32 devices in a mesh: cfg: 2 (over core), req: 16 (over z, y, x).
Axes of the slice: x: 2, y: 2, z: 4, core: 2. Of those that a mesh axis runs over, the one named last changes fastest.
Arguments:
- query_rows: bfloat16 [2, 8192, 2560], P('cfg', 'req'), may hold values from -32 to 32
- key_rows: bfloat16 [2, 8192, 2560], P('cfg', 'req'), may hold values from -6 to 6
- value_rows: bfloat16 [2, 8192, 2560], P('cfg', 'req'), may hold values from -600 to 600
- positions: int32 [3, 8192], P(None, 'req'), may hold values from 0 to 51
- latents: float32 [8192, 64], P('req', 'cfg'), may hold values from -6 to 6
- w_head: bfloat16 [2560, 64], replicated, may hold values from -0.125 to 0.125
- modulation: float32 [2, 2560], replicated, may hold values from -0.5 to 1
- guide_scale: float32 [1], replicated, may hold values from 4 to 6
- step_sizes: float32 [32], replicated, may hold values from -0.4 to -0.1
- lengths: int32 [32], replicated, may hold values from 1 to 512, 8192 in all
Outputs:
- next_latents: float32 [8192, 64], P('req', 'cfg')
The draws below stay inside these ranges and needn't reach their ends.
Inputs may be any that keep to these rules, and one draw needn't show every extreme that they name: Videos are laid end to end in the given order and their lengths sum to 8192.
All inputs are finite; a program needn't handle non-finite values.
Results may differ from the reference program's by a relative error of at most 0.0059.
Values may be sent and summed in bfloat16 or wider, within the bound.
No kernel may reach another device: no remote copies, remote signals or barrier semaphores. Data moves between devices by JAX's collectives and lax.ppermute only.
A program may use at most 128 MiB of HBM per device.

```python
import math
import jax
import jax.numpy as jnp
import numpy as np
from jax import lax

HD = 128
LATC = 64
LMAX = 512
ROWS = 512
HWD = 2560
TOKENS = 8192
NV = 32


def query_key_pair(key):
    full_shape = (2, TOKENS, HWD)
    query_seed = jax.random.fold_in(key, 101)
    key_seed = jax.random.fold_in(key, 102)
    query_draw = jnp.clip(jax.random.normal(query_seed, full_shape, jnp.float32), -6.0, 6.0)
    key_draw = jnp.clip(jax.random.normal(key_seed, full_shape, jnp.float32), -6.0, 6.0)
    return (query_draw, key_draw)


def draw_query_rows(key, part):
    return query_key_pair(key)[0].astype(jnp.bfloat16)


def draw_key_rows(key, part):
    return query_key_pair(key)[1].astype(jnp.bfloat16)


def draw_value_rows(key, part):
    base_seed = jax.random.fold_in(key, 201)
    row_seed = jax.random.fold_in(key, 202)
    column_seed = jax.random.fold_in(key, 203)
    base = jnp.clip(jax.random.normal(base_seed, (2, TOKENS, HWD), jnp.float32), -6.0, 6.0)
    row_scale = jnp.exp(jax.random.uniform(row_seed, (2, TOKENS, 1), jnp.float32, 0.0, math.log(10.0)))
    column_scale = jnp.exp(jax.random.uniform(column_seed, (1, 1, HWD), jnp.float32, 0.0, math.log(10.0)))
    return (base * row_scale * column_scale).astype(jnp.bfloat16)


def plant(entries, rng, smallest, largest):
    spot = [jax.random.randint(jax.random.fold_in(rng, axis), (), 0, length) for axis, length in enumerate(entries.shape)]
    widest = entries.shape.index(max(entries.shape))
    beside = spot[:widest] + [(spot[widest] + 1) % entries.shape[widest]] + spot[widest + 1:]
    return entries.at[tuple(spot)].set(smallest).at[tuple(beside)].set(largest)


def levels(own_key, shape, cuts, smallest, largest):
    level, own = 1.0, jax.random.fold_in(own_key, 6)
    for axis_at, blocks in cuts:
        draws = jnp.exp(jax.random.uniform(jax.random.fold_in(own, axis_at), (blocks,), jnp.float32, smallest / len(cuts), largest / len(cuts)))
        level = level * jnp.repeat(draws, shape[axis_at] // blocks).reshape([-1 if axis == axis_at else 1 for axis in range(len(shape))])
    return level


def length_profile(number_of, total, reach, skew):
    weights = [(1 << 20) // math.isqrt(rank ** skew) + 1 for rank in range(2, number_of + 1)]
    spare, given = total - reach - (number_of - 1), [1] * (number_of - 1)
    while spare > 0:
        candidates = [i for i in range(number_of - 1) if given[i] < reach]
        mass, left = sum([weights[i] for i in candidates]), spare
        for i in candidates:
            extra = min(reach - given[i], max(1, left * weights[i] // mass), spare)
            given[i] = given[i] + extra
            spare = spare - extra
    return np.array([reach] + given)


def ragged_sizes(own_key, count, total, most, skew):
    if count == 2:
        one = jax.random.randint(own_key, (), max(1, total - most), min(most, total - 1) + 1)
        return jnp.stack([one, total - one])
    sizes = jnp.asarray(length_profile(count, total, most, skew), jnp.int32)
    couples = (count - 1) // 2
    donor, receiver = sizes[1:1 + 2 * couples:2], sizes[2:2 + 2 * couples:2]
    margin = jnp.minimum(donor - 1, most - receiver)
    moved = jax.random.randint(jax.random.fold_in(own_key, 1), (couples,), 0, 1 << 20) % (margin + 1)
    sizes = sizes.at[1:1 + 2 * couples:2].set(donor - moved).at[2:2 + 2 * couples:2].set(receiver + moved)
    return sizes[jax.random.permutation(jax.random.fold_in(own_key, 2), count)]


def scatter_about(key, dims, scale, most, pieces=(), kind=jnp.bfloat16):
    array = jax.random.normal(key, dims, jnp.float32) * scale
    if len(pieces) > 0:
        array = levels(key, dims, pieces, -0.22, 0.18) * array
    return jnp.clip(array, min=-most, max=most).astype(kind)


def setup_inputs(seed: int = 0) -> dict:
    splits = jax.random.split(jax.random.key(seed), 11)
    query_rows = draw_query_rows(jax.random.fold_in(splits[10], 71), 0)
    key_rows = draw_key_rows(jax.random.fold_in(splits[10], 71), 0)
    value_rows = draw_value_rows(jax.random.fold_in(splits[10], 71), 0)
    positions = plant(jax.random.randint(splits[3], (3, TOKENS), 0, 52), jax.random.fold_in(splits[3], 1), 0, 51).astype(jnp.int32)
    latents = scatter_about(splits[4], (TOKENS, LATC), 1.0, 6.0, ((0, 16), (1, 2)), jnp.float32)
    w_head = scatter_about(splits[5], (HWD, LATC), HWD ** -0.5, 0.125)
    modulation = jnp.clip(jax.random.uniform(splits[6], (2, HWD), jnp.float32, -0.5, 1.0), -0.5, 1.0)
    guide_scale = jnp.clip(jax.random.uniform(splits[7], (1,), jnp.float32, 4.0, 6.0), 4.0, 6.0)
    step_sizes = jnp.clip(jax.random.uniform(splits[8], (NV,), jnp.float32, -0.4, -0.1), -0.4, -0.1)
    lengths = ragged_sizes(splits[9], NV, TOKENS, LMAX, 1).astype(jnp.int32)
    return dict(query_rows=query_rows, key_rows=key_rows, value_rows=value_rows, positions=positions, latents=latents, w_head=w_head, modulation=modulation, guide_scale=guide_scale, step_sizes=step_sizes, lengths=lengths)


masked_score = -1e+30
rope_theta = 10000.0

def angles(positions):
    pair_total = HD // 2
    side_pairs = HD // 6
    time_pairs = pair_total - 2 * side_pairs
    column = jnp.arange(pair_total, dtype=jnp.int32)
    in_time = column < time_pairs
    in_height = (column >= time_pairs) & (column < time_pairs + side_pairs)
    in_width = column >= time_pairs + side_pairs
    local_index = jnp.where(in_time, column, jnp.where(in_height, column - time_pairs, column - time_pairs - side_pairs))
    axis_pairs = jnp.where(in_time, time_pairs, side_pairs)
    frequency = jnp.exp(-(local_index.astype(jnp.float32) / axis_pairs.astype(jnp.float32)) * math.log(rope_theta))
    selector = jnp.stack([in_time, in_height, in_width]).astype(jnp.float32) * frequency[None, :]
    placed = positions.astype(jnp.float32)
    return placed[0][:, None] * selector[0][None, :] + placed[1][:, None] * selector[1][None, :] + placed[2][:, None] * selector[2][None, :]

def rotate(features, angle_table):
    row_total = features.shape[0]
    heads_here = features.shape[1] // HD
    paired = features.astype(jnp.float32).reshape(row_total, heads_here, HD // 2, 2)
    cosine = jnp.cos(angle_table)[:, None, :]
    sine_part = jnp.sin(angle_table)[:, None, :]
    real_part = paired[..., 0]
    imag_part = paired[..., 1]
    turned = jnp.stack([real_part * cosine - imag_part * sine_part, real_part * sine_part + imag_part * cosine], axis=-1)
    return turned.reshape(row_total, heads_here * HD).astype(jnp.bfloat16)

def video_of(global_rows, video_ends, row_count):
    inside = (global_rows >= 0) & (global_rows < row_count)
    counted = lax.optimization_barrier(jnp.sum((video_ends[None, :] <= global_rows[:, None]).astype(jnp.int32), axis=1))
    return jnp.where(inside, counted, -1).astype(jnp.int32)

def attend(query_block, window, first_row, video_ends, row_count):
    rows_here = query_block.shape[0]
    feature_count = query_block.shape[1]
    heads_here = feature_count // HD
    key_count = window.shape[0]
    query_video = video_of(first_row + jnp.arange(rows_here, dtype=jnp.int32), video_ends, row_count)
    key_first = first_row - (key_count - rows_here) // 2
    key_video = video_of(key_first + jnp.arange(key_count, dtype=jnp.int32), video_ends, row_count)
    same_video = query_video[:, None] == key_video[None, :]
    score_scale = 1.0 / math.sqrt(HD)
    query_heads = query_block.reshape(rows_here, heads_here, HD).transpose(1, 0, 2)
    key_heads = window[:, :feature_count].reshape(key_count, heads_here, HD).transpose(1, 0, 2)
    value_heads = window[:, feature_count:].reshape(key_count, heads_here, HD).transpose(1, 0, 2)

    def one_head(operands):
        query_head, key_head, value_head = operands
        scores = jnp.dot(query_head, key_head.T, preferred_element_type=jnp.float32) * score_scale
        scores = jnp.where(same_video, scores, masked_score)
        row_max = lax.optimization_barrier(jnp.max(scores, axis=1, keepdims=True))
        weights = jnp.exp(scores - row_max)
        denominator = lax.optimization_barrier(jnp.sum(weights, axis=1, keepdims=True))
        summed = jnp.dot(weights.astype(jnp.bfloat16), value_head, preferred_element_type=jnp.float32)
        return (summed / denominator).astype(jnp.bfloat16)
    outputs = lax.map(one_head, (query_heads, key_heads, value_heads))
    return outputs.transpose(1, 0, 2).reshape(rows_here, feature_count)

def project(attended, modulation, w_head):
    widened = attended.astype(jnp.float32)
    mean_square = lax.optimization_barrier(jnp.mean(widened * widened, axis=1, keepdims=True))
    normed = widened * lax.rsqrt(mean_square + 1e-06) * (1.0 + modulation[1][None, :]) + modulation[0][None, :]
    return jnp.dot(normed.astype(jnp.bfloat16), w_head, preferred_element_type=jnp.float32)

def step_rows(video_ids, step_sizes):
    video_count = step_sizes.shape[0]
    chosen = video_ids[:, None] == jnp.arange(video_count, dtype=jnp.int32)[None, :]
    return lax.optimization_barrier(jnp.sum(jnp.where(chosen, step_sizes[None, :], jnp.zeros_like(step_sizes)[None, :]), axis=1))

def reference(query_rows, key_rows, value_rows, positions, latents, w_head, modulation, guide_scale, step_sizes, lengths):
    row_count = TOKENS
    angle_table = angles(positions)
    video_ends = jnp.cumsum(lengths).astype(jnp.int32)
    margin_count = ROWS
    window_count = 3 * ROWS
    velocities = []
    for parity in range(2):
        query_rot = rotate(query_rows[parity], angle_table)
        key_rot = rotate(key_rows[parity], angle_table)
        joined = jnp.concatenate([key_rot, value_rows[parity]], axis=1)
        padded = jnp.pad(joined, ((margin_count, margin_count), (0, 0)))

        def one_block(block_index, query_rot=query_rot, padded=padded):
            first_row = (block_index * ROWS).astype(jnp.int32)
            query_block = lax.dynamic_slice_in_dim(query_rot, first_row, ROWS, 0)
            window = lax.dynamic_slice_in_dim(padded, first_row, window_count, 0)
            return attend(query_block, window, first_row, video_ends, row_count)
        attended = lax.map(one_block, jnp.arange(TOKENS // ROWS, dtype=jnp.int32)).reshape(TOKENS, HWD)
        velocities.append(project(attended, modulation, w_head))
    guided = velocities[1] + guide_scale[0] * (velocities[0] - velocities[1])
    video_ids = video_of(jnp.arange(TOKENS, dtype=jnp.int32), video_ends, row_count)
    return latents + step_rows(video_ids, step_sizes)[:, None] * guided
```

```python
import functools
import math

import jax
import jax.numpy as jnp
from jax import lax
from jax.experimental import pallas as pl
from jax.experimental.pallas import tpu as pltpu
from jax.sharding import PartitionSpec as P

HD = 128
TILE = 16
BLK = 128
rope_theta = 10000.0
NEG = -1e30
SCALE2 = math.log2(math.e) / math.sqrt(HD)
VMEM_LIMIT = 56 * 1024 * 1024

L_TILES, L_OWN_TILES, L_HEADS, L_FAR, L_OWN = 0, 1, 2, 3, 4
R_TILES, R_OWN_TILES, R_HEADS, R_FAR, R_OWN = 5, 6, 7, 8, 9


def angles(positions):
    pair_total = HD // 2
    side_pairs = HD // 6
    time_pairs = pair_total - 2 * side_pairs
    column = jnp.arange(HD, dtype=jnp.int32) // 2
    in_time = column < time_pairs
    in_height = (column >= time_pairs) & (column < time_pairs + side_pairs)
    in_width = column >= time_pairs + side_pairs
    local_index = jnp.where(
        in_time, column, jnp.where(in_height, column - time_pairs, column - time_pairs - side_pairs)
    )
    axis_pairs = jnp.where(in_time, time_pairs, side_pairs)
    frequency = jnp.exp(
        -(local_index.astype(jnp.float32) / axis_pairs.astype(jnp.float32)) * math.log(rope_theta)
    )
    selector = jnp.stack([in_time, in_height, in_width]).astype(jnp.float32) * frequency[None, :]
    placed = positions.astype(jnp.float32)
    return (
        placed[0][:, None] * selector[0][None, :]
        + placed[1][:, None] * selector[1][None, :]
        + placed[2][:, None] * selector[2][None, :]
    )


def boundary(at, row_count, ends, starts, heads):
    inside = (starts < at) & (ends > at)
    left = jnp.sum(jnp.where(inside, at - starts, 0))
    right = jnp.sum(jnp.where(inside, ends - at, 0))
    left_tiles = (left + TILE - 1) // TILE
    right_tiles = (right + TILE - 1) // TILE
    choice = jnp.arange(heads + 1, dtype=jnp.int32)
    load = jnp.maximum(left_tiles * choice, right_tiles * (heads - choice))
    best = jnp.argmin(load).astype(jnp.int32)
    return left, right, left_tiles, right_tiles, best


def dot_t(a, b):
    return lax.dot_general(a, b, (((1,), (1,)), ((), ())), preferred_element_type=jnp.float32)


def prep_kernel(scal, q_ref, k_ref, v_ref, cos_ref, sin_ref, qr_ref, kr_ref, xl_ref, xr_ref):
    h = pl.program_id(0)
    rows = q_ref.shape[0]
    even = lax.rem(lax.broadcasted_iota(jnp.int32, (rows, HD), 1), 2) == 0

    def turn(ref):
        x = ref[...].astype(jnp.float32)
        swapped = jnp.where(even, pltpu.roll(x, HD - 1, 1), pltpu.roll(x, 1, 1))
        return (x * cos_ref[...] + swapped * sin_ref[...]).astype(jnp.bfloat16)

    qr_ref[...] = turn(q_ref)
    kr_ref[...] = turn(k_ref)

    def send(out_ref, tiles, slot, first_row):
        def one(t, carry):
            at = pl.multiple_of(first_row + t * TILE, TILE)
            item = slot * tiles + t
            out_ref[item, 0:TILE] = qr_ref[pl.ds(at, TILE), :]
            out_ref[item, TILE : 2 * TILE] = kr_ref[pl.ds(at, TILE), :]
            out_ref[item, 2 * TILE : 3 * TILE] = v_ref[pl.ds(at, TILE), :]
            return carry

        lax.fori_loop(0, tiles, one, 0)

    @pl.when(h >= scal[L_HEADS])
    def _():
        send(xl_ref, scal[L_OWN_TILES], h - scal[L_HEADS], 0)

    @pl.when(h < scal[R_HEADS])
    def _():
        send(xr_ref, scal[R_OWN_TILES], h, rows - TILE * scal[R_OWN_TILES])


def attend_rows(q, k, v_ones, scores_of):
    s = scores_of(dot_t(q, k) * SCALE2)
    top = jnp.max(s, axis=1, keepdims=True)
    weight = jnp.exp2(s - top).astype(jnp.bfloat16)
    both = jnp.dot(weight, v_ones, preferred_element_type=jnp.float32)
    return (both[:, :HD] / both[:, HD:]).astype(jnp.bfloat16)


def with_total(z, sq, keep):
    added = z + pltpu.roll(z, HD // 2, 1)
    lane = lax.broadcasted_iota(jnp.int32, z.shape, 1)
    total = jnp.sum(sq, axis=1, keepdims=True)
    out = jnp.where(lane < HD // 2, added, jnp.where(lane == HD // 2, total, 0.0))
    return jnp.where(keep, out, 0.0)


def local_kernel(scal, q_ref, k_ref, v_ref, w_ref, qv_ref, kv_ref, out_ref, z_ref, sq_ref):
    h = pl.program_id(0)
    rows = q_ref.shape[0]

    @pl.when(h == 0)
    def _():
        z_ref[...] = jnp.zeros_like(z_ref)
        sq_ref[...] = jnp.zeros_like(sq_ref)

    k = k_ref[...]
    v_ones = jnp.concatenate([v_ref[...], jnp.ones((rows, HD), jnp.bfloat16)], axis=1)
    for j in range(rows // BLK):
        at = pl.ds(j * BLK, BLK)
        same = qv_ref[at, :] == kv_ref[...]
        o = attend_rows(q_ref[at, :], k, v_ones, lambda s: jnp.where(same, s, NEG))
        z_ref[at, :] += jnp.dot(o, w_ref[...], preferred_element_type=jnp.float32)
        wide = o.astype(jnp.float32)
        sq_ref[at, :] += wide * wide

    @pl.when(h == pl.num_programs(0) - 1)
    def _():
        row = lax.broadcasted_iota(jnp.int32, (rows, HD), 0)
        keep = (row >= scal[L_OWN]) & (row < rows - scal[R_OWN])
        out_ref[...] = with_total(z_ref[...], sq_ref[...], keep)


def straddle_kernel(
    scal, q_ref, k_ref, v_ref, xl_ref, xr_ref, w_ref, own_ref, toleft_ref, toright_ref, qs, ks, vs, zs, ss
):
    h = pl.program_id(0)
    rows = q_ref.shape[0]
    span = ks.shape[1]

    @pl.when(h == 0)
    def _():
        for side in range(2):
            qs[side] = jnp.zeros_like(qs[side])
            ks[side] = jnp.zeros_like(ks[side])
            vs[side, :, :HD] = jnp.zeros((span, HD), jnp.bfloat16)
            vs[side, :, HD:] = jnp.ones((span, HD), jnp.bfloat16)
            zs[side] = jnp.zeros_like(zs[side])
            ss[side] = jnp.zeros_like(ss[side])

    def work(side, x_ref, far_tiles, slot, own_at, far_at, left, right):
        qs[side, pl.ds(own_at, rows)] = q_ref[...]
        ks[side, pl.ds(own_at, rows)] = k_ref[...]
        vs[side, pl.ds(own_at, rows), :HD] = v_ref[...]

        def one(t, carry):
            at = pl.ds(pl.multiple_of(far_at + t * TILE, TILE), TILE)
            item = slot * far_tiles + t
            qs[side, at] = x_ref[item, 0:TILE]
            ks[side, at] = x_ref[item, TILE : 2 * TILE]
            vs[side, at, :HD] = x_ref[item, 2 * TILE : 3 * TILE]
            return carry

        lax.fori_loop(0, far_tiles, one, 0)
        left_tiles = (left + TILE - 1) // TILE
        right_tiles = (right + TILE - 1) // TILE
        first = rows - TILE * left_tiles
        blocks = (TILE * (left_tiles + right_tiles) + BLK - 1) // BLK
        for n in range(1, rows // BLK + 2):

            @pl.when(blocks == n)
            def _(n=n):
                width = n * BLK
                whole = pl.ds(pl.multiple_of(first, TILE), width)
                k = ks[side, whole]
                v_ones = vs[side, whole]
                place = first + lax.broadcasted_iota(jnp.int32, (1, width), 1)
                valid = (place >= rows - left) & (place < rows + right)
                bias = jnp.where(valid, 0.0, NEG)
                for j in range(n):
                    at = pl.ds(pl.multiple_of(first + j * BLK, TILE), BLK)
                    o = attend_rows(qs[side, at], k, v_ones, lambda s: s + bias)
                    zs[side, at] += jnp.dot(o, w_ref[...], preferred_element_type=jnp.float32)
                    wide = o.astype(jnp.float32)
                    ss[side, at] += wide * wide

    @pl.when((h < scal[L_HEADS]) & (scal[L_TILES] > 0))
    def _():
        work(0, xl_ref, scal[L_TILES], h, rows, rows - TILE * scal[L_TILES], scal[L_FAR], scal[L_OWN])

    @pl.when((h >= scal[R_HEADS]) & (scal[R_TILES] > 0))
    def _():
        work(1, xr_ref, scal[R_TILES], h - scal[R_HEADS], 0, rows, scal[R_OWN], scal[R_FAR])

    @pl.when(h == pl.num_programs(0) - 1)
    def _():
        row = lax.broadcasted_iota(jnp.int32, (rows, HD), 0)
        low, high = slice(0, rows), slice(rows, 2 * rows)
        own_ref[...] = with_total(zs[0, high], ss[0, high], row < scal[L_OWN]) + with_total(
            zs[1, low], ss[1, low], row >= rows - scal[R_OWN]
        )
        toleft_ref[...] = with_total(zs[0, low], ss[0, low], row >= rows - scal[L_FAR])
        toright_ref[...] = with_total(zs[1, high], ss[1, high], row < scal[R_FAR])


def step_rows(video_ids, step_sizes):
    chosen = video_ids[:, None] == jnp.arange(step_sizes.shape[0], dtype=jnp.int32)[None, :]
    return jnp.sum(jnp.where(chosen, step_sizes[None, :], 0.0), axis=1)


def per_device(
    query_rows, key_rows, value_rows, positions, latents, w_head, modulation,
    guide_scale, step_sizes, lengths,
):
    rows, features = query_rows.shape[1], query_rows.shape[2]
    heads = features // HD
    count = lax.axis_size("req")
    row_count = rows * count
    here = lax.axis_index("req")
    first_row = here * rows
    cap = max(
        min(max(a * n, b * (heads - n)) for n in range(heads + 1))
        for a in range(1, rows // TILE + 1)
        for b in [rows // TILE + 1 - a]
    )
    cap = -(-cap // 2) * 2

    angle = angles(positions)
    odd = (jnp.arange(HD, dtype=jnp.int32) % 2).astype(jnp.float32)
    cosine = jnp.cos(angle)
    sine = jnp.sin(angle) * (2.0 * odd - 1.0)[None, :]

    ends = jnp.cumsum(lengths)
    starts = ends - lengths
    ll, lr, llt, lrt, ln = boundary(first_row, row_count, ends, starts, heads)
    rl, rr, rlt, rrt, rn = boundary(first_row + rows, row_count, ends, starts, heads)
    scalars = jnp.stack([llt, lrt, ln, ll, lr, rrt, rlt, rn, rr, rl]).astype(jnp.int32)

    q, k, v = query_rows[0], key_rows[0], value_rows[0]
    head_block = pl.BlockSpec((rows, HD), lambda h, s: (0, h))
    table = pl.BlockSpec((rows, HD), lambda h, s: (0, 0))
    w_block = pl.BlockSpec((HD, HD), lambda h, s: (h, 0))
    box = pl.BlockSpec((cap, 3 * TILE, HD), lambda h, s: (0, 0, 0))
    box_shape = jax.ShapeDtypeStruct((cap, 3 * TILE, HD), jnp.bfloat16)
    params = pltpu.CompilerParams(
        dimension_semantics=("arbitrary",), vmem_limit_bytes=VMEM_LIMIT
    )
    q_rot, k_rot, box_left, box_right = pl.pallas_call(
        prep_kernel,
        out_shape=(
            jax.ShapeDtypeStruct(q.shape, q.dtype), jax.ShapeDtypeStruct(k.shape, k.dtype),
            box_shape, box_shape,
        ),
        grid_spec=pltpu.PrefetchScalarGridSpec(
            num_scalar_prefetch=1, grid=(heads,),
            in_specs=[head_block] * 3 + [table] * 2,
            out_specs=[head_block] * 2 + [box] * 2,
        ),
        compiler_params=params,
        name="rotate_and_pack",
    )(scalars, q, k, v, cosine, sine)

    to_right = [(i, i + 1) for i in range(count - 1)]
    to_left = [(i + 1, i) for i in range(count - 1)]
    from_left = lax.ppermute(box_right, "req", to_right)
    from_right = lax.ppermute(box_left, "req", to_left)

    scaled = (1.0 + modulation[1])[:, None] * w_head.astype(jnp.float32)
    high = lax.reduce_precision(scaled, 8, 7)
    w_both = jnp.concatenate([high, scaled - high], axis=1).astype(jnp.bfloat16)
    shift = jnp.dot(
        modulation[0][None, :], w_head.astype(jnp.float32), precision=lax.Precision.HIGHEST
    )
    own_rows = first_row + jnp.arange(rows, dtype=jnp.int32)
    video = jnp.sum((ends[None, :] <= own_rows[:, None]).astype(jnp.int32), axis=1)

    local = pl.pallas_call(
        local_kernel,
        out_shape=jax.ShapeDtypeStruct((rows, HD), jnp.float32),
        grid_spec=pltpu.PrefetchScalarGridSpec(
            num_scalar_prefetch=1, grid=(heads,),
            in_specs=[head_block] * 3 + [
                w_block,
                pl.BlockSpec((rows, 1), lambda h, s: (0, 0)),
                pl.BlockSpec((1, rows), lambda h, s: (0, 0)),
            ],
            out_specs=table,
            scratch_shapes=[pltpu.VMEM((rows, HD), jnp.float32)] * 2,
        ),
        compiler_params=params,
        cost_estimate=pl.CostEstimate(
            flops=heads * rows * rows * HD * 4, bytes_accessed=3 * rows * features * 2,
            transcendentals=heads * rows * rows,
        ),
        name="inner_videos",
    )(scalars, q_rot, k_rot, v, w_both, video[:, None], video[None, :])

    span = 2 * rows + BLK
    own, ret_left, ret_right = pl.pallas_call(
        straddle_kernel,
        out_shape=(jax.ShapeDtypeStruct((rows, HD), jnp.float32),) * 3,
        grid_spec=pltpu.PrefetchScalarGridSpec(
            num_scalar_prefetch=1, grid=(heads,),
            in_specs=[head_block] * 3 + [box] * 2 + [w_block],
            out_specs=[table] * 3,
            scratch_shapes=[
                pltpu.VMEM((2, span, HD), jnp.bfloat16),
                pltpu.VMEM((2, span, HD), jnp.bfloat16),
                pltpu.VMEM((2, span, 2 * HD), jnp.bfloat16),
                pltpu.VMEM((2, span, HD), jnp.float32),
                pltpu.VMEM((2, span, HD), jnp.float32),
            ],
        ),
        compiler_params=params,
        name="videos_across",
    )(scalars, q_rot, k_rot, v, from_left, from_right, w_both)

    back_right = lax.ppermute(ret_left, "req", to_left)
    back_left = lax.ppermute(ret_right, "req", to_right)
    total = local + own + back_right + back_left
    half = HD // 2
    scale = lax.rsqrt(total[:, half : half + 1] / features + 1e-06)
    velocity = total[:, :half] * scale + shift

    parity = lax.axis_index("cfg")
    partner = lax.ppermute(velocity, "cfg", [(0, 1), (1, 0)])
    conditional = jnp.where(parity == 0, velocity, partner)
    unconditional = jnp.where(parity == 0, partner, velocity)
    guided = unconditional + guide_scale[0] * (conditional - unconditional)
    width = latents.shape[1]
    mine = lax.dynamic_slice_in_dim(guided, parity * width, width, 1)
    return latents + step_rows(video, step_sizes)[:, None] * mine


def solution(mesh):
    in_specs = (
        P("cfg", "req", None), P("cfg", "req", None), P("cfg", "req", None),
        P(None, "req"), P("req", "cfg"), P(), P(), P(), P(), P(),
    )
    return jax.shard_map(
        per_device, mesh=mesh, in_specs=in_specs, out_specs=P("req", "cfg"), check_vma=False
    )
```

```python
import functools
import math

import jax
import jax.numpy as jnp
from jax import lax
from jax.experimental import pallas as pl
from jax.experimental.pallas import tpu as pltpu
from jax.sharding import PartitionSpec as P

HD = 128
TILE = 16
BLK = 128
CHUNK = 40
CHUNKS = 4
MORE = (48, 32)
rope_theta = 10000.0
NEG = -1e30
SCALE2 = math.log2(math.e) / math.sqrt(HD)
VMEM_LIMIT = 48 * 1024 * 1024

LB, RB, LROWS, RROWS, HEAD0, KEEP, EARLY, SOURCE = range(8)
SIDE = 16
PASS, DIRECT = 32, 36
ROW, TILES, FIRST, HEADS = range(4)
MOST = 40
SCALARS = 48


def sizes(rows, heads):
    tiles = rows // TILE
    cap = max(
        min(max(a * n, (tiles + 1 - a) * (heads - n)) for n in range(heads + 1))
        for a in range(1, tiles + 1)
    )
    padded = -(-cap // TILE) * TILE
    return cap, padded, 2 * padded


def angles(positions):
    pair_total = HD // 2
    side_pairs = HD // 6
    time_pairs = pair_total - 2 * side_pairs
    column = jnp.arange(HD, dtype=jnp.int32) // 2
    in_time = column < time_pairs
    in_height = (column >= time_pairs) & (column < time_pairs + side_pairs)
    in_width = column >= time_pairs + side_pairs
    local_index = jnp.where(
        in_time, column, jnp.where(in_height, column - time_pairs, column - time_pairs - side_pairs)
    )
    axis_pairs = jnp.where(in_time, time_pairs, side_pairs)
    frequency = jnp.exp(
        -(local_index.astype(jnp.float32) / axis_pairs.astype(jnp.float32)) * math.log(rope_theta)
    )
    selector = jnp.stack([in_time, in_height, in_width]).astype(jnp.float32) * frequency[None, :]
    placed = positions.astype(jnp.float32)
    return (
        placed[0][:, None] * selector[0][None, :]
        + placed[1][:, None] * selector[1][None, :]
        + placed[2][:, None] * selector[2][None, :]
    )


def plan_kernel(rows, heads, count, lengths, here_ref, out, ls, rs, split):
    cap, padded, _ = sizes(rows, heads)
    here = here_ref[0]

    def clear(b, carry):
        ls[b] = 0
        rs[b] = 0
        return carry

    lax.fori_loop(0, count + 3, clear, 0)

    def one_video(v, start):
        end = start + lengths[v]
        b = lax.div(end - 1, rows)
        at = b * rows

        @pl.when(start < at)
        def _():
            ls[b] = at - start
            rs[b] = end - at

        return end

    lax.fori_loop(0, lengths.shape[0], one_video, 0)
    budget = 3.0 * lax.broadcasted_iota(jnp.int32, (8, 128), 1).astype(jnp.float32)
    passed_on = jnp.where(
        budget >= cap + padded, jnp.float32(padded), jnp.float32(CHUNK * CHUNKS)
    )
    split[...] = jnp.zeros_like(split)

    def tiles_of(x):
        return lax.shift_right_logical(x + TILE - 1, 4)

    def one_boundary(b, carry):
        load, ok = carry
        lt = tiles_of(ls[b]).astype(jnp.float32)
        rt = tiles_of(rs[b]).astype(jnp.float32)
        direct = lax.rem(b, 2).astype(jnp.float32)
        limit = passed_on + direct * 1e6
        room = jnp.minimum(budget - load, limit)
        n = jnp.minimum(jnp.floor((room + 0.5) / jnp.maximum(lt, 1.0)), float(heads))
        n = jnp.where(lt > 0.0, n, 0.0)
        back = rt * (heads - n)
        good = (room >= 0.0) & (back <= limit)
        split[pl.ds(pl.multiple_of(b * 8, 8), 8)] = n
        return back, jnp.where(good, ok, 0.0)

    zero = jnp.zeros((8, 128), jnp.float32)
    load, ok = lax.fori_loop(1, count, one_boundary, (zero, zero + 1.0))
    ok = jnp.where(load <= budget, ok, 0.0)
    most = jnp.min(jnp.where(ok > 0.0, budget, 1e9))
    out[MOST] = most.astype(jnp.int32)

    def head_split(b):
        n = split[pl.ds(pl.multiple_of(b * 8, 8), 8)]
        return jnp.max(jnp.where(budget == most, n, 0.0)).astype(jnp.int32)

    even = lax.rem(here, 2) == 0
    beyond = jnp.where(even, here + 2, here - 1)
    n_left, n_right, n_beyond = head_split(here), head_split(here + 1), head_split(beyond)
    partner_passes = jnp.where(
        even,
        tiles_of(ls[beyond]) * n_beyond,
        tiles_of(rs[beyond]) * (heads - n_beyond),
    )
    direct_from = padded + partner_passes
    for side, b, n in ((0, here, n_left), (1, here + 1, n_right)):
        at = SIDE * side
        lt, rt = tiles_of(ls[b]), tiles_of(rs[b])
        direct = jnp.logical_not(even) if side == 0 else even
        out[at + LB], out[at + RB] = lt, rt
        out[at + LROWS], out[at + RROWS] = ls[b], rs[b]
        keep = n if side == 0 else jnp.where(lt > 0, heads - n, 0)
        far = lt if side == 0 else rt
        out[at + HEAD0] = 0 if side == 0 else n
        out[at + KEEP] = keep
        soon = lax.div(CHUNK * CHUNKS // 2, jnp.maximum(far, 1))
        out[at + EARLY] = jnp.where(direct, 0, jnp.minimum(keep, soon))
        out[at + SOURCE] = jnp.where(direct, direct_from, 0)
        to = jnp.where(direct, DIRECT, PASS)
        out[to + ROW] = 0 if side == 0 else rows - TILE * lt
        out[to + TILES] = rt if side == 0 else lt
        out[to + FIRST] = n if side == 0 else 0
        out[to + HEADS] = jnp.where(lt > 0, heads - n, 0) if side == 0 else n


def in_groups(low, high, step):
    groups = lax.div(jnp.maximum(high - low, 0), 4)

    def four(g, carry):
        step(low + 4 * g, 4)
        return carry

    def one(t, carry):
        step(t, 1)
        return carry

    lax.fori_loop(0, groups, four, 0)
    lax.fori_loop(low + 4 * groups, high, one, 0)


def lanes_of(h):
    return pl.ds(pl.multiple_of(h * HD, HD), HD)


def rows_of(t, group):
    return pl.ds(pl.multiple_of(t * TILE, TILE), group * TILE)


def turn(x, cosine, sine):
    wide = x.astype(jnp.float32)
    even = lax.rem(lax.broadcasted_iota(jnp.int32, wide.shape, 1), 2) == 0
    swapped = jnp.where(even, pltpu.roll(wide, HD - 1, 1), pltpu.roll(wide, 1, 1))
    return (wide * cosine + swapped * sine).astype(jnp.bfloat16)


def pack(scal, what, base, low, high, box, get):
    first_tile = lax.shift_right_logical(scal[what + ROW], 4)
    tiles = scal[what + TILES]

    def one_head(s, carry):
        start = base + s * tiles
        begin = jnp.clip(low - start, 0, tiles)
        end = jnp.clip(high - start, 0, tiles)
        lanes = lanes_of(scal[what + FIRST] + s)

        def step(t, group):
            q, k, v = get(rows_of(first_tile + t, group), lanes)
            item = pl.ds(start + t - low, group)
            box[item, 0:TILE] = q.reshape(group, TILE, HD)
            box[item, TILE : 2 * TILE] = k.reshape(group, TILE, HD)
            box[item, 2 * TILE : 3 * TILE] = v.reshape(group, TILE, HD)

        in_groups(begin, end, step)
        return carry

    lax.fori_loop(0, scal[what + HEADS], one_head, 0)


def first_kernel(scal, q_ref, k_ref, v_ref, cos_ref, sin_ref, *rest):
    outs, (box, sems) = rest[:CHUNKS], rest[CHUNKS:]

    def get(rows, lanes):
        cosine, sine = cos_ref[rows, :], sin_ref[rows, :]
        return (
            turn(q_ref[rows, lanes], cosine, sine),
            turn(k_ref[rows, lanes], cosine, sine),
            v_ref[rows, lanes],
        )

    limit = CHUNK * CHUNKS
    pack(scal, PASS, 0, 0, limit, box, get)
    pack(scal, DIRECT, scal[PASS + TILES] * scal[PASS + HEADS], 0, limit, box, get)
    copies = [
        pltpu.make_async_copy(box.at[pl.ds(i * CHUNK, CHUNK)], outs[i], sems.at[i])
        for i in range(CHUNKS)
    ]
    for copy in copies:
        copy.start()
    for copy in copies:
        copy.wait()


def second_kernel(scal, q_ref, k_ref, v_ref, cos_ref, sin_ref, qr_ref, kr_ref, *rest):
    outs, (box, sems) = rest[:-2], rest[-2:]
    heads = q_ref.shape[1] // HD
    cosine, sine = cos_ref[...], sin_ref[...]
    for h in range(heads):
        lanes = slice(h * HD, (h + 1) * HD)
        qr_ref[:, lanes] = turn(q_ref[:, lanes], cosine, sine)
        kr_ref[:, lanes] = turn(k_ref[:, lanes], cosine, sine)

    def get(rows, lanes):
        return qr_ref[rows, lanes], kr_ref[rows, lanes], v_ref[rows, lanes]

    low = CHUNK * CHUNKS
    high = low + box.shape[0]
    pack(scal, PASS, 0, low, high, box, get)
    pack(scal, DIRECT, scal[PASS + TILES] * scal[PASS + HEADS], low, high, box, get)
    at = 0
    copies = []
    for i, out in enumerate(outs):
        copies.append(pltpu.make_async_copy(box.at[pl.ds(at, out.shape[0])], out, sems.at[i]))
        at += out.shape[0]
    for copy in copies:
        copy.start()
    for copy in copies:
        copy.wait()


def dot_t(a, b):
    return lax.dot_general(a, b, (((1,), (1,)), ((), ())), preferred_element_type=jnp.float32)


def attend_rows(q, k, v_ones, masked):
    s = masked(dot_t(q, k))
    top = jnp.max(s, axis=1, keepdims=True)
    weight = jnp.exp2(s * SCALE2 - top * SCALE2).astype(jnp.bfloat16)
    both = jnp.dot(weight, v_ones, preferred_element_type=jnp.float32)
    return (both[:, :HD] / both[:, HD:]).astype(jnp.bfloat16)


def projected(o_ref, w_ref):
    z = jnp.dot(o_ref[...], w_ref[...], preferred_element_type=jnp.float32)
    z = z + pltpu.roll(z, HD // 2, 1)
    lane = lax.broadcasted_iota(jnp.int32, z.shape, 1)
    squares = jnp.zeros(z.shape, jnp.float32)
    for h in range(o_ref.shape[1] // HD):
        wide = o_ref[:, h * HD : (h + 1) * HD].astype(jnp.float32)
        squares = squares + wide * wide
    total = jnp.sum(squares, axis=1, keepdims=True)
    return jnp.where(lane < HD // 2, z, jnp.where(lane == HD // 2, total, 0.0))


def inner_kernel(scal, q_ref, k_ref, v_ref, w_ref, qv_ref, kv_ref, out_ref, o_ref):
    g = pl.program_id(0)
    rows, width = q_ref.shape
    first, last = scal[RROWS], rows - scal[SIDE + LROWS]

    @pl.when(g == 0)
    def _():
        o_ref[...] = jnp.zeros_like(o_ref)

    for j in range(rows // BLK):

        @pl.when((first < (j + 1) * BLK) & (last > j * BLK))
        def _(j=j):
            at = pl.ds(j * BLK, BLK)
            same = qv_ref[at, :] == kv_ref[...]
            for i in range(width // HD):
                lanes = slice(i * HD, (i + 1) * HD)
                ones = jnp.ones((rows, HD), jnp.bfloat16)
                v_ones = jnp.concatenate([v_ref[:, lanes], ones], axis=1)
                o_ref[at, pl.ds(pl.multiple_of(g * width + i * HD, HD), HD)] = attend_rows(
                    q_ref[at, lanes], k_ref[:, lanes], v_ones, lambda s: jnp.where(same, s, NEG)
                )

    @pl.when(g == pl.num_programs(0) - 1)
    def _():
        out_ref[...] = projected(o_ref, w_ref)


def across(scal, side, low, high, q_ref, k_ref, v_ref, items, w_ref, qs, ks, vs, o_ref, zz):
    rows = q_ref.shape[0]
    at = SIDE * side
    left, right = scal[at + LB], scal[at + RB]
    left_rows, right_rows = scal[at + LROWS], scal[at + RROWS]
    far = left if side == 0 else right
    lead = left * TILE - left_rows
    end = left * TILE + right_rows
    blocks = jnp.minimum(lax.div((left + right) * TILE + BLK - 1, BLK), rows // BLK)
    o_ref[...] = jnp.zeros_like(o_ref)

    def own_step(t, group):
        source = t if side == 0 else rows // TILE - left + t
        to = rows_of(left + t if side == 0 else t, group)
        return rows_of(source, group), to

    def one_head(n, s, carry):
        lanes = lanes_of(scal[at + HEAD0] + s)

        def own(t, group):
            source, to = own_step(t, group)
            qs[to, :] = q_ref[source, lanes]
            ks[to, :] = k_ref[source, lanes]
            vs[to, :HD] = v_ref[source, lanes]

        def foreign(t, group):
            item = pl.ds(scal[at + SOURCE] + s * far + t, group)
            to = rows_of(t if side == 0 else left + t, group)
            qs[to, :] = items[item, 0:TILE].reshape(group * TILE, HD)
            ks[to, :] = items[item, TILE : 2 * TILE].reshape(group * TILE, HD)
            vs[to, :HD] = items[item, 2 * TILE : 3 * TILE].reshape(group * TILE, HD)

        in_groups(0, right if side == 0 else left, own)
        in_groups(0, far, foreign)
        width = n * BLK
        if width == rows:

            @pl.when((left + right) * TILE > rows)
            def _():
                row = lax.broadcasted_iota(jnp.int32, (TILE, HD), 0)
                for ref in (qs, ks, vs):
                    first, last = ref[0:TILE, :HD], ref[rows : rows + TILE, :HD]
                    ref[0:TILE, :HD] = jnp.where(row < lead, last, first)

        place = lax.broadcasted_iota(jnp.int32, (1, width), 1)
        valid = ((place >= lead) & (place < end)) | (place + rows < end)
        bias = jnp.where(valid, 0.0, NEG)
        k, v_ones = ks[0:width, :], vs[0:width, :]
        for j in range(n):
            mine = slice(j * BLK, (j + 1) * BLK)
            o_ref[mine, lanes] = attend_rows(qs[mine, :], k, v_ones, lambda x: x + bias)
        return carry

    for n in range(1, rows // BLK + 1):

        @pl.when(blocks == n)
        def _(n=n):
            lax.fori_loop(low, high, functools.partial(one_head, n), 0)

    z = projected(o_ref, w_ref)
    zz[0:rows, :] = z
    zz[rows : 2 * rows, :] = z
    return zz[pl.ds(pl.multiple_of(left * TILE, TILE), rows), :]


def clear_rows(qs, ks, vs):
    qs[...] = jnp.zeros_like(qs)
    ks[...] = jnp.zeros_like(ks)
    vs[:, :HD] = jnp.zeros((vs.shape[0], HD), vs.dtype)
    vs[:, HD:] = jnp.ones((vs.shape[0], HD), vs.dtype)


def early_kernel(scal, q_ref, k_ref, v_ref, w_ref, *rest):
    half = CHUNKS // 2
    boxes, out_ref, items, sems, scratch = rest[:half], rest[half], rest[half + 1], rest[half + 2], rest[half + 3 :]
    copies = [
        pltpu.make_async_copy(box, items.at[pl.ds(i * CHUNK, CHUNK)], sems.at[i])
        for i, box in enumerate(boxes)
    ]
    for copy in copies:
        copy.start()
    clear_rows(*scratch[:3])
    for copy in copies:
        copy.wait()
    for side in range(2):
        out_ref[side] = across(
            scal, side, 0, scal[SIDE * side + EARLY], q_ref, k_ref, v_ref, items, w_ref, *scratch
        )


def late_kernel(places, scal, q_ref, k_ref, v_ref, w_ref, early_ref, inner_ref, *rest):
    boxes, rest = rest[: len(places)], rest[len(places) :]
    own_ref, left_ref, right_ref, items, sems, *scratch = rest
    rows = q_ref.shape[0]
    copies = [
        pltpu.make_async_copy(box, items.at[pl.ds(at, box.shape[0])], sems.at[i])
        for i, (at, box) in enumerate(zip(places, boxes))
    ]
    for copy in copies:
        copy.start()
    clear_rows(*scratch[:3])
    for copy in copies:
        copy.wait()
    row = lax.broadcasted_iota(jnp.int32, (rows, HD), 0)
    own = inner_ref[...]
    for side, back_ref in ((0, left_ref), (1, right_ref)):
        at = SIDE * side
        z = early_ref[side] + across(
            scal, side, scal[at + EARLY], scal[at + KEEP],
            q_ref, k_ref, v_ref, items, w_ref, *scratch,
        )
        of_left, of_right = row >= rows - scal[at + LROWS], row < scal[at + RROWS]
        own = jnp.where(of_right if side == 0 else of_left, z, own)
        back = jnp.where(of_left if side == 0 else of_right, z, 0.0)
        high = back.astype(jnp.bfloat16)
        low = (back - high.astype(jnp.float32)).astype(jnp.bfloat16).astype(jnp.float32)
        lane = lax.broadcasted_iota(jnp.int32, (rows, HD), 1)
        both = jnp.where(lane == HD // 2 + 1, pltpu.roll(low, 1, 1), high.astype(jnp.float32))
        back_ref[...] = both.astype(jnp.bfloat16)
    own_ref[...] = own


def step_rows(video_ids, step_sizes):
    chosen = video_ids[:, None] == jnp.arange(step_sizes.shape[0], dtype=jnp.int32)[None, :]
    return jnp.sum(jnp.where(chosen, step_sizes[None, :], 0.0), axis=1)


def call(kernel, name, scalars, operands, in_specs, outs, out_specs, scratch, cost=None, grid=()):
    return pl.pallas_call(
        kernel,
        out_shape=outs,
        grid_spec=pltpu.PrefetchScalarGridSpec(
            num_scalar_prefetch=1, grid=grid, in_specs=in_specs, out_specs=out_specs,
            scratch_shapes=scratch,
        ),
        compiler_params=pltpu.CompilerParams(vmem_limit_bytes=VMEM_LIMIT),
        cost_estimate=cost,
        name=name,
    )(scalars, *operands)


def per_device(
    query_rows, key_rows, value_rows, positions, latents, w_head, modulation,
    guide_scale, step_sizes, lengths,
):
    rows, features = query_rows.shape[1], query_rows.shape[2]
    heads = features // HD
    count = lax.axis_size("req")
    here = lax.axis_index("req")
    first_row = here * rows
    _, padded, room = sizes(rows, heads)
    early_items = CHUNK * CHUNKS
    last = room - early_items - sum(MORE)
    late_sizes = (*MORE, last)

    angle = angles(positions)
    odd = (jnp.arange(HD, dtype=jnp.int32) % 2).astype(jnp.float32)
    cosine = jnp.cos(angle)
    sine = jnp.sin(angle) * (2.0 * odd - 1.0)[None, :]

    smem = pl.BlockSpec(memory_space=pltpu.SMEM)
    vmem = pl.BlockSpec(memory_space=pltpu.VMEM)
    hbm = pl.BlockSpec(memory_space=pl.ANY)
    scalars = pl.pallas_call(
        functools.partial(plan_kernel, rows, heads, count),
        out_shape=jax.ShapeDtypeStruct((SCALARS,), jnp.int32),
        in_specs=[smem, smem],
        out_specs=smem,
        scratch_shapes=[
            pltpu.SMEM((count + 3,), jnp.int32),
            pltpu.SMEM((count + 3,), jnp.int32),
            pltpu.VMEM(((count + 3) * 8, 128), jnp.float32),
        ],
        name="plan",
    )(lengths, here.astype(jnp.int32)[None])

    q, k, v = query_rows[0], key_rows[0], value_rows[0]

    def box(items):
        return jax.ShapeDtypeStruct((items, 3 * TILE, HD), jnp.bfloat16)

    def box_scratch(items):
        return pltpu.VMEM((items, 3 * TILE, HD), jnp.bfloat16)

    first = call(
        first_kernel, "pack_first", scalars, (q, k, v, cosine, sine), [vmem] * 5,
        (box(CHUNK),) * CHUNKS, (hbm,) * CHUNKS,
        [box_scratch(early_items), pltpu.SemaphoreType.DMA((CHUNKS,))],
    )
    pairs = [(i, i ^ 1) for i in range(count)]
    onward = [(i, i + 2) for i in range(0, count - 2, 2)] + [(i + 2, i) for i in range(1, count - 2, 2)]
    got = [lax.ppermute(x, "req", pairs) for x in first]
    passed = [lax.ppermute(x, "req", onward) for x in got]

    q_rot, k_rot, *second = call(
        second_kernel, "turn_and_pack_rest", scalars, (q, k, v, cosine, sine), [vmem] * 5,
        (jax.ShapeDtypeStruct(q.shape, q.dtype), jax.ShapeDtypeStruct(k.shape, k.dtype),
         *[box(n) for n in late_sizes]),
        (vmem, vmem, *[hbm] * 3),
        [box_scratch(sum(late_sizes)), pltpu.SemaphoreType.DMA((3,))],
        cost=pl.CostEstimate(flops=0, bytes_accessed=40_000_000, transcendentals=0),
    )
    got.append(lax.ppermute(second[0], "req", pairs))

    scaled = (1.0 + modulation[1])[:, None] * w_head.astype(jnp.float32)
    high = lax.reduce_precision(scaled, 8, 7)
    w_both = jnp.concatenate([high, scaled - high], axis=1).astype(jnp.bfloat16)
    shift = jnp.dot(
        modulation[0][None, :], w_head.astype(jnp.float32), precision=lax.Precision.HIGHEST
    )
    own_rows = first_row + jnp.arange(rows, dtype=jnp.int32)
    video = jnp.sum((jnp.cumsum(lengths)[None, :] <= own_rows[:, None]).astype(jnp.int32), axis=1)
    steps = step_rows(video, step_sizes)

    group = next(n for n in (5, 4, 3, 2, 1) if heads % n == 0)
    head_block = pl.BlockSpec((rows, group * HD), lambda g, s: (0, g))
    result = jax.ShapeDtypeStruct((rows, HD), jnp.float32)
    inner = call(
        inner_kernel, "inner_videos", scalars,
        (q_rot, k_rot, v, w_both, video[:, None], video[None, :]),
        [head_block] * 3 + [vmem] * 3, result, vmem,
        [pltpu.VMEM((rows, features), jnp.bfloat16)], grid=(heads // group,),
        cost=pl.CostEstimate(
            flops=heads * rows * rows * HD * 4, bytes_accessed=60_000_000,
            transcendentals=heads * rows * rows,
        ),
    )

    work = [
        pltpu.VMEM((rows + TILE, HD), jnp.bfloat16),
        pltpu.VMEM((rows + TILE, HD), jnp.bfloat16),
        pltpu.VMEM((rows + TILE, 2 * HD), jnp.bfloat16),
        pltpu.VMEM((rows, features), jnp.bfloat16),
        pltpu.VMEM((2 * rows, HD), jnp.float32),
    ]
    half = CHUNKS // 2
    early = call(
        early_kernel, "videos_across_early", scalars, (q_rot, k_rot, v, w_both, *passed[:half]),
        [vmem] * 4 + [hbm] * half,
        jax.ShapeDtypeStruct((2, rows, HD), jnp.float32), vmem,
        [box_scratch(half * CHUNK), pltpu.SemaphoreType.DMA((half,)), *work],
    )

    most = scalars[MOST]
    nothing = lambda x: jnp.zeros_like(x)
    extra = lax.cond(
        most > early_items + MORE[0],
        lambda x: lax.ppermute(x, "req", pairs), nothing, second[1],
    )
    rest, passed_rest = lax.cond(
        most > early_items + sum(MORE),
        lambda x, y: (lax.ppermute(x, "req", pairs), lax.ppermute(y, "req", onward)),
        lambda x, y: (nothing(x), nothing(y)),
        second[2], got[-1][: padded - early_items],
    )
    boxes = [*passed, passed_rest, *got, extra, rest]
    places = [0]
    for x in boxes[:-1]:
        places.append(places[-1] + x.shape[0])
    own, to_left, to_right = call(
        functools.partial(late_kernel, tuple(places)), "videos_across", scalars,
        (q_rot, k_rot, v, w_both, early, inner, *boxes),
        [vmem] * 6 + [hbm] * len(boxes),
        (result, *[jax.ShapeDtypeStruct((rows, HD), jnp.bfloat16)] * 2), (vmem,) * 3,
        [box_scratch(padded + room), pltpu.SemaphoreType.DMA((len(boxes),)), *work],
    )

    back_right = lax.ppermute(to_left, "req", [(i + 1, i) for i in range(count - 1)])
    back_left = lax.ppermute(to_right, "req", [(i, i + 1) for i in range(count - 1)])
    total = own + back_right.astype(jnp.float32) + back_left.astype(jnp.float32)
    half = HD // 2
    squares = total[:, half : half + 1] + total[:, half + 1 : half + 2]
    velocity = total[:, :half] * lax.rsqrt(squares / features + 1e-06) + shift

    parity = lax.axis_index("cfg")
    partner = lax.ppermute(velocity, "cfg", [(0, 1), (1, 0)])
    conditional = jnp.where(parity == 0, velocity, partner)
    unconditional = jnp.where(parity == 0, partner, velocity)
    guided = unconditional + guide_scale[0] * (conditional - unconditional)
    width = latents.shape[1]
    mine = lax.dynamic_slice_in_dim(guided, parity * width, width, 1)
    return latents + steps[:, None] * mine


def solution(mesh):
    in_specs = (
        P("cfg", "req", None), P("cfg", "req", None), P("cfg", "req", None),
        P(None, "req"), P("req", "cfg"), P(), P(), P(), P(), P(),
    )
    return jax.shard_map(
        per_device, mesh=mesh, in_specs=in_specs, out_specs=P("req", "cfg"), check_vma=False
    )
```

```python
import functools
import math

import jax
import jax.numpy as jnp
from jax import lax
from jax.experimental import pallas as pl
from jax.experimental.pallas import tpu as pltpu
from jax.sharding import PartitionSpec as P

HD = 128
TILE = 16
BLK = 128
CHUNK = 40
CHUNKS = 4
MORE = (48, 32)
rope_theta = 10000.0
NEG = -1e30
SCALE2 = math.log2(math.e) / math.sqrt(HD)

LB, RB, LROWS, RROWS, HEAD0, KEEP, EARLY, SOURCE = range(8)
SIDE = 16
PASS, DIRECT = 32, 36
ROW, TILES, FIRST, HEADS = range(4)
MOST, PARITY = 40, 41
SCALARS = 48
MIB = 1024 * 1024


def sizes(rows, heads):
    tiles = rows // TILE
    cap = max(
        min(max(a * n, (tiles + 1 - a) * (heads - n)) for n in range(heads + 1))
        for a in range(1, tiles + 1)
    )
    padded = -(-cap // TILE) * TILE
    return cap, padded, 2 * padded


def angles(positions):
    pair_total = HD // 2
    side_pairs = HD // 6
    time_pairs = pair_total - 2 * side_pairs
    column = jnp.arange(HD, dtype=jnp.int32) // 2
    in_time = column < time_pairs
    in_height = (column >= time_pairs) & (column < time_pairs + side_pairs)
    in_width = column >= time_pairs + side_pairs
    local_index = jnp.where(
        in_time, column, jnp.where(in_height, column - time_pairs, column - time_pairs - side_pairs)
    )
    axis_pairs = jnp.where(in_time, time_pairs, side_pairs)
    frequency = jnp.exp(
        -(local_index.astype(jnp.float32) / axis_pairs.astype(jnp.float32)) * math.log(rope_theta)
    )
    selector = jnp.stack([in_time, in_height, in_width]).astype(jnp.float32) * frequency[None, :]
    placed = positions.astype(jnp.float32)
    return (
        placed[0][:, None] * selector[0][None, :]
        + placed[1][:, None] * selector[1][None, :]
        + placed[2][:, None] * selector[2][None, :]
    )


def plan_kernel(rows, heads, count, lengths, here_ref, out, ls, rs, split, least):
    cap, padded, _ = sizes(rows, heads)
    here = here_ref[0]

    def clear(b, carry):
        ls[b] = 0
        rs[b] = 0
        return carry

    lax.fori_loop(0, count + 3, clear, 0)

    def one_video(v, start):
        end = start + lengths[v]
        b = lax.div(end - 1, rows)
        at = b * rows

        @pl.when(start < at)
        def _():
            ls[b] = at - start
            rs[b] = end - at

        return end

    lax.fori_loop(0, lengths.shape[0], one_video, 0)
    budget = 3.0 * lax.broadcasted_iota(jnp.int32, (8, 128), 1).astype(jnp.float32)
    passed_on = jnp.where(
        budget >= cap + padded, jnp.float32(padded), jnp.float32(CHUNK * CHUNKS)
    )
    split[...] = jnp.zeros_like(split)

    def tiles_of(x):
        return lax.shift_right_logical(x + TILE - 1, 4)

    def eight(b):
        return pl.ds(pl.multiple_of(b * 8, 8), 8)

    def per_tile(x, tiles):
        return jnp.floor((x + 0.5) / jnp.maximum(tiles, 1.0))

    def facts(b):
        direct = lax.rem(b, 2).astype(jnp.float32)
        lt, rt = tiles_of(ls[b]).astype(jnp.float32), tiles_of(rs[b]).astype(jnp.float32)
        return lt, rt, passed_on + direct * 1e6

    def from_right(i, load):
        b = count - 1 - i
        lt, rt, limit = facts(b)
        room = jnp.minimum(budget - load, limit)
        n = jnp.where(rt > 0.0, jnp.maximum(heads - per_tile(room, rt), 0.0), 0.0)
        least[eight(b)] = jnp.where(room >= 0.0, n, 1e6)
        return lt * n

    def from_left(b, carry):
        load, ok = carry
        lt, rt, limit = facts(b)
        room = jnp.minimum(budget - load, limit)
        most = jnp.where(lt > 0.0, jnp.minimum(per_tile(room, lt), float(heads)), 0.0)
        low = least[eight(b)]
        even = jnp.floor(heads * rt / jnp.maximum(lt + rt, 1.0) + 0.5)
        n = jnp.minimum(most, jnp.maximum(low, even))
        split[eight(b)] = n
        return rt * (heads - n), jnp.where((room >= 0.0) & (low <= most), ok, 0.0)

    zero = jnp.zeros((8, 128), jnp.float32)
    lax.fori_loop(0, count - 1, from_right, zero)
    load, ok = lax.fori_loop(1, count, from_left, (zero, zero + 1.0))
    ok = jnp.where(load <= budget, ok, 0.0)
    most = jnp.min(jnp.where(ok > 0.0, budget, 1e9))
    out[MOST] = most.astype(jnp.int32)
    out[PARITY] = here_ref[1]

    def head_split(b):
        n = split[eight(b)]
        return jnp.max(jnp.where(budget == most, n, 0.0)).astype(jnp.int32)

    even = lax.rem(here, 2) == 0
    beyond = jnp.where(even, here + 2, here - 1)
    n_left, n_right, n_beyond = head_split(here), head_split(here + 1), head_split(beyond)
    partner_passes = jnp.where(
        even,
        tiles_of(ls[beyond]) * n_beyond,
        tiles_of(rs[beyond]) * (heads - n_beyond),
    )
    direct_from = padded + partner_passes
    for side, b, n in ((0, here, n_left), (1, here + 1, n_right)):
        at = SIDE * side
        lt, rt = tiles_of(ls[b]), tiles_of(rs[b])
        direct = jnp.logical_not(even) if side == 0 else even
        out[at + LB], out[at + RB] = lt, rt
        out[at + LROWS], out[at + RROWS] = ls[b], rs[b]
        keep = n if side == 0 else jnp.where(lt > 0, heads - n, 0)
        far = lt if side == 0 else rt
        out[at + HEAD0] = 0 if side == 0 else n
        out[at + KEEP] = keep
        soon = lax.div(CHUNK * CHUNKS // 2, jnp.maximum(far, 1))
        out[at + EARLY] = jnp.where(direct, 0, jnp.minimum(keep, soon))
        out[at + SOURCE] = jnp.where(direct, direct_from, 0)
        to = jnp.where(direct, DIRECT, PASS)
        out[to + ROW] = 0 if side == 0 else rows - TILE * lt
        out[to + TILES] = rt if side == 0 else lt
        out[to + FIRST] = n if side == 0 else 0
        out[to + HEADS] = jnp.where(lt > 0, heads - n, 0) if side == 0 else n


def in_groups(low, high, step):
    count = high - low

    def run(group, times):
        def body(i, carry):
            step(jnp.minimum(low + group * i, high - group), group)
            return carry

        lax.fori_loop(0, times, body, 0)

    run(8, jnp.where(count >= 8, lax.shift_right_logical(count + 7, 3), 0))
    run(2, jnp.where((count >= 2) & (count < 8), lax.shift_right_logical(count + 1, 1), 0))
    run(1, jnp.where(count == 1, 1, 0))


def lanes_of(h):
    return pl.ds(pl.multiple_of(h * HD, HD), HD)


def rows_of(t, group):
    return pl.ds(pl.multiple_of(t * TILE, TILE), group * TILE)


def turn(x, cosine, sine):
    wide = x.astype(jnp.float32)
    even = lax.rem(lax.broadcasted_iota(jnp.int32, wide.shape, 1), 2) == 0
    swapped = jnp.where(even, pltpu.roll(wide, HD - 1, 1), pltpu.roll(wide, 1, 1))
    return (wide * cosine + swapped * sine).astype(jnp.bfloat16)


def pack(scal, low, high, box, heads, get):
    base = 0
    for what in (PASS, DIRECT):
        first_tile = lax.shift_right_logical(scal[what + ROW], 4)
        tiles, first, count = scal[what + TILES], scal[what + FIRST], scal[what + HEADS]

        def one_head(i, carry):
            start = base + (pl.program_id(0) * heads + i - first) * tiles
            begin = jnp.clip(low - start, 0, tiles)
            end = jnp.clip(high - start, 0, tiles)
            lanes = lanes_of(i)

            def step(t, group):
                q, k, v = get(rows_of(first_tile + t, group), lanes)
                item = pl.ds(start + t - low, group)
                box[item, 0:TILE] = q.reshape(group, TILE, HD)
                box[item, TILE : 2 * TILE] = k.reshape(group, TILE, HD)
                box[item, 2 * TILE : 3 * TILE] = v.reshape(group, TILE, HD)

            in_groups(begin, end, step)
            return carry

        before = first - pl.program_id(0) * heads
        lax.fori_loop(
            jnp.clip(before, 0, heads), jnp.clip(before + count, 0, heads), one_head, 0
        )
        base = base + tiles * count


def send_off(box, outs, sems):
    @pl.when(pl.program_id(0) == pl.num_programs(0) - 1)
    def _():
        at, copies = 0, []
        for i, out in enumerate(outs):
            copies.append(pltpu.make_async_copy(box.at[pl.ds(at, out.shape[0])], out, sems.at[i]))
            at += out.shape[0]
        for copy in copies:
            copy.start()
        for copy in copies:
            copy.wait()


def first_kernel(scal, q_ref, k_ref, v_ref, cos_ref, sin_ref, *rest):
    outs, box, sems = rest[:-2], rest[-2], rest[-1]

    def get(rows, lanes):
        cosine, sine = cos_ref[rows, :], sin_ref[rows, :]
        return (
            turn(q_ref[rows, lanes], cosine, sine),
            turn(k_ref[rows, lanes], cosine, sine),
            v_ref[rows, lanes],
        )

    pack(scal, 0, CHUNK * CHUNKS, box, q_ref.shape[1] // HD, get)
    send_off(box, outs, sems)


def second_kernel(scal, q_ref, k_ref, v_ref, cos_ref, sin_ref, qr_ref, kr_ref, *rest):
    outs, box, sems = rest[:-2], rest[-2], rest[-1]
    heads = q_ref.shape[1] // HD
    cosine, sine = cos_ref[...], sin_ref[...]
    for h in range(heads):
        lanes = slice(h * HD, (h + 1) * HD)
        qr_ref[:, lanes] = turn(q_ref[:, lanes], cosine, sine)
        kr_ref[:, lanes] = turn(k_ref[:, lanes], cosine, sine)

    def get(rows, lanes):
        return qr_ref[rows, lanes], kr_ref[rows, lanes], v_ref[rows, lanes]

    low = CHUNK * CHUNKS
    pack(scal, low, low + box.shape[0], box, heads, get)
    send_off(box, outs, sems)


def dot_t(a, b):
    return lax.dot_general(a, b, (((1,), (1,)), ((), ())), preferred_element_type=jnp.float32)


def attend_rows(q, k, v_ones, masked):
    s = masked(dot_t(q, k))
    top = jnp.max(s, axis=1, keepdims=True)
    weight = jnp.exp2(s * SCALE2 - top * SCALE2).astype(jnp.bfloat16)
    both = jnp.dot(weight, v_ones, preferred_element_type=jnp.float32)
    return (both[:, :HD] / both[:, HD:]).astype(jnp.bfloat16)


def projected(o_ref, w_ref, out_ref, rows):
    for j in range(rows // BLK):
        at = slice(j * BLK, (j + 1) * BLK)
        z = jnp.dot(o_ref[at, :], w_ref[...], preferred_element_type=jnp.float32)
        z = z + pltpu.roll(z, HD // 2, 1)
        lane = lax.broadcasted_iota(jnp.int32, z.shape, 1)
        squares = jnp.zeros(z.shape, jnp.float32)
        for h in range(o_ref.shape[1] // HD):
            wide = o_ref[at, h * HD : (h + 1) * HD].astype(jnp.float32)
            squares = squares + wide * wide
        total = jnp.sum(squares, axis=1, keepdims=True)
        out_ref[at, :] = jnp.where(lane < HD // 2, z, jnp.where(lane == HD // 2, total, 0.0))


def inner_kernel(scal, q_ref, k_ref, v_ref, w_ref, qv_ref, kv_ref, out_ref, o_ref):
    g = pl.program_id(0)
    rows, width = q_ref.shape
    first, last = scal[RROWS], rows - scal[SIDE + LROWS]

    @pl.when(g == 0)
    def _():
        o_ref[...] = jnp.zeros_like(o_ref)

    for j in range(rows // BLK):

        @pl.when((first < (j + 1) * BLK) & (last > j * BLK))
        def _(j=j):
            at = pl.ds(j * BLK, BLK)
            same = qv_ref[at, :] == kv_ref[...]
            for i in range(width // HD):
                lanes = slice(i * HD, (i + 1) * HD)
                ones = jnp.ones((rows, HD), jnp.bfloat16)
                v_ones = jnp.concatenate([v_ref[:, lanes], ones], axis=1)
                o_ref[at, pl.ds(pl.multiple_of(g * width + i * HD, HD), HD)] = attend_rows(
                    q_ref[at, lanes], k_ref[:, lanes], v_ones, lambda s: jnp.where(same, s, NEG)
                )

    @pl.when(g == pl.num_programs(0) - 1)
    def _():
        projected(o_ref, w_ref, out_ref, rows)


def across(scal, side, low, high, q_ref, k_ref, v_ref, items, w_ref, qs, ks, vs, o_ref, zz):
    rows = q_ref.shape[0]
    at = SIDE * side
    left, right = scal[at + LB], scal[at + RB]
    left_rows, right_rows = scal[at + LROWS], scal[at + RROWS]
    far = left if side == 0 else right
    lead = left * TILE - left_rows
    end = left * TILE + right_rows
    blocks = jnp.minimum(lax.div((left + right) * TILE + BLK - 1, BLK), rows // BLK)
    def own_step(t, group):
        source = t if side == 0 else rows // TILE - left + t
        to = rows_of(left + t if side == 0 else t, group)
        return rows_of(source, group), to

    def one_head(n, s, carry):
        lanes = lanes_of(scal[at + HEAD0] + s)

        def own(t, group):
            source, to = own_step(t, group)
            qs[to, :] = q_ref[source, lanes]
            ks[to, :] = k_ref[source, lanes]
            vs[to, :HD] = v_ref[source, lanes]

        def foreign(t, group):
            item = pl.ds(scal[at + SOURCE] + s * far + t, group)
            to = rows_of(t if side == 0 else left + t, group)
            qs[to, :] = items[item, 0:TILE].reshape(group * TILE, HD)
            ks[to, :] = items[item, TILE : 2 * TILE].reshape(group * TILE, HD)
            vs[to, :HD] = items[item, 2 * TILE : 3 * TILE].reshape(group * TILE, HD)

        in_groups(0, right if side == 0 else left, own)
        in_groups(0, far, foreign)
        width = n * BLK
        if width == rows:

            @pl.when((left + right) * TILE > rows)
            def _():
                row = lax.broadcasted_iota(jnp.int32, (TILE, HD), 0)
                for ref in (qs, ks, vs):
                    first, last = ref[0:TILE, :HD], ref[rows : rows + TILE, :HD]
                    ref[0:TILE, :HD] = jnp.where(row < lead, last, first)

        place = lax.broadcasted_iota(jnp.int32, (1, width), 1)
        valid = ((place >= lead) & (place < end)) | (place + rows < end)
        bias = jnp.where(valid, 0.0, NEG)
        k, v_ones = ks[0:width, :], vs[0:width, :]
        for j in range(n):
            mine = slice(j * BLK, (j + 1) * BLK)
            o_ref[mine, lanes] = attend_rows(qs[mine, :], k, v_ones, lambda x: x + bias)
        return carry

    for n in range(1, rows // BLK + 1):

        @pl.when((blocks == n) & (high > low))
        def _(n=n):
            o_ref[0 : n * BLK, :] = jnp.zeros((n * BLK, o_ref.shape[1]), o_ref.dtype)
            lax.fori_loop(low, high, functools.partial(one_head, n), 0)
            projected(o_ref, w_ref, zz, n * BLK)
            zz[rows : 2 * rows, :] = zz[0:rows, :]

    @pl.when(high <= low)
    def _():
        zz[...] = jnp.zeros_like(zz)

    return zz[pl.ds(pl.multiple_of(left * TILE, TILE), rows), :]


def clear_rows(qs, ks, vs):
    qs[...] = jnp.zeros_like(qs)
    ks[...] = jnp.zeros_like(ks)
    vs[:, :HD] = jnp.zeros((vs.shape[0], HD), vs.dtype)
    vs[:, HD:] = jnp.ones((vs.shape[0], HD), vs.dtype)


def early_kernel(scal, q_ref, k_ref, v_ref, w_ref, *rest):
    half = CHUNKS // 2
    boxes, out_ref, items, sems, scratch = rest[:half], rest[half], rest[half + 1], rest[half + 2], rest[half + 3 :]
    copies = [
        pltpu.make_async_copy(box, items.at[pl.ds(i * CHUNK, CHUNK)], sems.at[i])
        for i, box in enumerate(boxes)
    ]
    for copy in copies:
        copy.start()
    clear_rows(*scratch[:3])
    for copy in copies:
        copy.wait()
    for side in range(2):
        out_ref[side] = across(
            scal, side, 0, scal[SIDE * side + EARLY], q_ref, k_ref, v_ref, items, w_ref, *scratch
        )


def late_kernel(places, scal, q_ref, k_ref, v_ref, w_ref, early_ref, inner_a, inner_b, *rest):
    boxes, rest = rest[: len(places)], rest[len(places) :]
    own_ref, left_ref, right_ref, items, sems, *scratch = rest
    rows = q_ref.shape[0]
    copies = [
        pltpu.make_async_copy(box, items.at[pl.ds(at, box.shape[0])], sems.at[i])
        for i, (at, box) in enumerate(zip(places, boxes))
    ]
    for copy in copies:
        copy.start()
    clear_rows(*scratch[:3])
    for copy in copies:
        copy.wait()
    row = lax.broadcasted_iota(jnp.int32, (rows, HD), 0)
    lane = lax.broadcasted_iota(jnp.int32, (rows, HD), 1)
    own = inner_a[...] + inner_b[...]
    for side, back_ref in ((0, left_ref), (1, right_ref)):
        at = SIDE * side
        z = early_ref[side] + across(
            scal, side, scal[at + EARLY], scal[at + KEEP],
            q_ref, k_ref, v_ref, items, w_ref, *scratch,
        )
        of_left, of_right = row >= rows - scal[at + LROWS], row < scal[at + RROWS]
        own = jnp.where(of_right if side == 0 else of_left, z, own)
        back = jnp.where(of_left if side == 0 else of_right, z, 0.0)
        high = back.astype(jnp.bfloat16).astype(jnp.float32)
        both = jnp.where(lane == HD // 2 + 1, pltpu.roll(back - high, 1, 1), high)
        back_ref[...] = both.T[: back_ref.shape[0]].astype(jnp.bfloat16)
    own_ref[...] = own.T[: own_ref.shape[0]]


def step_rows(video_ids, step_sizes):
    chosen = video_ids[:, None] == jnp.arange(step_sizes.shape[0], dtype=jnp.int32)[None, :]
    return jnp.sum(jnp.where(chosen, step_sizes[None, :], 0.0), axis=1)


def call(kernel, name, mib, scalars, operands, in_specs, outs, out_specs, scratch, cost=None, grid=()):
    return pl.pallas_call(
        kernel,
        out_shape=outs,
        grid_spec=pltpu.PrefetchScalarGridSpec(
            num_scalar_prefetch=1, grid=grid, in_specs=in_specs, out_specs=out_specs,
            scratch_shapes=scratch,
        ),
        compiler_params=pltpu.CompilerParams(vmem_limit_bytes=mib * MIB),
        cost_estimate=cost,
        name=name,
    )(scalars, *operands)


def per_device(
    query_rows, key_rows, value_rows, positions, latents, w_head, modulation,
    guide_scale, step_sizes, lengths,
):
    rows, features = query_rows.shape[1], query_rows.shape[2]
    heads = features // HD
    count = lax.axis_size("req")
    here = lax.axis_index("req")
    first_row = here * rows
    _, padded, room = sizes(rows, heads)
    early_items = CHUNK * CHUNKS
    last = room - early_items - sum(MORE)
    late_sizes = (*MORE, last)

    angle = angles(positions)
    odd = (jnp.arange(HD, dtype=jnp.int32) % 2).astype(jnp.float32)
    cosine = jnp.cos(angle)
    sine = jnp.sin(angle) * (2.0 * odd - 1.0)[None, :]

    smem = pl.BlockSpec(memory_space=pltpu.SMEM)
    vmem = pl.BlockSpec(memory_space=pltpu.VMEM)
    hbm = pl.BlockSpec(memory_space=pl.ANY)
    parity = lax.axis_index("cfg")
    tie = lax.optimization_barrier
    scalars = pl.pallas_call(
        functools.partial(plan_kernel, rows, heads, count),
        out_shape=jax.ShapeDtypeStruct((SCALARS,), jnp.int32),
        in_specs=[smem, smem],
        out_specs=smem,
        scratch_shapes=[
            pltpu.SMEM((count + 3,), jnp.int32),
            pltpu.SMEM((count + 3,), jnp.int32),
            pltpu.VMEM(((count + 3) * 8, 128), jnp.float32),
            pltpu.VMEM(((count + 3) * 8, 128), jnp.float32),
        ],
        name="plan",
    )(lengths, jnp.stack([here, parity]).astype(jnp.int32))

    q, k, v = query_rows[0], key_rows[0], value_rows[0]

    def box(items):
        return jax.ShapeDtypeStruct((items, 3 * TILE, HD), jnp.bfloat16)

    def box_scratch(items):
        return pltpu.VMEM((items, 3 * TILE, HD), jnp.bfloat16)

    group = next(n for n in (5, 4, 3, 2, 1) if heads % n == 0)
    steps = heads // group
    head_block = pl.BlockSpec((rows, group * HD), lambda g, s: (0, g))
    table = pl.BlockSpec((rows, HD), lambda g, s: (0, 0))
    first = call(
        first_kernel, "pack_first", 24, scalars, (q, k, v, cosine, sine),
        [head_block] * 3 + [table] * 2, (box(CHUNK),) * CHUNKS, (hbm,) * CHUNKS,
        [box_scratch(early_items), pltpu.SemaphoreType.DMA((CHUNKS,))], grid=(steps,),
    )
    pairs = [(i, i ^ 1) for i in range(count)]
    onward = [(i, i + 2) for i in range(0, count - 2, 2)] + [(i + 2, i) for i in range(1, count - 2, 2)]
    got = [lax.ppermute(x, "req", pairs) for x in first]

    after_first, _ = tie((scalars, first[0]))
    q_rot, k_rot, *second = call(
        second_kernel, "turn_and_pack_rest", 24, after_first, (q, k, v, cosine, sine),
        [head_block] * 3 + [table] * 2,
        (jax.ShapeDtypeStruct(q.shape, q.dtype), jax.ShapeDtypeStruct(k.shape, k.dtype),
         *[box(n) for n in late_sizes]),
        (head_block, head_block, *[hbm] * 3),
        [box_scratch(sum(late_sizes)), pltpu.SemaphoreType.DMA((3,))], grid=(steps,),
        cost=pl.CostEstimate(flops=0, bytes_accessed=40_000_000, transcendentals=0),
    )
    got.append(lax.ppermute(second[0], "req", pairs))

    scaled = (1.0 + modulation[1])[:, None] * w_head.astype(jnp.float32)
    high = lax.reduce_precision(scaled, 8, 7)
    w_both = jnp.concatenate([high, scaled - high], axis=1).astype(jnp.bfloat16)
    shift = jnp.dot(
        modulation[0][None, :], w_head.astype(jnp.float32), precision=lax.Precision.HIGHEST
    )
    own_rows = first_row + jnp.arange(rows, dtype=jnp.int32)
    video = jnp.sum((jnp.cumsum(lengths)[None, :] <= own_rows[:, None]).astype(jnp.int32), axis=1)
    step_of_row = step_rows(video, step_sizes)

    def inner(when, first_step, step_count):
        block = pl.BlockSpec((rows, group * HD), lambda g, s: (0, g + first_step))
        low = first_step * group * HD
        width = step_count * group * HD
        return call(
            inner_kernel, "inner_videos", 20, when,
            (q_rot, k_rot, v, w_both[low : low + width], video[:, None], video[None, :]),
            [block] * 3 + [vmem] * 3, jax.ShapeDtypeStruct((rows, HD), jnp.float32), vmem,
            [pltpu.VMEM((rows, width), jnp.bfloat16)], grid=(step_count,),
            cost=pl.CostEstimate(
                flops=heads * rows * rows * HD * 2, bytes_accessed=30_000_000,
                transcendentals=heads * rows * rows // 2,
            ),
        )

    when_a, got[0] = tie((scalars, got[0]))
    inner_a = inner(when_a, 0, steps // 2)
    got[1], inner_a = tie((got[1], inner_a))
    when_b, got[1] = tie((scalars, got[1]))
    inner_b = inner(when_b, steps // 2, steps - steps // 2)
    got[2], inner_b = tie((got[2], inner_b))
    when_early, got[3] = tie((scalars, got[3]))
    passed = [lax.ppermute(x, "req", onward) for x in got[:CHUNKS]]

    work = [
        pltpu.VMEM((rows + TILE, HD), jnp.bfloat16),
        pltpu.VMEM((rows + TILE, HD), jnp.bfloat16),
        pltpu.VMEM((rows + TILE, 2 * HD), jnp.bfloat16),
        pltpu.VMEM((rows, features), jnp.bfloat16),
        pltpu.VMEM((2 * rows, HD), jnp.float32),
    ]
    half = CHUNKS // 2
    early = call(
        early_kernel, "videos_across_early", 24, when_early, (q_rot, k_rot, v, w_both, *passed[:half]),
        [vmem] * 4 + [hbm] * half,
        jax.ShapeDtypeStruct((2, rows, HD), jnp.float32), vmem,
        [box_scratch(half * CHUNK), pltpu.SemaphoreType.DMA((half,)), *work],
        cost=pl.CostEstimate(flops=4_000_000_000, bytes_accessed=30_000_000, transcendentals=0),
    )

    lanes = HD // 2 + TILE
    sent_back = jax.ShapeDtypeStruct((lanes, rows), jnp.bfloat16)

    def late(boxes, places, q_rot, k_rot, v, early, inner_a, inner_b):
        return call(
            functools.partial(late_kernel, places), "videos_across", 32, scalars,
            (q_rot, k_rot, v, w_both, early, inner_a, inner_b, *boxes),
            [vmem] * 7 + [hbm] * len(boxes),
            (jax.ShapeDtypeStruct((lanes, rows), jnp.float32), sent_back, sent_back), (vmem,) * 3,
            [box_scratch(padded + room), pltpu.SemaphoreType.DMA((len(boxes),)), *work],
        )

    places = tuple(CHUNK * i for i in range(CHUNKS)) + tuple(
        padded + CHUNK * i for i in range(CHUNKS + 1)
    )

    def plain(passed, got, second, *others):
        return late([*passed, *got], places, *others)

    def more(passed, got, second, *others):
        extra = lax.ppermute(second[0], "req", pairs)
        return late([*passed, *got, extra], (*places, padded + early_items + MORE[0]), *others)

    def all_of_it(passed, got, second, *others):
        extra = [lax.ppermute(x, "req", pairs) for x in second]
        passed_rest = lax.ppermute(got[-1][: padded - early_items], "req", onward)
        at = padded + early_items + MORE[0]
        return late(
            [*passed, *got, *extra, passed_rest], (*places, at, at + MORE[1], early_items), *others
        )

    most = scalars[MOST]
    level = (most > early_items + MORE[0]).astype(jnp.int32) + (most > early_items + sum(MORE))
    own, to_left, to_right = lax.switch(
        level, [plain, more, all_of_it], passed, got, second[1:],
        q_rot, k_rot, v, early, inner_a, inner_b,
    )

    back_right = lax.ppermute(to_left, "req", [(i + 1, i) for i in range(count - 1)])
    back_left = lax.ppermute(to_right, "req", [(i, i + 1) for i in range(count - 1)])
    total = own + back_right.astype(jnp.float32) + back_left.astype(jnp.float32)
    values = HD // 2
    squares = total[values : values + 1] + total[values + 1 : values + 2]
    velocity = total[:values] * lax.rsqrt(squares / features + 1e-06) + shift.T

    width = latents.shape[1]
    mine = lax.dynamic_slice_in_dim(velocity, parity * width, width, 0)
    theirs = lax.dynamic_slice_in_dim(velocity, (1 - parity) * width, width, 0)
    partner = lax.ppermute(theirs, "cfg", [(0, 1), (1, 0)])
    conditional = jnp.where(parity == 0, mine, partner)
    unconditional = jnp.where(parity == 0, partner, mine)
    guided = unconditional + guide_scale[0] * (conditional - unconditional)
    return (latents.T + step_of_row[None, :] * guided).T


def solution(mesh):
    in_specs = (
        P("cfg", "req", None), P("cfg", "req", None), P("cfg", "req", None),
        P(None, "req"), P("req", "cfg"), P(), P(), P(), P(), P(),
    )
    return jax.shard_map(
        per_device, mesh=mesh, in_specs=in_specs, out_specs=P("req", "cfg"), check_vma=False
    )
```

```python
import functools
import math

import jax
import jax.numpy as jnp
import numpy
from jax import lax
from jax.experimental import pallas as pl
from jax.experimental.pallas import tpu as pltpu
from jax.sharding import PartitionSpec as P

HD = 128
TILE = 16
BLK = 128
CHUNK = 40
CHUNKS = 4
MORE = (64, 32, 32)
rope_theta = 10000.0
NEG = -1e30
SCALE2 = math.log2(math.e) / math.sqrt(HD)

PASS, DIRECT = 0, 16
LB, RB, LROWS, RROWS, HEAD0, KEEP, EARLY, SOURCE = range(8)
OWN_FROM, OWN_TO, OWN, FAR_TO, FAR, SIDE = range(8, 14)
SEND = 32
ROW, TILES, FIRST, HEADS = range(4)
MOST, INNER_FROM, INNER_TO = 40, 41, 42
SCALARS = 48
MIB = 1024 * 1024


def sizes(rows, heads):
    tiles = rows // TILE
    cap = max(
        min(max(a * n, (tiles + 1 - a) * (heads - n)) for n in range(heads + 1))
        for a in range(1, tiles + 1)
    )
    padded = -(-cap // TILE) * TILE
    return cap, padded, 2 * padded


def angles(positions):
    pair_total = HD // 2
    side_pairs = HD // 6
    time_pairs = pair_total - 2 * side_pairs
    column = jnp.arange(HD, dtype=jnp.int32) // 2
    in_time = column < time_pairs
    in_height = (column >= time_pairs) & (column < time_pairs + side_pairs)
    in_width = column >= time_pairs + side_pairs
    local_index = jnp.where(
        in_time, column, jnp.where(in_height, column - time_pairs, column - time_pairs - side_pairs)
    )
    axis_pairs = jnp.where(in_time, time_pairs, side_pairs)
    frequency = jnp.exp(
        -(local_index.astype(jnp.float32) / axis_pairs.astype(jnp.float32)) * math.log(rope_theta)
    )
    selector = jnp.stack([in_time, in_height, in_width]).astype(jnp.float32) * frequency[None, :]
    placed = positions.astype(jnp.float32)
    return (
        placed[0][:, None] * selector[0][None, :]
        + placed[1][:, None] * selector[1][None, :]
        + placed[2][:, None] * selector[2][None, :]
    )


def plan_kernel(rows, heads, count, lengths, out, ls, rs, split, least):
    cap, padded, _ = sizes(rows, heads)
    here = lax.axis_index("req")

    def clear(b, carry):
        ls[b] = 0
        rs[b] = 0
        return carry

    lax.fori_loop(0, count + 3, clear, 0)

    def one_video(v, start):
        end = start + lengths[v]
        b = lax.div(end - 1, rows)
        at = b * rows

        @pl.when(start < at)
        def _():
            ls[b] = at - start
            rs[b] = end - at

        return end

    lax.fori_loop(0, lengths.shape[0], one_video, 0)
    budget = 3.0 * lax.broadcasted_iota(jnp.int32, (8, 128), 1).astype(jnp.float32)
    passed_on = jnp.where(
        budget >= cap + padded, jnp.float32(padded), jnp.float32(CHUNK * CHUNKS)
    )
    split[...] = jnp.zeros_like(split)

    def tiles_of(x):
        return lax.shift_right_logical(x + TILE - 1, 4)

    def eight(b):
        return pl.ds(pl.multiple_of(b * 8, 8), 8)

    def per_tile(x, tiles):
        return jnp.floor((x + 0.5) / jnp.maximum(tiles, 1.0))

    def facts(b):
        direct = lax.rem(b, 2).astype(jnp.float32)
        lt, rt = tiles_of(ls[b]).astype(jnp.float32), tiles_of(rs[b]).astype(jnp.float32)
        return lt, rt, passed_on + direct * 1e6

    def from_right(i, load):
        b = count - 1 - i
        lt, rt, limit = facts(b)
        room = jnp.minimum(budget - load, limit)
        n = jnp.where(rt > 0.0, jnp.maximum(heads - per_tile(room, rt), 0.0), 0.0)
        least[eight(b)] = jnp.where(room >= 0.0, n, 1e6)
        return lt * n

    def from_left(b, carry):
        load, ok = carry
        lt, rt, limit = facts(b)
        room = jnp.minimum(budget - load, limit)
        most = jnp.where(lt > 0.0, jnp.minimum(per_tile(room, lt), float(heads)), 0.0)
        low = least[eight(b)]
        even = jnp.floor(heads * rt / jnp.maximum(lt + rt, 1.0) + 0.5)
        n = jnp.minimum(most, jnp.maximum(low, even))
        split[eight(b)] = n
        return rt * (heads - n), jnp.where((room >= 0.0) & (low <= most), ok, 0.0)

    zero = jnp.zeros((8, 128), jnp.float32)
    lax.fori_loop(0, count - 1, from_right, zero)
    load, ok = lax.fori_loop(1, count, from_left, (zero, zero + 1.0))
    ok = jnp.where(load <= budget, ok, 0.0)
    most = jnp.min(jnp.where(ok > 0.0, budget, 1e9))
    out[MOST] = most.astype(jnp.int32)

    def head_split(b):
        n = split[eight(b)]
        return jnp.max(jnp.where(budget == most, n, 0.0)).astype(jnp.int32)

    even = lax.rem(here, 2) == 0
    beyond = jnp.where(even, here + 2, here - 1)
    n_left, n_right, n_beyond = head_split(here), head_split(here + 1), head_split(beyond)
    partner_passes = jnp.where(
        even,
        tiles_of(ls[beyond]) * n_beyond,
        tiles_of(rs[beyond]) * (heads - n_beyond),
    )
    for side, b, n in ((0, here, n_left), (1, here + 1, n_right)):
        direct = jnp.logical_not(even) if side == 0 else even
        at = jnp.where(direct, DIRECT, PASS)
        lt, rt = tiles_of(ls[b]), tiles_of(rs[b])
        none = jnp.where(lt > 0, 0, heads)
        keep = n if side == 0 else jnp.maximum(heads - n - none, 0)
        far = lt if side == 0 else rt
        out[at + LB], out[at + RB] = lt, rt
        out[at + LROWS], out[at + RROWS] = ls[b], rs[b]
        out[at + HEAD0] = 0 if side == 0 else n
        out[at + KEEP] = keep
        out[at + EARLY] = jnp.minimum(keep, lax.div(CHUNK * CHUNKS // 2, jnp.maximum(far, 1)))
        out[at + SOURCE] = jnp.where(direct, partner_passes, 0)
        out[at + OWN_FROM] = 0 if side == 0 else rows // TILE - lt
        out[at + OWN_TO] = lt if side == 0 else 0
        out[at + OWN] = rt if side == 0 else lt
        out[at + FAR_TO] = 0 if side == 0 else lt
        out[at + FAR] = far
        out[at + SIDE] = side
        to = SEND + jnp.where(direct, 4, 0)
        out[to + ROW] = 0 if side == 0 else rows - TILE * lt
        out[to + TILES] = rt if side == 0 else lt
        out[to + FIRST] = n if side == 0 else 0
        out[to + HEADS] = jnp.maximum(heads - n - none, 0) if side == 0 else n
    out[INNER_FROM] = rs[here]
    out[INNER_TO] = rows - ls[here + 1]


def in_groups(low, high, step):
    count = high - low

    def run(group, times):
        def body(i, carry):
            step(jnp.minimum(low + group * i, high - group), group)
            return carry

        lax.fori_loop(0, times, body, 0)

    run(8, jnp.where(count >= 8, lax.shift_right_logical(count + 7, 3), 0))
    run(2, jnp.where((count >= 2) & (count < 8), lax.shift_right_logical(count + 1, 1), 0))
    run(1, jnp.where(count == 1, 1, 0))


def lanes_of(h):
    return pl.ds(pl.multiple_of(h * HD, HD), HD)


def rows_of(t, group):
    return pl.ds(pl.multiple_of(t * TILE, TILE), group * TILE)


def turn(x, cosine, sine):
    wide = x.astype(jnp.float32)
    even = lax.rem(lax.broadcasted_iota(jnp.int32, wide.shape, 1), 2) == 0
    swapped = jnp.where(even, pltpu.roll(wide, HD - 1, 1), pltpu.roll(wide, 1, 1))
    return (wide * cosine + swapped * sine).astype(jnp.bfloat16)


def pack(scal, low, high, box, heads, get):
    base = 0
    for what in (SEND, SEND + 4):
        first_tile = lax.shift_right_logical(scal[what + ROW], 4)
        tiles, first, count = scal[what + TILES], scal[what + FIRST], scal[what + HEADS]

        def one_head(i, carry):
            start = base + (pl.program_id(0) * heads + i - first) * tiles
            begin = jnp.clip(low - start, 0, tiles)
            end = jnp.clip(high - start, 0, tiles)
            lanes = lanes_of(i)

            def step(t, group):
                q, k, v = get(rows_of(first_tile + t, group), lanes)
                item = pl.ds(start + t - low, group)
                box[item, 0:TILE] = q.reshape(group, TILE, HD)
                box[item, TILE : 2 * TILE] = k.reshape(group, TILE, HD)
                box[item, 2 * TILE : 3 * TILE] = v.reshape(group, TILE, HD)

            in_groups(begin, end, step)
            return carry

        before = first - pl.program_id(0) * heads
        lax.fori_loop(
            jnp.clip(before, 0, heads), jnp.clip(before + count, 0, heads), one_head, 0
        )
        base = base + tiles * count


def send_off(box, outs, sems):
    @pl.when(pl.program_id(0) == pl.num_programs(0) - 1)
    def _():
        at, copies = 0, []
        for i, out in enumerate(outs):
            copies.append(pltpu.make_async_copy(box.at[pl.ds(at, out.shape[0])], out, sems.at[i]))
            at += out.shape[0]
        for copy in copies:
            copy.start()
        for copy in copies:
            copy.wait()


def first_kernel(scal, q_ref, k_ref, v_ref, cos_ref, sin_ref, *rest):
    outs, box, sems = rest[:-2], rest[-2], rest[-1]

    def get(rows, lanes):
        cosine, sine = cos_ref[rows, :], sin_ref[rows, :]
        return (
            turn(q_ref[rows, lanes], cosine, sine),
            turn(k_ref[rows, lanes], cosine, sine),
            v_ref[rows, lanes],
        )

    pack(scal, 0, CHUNK * CHUNKS, box, q_ref.shape[1] // HD, get)
    send_off(box, outs, sems)


def second_kernel(
    scal, q_ref, k_ref, v_ref, cos_ref, sin_ref, swap_ref, wt_ref, mod_ref, qr_ref, kr_ref, w_ref, shift_ref, *rest
):
    outs, box, sems = rest[:-2], rest[-2], rest[-1]
    rows = q_ref.shape[0]
    heads = q_ref.shape[1] // HD
    wide = swap_ref.shape[0]

    @pl.when(pl.program_id(0) == 0)
    def _():
        w = wt_ref[...].astype(jnp.float32)
        scaled = w * (1.0 + mod_ref[1:2, :])
        high = scaled.astype(jnp.bfloat16)
        low = (scaled - high.astype(jnp.float32)).astype(jnp.bfloat16)
        w_ref[...] = jnp.concatenate([high, low], axis=0)
        shift = jnp.sum(w * mod_ref[0:1, :], axis=1, keepdims=True)
        shift_ref[...] = jnp.broadcast_to(shift, shift_ref.shape)

    for source, to in ((q_ref, qr_ref), (k_ref, kr_ref)):
        for h in range(0, heads, wide // HD):
            for j in range(rows // BLK):
                at = slice(j * BLK, (j + 1) * BLK)
                x = source[at, h * HD : h * HD + wide]
                swapped = jnp.dot(x, swap_ref[: x.shape[1], : x.shape[1]], preferred_element_type=jnp.float32)
                for i in range(x.shape[1] // HD):
                    lanes = slice(i * HD, (i + 1) * HD)
                    to[at, (h + i) * HD : (h + i + 1) * HD] = (
                        x[:, lanes].astype(jnp.float32) * cos_ref[at, :] + swapped[:, lanes] * sin_ref[at, :]
                    ).astype(jnp.bfloat16)

    def get(rows, lanes):
        return qr_ref[rows, lanes], kr_ref[rows, lanes], v_ref[rows, lanes]

    low = CHUNK * CHUNKS
    pack(scal, low, low + box.shape[0], box, heads, get)
    send_off(box, outs, sems)


def dot_t(a, b):
    return lax.dot_general(a, b, (((1,), (1,)), ((), ())), preferred_element_type=jnp.float32)


def attend_rows(q, k, v_ones, masked):
    s = masked(dot_t(q, k))
    top = jnp.max(s, axis=1, keepdims=True)
    weight = jnp.exp2(s * SCALE2 - top * SCALE2).astype(jnp.bfloat16)
    both = jnp.dot(weight, v_ones, preferred_element_type=jnp.float32)
    return (both[:, :HD] / both[:, HD:]).astype(jnp.bfloat16)


def projected(o_ref, w_ref, out_ref, rows):
    for j in range(rows // BLK):
        at = slice(j * BLK, (j + 1) * BLK)
        z = dot_t(o_ref[at, :], w_ref[...])
        z = z + pltpu.roll(z, HD // 2, 1)
        lane = lax.broadcasted_iota(jnp.int32, z.shape, 1)
        squares = jnp.zeros(z.shape, jnp.float32)
        for h in range(o_ref.shape[1] // HD):
            wide = o_ref[at, h * HD : (h + 1) * HD].astype(jnp.float32)
            squares = squares + wide * wide
        total = jnp.sum(squares, axis=1, keepdims=True)
        out_ref[at, :] = jnp.where(lane < HD // 2, z, jnp.where(lane == HD // 2, total, 0.0))


def inner_kernel(scal, q_ref, k_ref, v_ref, w_ref, qv_ref, kv_ref, out_ref, o_ref):
    g = pl.program_id(0)
    rows, width = q_ref.shape
    ones = jnp.ones((rows, HD), jnp.bfloat16)
    for j in range(rows // BLK):
        at = pl.ds(j * BLK, BLK)
        same = qv_ref[at, :] == kv_ref[...]
        for i in range(width // HD):
            lanes = slice(i * HD, (i + 1) * HD)
            v_ones = jnp.concatenate([v_ref[:, lanes], ones], axis=1)
            o_ref[at, pl.ds(pl.multiple_of(g * width + i * HD, HD), HD)] = attend_rows(
                q_ref[at, lanes], k_ref[:, lanes], v_ones, lambda s: jnp.where(same, s, NEG)
            )

    @pl.when(g == pl.num_programs(0) - 1)
    def _():
        projected(o_ref, w_ref, out_ref, rows)


def across(scal, at, low, high, q_ref, k_ref, v_ref, items, w_ref, qs, ks, vs, o_ref, zz):
    rows = q_ref.shape[0]
    left, right = scal[at + LB], scal[at + RB]
    lead = left * TILE - scal[at + LROWS]
    end = left * TILE + scal[at + RROWS]
    blocks = jnp.minimum(lax.div((left + right) * TILE + BLK - 1, BLK), rows // BLK)

    def two_heads(n, i, carry):
        heads = [jnp.minimum(low + 2 * i + u, high - 1) for u in range(2)]

        def own(t, group):
            source = rows_of(scal[at + OWN_FROM] + t, group)
            to = rows_of(scal[at + OWN_TO] + t, group)
            for u, s in enumerate(heads):
                lanes = lanes_of(scal[at + HEAD0] + s)
                qs[u, to, :] = q_ref[source, lanes]
                ks[u, to, :] = k_ref[source, lanes]
                vs[u, to, :HD] = v_ref[source, lanes]

        def foreign(t, group):
            to = rows_of(scal[at + FAR_TO] + t, group)
            for u, s in enumerate(heads):
                item = pl.ds(scal[at + SOURCE] + s * scal[at + FAR] + t, group)
                qs[u, to, :] = items[item, 0:TILE].reshape(group * TILE, HD)
                ks[u, to, :] = items[item, TILE : 2 * TILE].reshape(group * TILE, HD)
                vs[u, to, :HD] = items[item, 2 * TILE : 3 * TILE].reshape(group * TILE, HD)

        in_groups(0, scal[at + OWN], own)
        in_groups(0, scal[at + FAR], foreign)
        width = n * BLK
        if width == rows:

            @pl.when((left + right) * TILE > rows)
            def _():
                row = lax.broadcasted_iota(jnp.int32, (TILE, HD), 0)
                for ref in (qs, ks, vs):
                    for u in range(2):
                        first, last = ref[u, 0:TILE, :HD], ref[u, rows : rows + TILE, :HD]
                        ref[u, 0:TILE, :HD] = jnp.where(row < lead, last, first)

        place = lax.broadcasted_iota(jnp.int32, (1, width), 1)
        valid = ((place >= lead) & (place < end)) | (place + rows < end)
        bias = jnp.where(valid, 0.0, NEG)
        for j in range(n):
            mine = slice(j * BLK, (j + 1) * BLK)
            for u, s in enumerate(heads):
                o_ref[mine, lanes_of(scal[at + HEAD0] + s)] = attend_rows(
                    qs[u, mine, :], ks[u, 0:width, :], vs[u, 0:width, :], lambda x: x + bias
                )
        return carry

    for n in range(1, rows // BLK + 1):

        @pl.when((blocks == n) & (high > low))
        def _(n=n):
            o_ref[0 : n * BLK, :] = jnp.zeros((n * BLK, o_ref.shape[1]), o_ref.dtype)
            lax.fori_loop(
                0, lax.shift_right_logical(high - low + 1, 1), functools.partial(two_heads, n), 0
            )
            projected(o_ref, w_ref, zz, n * BLK)
            zz[rows : 2 * rows, :] = zz[0:rows, :]

    @pl.when(high <= low)
    def _():
        zz[...] = jnp.zeros_like(zz)

    return zz[pl.ds(pl.multiple_of(left * TILE, TILE), rows), :]


def fetch(scal, at, low, high, places, boxes, items, sems, qs, ks, vs):
    begin = scal[at + SOURCE] + low * scal[at + FAR]
    end = scal[at + SOURCE] + high * scal[at + FAR]
    copies = [
        pltpu.make_async_copy(box, items.at[pl.ds(place, box.shape[0])], sems.at[i])
        for i, (place, box) in enumerate(zip(places, boxes))
    ]
    needed = [(begin < place + box.shape[0]) & (end > place) for place, box in zip(places, boxes)]
    for copy, need in zip(copies, needed):
        pl.when(need)(copy.start)
    qs[...] = jnp.zeros_like(qs)
    ks[...] = jnp.zeros_like(ks)
    vs[:, :, :HD] = jnp.zeros((*vs.shape[:2], HD), vs.dtype)
    vs[:, :, HD:] = jnp.ones((*vs.shape[:2], HD), vs.dtype)
    for copy, need in zip(copies, needed):
        pl.when(need)(copy.wait)


def of_boundary(scal, at, shape, mine):
    row = lax.broadcasted_iota(jnp.int32, shape, 0)
    tail = jnp.where(row >= shape[0] - scal[at + LROWS], 1, 0)
    head = jnp.where(row < scal[at + RROWS], 1, 0)
    right_is_mine = (scal[at + SIDE] == 0) == mine
    return jnp.where(right_is_mine, head, tail) == 1


def send_back(scal, at, z, back_ref):
    lane = lax.broadcasted_iota(jnp.int32, z.shape, 1)
    back = jnp.where(of_boundary(scal, at, z.shape, False), z, 0.0)
    high = back.astype(jnp.bfloat16).astype(jnp.float32)
    both = jnp.where(lane == HD // 2 + 1, pltpu.roll(back - high, 1, 1), high)
    back_ref[...] = both.T[: back_ref.shape[0]].astype(jnp.bfloat16)


def early_kernel(places, scal, q_ref, k_ref, v_ref, w_ref, *rest):
    boxes, (out_ref, items, sems, *scratch) = rest[: len(places)], rest[len(places) :]
    high = scal[PASS + EARLY]
    fetch(scal, PASS, 0, high, places, boxes, items, sems, *scratch[:3])
    out_ref[...] = across(scal, PASS, 0, high, q_ref, k_ref, v_ref, items, w_ref, *scratch)


def direct_kernel(places, scal, q_ref, k_ref, v_ref, w_ref, *rest):
    boxes, (out_ref, back_ref, items, sems, *scratch) = rest[: len(places)], rest[len(places) :]
    high = scal[DIRECT + KEEP]
    fetch(scal, DIRECT, 0, high, places, boxes, items, sems, *scratch[:3])
    z = across(scal, DIRECT, 0, high, q_ref, k_ref, v_ref, items, w_ref, *scratch)
    out_ref[...] = z
    send_back(scal, DIRECT, z, back_ref)


def last_kernel(places, scal, q_ref, k_ref, v_ref, w_ref, early_ref, direct_ref, inner_a, inner_b, *rest):
    boxes, (own_ref, back_ref, items, sems, *scratch) = rest[: len(places)], rest[len(places) :]
    low, high = scal[PASS + EARLY], scal[PASS + KEEP]
    fetch(scal, PASS, low, high, places, boxes, items, sems, *scratch[:3])
    z = across(scal, PASS, low, high, q_ref, k_ref, v_ref, items, w_ref, *scratch)
    z = z + early_ref[...]
    send_back(scal, PASS, z, back_ref)
    own = inner_a[...] + inner_b[...]
    own = jnp.where(of_boundary(scal, DIRECT, z.shape, True), direct_ref[...], own)
    own = jnp.where(of_boundary(scal, PASS, z.shape, True), z, own)
    own_ref[...] = own.T[: own_ref.shape[0]]


def step_rows(video_ids, step_sizes):
    chosen = video_ids[:, None] == jnp.arange(step_sizes.shape[0], dtype=jnp.int32)[None, :]
    return jnp.sum(jnp.where(chosen, step_sizes[None, :], 0.0), axis=1)


def call(kernel, name, mib, scalars, operands, in_specs, outs, out_specs, scratch, cost=None, grid=()):
    return pl.pallas_call(
        kernel,
        out_shape=outs,
        grid_spec=pltpu.PrefetchScalarGridSpec(
            num_scalar_prefetch=1, grid=grid, in_specs=in_specs, out_specs=out_specs,
            scratch_shapes=scratch,
        ),
        compiler_params=pltpu.CompilerParams(vmem_limit_bytes=mib * MIB),
        cost_estimate=cost,
        name=name,
    )(scalars, *operands)


def per_device(
    query_rows, key_rows, value_rows, positions, latents, w_head, modulation,
    guide_scale, step_sizes, lengths,
):
    rows, features = query_rows.shape[1], query_rows.shape[2]
    heads = features // HD
    count = lax.axis_size("req")
    here = lax.axis_index("req")
    first_row = here * rows
    _, padded, room = sizes(rows, heads)
    early_items = CHUNK * CHUNKS
    late_sizes = (*MORE, room - early_items - sum(MORE))

    angle = angles(positions)
    odd = (jnp.arange(HD, dtype=jnp.int32) % 2).astype(jnp.float32)
    cosine = jnp.cos(angle)
    sine = jnp.sin(angle) * (2.0 * odd - 1.0)[None, :]

    smem = pl.BlockSpec(memory_space=pltpu.SMEM)
    vmem = pl.BlockSpec(memory_space=pltpu.VMEM)
    hbm = pl.BlockSpec(memory_space=pl.ANY)
    parity = lax.axis_index("cfg")
    tie = lax.optimization_barrier
    scalars = pl.pallas_call(
        functools.partial(plan_kernel, rows, heads, count),
        out_shape=jax.ShapeDtypeStruct((SCALARS,), jnp.int32),
        in_specs=[smem],
        out_specs=smem,
        scratch_shapes=[
            pltpu.SMEM((count + 3,), jnp.int32),
            pltpu.SMEM((count + 3,), jnp.int32),
            pltpu.VMEM(((count + 3) * 8, 128), jnp.float32),
            pltpu.VMEM(((count + 3) * 8, 128), jnp.float32),
        ],
        name="plan",
    )(lengths)

    q, k, v = query_rows[0], key_rows[0], value_rows[0]

    def box(items):
        return jax.ShapeDtypeStruct((items, 3 * TILE, HD), jnp.bfloat16)

    def box_scratch(items):
        return pltpu.VMEM((items, 3 * TILE, HD), jnp.bfloat16)

    group = next(n for n in (5, 4, 3, 2, 1) if heads % n == 0)
    steps = heads // group
    head_block = pl.BlockSpec((rows, group * HD), lambda g, s: (0, g))
    table = pl.BlockSpec((rows, HD), lambda g, s: (0, 0))
    first = call(
        first_kernel, "pack_first", 56, scalars, (q, k, v, cosine, sine),
        [head_block] * 3 + [table] * 2, (box(CHUNK),) * CHUNKS, (hbm,) * CHUNKS,
        [box_scratch(early_items), pltpu.SemaphoreType.DMA((CHUNKS,))], grid=(steps,),
    )
    pairs = [(i, i ^ 1) for i in range(count)]
    onward = [(i, i + 2) for i in range(0, count - 2, 2)] + [(i + 2, i) for i in range(1, count - 2, 2)]
    got = [lax.ppermute(x, "req", pairs) for x in first]

    after_first, _ = tie((scalars, first[0]))
    swap = jnp.asarray(numpy.eye(2 * HD)[numpy.arange(2 * HD) ^ 1], jnp.bfloat16)
    q_rot, k_rot, w_both, shift, *second = call(
        second_kernel, "turn_and_pack_rest", 32, after_first,
        (q, k, v, cosine, sine, swap, w_head.T, modulation),
        [head_block] * 3 + [table] * 2 + [vmem] * 3,
        (jax.ShapeDtypeStruct(q.shape, q.dtype), jax.ShapeDtypeStruct(k.shape, k.dtype),
         jax.ShapeDtypeStruct((HD, features), jnp.bfloat16),
         jax.ShapeDtypeStruct((HD // 2, HD), jnp.float32),
         *[box(n) for n in late_sizes]),
        (head_block, head_block, vmem, vmem, *[hbm] * len(late_sizes)),
        [box_scratch(sum(late_sizes)), pltpu.SemaphoreType.DMA((len(late_sizes),))], grid=(steps,),
        cost=pl.CostEstimate(flops=0, bytes_accessed=20_000_000, transcendentals=0),
    )
    got.append(lax.ppermute(second[0], "req", pairs))

    own_rows = first_row + jnp.arange(rows, dtype=jnp.int32)
    video = jnp.sum((jnp.cumsum(lengths)[None, :] <= own_rows[:, None]).astype(jnp.int32), axis=1)
    step_of_row = step_rows(video, step_sizes)

    def inner(when, first_step, step_count):
        block = pl.BlockSpec((rows, group * HD), lambda g, s: (0, g + first_step))
        width = step_count * group * HD
        return call(
            inner_kernel, "inner_videos", 20, when,
            (q_rot, k_rot, v, w_both, video[:, None], video[None, :]),
            [block] * 3 + [pl.BlockSpec((HD, width), lambda g, s: (0, first_step // step_count))] + [vmem] * 2, jax.ShapeDtypeStruct((rows, HD), jnp.float32), vmem,
            [pltpu.VMEM((rows, width), jnp.bfloat16)], grid=(step_count,),
            cost=pl.CostEstimate(
                flops=heads * rows * rows * HD * 2, bytes_accessed=20_000_000,
                transcendentals=heads * rows * rows // 2,
            ),
        )

    when_a, got[0] = tie((scalars, got[0]))
    inner_a = inner(when_a, 0, steps // 2)
    got[1], inner_a = tie((got[1], inner_a))
    when_b, got[1] = tie((scalars, got[1]))
    inner_b = inner(when_b, steps // 2, steps - steps // 2)
    got[2], inner_b = tie((got[2], inner_b))
    when_early, got[3] = tie((scalars, got[3]))
    passed = [lax.ppermute(x, "req", onward) for x in got[:CHUNKS]]

    work = [
        pltpu.VMEM((2, rows + TILE, HD), jnp.bfloat16),
        pltpu.VMEM((2, rows + TILE, HD), jnp.bfloat16),
        pltpu.VMEM((2, rows + TILE, 2 * HD), jnp.bfloat16),
        pltpu.VMEM((rows, features), jnp.bfloat16),
        pltpu.VMEM((2 * rows, HD), jnp.float32),
    ]
    partial = jax.ShapeDtypeStruct((rows, HD), jnp.float32)
    lanes = HD // 2 + TILE
    sent_back = jax.ShapeDtypeStruct((lanes, rows), jnp.bfloat16)

    def on_videos_across(kernel, name, when, boxes, outs, others=(), q_rot=q_rot, k_rot=k_rot, v=v, w_both=w_both):
        places = [0]
        for x in boxes:
            places.append(places[-1] + x.shape[0])
        return call(
            functools.partial(kernel, tuple(places[:-1])), name, 24, when,
            (q_rot, k_rot, v, w_both, *others, *boxes),
            [vmem] * (4 + len(others)) + [hbm] * len(boxes),
            outs, jax.tree.map(lambda _: vmem, outs),
            [box_scratch(places[-1]), pltpu.SemaphoreType.DMA((len(boxes),)), *work],
            cost=pl.CostEstimate(flops=4_000_000_000, bytes_accessed=20_000_000, transcendentals=0),
        )

    early = on_videos_across(
        early_kernel, "videos_across_early", when_early, passed[: CHUNKS // 2], partial
    )

    def direct(pieces):
        def branch(got, second, *others):
            extra = [lax.ppermute(x, "req", pairs) for x in second[:pieces]]
            rest = got[-1][: padded - early_items]
            if pieces == len(second):
                rest = lax.ppermute(rest, "req", onward)
            return *on_videos_across(
                direct_kernel, "videos_across_direct", scalars, [*got, *extra],
                (partial, sent_back), (), *others,
            ), rest

        return branch

    most = scalars[MOST]
    limits = [early_items + sum(MORE[: i + 1]) for i in range(len(MORE))]
    level = sum((most > limit).astype(jnp.int32) for limit in limits)
    direct_z, to_direct, passed_rest = lax.switch(
        level, [direct(i) for i in range(len(MORE) + 1)], got, second[1:], q_rot, k_rot, v, w_both
    )
    back_direct = lax.ppermute(to_direct, "req", pairs)
    own, to_beyond = on_videos_across(
        last_kernel, "videos_across_last", scalars, [*passed, passed_rest],
        (jax.ShapeDtypeStruct((lanes, rows), jnp.float32), sent_back),
        (early, direct_z, inner_a, inner_b),
    )
    beyond = [(i, i + 1) for i in range(1, count - 1, 2)] + [(i + 1, i) for i in range(1, count - 1, 2)]
    back_beyond = lax.ppermute(to_beyond, "req", beyond)
    total = own + back_direct.astype(jnp.float32) + back_beyond.astype(jnp.float32)
    values = HD // 2
    squares = total[values : values + 1] + total[values + 1 : values + 2]
    velocity = total[:values] * lax.rsqrt(squares / features + 1e-06) + shift[:, :1]

    width = latents.shape[1]
    mine = lax.dynamic_slice_in_dim(velocity, parity * width, width, 0)
    theirs = lax.dynamic_slice_in_dim(velocity, (1 - parity) * width, width, 0)
    partner = lax.ppermute(theirs, "cfg", [(0, 1), (1, 0)])
    conditional = jnp.where(parity == 0, mine, partner)
    unconditional = jnp.where(parity == 0, partner, mine)
    guided = unconditional + guide_scale[0] * (conditional - unconditional)
    return (latents.T + step_of_row[None, :] * guided).T


def solution(mesh):
    in_specs = (
        P("cfg", "req", None), P("cfg", "req", None), P("cfg", "req", None),
        P(None, "req"), P("req", "cfg"), P(), P(), P(), P(), P(),
    )
    return jax.shard_map(
        per_device, mesh=mesh, in_specs=in_specs, out_specs=P("req", "cfg"), check_vma=False
    )
```

```python
import functools
import math

import jax
import jax.numpy as jnp
import numpy
from jax import lax
from jax.experimental import pallas as pl
from jax.experimental.pallas import tpu as pltpu
from jax.sharding import PartitionSpec as P

HD = 128
TILE = 16
BLK = 128
CHUNKS = 4
MORE = (48, 32, 32)
rope_theta = 10000.0
NEG = -1e30
SCALE2 = math.log2(math.e) / math.sqrt(HD)

PASS, DIRECT = 0, 16
LB, RB, LROWS, RROWS, HEAD0, KEEP, EARLY, SOURCE = range(8)
OWN_FROM, OWN_TO, OWN, FAR_TO, FAR, SIDE = range(8, 14)
SEND = 32
ROW, TILES, FIRST, HEADS = range(4)
MOST, INNER_FROM, INNER_TO = 40, 41, 42
SCALARS = 48
MIB = 1024 * 1024


def sizes(rows, heads):
    tiles = rows // TILE
    cap = max(
        min(max(a * n, (tiles + 1 - a) * (heads - n)) for n in range(heads + 1))
        for a in range(1, tiles + 1)
    )
    padded = -(-cap // TILE) * TILE
    return cap, padded, 2 * padded


def angles(positions):
    pair_total = HD // 2
    side_pairs = HD // 6
    time_pairs = pair_total - 2 * side_pairs
    column = jnp.arange(HD, dtype=jnp.int32) // 2
    in_time = column < time_pairs
    in_height = (column >= time_pairs) & (column < time_pairs + side_pairs)
    in_width = column >= time_pairs + side_pairs
    local_index = jnp.where(
        in_time, column, jnp.where(in_height, column - time_pairs, column - time_pairs - side_pairs)
    )
    axis_pairs = jnp.where(in_time, time_pairs, side_pairs)
    frequency = jnp.exp(
        -(local_index.astype(jnp.float32) / axis_pairs.astype(jnp.float32)) * math.log(rope_theta)
    )
    selector = jnp.stack([in_time, in_height, in_width]).astype(jnp.float32) * frequency[None, :]
    placed = positions.astype(jnp.float32)
    return (
        placed[0][:, None] * selector[0][None, :]
        + placed[1][:, None] * selector[1][None, :]
        + placed[2][:, None] * selector[2][None, :]
    )


def plan_kernel(rows, heads, count, lengths, out, ls, rs, split, least):
    cap, padded, _ = sizes(rows, heads)
    here = lax.axis_index("req")

    def clear(b, carry):
        ls[b] = 0
        rs[b] = 0
        return carry

    lax.fori_loop(0, count + 3, clear, 0)

    def one_video(v, start):
        end = start + lengths[v]
        b = lax.div(end - 1, rows)
        at = b * rows

        @pl.when(start < at)
        def _():
            ls[b] = at - start
            rs[b] = end - at

        return end

    lax.fori_loop(0, lengths.shape[0], one_video, 0)
    budget = 3.0 * lax.broadcasted_iota(jnp.int32, (8, 128), 1).astype(jnp.float32)
    split[...] = jnp.zeros_like(split)

    def tiles_of(x):
        return lax.shift_right_logical(x + TILE - 1, 4)

    def eight(b):
        return pl.ds(pl.multiple_of(b * 8, 8), 8)

    def per_tile(x, tiles):
        return jnp.floor((x + 0.5) / jnp.maximum(tiles, 1.0))

    def facts(b):
        direct = lax.rem(b, 2).astype(jnp.float32)
        lt, rt = tiles_of(ls[b]).astype(jnp.float32), tiles_of(rs[b]).astype(jnp.float32)
        return lt, rt, padded + direct * 1e6

    def from_right(i, load):
        b = count - 1 - i
        lt, rt, limit = facts(b)
        room = jnp.minimum(budget - load, limit)
        n = jnp.where(rt > 0.0, jnp.maximum(heads - per_tile(room, rt), 0.0), 0.0)
        least[eight(b)] = jnp.where(room >= 0.0, n, 1e6)
        return lt * n

    def from_left(b, carry):
        load, ok = carry
        lt, rt, limit = facts(b)
        room = jnp.minimum(budget - load, limit)
        most = jnp.where(lt > 0.0, jnp.minimum(per_tile(room, lt), float(heads)), 0.0)
        low = least[eight(b)]
        even = jnp.floor(heads * rt / jnp.maximum(lt + rt, 1.0) + 0.5)
        n = jnp.minimum(most, jnp.maximum(low, even))
        split[eight(b)] = n
        return rt * (heads - n), jnp.where((room >= 0.0) & (low <= most), ok, 0.0)

    zero = jnp.zeros((8, 128), jnp.float32)
    lax.fori_loop(0, count - 1, from_right, zero)
    load, ok = lax.fori_loop(1, count, from_left, (zero, zero + 1.0))
    ok = jnp.where(load <= budget, ok, 0.0)
    most = jnp.min(jnp.where(ok > 0.0, budget, 1e9))
    out[MOST] = most.astype(jnp.int32)

    def head_split(b):
        n = split[eight(b)]
        return jnp.max(jnp.where(budget == most, n, 0.0)).astype(jnp.int32)

    even = lax.rem(here, 2) == 0
    beyond = jnp.where(even, here + 2, here - 1)
    n_left, n_right, n_beyond = head_split(here), head_split(here + 1), head_split(beyond)
    partner_passes = jnp.where(
        even,
        tiles_of(ls[beyond]) * n_beyond,
        tiles_of(rs[beyond]) * (heads - n_beyond),
    )
    for side, b, n in ((0, here, n_left), (1, here + 1, n_right)):
        direct = jnp.logical_not(even) if side == 0 else even
        at = jnp.where(direct, DIRECT, PASS)
        lt, rt = tiles_of(ls[b]), tiles_of(rs[b])
        none = jnp.where(lt > 0, 0, heads)
        keep = n if side == 0 else jnp.maximum(heads - n - none, 0)
        far = lt if side == 0 else rt
        out[at + LB], out[at + RB] = lt, rt
        out[at + LROWS], out[at + RROWS] = ls[b], rs[b]
        out[at + HEAD0] = 0 if side == 0 else n
        out[at + KEEP] = keep
        source = jnp.where(direct, partner_passes, 0)
        there = jnp.where(direct, padded + MORE[0], padded // CHUNKS * (CHUNKS - 1)) - source
        out[at + EARLY] = jnp.minimum(keep, lax.div(jnp.maximum(there, 0), jnp.maximum(far, 1)))
        out[at + SOURCE] = source
        out[at + OWN_FROM] = 0 if side == 0 else rows // TILE - lt
        out[at + OWN_TO] = lt if side == 0 else 0
        out[at + OWN] = rt if side == 0 else lt
        out[at + FAR_TO] = 0 if side == 0 else lt
        out[at + FAR] = far
        out[at + SIDE] = side
        to = SEND + jnp.where(direct, 4, 0)
        out[to + ROW] = 0 if side == 0 else rows - TILE * lt
        out[to + TILES] = rt if side == 0 else lt
        out[to + FIRST] = n if side == 0 else 0
        out[to + HEADS] = jnp.maximum(heads - n - none, 0) if side == 0 else n
    out[INNER_FROM] = rs[here]
    out[INNER_TO] = rows - ls[here + 1]


def in_groups(low, high, step):
    count = high - low

    def run(group, times):
        def body(i, carry):
            step(jnp.minimum(low + group * i, high - group), group)
            return carry

        lax.fori_loop(0, times, body, 0)

    run(8, jnp.where(count >= 8, lax.shift_right_logical(count + 7, 3), 0))
    run(2, jnp.where((count >= 2) & (count < 8), lax.shift_right_logical(count + 1, 1), 0))
    run(1, jnp.where(count == 1, 1, 0))


def lanes_of(h):
    return pl.ds(pl.multiple_of(h * HD, HD), HD)


def rows_of(t, group):
    return pl.ds(pl.multiple_of(t * TILE, TILE), group * TILE)


def turn(x, cosine, sine):
    wide = x.astype(jnp.float32)
    even = lax.rem(lax.broadcasted_iota(jnp.int32, wide.shape, 1), 2) == 0
    swapped = jnp.where(even, pltpu.roll(wide, HD - 1, 1), pltpu.roll(wide, 1, 1))
    return (wide * cosine + swapped * sine).astype(jnp.bfloat16)


def pack(scal, low, high, box, heads, get):
    base = 0
    for what in (SEND, SEND + 4):
        first_tile = lax.shift_right_logical(scal[what + ROW], 4)
        tiles, first, count = scal[what + TILES], scal[what + FIRST], scal[what + HEADS]

        def one_head(i, carry):
            start = base + (pl.program_id(0) * heads + i - first) * tiles
            begin = jnp.clip(low - start, 0, tiles)
            end = jnp.clip(high - start, 0, tiles)
            lanes = lanes_of(i)

            def step(t, group):
                q, k, v = get(rows_of(first_tile + t, group), lanes)
                item = pl.ds(start + t - low, group)
                box[item, 0:TILE] = q.reshape(group, TILE, HD)
                box[item, TILE : 2 * TILE] = k.reshape(group, TILE, HD)
                box[item, 2 * TILE : 3 * TILE] = v.reshape(group, TILE, HD)

            in_groups(begin, end, step)
            return carry

        before = first - pl.program_id(0) * heads
        lax.fori_loop(
            jnp.clip(before, 0, heads), jnp.clip(before + count, 0, heads), one_head, 0
        )
        base = base + tiles * count


def send_off(box, outs, sems):
    @pl.when(pl.program_id(0) == pl.num_programs(0) - 1)
    def _():
        at, copies = 0, []
        for i, out in enumerate(outs):
            copies.append(pltpu.make_async_copy(box.at[pl.ds(at, out.shape[0])], out, sems.at[i]))
            at += out.shape[0]
        for copy in copies:
            copy.start()
        for copy in copies:
            copy.wait()


def first_kernel(scal, q_ref, k_ref, v_ref, cos_ref, sin_ref, *rest):
    outs, box, sems = rest[:-2], rest[-2], rest[-1]

    def get(rows, lanes):
        cosine, sine = cos_ref[rows, :], sin_ref[rows, :]
        return (
            turn(q_ref[rows, lanes], cosine, sine),
            turn(k_ref[rows, lanes], cosine, sine),
            v_ref[rows, lanes],
        )

    pack(scal, 0, box.shape[0], box, q_ref.shape[1] // HD, get)
    send_off(box, outs, sems)


def second_kernel(
    low, scal, q_ref, k_ref, v_ref, cos_ref, sin_ref, swap_ref, wt_ref, mod_ref, qr_ref, kr_ref, w_ref, shift_ref, *rest
):
    outs, box, sems = rest[:-2], rest[-2], rest[-1]
    rows = q_ref.shape[0]
    heads = q_ref.shape[1] // HD
    wide = swap_ref.shape[0]

    @pl.when(pl.program_id(0) == 0)
    def _():
        w = wt_ref[...].astype(jnp.float32)
        scaled = w * (1.0 + mod_ref[1:2, :])
        high = scaled.astype(jnp.bfloat16)
        low = (scaled - high.astype(jnp.float32)).astype(jnp.bfloat16)
        w_ref[...] = jnp.concatenate([high, low], axis=0)
        shift = jnp.sum(w * mod_ref[0:1, :], axis=1, keepdims=True)
        shift_ref[...] = jnp.broadcast_to(shift, shift_ref.shape)

    for source, to in ((q_ref, qr_ref), (k_ref, kr_ref)):
        for h in range(0, heads, wide // HD):
            for j in range(rows // BLK):
                at = slice(j * BLK, (j + 1) * BLK)
                x = source[at, h * HD : h * HD + wide]
                swapped = jnp.dot(x, swap_ref[: x.shape[1], : x.shape[1]], preferred_element_type=jnp.float32)
                for i in range(x.shape[1] // HD):
                    lanes = slice(i * HD, (i + 1) * HD)
                    to[at, (h + i) * HD : (h + i + 1) * HD] = (
                        x[:, lanes].astype(jnp.float32) * cos_ref[at, :] + swapped[:, lanes] * sin_ref[at, :]
                    ).astype(jnp.bfloat16)

    def get(rows, lanes):
        return qr_ref[rows, lanes], kr_ref[rows, lanes], v_ref[rows, lanes]

    pack(scal, low, low + box.shape[0], box, heads, get)
    send_off(box, outs, sems)


def dot_t(a, b):
    return lax.dot_general(a, b, (((1,), (1,)), ((), ())), preferred_element_type=jnp.float32)


def attend_rows(q, k, v_ones, masked):
    s = masked(dot_t(q, k))
    top = jnp.max(s, axis=1, keepdims=True)
    weight = jnp.exp2(s * SCALE2 - top * SCALE2).astype(jnp.bfloat16)
    both = jnp.dot(weight, v_ones, preferred_element_type=jnp.float32)
    return (both[:, :HD] / both[:, HD:]).astype(jnp.bfloat16)


def projected(o_ref, w_ref, out_ref, rows):
    for j in range(rows // BLK):
        at = slice(j * BLK, (j + 1) * BLK)
        z = dot_t(o_ref[at, :], w_ref[...])
        z = z + pltpu.roll(z, HD // 2, 1)
        lane = lax.broadcasted_iota(jnp.int32, z.shape, 1)
        squares = jnp.zeros(z.shape, jnp.float32)
        for h in range(o_ref.shape[1] // HD):
            wide = o_ref[at, h * HD : (h + 1) * HD].astype(jnp.float32)
            squares = squares + wide * wide
        total = jnp.sum(squares, axis=1, keepdims=True)
        out_ref[at, :] = jnp.where(lane < HD // 2, z, jnp.where(lane == HD // 2, total, 0.0))


def inner_kernel(scal, q_ref, k_ref, v_ref, w_ref, qv_ref, kv_ref, out_ref, o_ref):
    g = pl.program_id(0)
    rows, width = q_ref.shape
    ones = jnp.ones((rows, HD), jnp.bfloat16)
    for j in range(rows // BLK):
        at = pl.ds(j * BLK, BLK)
        same = qv_ref[at, :] == kv_ref[...]
        for i in range(width // HD):
            lanes = slice(i * HD, (i + 1) * HD)
            v_ones = jnp.concatenate([v_ref[:, lanes], ones], axis=1)
            o_ref[at, pl.ds(pl.multiple_of(g * width + i * HD, HD), HD)] = attend_rows(
                q_ref[at, lanes], k_ref[:, lanes], v_ones, lambda s: jnp.where(same, s, NEG)
            )

    @pl.when(g == pl.num_programs(0) - 1)
    def _():
        projected(o_ref, w_ref, out_ref, rows)


def across(scal, at, offset, low, high, q_ref, k_ref, v_ref, items, w_ref, qs, ks, vs, o_ref, zz):
    rows = q_ref.shape[0]
    left, right = scal[at + LB], scal[at + RB]
    lead = left * TILE - scal[at + LROWS]
    end = left * TILE + scal[at + RROWS]
    blocks = jnp.minimum(lax.div((left + right) * TILE + BLK - 1, BLK), rows // BLK)

    def two_heads(n, i, carry):
        heads = [jnp.minimum(low + 2 * i + u, high - 1) for u in range(2)]

        def own(t, group):
            source = rows_of(scal[at + OWN_FROM] + t, group)
            to = rows_of(scal[at + OWN_TO] + t, group)
            for u, s in enumerate(heads):
                lanes = lanes_of(scal[at + HEAD0] + s)
                qs[u, to, :] = q_ref[source, lanes]
                ks[u, to, :] = k_ref[source, lanes]
                vs[u, to, :HD] = v_ref[source, lanes]

        def foreign(t, group):
            to = rows_of(scal[at + FAR_TO] + t, group)
            for u, s in enumerate(heads):
                item = pl.ds(scal[at + SOURCE] + offset + s * scal[at + FAR] + t, group)
                qs[u, to, :] = items[item, 0:TILE].reshape(group * TILE, HD)
                ks[u, to, :] = items[item, TILE : 2 * TILE].reshape(group * TILE, HD)
                vs[u, to, :HD] = items[item, 2 * TILE : 3 * TILE].reshape(group * TILE, HD)

        in_groups(0, scal[at + OWN], own)
        in_groups(0, scal[at + FAR], foreign)
        width = n * BLK
        if width == rows:

            @pl.when((left + right) * TILE > rows)
            def _():
                row = lax.broadcasted_iota(jnp.int32, (TILE, HD), 0)
                for ref in (qs, ks, vs):
                    for u in range(2):
                        first, last = ref[u, 0:TILE, :HD], ref[u, rows : rows + TILE, :HD]
                        ref[u, 0:TILE, :HD] = jnp.where(row < lead, last, first)

        place = lax.broadcasted_iota(jnp.int32, (1, width), 1)
        valid = ((place >= lead) & (place < end)) | (place + rows < end)
        bias = jnp.where(valid, 0.0, NEG)
        for j in range(n):
            mine = slice(j * BLK, (j + 1) * BLK)
            for u, s in enumerate(heads):
                o_ref[mine, lanes_of(scal[at + HEAD0] + s)] = attend_rows(
                    qs[u, mine, :], ks[u, 0:width, :], vs[u, 0:width, :], lambda x: x + bias
                )
        return carry

    for n in range(1, rows // BLK + 1):

        @pl.when((blocks == n) & (high > low))
        def _(n=n):
            o_ref[0 : n * BLK, :] = jnp.zeros((n * BLK, o_ref.shape[1]), o_ref.dtype)
            lax.fori_loop(
                0, lax.shift_right_logical(high - low + 1, 1), functools.partial(two_heads, n), 0
            )
            projected(o_ref, w_ref, zz, n * BLK)
            zz[rows : 2 * rows, :] = zz[0:rows, :]

    @pl.when(high <= low)
    def _():
        zz[...] = jnp.zeros_like(zz)

    return zz[pl.ds(pl.multiple_of(left * TILE, TILE), rows), :]


def fetch(scal, at, offset, low, high, places, boxes, items, sems, qs, ks, vs):
    begin = scal[at + SOURCE] + offset + low * scal[at + FAR]
    end = scal[at + SOURCE] + offset + high * scal[at + FAR]
    copies = [
        pltpu.make_async_copy(box, items.at[pl.ds(place, box.shape[0])], sems.at[i])
        for i, (place, box) in enumerate(zip(places, boxes))
    ]
    needed = [(high > low) & (begin < place + box.shape[0]) & (end > place) for place, box in zip(places, boxes)]
    for copy, need in zip(copies, needed):
        pl.when(need)(copy.start)
    qs[...] = jnp.zeros_like(qs)
    ks[...] = jnp.zeros_like(ks)
    vs[:, :, :HD] = jnp.zeros((*vs.shape[:2], HD), vs.dtype)
    vs[:, :, HD:] = jnp.ones((*vs.shape[:2], HD), vs.dtype)
    for copy, need in zip(copies, needed):
        pl.when(need)(copy.wait)


def of_boundary(scal, at, shape, mine):
    row = lax.broadcasted_iota(jnp.int32, shape, 0)
    tail = jnp.where(row >= shape[0] - scal[at + LROWS], 1, 0)
    head = jnp.where(row < scal[at + RROWS], 1, 0)
    right_is_mine = (scal[at + SIDE] == 0) == mine
    return jnp.where(right_is_mine, head, tail) == 1


def send_back(scal, at, z, back_ref):
    lane = lax.broadcasted_iota(jnp.int32, z.shape, 1)
    back = jnp.where(of_boundary(scal, at, z.shape, False), z, 0.0)
    high = back.astype(jnp.bfloat16).astype(jnp.float32)
    both = jnp.where(lane == HD // 2 + 1, pltpu.roll(back - high, 1, 1), high)
    back_ref[...] = both.T[: back_ref.shape[0]].astype(jnp.bfloat16)


def early_kernel(places, at, scal, q_ref, k_ref, v_ref, w_ref, *rest):
    boxes, (out_ref, items, sems, *scratch) = rest[: len(places)], rest[len(places) :]
    high = scal[at + EARLY]
    fetch(scal, at, 0, 0, high, places, boxes, items, sems, *scratch[:3])
    out_ref[...] = across(scal, at, 0, 0, high, q_ref, k_ref, v_ref, items, w_ref, *scratch)


def last_kernel(
    places, passed_before, offset, scal, q_ref, k_ref, v_ref, w_ref, passed_ref, direct_ref, inner_a, inner_b, *rest
):
    boxes, rest = rest[: len(places)], rest[len(places) :]
    own_ref, pass_back_ref, direct_back_ref, items, sems, *scratch = rest

    def remaining(at, offset):
        low, high = scal[at + EARLY], scal[at + KEEP]
        fetch(scal, at, offset, low, high, places, boxes, items, sems, *scratch[:3])
        return across(scal, at, offset, low, high, q_ref, k_ref, v_ref, items, w_ref, *scratch)

    direct_z = direct_ref[...]
    if offset is not None:
        direct_z = direct_z + remaining(DIRECT, offset)
    passed_z = passed_ref[...] + remaining(PASS, -passed_before)
    send_back(scal, PASS, passed_z, pass_back_ref)
    send_back(scal, DIRECT, direct_z, direct_back_ref)
    own = inner_a[...] + inner_b[...]
    own = jnp.where(of_boundary(scal, DIRECT, own.shape, True), direct_z, own)
    own = jnp.where(of_boundary(scal, PASS, own.shape, True), passed_z, own)
    own_ref[...] = own.T[: own_ref.shape[0]]


def step_rows(video_ids, step_sizes):
    chosen = video_ids[:, None] == jnp.arange(step_sizes.shape[0], dtype=jnp.int32)[None, :]
    return jnp.sum(jnp.where(chosen, step_sizes[None, :], 0.0), axis=1)


def call(kernel, name, mib, scalars, operands, in_specs, outs, out_specs, scratch, grid=()):
    return pl.pallas_call(
        kernel,
        out_shape=outs,
        grid_spec=pltpu.PrefetchScalarGridSpec(
            num_scalar_prefetch=1, grid=grid, in_specs=in_specs, out_specs=out_specs,
            scratch_shapes=scratch,
        ),
        compiler_params=pltpu.CompilerParams(vmem_limit_bytes=mib * MIB),
        cost_estimate=pl.CostEstimate(flops=1, bytes_accessed=1, transcendentals=0),
        name=name,
    )(scalars, *operands)


def per_device(
    query_rows, key_rows, value_rows, positions, latents, w_head, modulation,
    guide_scale, step_sizes, lengths,
):
    rows, features = query_rows.shape[1], query_rows.shape[2]
    heads = features // HD
    count = lax.axis_size("req")
    here = lax.axis_index("req")
    first_row = here * rows
    _, padded, room = sizes(rows, heads)
    chunk = padded // CHUNKS
    late_sizes = (*[chunk] * (CHUNKS - 1), *MORE, room - padded - sum(MORE))

    angle = angles(positions)
    odd = (jnp.arange(HD, dtype=jnp.int32) % 2).astype(jnp.float32)
    cosine = jnp.cos(angle)
    sine = jnp.sin(angle) * (2.0 * odd - 1.0)[None, :]

    smem = pl.BlockSpec(memory_space=pltpu.SMEM)
    vmem = pl.BlockSpec(memory_space=pltpu.VMEM)
    hbm = pl.BlockSpec(memory_space=pl.ANY)
    parity = lax.axis_index("cfg")
    tie = lax.optimization_barrier
    scalars = pl.pallas_call(
        functools.partial(plan_kernel, rows, heads, count),
        out_shape=jax.ShapeDtypeStruct((SCALARS,), jnp.int32),
        in_specs=[smem],
        out_specs=smem,
        scratch_shapes=[
            pltpu.SMEM((count + 3,), jnp.int32),
            pltpu.SMEM((count + 3,), jnp.int32),
            pltpu.VMEM(((count + 3) * 8, 128), jnp.float32),
            pltpu.VMEM(((count + 3) * 8, 128), jnp.float32),
        ],
        name="plan",
    )(lengths)

    q, k, v = query_rows[0], key_rows[0], value_rows[0]

    def box(items):
        return jax.ShapeDtypeStruct((items, 3 * TILE, HD), jnp.bfloat16)

    def box_scratch(items):
        return pltpu.VMEM((items, 3 * TILE, HD), jnp.bfloat16)

    group = next(n for n in (5, 4, 3, 2, 1) if heads % n == 0)
    steps = heads // group
    head_block = pl.BlockSpec((rows, group * HD), lambda g, s: (0, g))
    table = pl.BlockSpec((rows, HD), lambda g, s: (0, 0))
    first = call(
        first_kernel, "pack_first", 56, scalars, (q, k, v, cosine, sine),
        [head_block] * 3 + [table] * 2, (box(chunk),), (hbm,),
        [box_scratch(chunk), pltpu.SemaphoreType.DMA((1,))], grid=(steps,),
    )
    pairs = [(i, i ^ 1) for i in range(count)]
    onward = [(i, i + 2) for i in range(0, count - 2, 2)] + [(i + 2, i) for i in range(1, count - 2, 2)]
    got = [lax.ppermute(first[0], "req", pairs)]

    after_first, _ = tie((scalars, first[0]))
    swap = jnp.asarray(numpy.eye(2 * HD)[numpy.arange(2 * HD) ^ 1], jnp.bfloat16)
    q_rot, k_rot, w_both, shift, *second = call(
        functools.partial(second_kernel, chunk), "turn_and_pack_rest", 32, after_first,
        (q, k, v, cosine, sine, swap, w_head.T, modulation),
        [head_block] * 3 + [table] * 2 + [vmem] * 3,
        (jax.ShapeDtypeStruct(q.shape, q.dtype), jax.ShapeDtypeStruct(k.shape, k.dtype),
         jax.ShapeDtypeStruct((HD, features), jnp.bfloat16),
         jax.ShapeDtypeStruct((HD // 2, HD), jnp.float32),
         *[box(n) for n in late_sizes]),
        (head_block, head_block, vmem, vmem, *[hbm] * len(late_sizes)),
        [box_scratch(sum(late_sizes)), pltpu.SemaphoreType.DMA((len(late_sizes),))], grid=(steps,),
    )
    got += [lax.ppermute(x, "req", pairs) for x in second[:CHUNKS]]
    second = second[CHUNKS:]

    own_rows = first_row + jnp.arange(rows, dtype=jnp.int32)
    video = jnp.sum((jnp.cumsum(lengths)[None, :] <= own_rows[:, None]).astype(jnp.int32), axis=1)
    step_of_row = step_rows(video, step_sizes)

    def inner(when, first_step, step_count):
        block = pl.BlockSpec((rows, group * HD), lambda g, s: (0, g + first_step))
        width = step_count * group * HD
        return call(
            inner_kernel, "inner_videos", 20, when,
            (q_rot, k_rot, v, w_both, video[:, None], video[None, :]),
            [block] * 3 + [pl.BlockSpec((HD, width), lambda g, s: (0, first_step // step_count))] + [vmem] * 2, jax.ShapeDtypeStruct((rows, HD), jnp.float32), vmem,
            [pltpu.VMEM((rows, width), jnp.bfloat16)], grid=(step_count,),
        )

    inner_a = inner(scalars, 0, steps // 2)
    got[0], inner_a = tie((got[0], inner_a))
    when_b, got[0] = tie((scalars, got[0]))
    inner_b = inner(when_b, steps // 2, steps - steps // 2)
    got[1], inner_b = tie((got[1], inner_b))
    when_early, got[3] = tie((scalars, got[3]))
    passed = [lax.ppermute(x, "req", onward) for x in got[:CHUNKS]]

    work = [
        pltpu.VMEM((2, rows + TILE, HD), jnp.bfloat16),
        pltpu.VMEM((2, rows + TILE, HD), jnp.bfloat16),
        pltpu.VMEM((2, rows + TILE, 2 * HD), jnp.bfloat16),
        pltpu.VMEM((rows, features), jnp.bfloat16),
        pltpu.VMEM((2 * rows, HD), jnp.float32),
    ]
    partial = jax.ShapeDtypeStruct((rows, HD), jnp.float32)
    lanes = HD // 2 + TILE
    sent_back = jax.ShapeDtypeStruct((lanes, rows), jnp.bfloat16)

    def on_videos_across(kernel, name, when, boxes, outs, others, q_rot, k_rot, v, w_both):
        places = [0]
        for x in boxes:
            places.append(places[-1] + x.shape[0])
        return call(
            kernel(tuple(places[:-1])), name, 24, when, (q_rot, k_rot, v, w_both, *others, *boxes),
            [vmem] * (4 + len(others)) + [hbm] * len(boxes), outs, jax.tree.map(lambda _: vmem, outs),
            [box_scratch(places[-1]), pltpu.SemaphoreType.DMA((len(boxes),)), *work],
        )

    def early_on(at, name, when, boxes):
        return on_videos_across(
            lambda places: functools.partial(early_kernel, places, at), name, when, boxes,
            partial, (), q_rot, k_rot, v, w_both,
        )

    early = early_on(PASS, "videos_across_early", when_early, passed[: CHUNKS - 1])
    when_direct, early = tie((scalars, early))
    direct_z = early_on(DIRECT, "videos_across_direct", when_direct, got)

    def last(pieces):
        def branch(passed, got, second, q_rot, k_rot, v, w_both, *others):
            boxes, offset = passed[CHUNKS - 2 :], None
            if pieces:
                boxes = [*boxes, *got, *[lax.ppermute(x, "req", pairs) for x in second[:pieces]]]
                offset = 2 * chunk
            return on_videos_across(
                lambda places: functools.partial(last_kernel, places, chunk * (CHUNKS - 2), offset),
                "videos_across_last", scalars, boxes,
                (jax.ShapeDtypeStruct((lanes, rows), jnp.float32), sent_back, sent_back),
                others, q_rot, k_rot, v, w_both,
            )

        return branch

    most = scalars[MOST]
    limits = [padded + sum(MORE[: i + 1]) for i in range(len(MORE))]
    level = sum((most > limit).astype(jnp.int32) for limit in limits)
    level, direct_z = tie((level, direct_z))
    own, to_beyond, to_direct = lax.switch(
        level, [last(i) for i in range(len(MORE) + 1)], passed, got, second,
        q_rot, k_rot, v, w_both, early, direct_z, inner_a, inner_b,
    )
    back_direct = lax.ppermute(to_direct, "req", pairs)
    beyond = [(i, i + 1) for i in range(1, count - 1, 2)] + [(i + 1, i) for i in range(1, count - 1, 2)]
    back_beyond = lax.ppermute(to_beyond, "req", beyond)
    total = own + back_direct.astype(jnp.float32) + back_beyond.astype(jnp.float32)
    values = HD // 2
    squares = total[values : values + 1] + total[values + 1 : values + 2]
    velocity = total[:values] * lax.rsqrt(squares / features + 1e-06) + shift[:, :1]

    width = latents.shape[1]
    mine = lax.dynamic_slice_in_dim(velocity, parity * width, width, 0)
    theirs = lax.dynamic_slice_in_dim(velocity, (1 - parity) * width, width, 0)
    partner = lax.ppermute(theirs, "cfg", [(0, 1), (1, 0)])
    conditional = jnp.where(parity == 0, mine, partner)
    unconditional = jnp.where(parity == 0, partner, mine)
    guided = unconditional + guide_scale[0] * (conditional - unconditional)
    return (latents.T + step_of_row[None, :] * guided).T


def solution(mesh):
    in_specs = (
        P("cfg", "req", None), P("cfg", "req", None), P("cfg", "req", None),
        P(None, "req"), P("req", "cfg"), P(), P(), P(), P(), P(),
    )
    return jax.shard_map(
        per_device, mesh=mesh, in_specs=in_specs, out_specs=P("req", "cfg"), check_vma=False
    )
```

```python
import functools
import math

import jax
import jax.numpy as jnp
import numpy
from jax import lax
from jax.experimental import pallas as pl
from jax.experimental.pallas import tpu as pltpu
from jax.sharding import PartitionSpec as P

HD = 128
TILE = 16
BLK = 128
CHUNKS = 4
MORE = (48, 32, 32)
rope_theta = 10000.0
NEG = -1e30
SCALE2 = math.log2(math.e) / math.sqrt(HD)

PASS, DIRECT = 0, 16
LB, RB, LROWS, RROWS, HEAD0, KEEP, EARLY, SOURCE = range(8)
OWN_FROM, OWN_TO, OWN, FAR_TO, FAR, SIDE = range(8, 14)
SEND = 32
ROW, TILES, FIRST, HEADS = range(4)
MOST, INNER_FROM, INNER_TO = 40, 41, 42
SCALARS = 48
MIB = 1024 * 1024


def sizes(rows, heads):
    tiles = rows // TILE
    cap = max(
        min(max(a * n, (tiles + 1 - a) * (heads - n)) for n in range(heads + 1))
        for a in range(1, tiles + 1)
    )
    padded = -(-cap // TILE) * TILE
    return cap, padded, 2 * padded


def angles(positions):
    pair_total = HD // 2
    side_pairs = HD // 6
    time_pairs = pair_total - 2 * side_pairs
    column = jnp.arange(HD, dtype=jnp.int32) // 2
    in_time = column < time_pairs
    in_height = (column >= time_pairs) & (column < time_pairs + side_pairs)
    in_width = column >= time_pairs + side_pairs
    local_index = jnp.where(
        in_time, column, jnp.where(in_height, column - time_pairs, column - time_pairs - side_pairs)
    )
    axis_pairs = jnp.where(in_time, time_pairs, side_pairs)
    frequency = jnp.exp(
        -(local_index.astype(jnp.float32) / axis_pairs.astype(jnp.float32)) * math.log(rope_theta)
    )
    selector = jnp.stack([in_time, in_height, in_width]).astype(jnp.float32) * frequency[None, :]
    placed = positions.astype(jnp.float32)
    return (
        placed[0][:, None] * selector[0][None, :]
        + placed[1][:, None] * selector[1][None, :]
        + placed[2][:, None] * selector[2][None, :]
    )


def plan_kernel(rows, heads, count, lengths, out, ls, rs, split, least):
    cap, padded, _ = sizes(rows, heads)
    here = lax.axis_index("req")

    def clear(b, carry):
        ls[b] = 0
        rs[b] = 0
        return carry

    lax.fori_loop(0, count + 3, clear, 0)

    def one_video(v, start):
        end = start + lengths[v]
        b = lax.div(end - 1, rows)
        at = b * rows

        @pl.when(start < at)
        def _():
            ls[b] = at - start
            rs[b] = end - at

        return end

    lax.fori_loop(0, lengths.shape[0], one_video, 0)
    budget = 3.0 * lax.broadcasted_iota(jnp.int32, (8, 128), 1).astype(jnp.float32)
    split[...] = jnp.zeros_like(split)

    def tiles_of(x):
        return lax.shift_right_logical(x + TILE - 1, 4)

    def eight(b):
        return pl.ds(pl.multiple_of(b * 8, 8), 8)

    def per_tile(x, tiles):
        return jnp.floor((x + 0.5) / jnp.maximum(tiles, 1.0))

    def facts(b):
        direct = lax.rem(b, 2).astype(jnp.float32)
        lt, rt = tiles_of(ls[b]).astype(jnp.float32), tiles_of(rs[b]).astype(jnp.float32)
        return lt, rt, padded + direct * 1e6

    def from_right(i, load):
        b = count - 1 - i
        lt, rt, limit = facts(b)
        room = jnp.minimum(budget - load, limit)
        n = jnp.where(rt > 0.0, jnp.maximum(heads - per_tile(room, rt), 0.0), 0.0)
        least[eight(b)] = jnp.where(room >= 0.0, n, 1e6)
        return lt * n

    def from_left(b, carry):
        load, ok = carry
        lt, rt, limit = facts(b)
        room = jnp.minimum(budget - load, limit)
        most = jnp.where(lt > 0.0, jnp.minimum(per_tile(room, lt), float(heads)), 0.0)
        low = least[eight(b)]
        even = jnp.floor(heads * rt / jnp.maximum(lt + rt, 1.0) + 0.5)
        n = jnp.minimum(most, jnp.maximum(low, even))
        split[eight(b)] = n
        return rt * (heads - n), jnp.where((room >= 0.0) & (low <= most), ok, 0.0)

    zero = jnp.zeros((8, 128), jnp.float32)
    lax.fori_loop(0, count - 1, from_right, zero)
    load, ok = lax.fori_loop(1, count, from_left, (zero, zero + 1.0))
    ok = jnp.where(load <= budget, ok, 0.0)
    most = jnp.min(jnp.where(ok > 0.0, budget, 1e9))
    out[MOST] = most.astype(jnp.int32)

    def head_split(b):
        n = split[eight(b)]
        return jnp.max(jnp.where(budget == most, n, 0.0)).astype(jnp.int32)

    even = lax.rem(here, 2) == 0
    beyond = jnp.where(even, here + 2, here - 1)
    n_left, n_right, n_beyond = head_split(here), head_split(here + 1), head_split(beyond)
    partner_passes = jnp.where(
        even,
        tiles_of(ls[beyond]) * n_beyond,
        tiles_of(rs[beyond]) * (heads - n_beyond),
    )
    for side, b, n in ((0, here, n_left), (1, here + 1, n_right)):
        direct = jnp.logical_not(even) if side == 0 else even
        at = jnp.where(direct, DIRECT, PASS)
        lt, rt = tiles_of(ls[b]), tiles_of(rs[b])
        none = jnp.where(lt > 0, 0, heads)
        keep = n if side == 0 else jnp.maximum(heads - n - none, 0)
        far = lt if side == 0 else rt
        out[at + LB], out[at + RB] = lt, rt
        out[at + LROWS], out[at + RROWS] = ls[b], rs[b]
        out[at + HEAD0] = 0 if side == 0 else n
        out[at + KEEP] = keep
        source = jnp.where(direct, partner_passes, 0)
        there = jnp.where(direct, padded + MORE[0], padded // CHUNKS * (CHUNKS - 1)) - source
        out[at + EARLY] = jnp.minimum(keep, lax.div(jnp.maximum(there, 0), jnp.maximum(far, 1)))
        out[at + SOURCE] = source
        out[at + OWN_FROM] = 0 if side == 0 else rows // TILE - lt
        out[at + OWN_TO] = lt if side == 0 else 0
        out[at + OWN] = rt if side == 0 else lt
        out[at + FAR_TO] = 0 if side == 0 else lt
        out[at + FAR] = far
        out[at + SIDE] = side
        to = SEND + jnp.where(direct, 4, 0)
        out[to + ROW] = 0 if side == 0 else rows - TILE * lt
        out[to + TILES] = rt if side == 0 else lt
        out[to + FIRST] = n if side == 0 else 0
        out[to + HEADS] = jnp.maximum(heads - n - none, 0) if side == 0 else n
    out[INNER_FROM] = rs[here]
    out[INNER_TO] = rows - ls[here + 1]


def in_groups(low, high, step):
    count = high - low

    def run(group, times):
        def body(i, carry):
            step(jnp.minimum(low + group * i, high - group), group)
            return carry

        lax.fori_loop(0, times, body, 0)

    run(8, jnp.where(count >= 8, lax.shift_right_logical(count + 7, 3), 0))
    run(2, jnp.where((count >= 2) & (count < 8), lax.shift_right_logical(count + 1, 1), 0))
    run(1, jnp.where(count == 1, 1, 0))


def lanes_of(h):
    return pl.ds(pl.multiple_of(h * HD, HD), HD)


def rows_of(t, group):
    return pl.ds(pl.multiple_of(t * TILE, TILE), group * TILE)


def turn(x, cosine, sine):
    wide = x.astype(jnp.float32)
    even = lax.rem(lax.broadcasted_iota(jnp.int32, wide.shape, 1), 2) == 0
    swapped = jnp.where(even, pltpu.roll(wide, HD - 1, 1), pltpu.roll(wide, 1, 1))
    return (wide * cosine + swapped * sine).astype(jnp.bfloat16)


def pack(scal, low, high, box, heads, get):
    base = 0
    for what in (SEND, SEND + 4):
        first_tile = lax.shift_right_logical(scal[what + ROW], 4)
        tiles, first, count = scal[what + TILES], scal[what + FIRST], scal[what + HEADS]

        def one_head(i, carry):
            start = base + (pl.program_id(0) * heads + i - first) * tiles
            begin = jnp.clip(low - start, 0, tiles)
            end = jnp.clip(high - start, 0, tiles)
            lanes = lanes_of(i)

            def step(t, group):
                q, k, v = get(rows_of(first_tile + t, group), lanes)
                item = pl.ds(start + t - low, group)
                box[item, 0:TILE] = q.reshape(group, TILE, HD)
                box[item, TILE : 2 * TILE] = k.reshape(group, TILE, HD)
                box[item, 2 * TILE : 3 * TILE] = v.reshape(group, TILE, HD)

            in_groups(begin, end, step)
            return carry

        before = first - pl.program_id(0) * heads
        lax.fori_loop(
            jnp.clip(before, 0, heads), jnp.clip(before + count, 0, heads), one_head, 0
        )
        base = base + tiles * count


def send_off(box, outs, sems):
    @pl.when(pl.program_id(0) == pl.num_programs(0) - 1)
    def _():
        at, copies = 0, []
        for i, out in enumerate(outs):
            copies.append(pltpu.make_async_copy(box.at[pl.ds(at, out.shape[0])], out, sems.at[i]))
            at += out.shape[0]
        for copy in copies:
            copy.start()
        for copy in copies:
            copy.wait()


def first_kernel(scal, q_ref, k_ref, v_ref, cos_ref, sin_ref, *rest):
    outs, box, sems = rest[:-2], rest[-2], rest[-1]

    def get(rows, lanes):
        cosine, sine = cos_ref[rows, :], sin_ref[rows, :]
        return (
            turn(q_ref[rows, lanes], cosine, sine),
            turn(k_ref[rows, lanes], cosine, sine),
            v_ref[rows, lanes],
        )

    pack(scal, 0, box.shape[0], box, q_ref.shape[1] // HD, get)
    send_off(box, outs, sems)


def second_kernel(
    low, scal, q_ref, k_ref, v_ref, cos_ref, sin_ref, swap_ref, wt_ref, mod_ref, qr_ref, kr_ref, w_ref, shift_ref, *rest
):
    outs, box, sems = rest[:-2], rest[-2], rest[-1]
    rows = q_ref.shape[0]
    heads = q_ref.shape[1] // HD
    wide = swap_ref.shape[0]

    @pl.when(pl.program_id(0) == 0)
    def _():
        w = wt_ref[...].astype(jnp.float32)
        scaled = w * (1.0 + mod_ref[1:2, :])
        high = scaled.astype(jnp.bfloat16)
        low = (scaled - high.astype(jnp.float32)).astype(jnp.bfloat16)
        w_ref[...] = jnp.concatenate([high, low], axis=0)
        shift = jnp.sum(w * mod_ref[0:1, :], axis=1, keepdims=True)
        shift_ref[...] = jnp.broadcast_to(shift, shift_ref.shape)

    for source, to in ((q_ref, qr_ref), (k_ref, kr_ref)):
        for h in range(0, heads, wide // HD):
            for j in range(rows // BLK):
                at = slice(j * BLK, (j + 1) * BLK)
                x = source[at, h * HD : h * HD + wide]
                swapped = jnp.dot(x, swap_ref[: x.shape[1], : x.shape[1]], preferred_element_type=jnp.float32)
                for i in range(x.shape[1] // HD):
                    lanes = slice(i * HD, (i + 1) * HD)
                    to[at, (h + i) * HD : (h + i + 1) * HD] = (
                        x[:, lanes].astype(jnp.float32) * cos_ref[at, :] + swapped[:, lanes] * sin_ref[at, :]
                    ).astype(jnp.bfloat16)

    def get(rows, lanes):
        return qr_ref[rows, lanes], kr_ref[rows, lanes], v_ref[rows, lanes]

    pack(scal, low, low + box.shape[0], box, heads, get)
    send_off(box, outs, sems)


def dot_t(a, b):
    return lax.dot_general(a, b, (((1,), (1,)), ((), ())), preferred_element_type=jnp.float32)


def attend_rows(q, k, v_ones, masked):
    s = masked(dot_t(q, k))
    top = jnp.max(s, axis=1, keepdims=True)
    weight = jnp.exp2(s * SCALE2 - top * SCALE2).astype(jnp.bfloat16)
    both = jnp.dot(weight, v_ones, preferred_element_type=jnp.float32)
    return (both[:, :HD] / both[:, HD:]).astype(jnp.bfloat16)


def projected(o_ref, w_ref, out_ref, rows):
    for j in range(rows // BLK):
        at = slice(j * BLK, (j + 1) * BLK)
        z = dot_t(o_ref[at, :], w_ref[...])
        z = z + pltpu.roll(z, HD // 2, 1)
        lane = lax.broadcasted_iota(jnp.int32, z.shape, 1)
        squares = jnp.zeros(z.shape, jnp.float32)
        for h in range(o_ref.shape[1] // HD):
            wide = o_ref[at, h * HD : (h + 1) * HD].astype(jnp.float32)
            squares = squares + wide * wide
        total = jnp.sum(squares, axis=1, keepdims=True)
        out_ref[at, :] = jnp.where(lane < HD // 2, z, jnp.where(lane == HD // 2, total, 0.0))


def inner_kernel(scal, q_ref, k_ref, v_ref, w_ref, qv_ref, kv_ref, out_ref, o_ref):
    g = pl.program_id(0)
    rows, width = q_ref.shape
    ones = jnp.ones((rows, HD), jnp.bfloat16)
    for j in range(rows // BLK):
        at = pl.ds(j * BLK, BLK)
        same = qv_ref[at, :] == kv_ref[...]
        for i in range(width // HD):
            lanes = slice(i * HD, (i + 1) * HD)
            v_ones = jnp.concatenate([v_ref[:, lanes], ones], axis=1)
            o_ref[at, pl.ds(pl.multiple_of(g * width + i * HD, HD), HD)] = attend_rows(
                q_ref[at, lanes], k_ref[:, lanes], v_ones, lambda s: jnp.where(same, s, NEG)
            )

    @pl.when(g == pl.num_programs(0) - 1)
    def _():
        projected(o_ref, w_ref, out_ref, rows)


def across(scal, at, offset, low, high, q_ref, k_ref, v_ref, items, w_ref, qs, ks, vs, o_ref, zz):
    rows = q_ref.shape[0]
    left, right = scal[at + LB], scal[at + RB]
    lead = left * TILE - scal[at + LROWS]
    end = left * TILE + scal[at + RROWS]
    blocks = jnp.minimum(lax.div((left + right) * TILE + BLK - 1, BLK), rows // BLK)

    def two_heads(n, i, carry):
        heads = [jnp.minimum(low + 2 * i + u, high - 1) for u in range(2)]

        def own(t, group):
            source = rows_of(scal[at + OWN_FROM] + t, group)
            to = rows_of(scal[at + OWN_TO] + t, group)
            for u, s in enumerate(heads):
                lanes = lanes_of(scal[at + HEAD0] + s)
                qs[u, to, :] = q_ref[source, lanes]
                ks[u, to, :] = k_ref[source, lanes]
                vs[u, to, :HD] = v_ref[source, lanes]

        def foreign(t, group):
            to = rows_of(scal[at + FAR_TO] + t, group)
            for u, s in enumerate(heads):
                item = pl.ds(scal[at + SOURCE] + offset + s * scal[at + FAR] + t, group)
                qs[u, to, :] = items[item, 0:TILE].reshape(group * TILE, HD)
                ks[u, to, :] = items[item, TILE : 2 * TILE].reshape(group * TILE, HD)
                vs[u, to, :HD] = items[item, 2 * TILE : 3 * TILE].reshape(group * TILE, HD)

        in_groups(0, scal[at + OWN], own)
        in_groups(0, scal[at + FAR], foreign)
        width = n * BLK
        if width == rows:

            @pl.when((left + right) * TILE > rows)
            def _():
                row = lax.broadcasted_iota(jnp.int32, (TILE, HD), 0)
                for ref in (qs, ks, vs):
                    for u in range(2):
                        first, last = ref[u, 0:TILE, :HD], ref[u, rows : rows + TILE, :HD]
                        ref[u, 0:TILE, :HD] = jnp.where(row < lead, last, first)

        place = lax.broadcasted_iota(jnp.int32, (1, width), 1)
        valid = ((place >= lead) & (place < end)) | (place + rows < end)
        bias = jnp.where(valid, 0.0, NEG)
        for j in range(n):
            mine = slice(j * BLK, (j + 1) * BLK)
            for u, s in enumerate(heads):
                o_ref[mine, lanes_of(scal[at + HEAD0] + s)] = attend_rows(
                    qs[u, mine, :], ks[u, 0:width, :], vs[u, 0:width, :], lambda x: x + bias
                )
        return carry

    for n in range(1, rows // BLK + 1):

        @pl.when((blocks == n) & (high > low))
        def _(n=n):
            o_ref[0 : n * BLK, :] = jnp.zeros((n * BLK, o_ref.shape[1]), o_ref.dtype)
            lax.fori_loop(
                0, lax.shift_right_logical(high - low + 1, 1), functools.partial(two_heads, n), 0
            )
            projected(o_ref, w_ref, zz, n * BLK)
            zz[rows : 2 * rows, :] = zz[0:rows, :]

    @pl.when(high <= low)
    def _():
        zz[...] = jnp.zeros_like(zz)

    return zz[pl.ds(pl.multiple_of(left * TILE, TILE), rows), :]


def fetch(scal, at, offset, low, high, places, boxes, items, sems, qs, ks, vs):
    begin = scal[at + SOURCE] + offset + low * scal[at + FAR]
    end = scal[at + SOURCE] + offset + high * scal[at + FAR]
    copies = [
        pltpu.make_async_copy(box, items.at[pl.ds(place, box.shape[0])], sems.at[i])
        for i, (place, box) in enumerate(zip(places, boxes))
    ]
    needed = [(high > low) & (begin < place + box.shape[0]) & (end > place) for place, box in zip(places, boxes)]
    for copy, need in zip(copies, needed):
        pl.when(need)(copy.start)
    qs[...] = jnp.zeros_like(qs)
    ks[...] = jnp.zeros_like(ks)
    vs[:, :, :HD] = jnp.zeros((*vs.shape[:2], HD), vs.dtype)
    vs[:, :, HD:] = jnp.ones((*vs.shape[:2], HD), vs.dtype)
    for copy, need in zip(copies, needed):
        pl.when(need)(copy.wait)


def of_boundary(scal, at, shape, mine):
    row = lax.broadcasted_iota(jnp.int32, shape, 0)
    tail = jnp.where(row >= shape[0] - scal[at + LROWS], 1, 0)
    head = jnp.where(row < scal[at + RROWS], 1, 0)
    right_is_mine = (scal[at + SIDE] == 0) == mine
    return jnp.where(right_is_mine, head, tail) == 1


def send_back(scal, at, z, back_ref):
    lane = lax.broadcasted_iota(jnp.int32, z.shape, 1)
    back = jnp.where(of_boundary(scal, at, z.shape, False), z, 0.0)
    high = back.astype(jnp.bfloat16).astype(jnp.float32)
    both = jnp.where(lane == HD // 2 + 1, pltpu.roll(back - high, 1, 1), high)
    back_ref[...] = both.T[: back_ref.shape[0]].astype(jnp.bfloat16)


def early_kernel(places, at, scal, q_ref, k_ref, v_ref, w_ref, *rest):
    boxes, (out_ref, items, sems, *scratch) = rest[: len(places)], rest[len(places) :]
    high = scal[at + EARLY]
    fetch(scal, at, 0, 0, high, places, boxes, items, sems, *scratch[:3])
    out_ref[...] = across(scal, at, 0, 0, high, q_ref, k_ref, v_ref, items, w_ref, *scratch)


def last_kernel(
    places, passed_before, offset, scal, q_ref, k_ref, v_ref, w_ref, passed_ref, direct_ref, inner_a, inner_b, *rest
):
    boxes, rest = rest[: len(places)], rest[len(places) :]
    own_ref, pass_back_ref, direct_back_ref, items, sems, *scratch = rest

    def remaining(at, offset):
        low, high = scal[at + EARLY], scal[at + KEEP]
        fetch(scal, at, offset, low, high, places, boxes, items, sems, *scratch[:3])
        return across(scal, at, offset, low, high, q_ref, k_ref, v_ref, items, w_ref, *scratch)

    direct_z = direct_ref[...]
    if offset is not None:
        direct_z = direct_z + remaining(DIRECT, offset)
    passed_z = passed_ref[...] + remaining(PASS, -passed_before)
    send_back(scal, PASS, passed_z, pass_back_ref)
    send_back(scal, DIRECT, direct_z, direct_back_ref)
    own = inner_a[...] + inner_b[...]
    own = jnp.where(of_boundary(scal, DIRECT, own.shape, True), direct_z, own)
    own = jnp.where(of_boundary(scal, PASS, own.shape, True), passed_z, own)
    own_ref[...] = own.T[: own_ref.shape[0]]


def step_rows(video_ids, step_sizes):
    chosen = video_ids[:, None] == jnp.arange(step_sizes.shape[0], dtype=jnp.int32)[None, :]
    return jnp.sum(jnp.where(chosen, step_sizes[None, :], 0.0), axis=1)


def call(kernel, name, mib, scalars, operands, in_specs, outs, out_specs, scratch, grid=()):
    return pl.pallas_call(
        kernel,
        out_shape=outs,
        grid_spec=pltpu.PrefetchScalarGridSpec(
            num_scalar_prefetch=1, grid=grid, in_specs=in_specs, out_specs=out_specs,
            scratch_shapes=scratch,
        ),
        compiler_params=pltpu.CompilerParams(vmem_limit_bytes=mib * MIB),
        cost_estimate=pl.CostEstimate(flops=1, bytes_accessed=1, transcendentals=0),
        name=name,
    )(scalars, *operands)


def per_device(
    query_rows, key_rows, value_rows, positions, latents, w_head, modulation,
    guide_scale, step_sizes, lengths,
):
    rows, features = query_rows.shape[1], query_rows.shape[2]
    heads = features // HD
    count = lax.axis_size("req")
    here = lax.axis_index("req")
    first_row = here * rows
    _, padded, room = sizes(rows, heads)
    chunk = padded // CHUNKS
    late_sizes = (*[chunk] * (CHUNKS - 1), *MORE, room - padded - sum(MORE))

    angle = angles(positions)
    odd = (jnp.arange(HD, dtype=jnp.int32) % 2).astype(jnp.float32)
    cosine = jnp.cos(angle)
    sine = jnp.sin(angle) * (2.0 * odd - 1.0)[None, :]

    smem = pl.BlockSpec(memory_space=pltpu.SMEM)
    vmem = pl.BlockSpec(memory_space=pltpu.VMEM)
    hbm = pl.BlockSpec(memory_space=pl.ANY)
    parity = lax.axis_index("cfg")
    tie = lax.optimization_barrier
    scalars = pl.pallas_call(
        functools.partial(plan_kernel, rows, heads, count),
        out_shape=jax.ShapeDtypeStruct((SCALARS,), jnp.int32),
        in_specs=[smem],
        out_specs=smem,
        scratch_shapes=[
            pltpu.SMEM((count + 3,), jnp.int32),
            pltpu.SMEM((count + 3,), jnp.int32),
            pltpu.VMEM(((count + 3) * 8, 128), jnp.float32),
            pltpu.VMEM(((count + 3) * 8, 128), jnp.float32),
        ],
        name="plan",
    )(lengths)

    q, k, v = query_rows[0], key_rows[0], value_rows[0]

    def box(items):
        return jax.ShapeDtypeStruct((items, 3 * TILE, HD), jnp.bfloat16)

    def box_scratch(items):
        return pltpu.VMEM((items, 3 * TILE, HD), jnp.bfloat16)

    group = next(n for n in (5, 4, 3, 2, 1) if heads % n == 0)
    steps = heads // group
    head_block = pl.BlockSpec((rows, group * HD), lambda g, s: (0, g))
    table = pl.BlockSpec((rows, HD), lambda g, s: (0, 0))
    first = call(
        first_kernel, "pack_first", 56, scalars, (q, k, v, cosine, sine),
        [head_block] * 3 + [table] * 2, (box(chunk),), (hbm,),
        [box_scratch(chunk), pltpu.SemaphoreType.DMA((1,))], grid=(steps,),
    )
    pairs = [(i, i ^ 1) for i in range(count)]
    onward = [(i, i + 2) for i in range(0, count - 2, 2)] + [(i + 2, i) for i in range(1, count - 2, 2)]
    got = [lax.ppermute(first[0], "req", pairs)]

    after_first, _ = tie((scalars, first[0]))
    swap = jnp.asarray(numpy.eye(2 * HD)[numpy.arange(2 * HD) ^ 1], jnp.bfloat16)
    q_rot, k_rot, w_both, shift, *second = call(
        functools.partial(second_kernel, chunk), "turn_and_pack_rest", 32, after_first,
        (q, k, v, cosine, sine, swap, w_head.T, modulation),
        [head_block] * 3 + [table] * 2 + [vmem] * 3,
        (jax.ShapeDtypeStruct(q.shape, q.dtype), jax.ShapeDtypeStruct(k.shape, k.dtype),
         jax.ShapeDtypeStruct((HD, features), jnp.bfloat16),
         jax.ShapeDtypeStruct((HD // 2, HD), jnp.float32),
         *[box(n) for n in late_sizes]),
        (head_block, head_block, vmem, vmem, *[hbm] * len(late_sizes)),
        [box_scratch(sum(late_sizes)), pltpu.SemaphoreType.DMA((len(late_sizes),))], grid=(steps,),
    )
    got += [lax.ppermute(x, "req", pairs) for x in second[:CHUNKS]]
    second = second[CHUNKS:]

    own_rows = first_row + jnp.arange(rows, dtype=jnp.int32)
    video = jnp.sum((jnp.cumsum(lengths)[None, :] <= own_rows[:, None]).astype(jnp.int32), axis=1)
    step_of_row = step_rows(video, step_sizes)

    def inner(when, first_step, step_count):
        block = pl.BlockSpec((rows, group * HD), lambda g, s: (0, g + first_step))
        width = step_count * group * HD
        return call(
            inner_kernel, "inner_videos", 20, when,
            (q_rot, k_rot, v, w_both, video[:, None], video[None, :]),
            [block] * 3 + [pl.BlockSpec((HD, width), lambda g, s: (0, first_step // step_count))] + [vmem] * 2, jax.ShapeDtypeStruct((rows, HD), jnp.float32), vmem,
            [pltpu.VMEM((rows, width), jnp.bfloat16)], grid=(step_count,),
        )

    inner_a = inner(scalars, 0, steps // 2)
    got[0], inner_a = tie((got[0], inner_a))
    when_b, got[1] = tie((scalars, got[1]))
    inner_b = inner(when_b, steps // 2, steps - steps // 2)
    got[1], inner_b = tie((got[1], inner_b))
    when_early, got[3] = tie((scalars, got[3]))
    passed = [lax.ppermute(x, "req", onward) for x in got[:CHUNKS]]

    work = [
        pltpu.VMEM((2, rows + TILE, HD), jnp.bfloat16),
        pltpu.VMEM((2, rows + TILE, HD), jnp.bfloat16),
        pltpu.VMEM((2, rows + TILE, 2 * HD), jnp.bfloat16),
        pltpu.VMEM((rows, features), jnp.bfloat16),
        pltpu.VMEM((2 * rows, HD), jnp.float32),
    ]
    partial = jax.ShapeDtypeStruct((rows, HD), jnp.float32)
    lanes = HD // 2 + TILE
    sent_back = jax.ShapeDtypeStruct((lanes, rows), jnp.bfloat16)

    def on_videos_across(kernel, name, when, boxes, outs, others, q_rot, k_rot, v, w_both):
        places = [0]
        for x in boxes:
            places.append(places[-1] + x.shape[0])
        return call(
            kernel(tuple(places[:-1])), name, 24, when, (q_rot, k_rot, v, w_both, *others, *boxes),
            [vmem] * (4 + len(others)) + [hbm] * len(boxes), outs, jax.tree.map(lambda _: vmem, outs),
            [box_scratch(places[-1]), pltpu.SemaphoreType.DMA((len(boxes),)), *work],
        )

    def early_on(at, name, when, boxes):
        return on_videos_across(
            lambda places: functools.partial(early_kernel, places, at), name, when, boxes,
            partial, (), q_rot, k_rot, v, w_both,
        )

    early = early_on(PASS, "videos_across_early", when_early, passed[: CHUNKS - 1])
    when_direct, early = tie((scalars, early))
    direct_z = early_on(DIRECT, "videos_across_direct", when_direct, got)

    def last(pieces):
        def branch(passed, got, second, q_rot, k_rot, v, w_both, *others):
            boxes, offset = passed[CHUNKS - 2 :], None
            if pieces:
                boxes = [*boxes, *got, *[lax.ppermute(x, "req", pairs) for x in second[:pieces]]]
                offset = 2 * chunk
            return on_videos_across(
                lambda places: functools.partial(last_kernel, places, chunk * (CHUNKS - 2), offset),
                "videos_across_last", scalars, boxes,
                (jax.ShapeDtypeStruct((lanes, rows), jnp.float32), sent_back, sent_back),
                others, q_rot, k_rot, v, w_both,
            )

        return branch

    most = scalars[MOST]
    limits = [padded + sum(MORE[: i + 1]) for i in range(len(MORE))]
    level = sum((most > limit).astype(jnp.int32) for limit in limits)
    level, direct_z = tie((level, direct_z))
    own, to_beyond, to_direct = lax.switch(
        level, [last(i) for i in range(len(MORE) + 1)], passed, got, second,
        q_rot, k_rot, v, w_both, early, direct_z, inner_a, inner_b,
    )
    back_direct = lax.ppermute(to_direct, "req", pairs)
    beyond = [(i, i + 1) for i in range(1, count - 1, 2)] + [(i + 1, i) for i in range(1, count - 1, 2)]
    back_beyond = lax.ppermute(to_beyond, "req", beyond)
    total = own + back_direct.astype(jnp.float32) + back_beyond.astype(jnp.float32)
    values = HD // 2
    squares = total[values : values + 1] + total[values + 1 : values + 2]
    velocity = total[:values] * lax.rsqrt(squares / features + 1e-06) + shift[:, :1]

    width = latents.shape[1]
    mine = lax.dynamic_slice_in_dim(velocity, parity * width, width, 0)
    theirs = lax.dynamic_slice_in_dim(velocity, (1 - parity) * width, width, 0)
    partner = lax.ppermute(theirs, "cfg", [(0, 1), (1, 0)])
    conditional = jnp.where(parity == 0, mine, partner)
    unconditional = jnp.where(parity == 0, partner, mine)
    guided = unconditional + guide_scale[0] * (conditional - unconditional)
    return (latents.T + step_of_row[None, :] * guided).T


def solution(mesh):
    in_specs = (
        P("cfg", "req", None), P("cfg", "req", None), P("cfg", "req", None),
        P(None, "req"), P("req", "cfg"), P(), P(), P(), P(), P(),
    )
    return jax.shard_map(
        per_device, mesh=mesh, in_specs=in_specs, out_specs=P("req", "cfg"), check_vma=False
    )
```

```python
import functools
import math

import jax
import jax.numpy as jnp
import numpy
from jax import lax
from jax.experimental import pallas as pl
from jax.experimental.pallas import tpu as pltpu
from jax.sharding import PartitionSpec as P

HD = 128
TILE = 16
BLK = 128
CHUNKS = 4
MORE = 48
EXTRA = 32
EARLY_CHUNKS = 2
rope_theta = 10000.0
NEG = -1e30
SCALE2 = math.log2(math.e) / math.sqrt(HD)

PASS, DIRECT = 0, 16
LB, RB, LROWS, RROWS, HEAD0, KEEP, EARLY, SOURCE = range(8)
OWN_FROM, OWN_TO, OWN, FAR_TO, FAR, SIDE = range(8, 14)
SEND = 32
ROW, TILES, FIRST, HEADS = range(4)
MOST, INNER_FROM, INNER_TO = 40, 41, 42
SCALARS = 48
MIB = 1024 * 1024


def sizes(rows, heads):
    tiles = rows // TILE
    cap = max(
        min(max(a * n, (tiles + 1 - a) * (heads - n)) for n in range(heads + 1))
        for a in range(1, tiles + 1)
    )
    padded = -(-cap // TILE) * TILE
    return cap, padded, 2 * padded


def angles(positions):
    pair_total = HD // 2
    side_pairs = HD // 6
    time_pairs = pair_total - 2 * side_pairs
    column = jnp.arange(HD, dtype=jnp.int32) // 2
    in_time = column < time_pairs
    in_height = (column >= time_pairs) & (column < time_pairs + side_pairs)
    in_width = column >= time_pairs + side_pairs
    local_index = jnp.where(
        in_time, column, jnp.where(in_height, column - time_pairs, column - time_pairs - side_pairs)
    )
    axis_pairs = jnp.where(in_time, time_pairs, side_pairs)
    frequency = jnp.exp(
        -(local_index.astype(jnp.float32) / axis_pairs.astype(jnp.float32)) * math.log(rope_theta)
    )
    selector = jnp.stack([in_time, in_height, in_width]).astype(jnp.float32) * frequency[None, :]
    placed = positions.astype(jnp.float32)
    return (
        placed[0][:, None] * selector[0][None, :]
        + placed[1][:, None] * selector[1][None, :]
        + placed[2][:, None] * selector[2][None, :]
    )


def plan_kernel(rows, heads, count, lengths, out, ls, rs, split, least):
    cap, padded, _ = sizes(rows, heads)
    here = lax.axis_index("req")

    def clear(b, carry):
        ls[b] = 0
        rs[b] = 0
        return carry

    lax.fori_loop(0, count + 3, clear, 0)

    def one_video(v, start):
        end = start + lengths[v]
        b = lax.div(end - 1, rows)
        at = b * rows

        @pl.when(start < at)
        def _():
            ls[b] = at - start
            rs[b] = end - at

        return end

    lax.fori_loop(0, lengths.shape[0], one_video, 0)
    budget = 3.0 * lax.broadcasted_iota(jnp.int32, (8, 128), 1).astype(jnp.float32)
    split[...] = jnp.zeros_like(split)

    def tiles_of(x):
        return lax.shift_right_logical(x + TILE - 1, 4)

    def eight(b):
        return pl.ds(pl.multiple_of(b * 8, 8), 8)

    def per_tile(x, tiles):
        return jnp.floor((x + 0.5) / jnp.maximum(tiles, 1.0))

    def facts(b):
        direct = lax.rem(b, 2).astype(jnp.float32)
        lt, rt = tiles_of(ls[b]).astype(jnp.float32), tiles_of(rs[b]).astype(jnp.float32)
        return lt, rt, padded + direct * 1e6

    def from_right(i, load):
        b = count - 1 - i
        lt, rt, limit = facts(b)
        room = jnp.minimum(budget - load, limit)
        n = jnp.where(rt > 0.0, jnp.maximum(heads - per_tile(room, rt), 0.0), 0.0)
        least[eight(b)] = jnp.where(room >= 0.0, n, 1e6)
        return lt * n

    def from_left(b, carry):
        load, ok = carry
        lt, rt, limit = facts(b)
        room = jnp.minimum(budget - load, limit)
        most = jnp.where(lt > 0.0, jnp.minimum(per_tile(room, lt), float(heads)), 0.0)
        low = least[eight(b)]
        even = jnp.floor(heads * rt / jnp.maximum(lt + rt, 1.0) + 0.5)
        n = jnp.minimum(most, jnp.maximum(low, even))
        split[eight(b)] = n
        return rt * (heads - n), jnp.where((room >= 0.0) & (low <= most), ok, 0.0)

    zero = jnp.zeros((8, 128), jnp.float32)
    lax.fori_loop(0, count - 1, from_right, zero)
    load, ok = lax.fori_loop(1, count, from_left, (zero, zero + 1.0))
    ok = jnp.where(load <= budget, ok, 0.0)
    most = jnp.min(jnp.where(ok > 0.0, budget, 1e9))
    out[MOST] = most.astype(jnp.int32)

    def head_split(b):
        n = split[eight(b)]
        return jnp.max(jnp.where(budget == most, n, 0.0)).astype(jnp.int32)

    even = lax.rem(here, 2) == 0
    beyond = jnp.where(even, here + 2, here - 1)
    n_left, n_right, n_beyond = head_split(here), head_split(here + 1), head_split(beyond)
    partner_passes = jnp.where(
        even,
        tiles_of(ls[beyond]) * n_beyond,
        tiles_of(rs[beyond]) * (heads - n_beyond),
    )
    for side, b, n in ((0, here, n_left), (1, here + 1, n_right)):
        direct = jnp.logical_not(even) if side == 0 else even
        at = jnp.where(direct, DIRECT, PASS)
        lt, rt = tiles_of(ls[b]), tiles_of(rs[b])
        none = jnp.where(lt > 0, 0, heads)
        keep = n if side == 0 else jnp.maximum(heads - n - none, 0)
        far = lt if side == 0 else rt
        out[at + LB], out[at + RB] = lt, rt
        out[at + LROWS], out[at + RROWS] = ls[b], rs[b]
        out[at + HEAD0] = 0 if side == 0 else n
        out[at + KEEP] = keep
        source = jnp.where(direct, partner_passes, 0)
        there = jnp.where(direct, padded + MORE, padded // CHUNKS * EARLY_CHUNKS) - source
        out[at + EARLY] = jnp.minimum(keep, lax.div(jnp.maximum(there, 0), jnp.maximum(far, 1)))
        out[at + SOURCE] = source
        out[at + OWN_FROM] = 0 if side == 0 else rows // TILE - lt
        out[at + OWN_TO] = lt if side == 0 else 0
        out[at + OWN] = rt if side == 0 else lt
        out[at + FAR_TO] = 0 if side == 0 else lt
        out[at + FAR] = far
        out[at + SIDE] = side
        to = SEND + jnp.where(direct, 4, 0)
        out[to + ROW] = 0 if side == 0 else rows - TILE * lt
        out[to + TILES] = rt if side == 0 else lt
        out[to + FIRST] = n if side == 0 else 0
        out[to + HEADS] = jnp.maximum(heads - n - none, 0) if side == 0 else n
    out[INNER_FROM] = rs[here]
    out[INNER_TO] = rows - ls[here + 1]


def in_groups(low, high, step):
    count = high - low

    def run(group, times):
        def body(i, carry):
            step(jnp.minimum(low + group * i, high - group), group)
            return carry

        lax.fori_loop(0, times, body, 0)

    run(8, jnp.where(count >= 8, lax.shift_right_logical(count + 7, 3), 0))
    run(2, jnp.where((count >= 2) & (count < 8), lax.shift_right_logical(count + 1, 1), 0))
    run(1, jnp.where(count == 1, 1, 0))


def lanes_of(h):
    return pl.ds(pl.multiple_of(h * HD, HD), HD)


def rows_of(t, group):
    return pl.ds(pl.multiple_of(t * TILE, TILE), group * TILE)


def turn(x, cosine, sine):
    wide = x.astype(jnp.float32)
    even = lax.rem(lax.broadcasted_iota(jnp.int32, wide.shape, 1), 2) == 0
    swapped = jnp.where(even, pltpu.roll(wide, HD - 1, 1), pltpu.roll(wide, 1, 1))
    return (wide * cosine + swapped * sine).astype(jnp.bfloat16)


def pack(scal, low, high, box, heads, get):
    base = 0
    for what in (SEND, SEND + 4):
        first_tile = lax.shift_right_logical(scal[what + ROW], 4)
        tiles, first, count = scal[what + TILES], scal[what + FIRST], scal[what + HEADS]

        def one_head(i, carry):
            start = base + (pl.program_id(0) * heads + i - first) * tiles
            begin = jnp.clip(low - start, 0, tiles)
            end = jnp.clip(high - start, 0, tiles)
            lanes = lanes_of(i)

            def step(t, group):
                q, k, v = get(rows_of(first_tile + t, group), lanes)
                item = pl.ds(start + t - low, group)
                box[item, 0:TILE] = q.reshape(group, TILE, HD)
                box[item, TILE : 2 * TILE] = k.reshape(group, TILE, HD)
                box[item, 2 * TILE : 3 * TILE] = v.reshape(group, TILE, HD)

            in_groups(begin, end, step)
            return carry

        before = first - pl.program_id(0) * heads
        lax.fori_loop(
            jnp.clip(before, 0, heads), jnp.clip(before + count, 0, heads), one_head, 0
        )
        base = base + tiles * count


def send_off(box, outs, sems):
    @pl.when(pl.program_id(0) == pl.num_programs(0) - 1)
    def _():
        at, copies = 0, []
        for i, out in enumerate(outs):
            copies.append(pltpu.make_async_copy(box.at[pl.ds(at, out.shape[0])], out, sems.at[i]))
            at += out.shape[0]
        for copy in copies:
            copy.start()
        for copy in copies:
            copy.wait()


def first_kernel(scal, q_ref, k_ref, v_ref, cos_ref, sin_ref, *rest):
    outs, box, sems = rest[:-2], rest[-2], rest[-1]

    def get(rows, lanes):
        cosine, sine = cos_ref[rows, :], sin_ref[rows, :]
        return (
            turn(q_ref[rows, lanes], cosine, sine),
            turn(k_ref[rows, lanes], cosine, sine),
            v_ref[rows, lanes],
        )

    pack(scal, 0, box.shape[0], box, q_ref.shape[1] // HD, get)
    send_off(box, outs, sems)


def second_kernel(
    low, scal, q_ref, k_ref, v_ref, cos_ref, sin_ref, swap_ref, wt_ref, mod_ref, qr_ref, kr_ref, w_ref, shift_ref, *rest
):
    outs, box, sems = rest[:-3], rest[-2], rest[-1]
    rows = q_ref.shape[0]
    heads = q_ref.shape[1] // HD
    wide = swap_ref.shape[0]

    @pl.when(pl.program_id(0) == 0)
    def _():
        w = wt_ref[...].astype(jnp.float32)
        scaled = w * (1.0 + mod_ref[1:2, :])
        high = scaled.astype(jnp.bfloat16)
        low = (scaled - high.astype(jnp.float32)).astype(jnp.bfloat16)
        w_ref[...] = jnp.concatenate([high, low], axis=0)
        shift = jnp.sum(w * mod_ref[0:1, :], axis=1, keepdims=True)
        shift_ref[...] = jnp.broadcast_to(shift, shift_ref.shape)

    for source, to in ((q_ref, qr_ref), (k_ref, kr_ref)):
        for h in range(0, heads, wide // HD):
            for j in range(rows // BLK):
                at = slice(j * BLK, (j + 1) * BLK)
                x = source[at, h * HD : h * HD + wide]
                swapped = jnp.dot(x, swap_ref[: x.shape[1], : x.shape[1]], preferred_element_type=jnp.float32)
                for i in range(x.shape[1] // HD):
                    lanes = slice(i * HD, (i + 1) * HD)
                    to[at, (h + i) * HD : (h + i + 1) * HD] = (
                        x[:, lanes].astype(jnp.float32) * cos_ref[at, :] + swapped[:, lanes] * sin_ref[at, :]
                    ).astype(jnp.bfloat16)

    def get(rows, lanes):
        return qr_ref[rows, lanes], kr_ref[rows, lanes], v_ref[rows, lanes]

    pack(scal, low, low + box.shape[0], box, heads, get)
    send_off(box, outs, sems)


def dot_t(a, b):
    return lax.dot_general(a, b, (((1,), (1,)), ((), ())), preferred_element_type=jnp.float32)


def attend_rows(q, k, v_ones, masked):
    s = masked(dot_t(q, k))
    top = jnp.max(s, axis=1, keepdims=True)
    weight = jnp.exp2(s * SCALE2 - top * SCALE2).astype(jnp.bfloat16)
    both = jnp.dot(weight, v_ones, preferred_element_type=jnp.float32)
    return (both[:, :HD] / both[:, HD:]).astype(jnp.bfloat16)


def projected(o_ref, w_ref, out_ref, rows):
    for j in range(rows // BLK):
        at = slice(j * BLK, (j + 1) * BLK)
        z = dot_t(o_ref[at, :], w_ref[...])
        z = z + pltpu.roll(z, HD // 2, 1)
        lane = lax.broadcasted_iota(jnp.int32, z.shape, 1)
        squares = jnp.zeros(z.shape, jnp.float32)
        for h in range(o_ref.shape[1] // HD):
            wide = o_ref[at, h * HD : (h + 1) * HD].astype(jnp.float32)
            squares = squares + wide * wide
        total = jnp.sum(squares, axis=1, keepdims=True)
        out_ref[at, :] = jnp.where(lane < HD // 2, z, jnp.where(lane == HD // 2, total, 0.0))


def inner_kernel(scal, q_ref, k_ref, v_ref, w_ref, qv_ref, kv_ref, out_ref, o_ref):
    g = pl.program_id(0)
    rows, width = q_ref.shape
    ones = jnp.ones((rows, HD), jnp.bfloat16)
    for j in range(rows // BLK):
        at = pl.ds(j * BLK, BLK)
        same = qv_ref[at, :] == kv_ref[...]
        for i in range(width // HD):
            lanes = slice(i * HD, (i + 1) * HD)
            v_ones = jnp.concatenate([v_ref[:, lanes], ones], axis=1)
            o_ref[at, pl.ds(pl.multiple_of(g * width + i * HD, HD), HD)] = attend_rows(
                q_ref[at, lanes], k_ref[:, lanes], v_ones, lambda s: jnp.where(same, s, NEG)
            )

    @pl.when(g == pl.num_programs(0) - 1)
    def _():
        projected(o_ref, w_ref, out_ref, rows)


def across(scal, at, offset, low, high, q_ref, k_ref, v_ref, items, w_ref, qs, ks, vs, o_ref, zz):
    rows = q_ref.shape[0]
    left, right = scal[at + LB], scal[at + RB]
    lead = left * TILE - scal[at + LROWS]
    end = left * TILE + scal[at + RROWS]
    blocks = jnp.minimum(lax.div((left + right) * TILE + BLK - 1, BLK), rows // BLK)

    def two_heads(n, i, carry):
        heads = [jnp.minimum(low + 2 * i + u, high - 1) for u in range(2)]

        def own(t, group):
            source = rows_of(scal[at + OWN_FROM] + t, group)
            to = rows_of(scal[at + OWN_TO] + t, group)
            for u, s in enumerate(heads):
                lanes = lanes_of(scal[at + HEAD0] + s)
                qs[u, to, :] = q_ref[source, lanes]
                ks[u, to, :] = k_ref[source, lanes]
                vs[u, to, :HD] = v_ref[source, lanes]

        def foreign(t, group):
            to = rows_of(scal[at + FAR_TO] + t, group)
            for u, s in enumerate(heads):
                item = pl.ds(scal[at + SOURCE] + offset + s * scal[at + FAR] + t, group)
                qs[u, to, :] = items[item, 0:TILE].reshape(group * TILE, HD)
                ks[u, to, :] = items[item, TILE : 2 * TILE].reshape(group * TILE, HD)
                vs[u, to, :HD] = items[item, 2 * TILE : 3 * TILE].reshape(group * TILE, HD)

        in_groups(0, scal[at + OWN], own)
        in_groups(0, scal[at + FAR], foreign)
        width = n * BLK
        if width == rows:

            @pl.when((left + right) * TILE > rows)
            def _():
                row = lax.broadcasted_iota(jnp.int32, (TILE, HD), 0)
                for ref in (qs, ks, vs):
                    for u in range(2):
                        first, last = ref[u, 0:TILE, :HD], ref[u, rows : rows + TILE, :HD]
                        ref[u, 0:TILE, :HD] = jnp.where(row < lead, last, first)

        place = lax.broadcasted_iota(jnp.int32, (1, width), 1)
        valid = ((place >= lead) & (place < end)) | (place + rows < end)
        bias = jnp.where(valid, 0.0, NEG)
        for j in range(n):
            mine = slice(j * BLK, (j + 1) * BLK)
            for u, s in enumerate(heads):
                o_ref[mine, lanes_of(scal[at + HEAD0] + s)] = attend_rows(
                    qs[u, mine, :], ks[u, 0:width, :], vs[u, 0:width, :], lambda x: x + bias
                )
        return carry

    for n in range(1, rows // BLK + 1):

        @pl.when((blocks == n) & (high > low))
        def _(n=n):
            o_ref[0 : n * BLK, :] = jnp.zeros((n * BLK, o_ref.shape[1]), o_ref.dtype)
            lax.fori_loop(
                0, lax.shift_right_logical(high - low + 1, 1), functools.partial(two_heads, n), 0
            )
            projected(o_ref, w_ref, zz, n * BLK)
            zz[rows : 2 * rows, :] = zz[0:rows, :]

    @pl.when(high <= low)
    def _():
        zz[...] = jnp.zeros_like(zz)

    return zz[pl.ds(pl.multiple_of(left * TILE, TILE), rows), :]


def fetch(scal, at, offset, low, high, places, boxes, items, sems, qs, ks, vs):
    begin = scal[at + SOURCE] + offset + low * scal[at + FAR]
    end = scal[at + SOURCE] + offset + high * scal[at + FAR]
    copies = [
        pltpu.make_async_copy(box, items.at[pl.ds(place, box.shape[0])], sems.at[i])
        for i, (place, box) in enumerate(zip(places, boxes))
    ]
    needed = [(high > low) & (begin < place + box.shape[0]) & (end > place) for place, box in zip(places, boxes)]
    for copy, need in zip(copies, needed):
        pl.when(need)(copy.start)
    qs[...] = jnp.zeros_like(qs)
    ks[...] = jnp.zeros_like(ks)
    vs[:, :, :HD] = jnp.zeros((*vs.shape[:2], HD), vs.dtype)
    vs[:, :, HD:] = jnp.ones((*vs.shape[:2], HD), vs.dtype)
    for copy, need in zip(copies, needed):
        pl.when(need)(copy.wait)


def of_boundary(scal, at, shape, mine):
    row = lax.broadcasted_iota(jnp.int32, shape, 0)
    tail = jnp.where(row >= shape[0] - scal[at + LROWS], 1, 0)
    head = jnp.where(row < scal[at + RROWS], 1, 0)
    right_is_mine = (scal[at + SIDE] == 0) == mine
    return jnp.where(right_is_mine, head, tail) == 1


def send_back(scal, at, z, back_ref):
    lane = lax.broadcasted_iota(jnp.int32, z.shape, 1)
    back = jnp.where(of_boundary(scal, at, z.shape, False), z, 0.0)
    high = back.astype(jnp.bfloat16).astype(jnp.float32)
    both = jnp.where(lane == HD // 2 + 1, pltpu.roll(back - high, 1, 1), high)
    back_ref[...] = both.T[: back_ref.shape[0]].astype(jnp.bfloat16)


def early_kernel(places, at, scal, q_ref, k_ref, v_ref, w_ref, *rest):
    boxes, (out_ref, items, sems, *scratch) = rest[: len(places)], rest[len(places) :]
    high = scal[at + EARLY]
    fetch(scal, at, 0, 0, high, places, boxes, items, sems, *scratch[:3])
    out_ref[...] = across(scal, at, 0, 0, high, q_ref, k_ref, v_ref, items, w_ref, *scratch)


def last_kernel(
    places, offsets, scal, q_ref, k_ref, v_ref, w_ref, passed_ref, direct_ref, inner_a, inner_b, *rest
):
    boxes, rest = rest[: len(places)], rest[len(places) :]
    own_ref, pass_back_ref, direct_back_ref, items, sems, *scratch = rest

    def remaining(at, offset):
        low, high = scal[at + EARLY], scal[at + KEEP]
        fetch(scal, at, offset, low, high, places, boxes, items, sems, *scratch[:3])
        return across(scal, at, offset, low, high, q_ref, k_ref, v_ref, items, w_ref, *scratch)

    direct_z = direct_ref[...] + remaining(DIRECT, offsets[1])
    send_back(scal, DIRECT, direct_z, direct_back_ref)
    passed_z = passed_ref[...] + remaining(PASS, offsets[0])
    send_back(scal, PASS, passed_z, pass_back_ref)
    own = inner_a[...] + inner_b[...]
    own = jnp.where(of_boundary(scal, DIRECT, own.shape, True), direct_z, own)
    own = jnp.where(of_boundary(scal, PASS, own.shape, True), passed_z, own)
    own_ref[...] = own.T[: own_ref.shape[0]]


def step_rows(video_ids, step_sizes):
    chosen = video_ids[:, None] == jnp.arange(step_sizes.shape[0], dtype=jnp.int32)[None, :]
    return jnp.sum(jnp.where(chosen, step_sizes[None, :], 0.0), axis=1)


def call(kernel, name, mib, scalars, operands, in_specs, outs, out_specs, scratch, grid=()):
    return pl.pallas_call(
        kernel,
        out_shape=outs,
        grid_spec=pltpu.PrefetchScalarGridSpec(
            num_scalar_prefetch=1, grid=grid, in_specs=in_specs, out_specs=out_specs,
            scratch_shapes=scratch,
        ),
        compiler_params=pltpu.CompilerParams(vmem_limit_bytes=mib * MIB),
        cost_estimate=pl.CostEstimate(flops=1, bytes_accessed=1, transcendentals=0),
        name=name,
    )(scalars, *operands)


def per_device(
    query_rows, key_rows, value_rows, positions, latents, w_head, modulation,
    guide_scale, step_sizes, lengths,
):
    rows, features = query_rows.shape[1], query_rows.shape[2]
    heads = features // HD
    count = lax.axis_size("req")
    here = lax.axis_index("req")
    first_row = here * rows
    _, padded, room = sizes(rows, heads)
    chunk = padded // CHUNKS
    late_sizes = (*[chunk] * (CHUNKS - 1), MORE, room - padded - MORE)

    angle = angles(positions)
    odd = (jnp.arange(HD, dtype=jnp.int32) % 2).astype(jnp.float32)
    cosine = jnp.cos(angle)
    sine = jnp.sin(angle) * (2.0 * odd - 1.0)[None, :]

    smem = pl.BlockSpec(memory_space=pltpu.SMEM)
    vmem = pl.BlockSpec(memory_space=pltpu.VMEM)
    hbm = pl.BlockSpec(memory_space=pl.ANY)
    parity = lax.axis_index("cfg")
    tie = lax.optimization_barrier
    scalars = pl.pallas_call(
        functools.partial(plan_kernel, rows, heads, count),
        out_shape=jax.ShapeDtypeStruct((SCALARS,), jnp.int32),
        in_specs=[smem],
        out_specs=smem,
        scratch_shapes=[
            pltpu.SMEM((count + 3,), jnp.int32),
            pltpu.SMEM((count + 3,), jnp.int32),
            pltpu.VMEM(((count + 3) * 8, 128), jnp.float32),
            pltpu.VMEM(((count + 3) * 8, 128), jnp.float32),
        ],
        name="plan",
    )(lengths)

    q, k, v = query_rows[0], key_rows[0], value_rows[0]

    def box(items):
        return jax.ShapeDtypeStruct((items, 3 * TILE, HD), jnp.bfloat16)

    def box_scratch(items):
        return pltpu.VMEM((items, 3 * TILE, HD), jnp.bfloat16)

    group = next(n for n in (5, 4, 3, 2, 1) if heads % n == 0)
    steps = heads // group
    head_block = pl.BlockSpec((rows, group * HD), lambda g, s: (0, g))
    table = pl.BlockSpec((rows, HD), lambda g, s: (0, 0))
    first = call(
        first_kernel, "pack_first", 56, scalars, (q, k, v, cosine, sine),
        [head_block] * 3 + [table] * 2, (box(chunk),), (hbm,),
        [box_scratch(chunk), pltpu.SemaphoreType.DMA((1,))], grid=(steps,),
    )
    pairs = [(i, i ^ 1) for i in range(count)]
    onward = [(i, i + 2) for i in range(0, count - 2, 2)] + [(i + 2, i) for i in range(1, count - 2, 2)]
    got = [lax.ppermute(first[0], "req", pairs)]

    after_first, _ = tie((scalars, first[0]))
    swap = jnp.asarray(numpy.eye(2 * HD)[numpy.arange(2 * HD) ^ 1], jnp.bfloat16)
    q_rot, k_rot, w_both, shift, *second = call(
        functools.partial(second_kernel, chunk), "turn_and_pack_rest", 32, after_first,
        (q, k, v, cosine, sine, swap, w_head.T, modulation),
        [head_block] * 3 + [table] * 2 + [vmem] * 3,
        (jax.ShapeDtypeStruct(q.shape, q.dtype), jax.ShapeDtypeStruct(k.shape, k.dtype),
         jax.ShapeDtypeStruct((HD, features), jnp.bfloat16),
         jax.ShapeDtypeStruct((HD // 2, HD), jnp.float32),
         *[box(n) for n in late_sizes], box(late_sizes[-1])),
        (head_block, head_block, vmem, vmem, *[hbm] * (len(late_sizes) + 1)),
        [box_scratch(sum(late_sizes)), pltpu.SemaphoreType.DMA((len(late_sizes),))], grid=(steps,),
    )
    got += [lax.ppermute(x, "req", pairs) for x in second[: CHUNKS - 1]]
    got[1], second[CHUNKS - 1] = tie((got[1], second[CHUNKS - 1]))
    got.append(lax.ppermute(second[CHUNKS - 1], "req", pairs))
    more, arriving = second[CHUNKS:]

    own_rows = first_row + jnp.arange(rows, dtype=jnp.int32)
    video = jnp.sum((jnp.cumsum(lengths)[None, :] <= own_rows[:, None]).astype(jnp.int32), axis=1)
    step_of_row = step_rows(video, step_sizes)

    def inner(when, first_step, step_count):
        block = pl.BlockSpec((rows, group * HD), lambda g, s: (0, g + first_step))
        width = step_count * group * HD
        return call(
            inner_kernel, "inner_videos", 20, when,
            (q_rot, k_rot, v, w_both, video[:, None], video[None, :]),
            [block] * 3 + [pl.BlockSpec((HD, width), lambda g, s: (0, first_step // step_count))] + [vmem] * 2, jax.ShapeDtypeStruct((rows, HD), jnp.float32), vmem,
            [pltpu.VMEM((rows, width), jnp.bfloat16)], grid=(step_count,),
        )

    when_a, got[0] = tie((scalars, got[0]))
    inner_a = inner(when_a, 0, steps // 2)
    got[1], inner_a = tie((got[1], inner_a))
    passed = [lax.ppermute(x, "req", onward) for x in got[:2]]
    when_b, passed[0], got[2], inner_a = tie((scalars, passed[0], got[2], inner_a))
    inner_b = inner(when_b, steps // 2, steps - steps // 2)
    got[3], inner_b = tie((got[3], inner_b))
    when_early, got[3] = tie((scalars, got[3]))
    passed += [lax.ppermute(x, "req", onward) for x in got[2:CHUNKS]]

    work = [
        pltpu.VMEM((2, rows + TILE, HD), jnp.bfloat16),
        pltpu.VMEM((2, rows + TILE, HD), jnp.bfloat16),
        pltpu.VMEM((2, rows + TILE, 2 * HD), jnp.bfloat16),
        pltpu.VMEM((rows, features), jnp.bfloat16),
        pltpu.VMEM((2 * rows, HD), jnp.float32),
    ]
    partial = jax.ShapeDtypeStruct((rows, HD), jnp.float32)
    lanes = HD // 2 + TILE
    sent_back = jax.ShapeDtypeStruct((lanes, rows), jnp.bfloat16)

    def on_videos_across(kernel, name, when, boxes, outs, others=()):
        places = [0]
        for x in boxes:
            places.append(places[-1] + x.shape[0])
        return call(
            kernel(tuple(places[:-1])), name, 24, when, (q_rot, k_rot, v, w_both, *others, *boxes),
            [vmem] * (4 + len(others)) + [hbm] * len(boxes), outs, jax.tree.map(lambda _: vmem, outs),
            [box_scratch(places[-1]), pltpu.SemaphoreType.DMA((len(boxes),)), *work],
        )

    def early_on(at, name, when, boxes):
        return on_videos_across(
            lambda places: functools.partial(early_kernel, places, at), name, when, boxes,
            partial,
        )

    early = early_on(PASS, "videos_across_early", when_early, passed[:EARLY_CHUNKS])
    when_direct, early, passed[2] = tie((scalars, early, passed[2]))
    direct_z = early_on(DIRECT, "videos_across_direct", when_direct, got)

    pieces = jnp.maximum(scalars[MOST] - padded - MORE + EXTRA - 1, 0) // EXTRA
    pieces, direct_z = tie((pieces, direct_z))

    def one_more(i, arrived):
        piece = lax.dynamic_slice_in_dim(more, i * EXTRA, EXTRA, 0)
        piece = lax.ppermute(piece, "req", pairs)
        return lax.dynamic_update_slice_in_dim(arrived, piece, i * EXTRA, 0)

    arrived = lax.fori_loop(0, pieces, one_more, arriving)
    before = EARLY_CHUNKS - 1
    offsets = (-chunk * before, chunk * (CHUNKS - before))
    own, to_beyond, to_direct = on_videos_across(
        lambda places: functools.partial(last_kernel, places, offsets), "videos_across_last", scalars,
        [*passed[before:], *got, arrived],
        (jax.ShapeDtypeStruct((lanes, rows), jnp.float32), sent_back, sent_back),
        (early, direct_z, inner_a, inner_b),
    )
    back_direct = lax.ppermute(to_direct, "req", pairs)
    beyond = [(i, i + 1) for i in range(1, count - 1, 2)] + [(i + 1, i) for i in range(1, count - 1, 2)]
    back_beyond = lax.ppermute(to_beyond, "req", beyond)
    total = own + back_direct.astype(jnp.float32) + back_beyond.astype(jnp.float32)
    values = HD // 2
    squares = total[values : values + 1] + total[values + 1 : values + 2]
    velocity = total[:values] * lax.rsqrt(squares / features + 1e-06) + shift[:, :1]

    width = latents.shape[1]
    mine = lax.dynamic_slice_in_dim(velocity, parity * width, width, 0)
    theirs = lax.dynamic_slice_in_dim(velocity, (1 - parity) * width, width, 0)
    partner = lax.ppermute(theirs, "cfg", [(0, 1), (1, 0)])
    conditional = jnp.where(parity == 0, mine, partner)
    unconditional = jnp.where(parity == 0, partner, mine)
    guided = unconditional + guide_scale[0] * (conditional - unconditional)
    return (latents.T + step_of_row[None, :] * guided).T


def solution(mesh):
    in_specs = (
        P("cfg", "req", None), P("cfg", "req", None), P("cfg", "req", None),
        P(None, "req"), P("req", "cfg"), P(), P(), P(), P(), P(),
    )
    return jax.shard_map(
        per_device, mesh=mesh, in_specs=in_specs, out_specs=P("req", "cfg"), check_vma=False
    )
```

```python
import functools
import math

import jax
import jax.numpy as jnp
import numpy
from jax import lax
from jax.experimental import pallas as pl
from jax.experimental.pallas import tpu as pltpu
from jax.sharding import PartitionSpec as P

HD = 128
TILE = 16
BLK = 128
CHUNKS = 4
MORE = 48
EXTRA = 32
EARLY_CHUNKS = 2
rope_theta = 10000.0
NEG = -1e30
SCALE2 = math.log2(math.e) / math.sqrt(HD)

PASS, DIRECT = 0, 16
LB, RB, LROWS, RROWS, HEAD0, KEEP, EARLY, SOURCE = range(8)
OWN_FROM, OWN_TO, OWN, FAR_TO, FAR, SIDE = range(8, 14)
SEND = 32
ROW, TILES, FIRST, HEADS = range(4)
MOST, INNER_FROM, INNER_TO = 40, 41, 42
SCALARS = 48
MIB = 1024 * 1024


def sizes(rows, heads):
    tiles = rows // TILE
    cap = max(
        min(max(a * n, (tiles + 1 - a) * (heads - n)) for n in range(heads + 1))
        for a in range(1, tiles + 1)
    )
    padded = -(-cap // TILE) * TILE
    return cap, padded, 2 * padded


def angles(positions):
    pair_total = HD // 2
    side_pairs = HD // 6
    time_pairs = pair_total - 2 * side_pairs
    column = jnp.arange(HD, dtype=jnp.int32) // 2
    in_time = column < time_pairs
    in_height = (column >= time_pairs) & (column < time_pairs + side_pairs)
    in_width = column >= time_pairs + side_pairs
    local_index = jnp.where(
        in_time, column, jnp.where(in_height, column - time_pairs, column - time_pairs - side_pairs)
    )
    axis_pairs = jnp.where(in_time, time_pairs, side_pairs)
    frequency = jnp.exp(
        -(local_index.astype(jnp.float32) / axis_pairs.astype(jnp.float32)) * math.log(rope_theta)
    )
    selector = jnp.stack([in_time, in_height, in_width]).astype(jnp.float32) * frequency[None, :]
    placed = positions.astype(jnp.float32)
    return (
        placed[0][:, None] * selector[0][None, :]
        + placed[1][:, None] * selector[1][None, :]
        + placed[2][:, None] * selector[2][None, :]
    )


def plan_kernel(rows, heads, count, lengths, out, ls, rs, split, least):
    cap, padded, _ = sizes(rows, heads)
    here = lax.axis_index("req")

    def clear(b, carry):
        ls[b] = 0
        rs[b] = 0
        return carry

    lax.fori_loop(0, count + 3, clear, 0)

    def one_video(v, start):
        end = start + lengths[v]
        b = lax.div(end - 1, rows)
        at = b * rows

        @pl.when(start < at)
        def _():
            ls[b] = at - start
            rs[b] = end - at

        return end

    lax.fori_loop(0, lengths.shape[0], one_video, 0)
    budget = 3.0 * lax.broadcasted_iota(jnp.int32, (8, 128), 1).astype(jnp.float32)
    split[...] = jnp.zeros_like(split)

    def tiles_of(x):
        return lax.shift_right_logical(x + TILE - 1, 4)

    def eight(b):
        return pl.ds(pl.multiple_of(b * 8, 8), 8)

    def per_tile(x, tiles):
        return jnp.floor((x + 0.5) / jnp.maximum(tiles, 1.0))

    def facts(b):
        direct = lax.rem(b, 2).astype(jnp.float32)
        lt, rt = tiles_of(ls[b]).astype(jnp.float32), tiles_of(rs[b]).astype(jnp.float32)
        return lt, rt, padded + direct * 1e6

    def from_right(i, load):
        b = count - 1 - i
        lt, rt, limit = facts(b)
        room = jnp.minimum(budget - load, limit)
        n = jnp.where(rt > 0.0, jnp.maximum(heads - per_tile(room, rt), 0.0), 0.0)
        least[eight(b)] = jnp.where(room >= 0.0, n, 1e6)
        return lt * n

    def from_left(b, carry):
        load, ok = carry
        lt, rt, limit = facts(b)
        room = jnp.minimum(budget - load, limit)
        most = jnp.where(lt > 0.0, jnp.minimum(per_tile(room, lt), float(heads)), 0.0)
        low = least[eight(b)]
        even = jnp.floor(heads * rt / jnp.maximum(lt + rt, 1.0) + 0.5)
        n = jnp.minimum(most, jnp.maximum(low, even))
        split[eight(b)] = n
        return rt * (heads - n), jnp.where((room >= 0.0) & (low <= most), ok, 0.0)

    zero = jnp.zeros((8, 128), jnp.float32)
    lax.fori_loop(0, count - 1, from_right, zero)
    load, ok = lax.fori_loop(1, count, from_left, (zero, zero + 1.0))
    ok = jnp.where(load <= budget, ok, 0.0)
    most = jnp.min(jnp.where(ok > 0.0, budget, 1e9))
    out[MOST] = most.astype(jnp.int32)

    def head_split(b):
        n = split[eight(b)]
        return jnp.max(jnp.where(budget == most, n, 0.0)).astype(jnp.int32)

    even = lax.rem(here, 2) == 0
    beyond = jnp.where(even, here + 2, here - 1)
    n_left, n_right, n_beyond = head_split(here), head_split(here + 1), head_split(beyond)
    partner_passes = jnp.where(
        even,
        tiles_of(ls[beyond]) * n_beyond,
        tiles_of(rs[beyond]) * (heads - n_beyond),
    )
    for side, b, n in ((0, here, n_left), (1, here + 1, n_right)):
        direct = jnp.logical_not(even) if side == 0 else even
        at = jnp.where(direct, DIRECT, PASS)
        lt, rt = tiles_of(ls[b]), tiles_of(rs[b])
        none = jnp.where(lt > 0, 0, heads)
        keep = n if side == 0 else jnp.maximum(heads - n - none, 0)
        far = lt if side == 0 else rt
        out[at + LB], out[at + RB] = lt, rt
        out[at + LROWS], out[at + RROWS] = ls[b], rs[b]
        out[at + HEAD0] = 0 if side == 0 else n
        out[at + KEEP] = keep
        source = jnp.where(direct, partner_passes, 0)
        there = jnp.where(direct, padded + MORE, padded // CHUNKS * EARLY_CHUNKS) - source
        out[at + EARLY] = jnp.minimum(keep, lax.div(jnp.maximum(there, 0), jnp.maximum(far, 1)))
        out[at + SOURCE] = source
        out[at + OWN_FROM] = 0 if side == 0 else rows // TILE - lt
        out[at + OWN_TO] = lt if side == 0 else 0
        out[at + OWN] = rt if side == 0 else lt
        out[at + FAR_TO] = 0 if side == 0 else lt
        out[at + FAR] = far
        out[at + SIDE] = side
        to = SEND + jnp.where(direct, 4, 0)
        out[to + ROW] = 0 if side == 0 else rows - TILE * lt
        out[to + TILES] = rt if side == 0 else lt
        out[to + FIRST] = n if side == 0 else 0
        out[to + HEADS] = jnp.maximum(heads - n - none, 0) if side == 0 else n
    out[INNER_FROM] = rs[here]
    out[INNER_TO] = rows - ls[here + 1]


def in_groups(low, high, step):
    count = high - low

    def run(group, times):
        def body(i, carry):
            step(jnp.minimum(low + group * i, high - group), group)
            return carry

        lax.fori_loop(0, times, body, 0)

    run(8, jnp.where(count >= 8, lax.shift_right_logical(count + 7, 3), 0))
    run(2, jnp.where((count >= 2) & (count < 8), lax.shift_right_logical(count + 1, 1), 0))
    run(1, jnp.where(count == 1, 1, 0))


def lanes_of(h):
    return pl.ds(pl.multiple_of(h * HD, HD), HD)


def rows_of(t, group):
    return pl.ds(pl.multiple_of(t * TILE, TILE), group * TILE)


def turn(x, cosine, sine):
    wide = x.astype(jnp.float32)
    even = lax.rem(lax.broadcasted_iota(jnp.int32, wide.shape, 1), 2) == 0
    swapped = jnp.where(even, pltpu.roll(wide, HD - 1, 1), pltpu.roll(wide, 1, 1))
    return (wide * cosine + swapped * sine).astype(jnp.bfloat16)


def pack(scal, low, high, box, heads, get):
    base = 0
    for what in (SEND, SEND + 4):
        first_tile = lax.shift_right_logical(scal[what + ROW], 4)
        tiles, first, count = scal[what + TILES], scal[what + FIRST], scal[what + HEADS]

        def one_head(i, carry):
            start = base + (pl.program_id(0) * heads + i - first) * tiles
            begin = jnp.clip(low - start, 0, tiles)
            end = jnp.clip(high - start, 0, tiles)
            lanes = lanes_of(i)

            def step(t, group):
                q, k, v = get(rows_of(first_tile + t, group), lanes)
                item = pl.ds(start + t - low, group)
                box[item, 0:TILE] = q.reshape(group, TILE, HD)
                box[item, TILE : 2 * TILE] = k.reshape(group, TILE, HD)
                box[item, 2 * TILE : 3 * TILE] = v.reshape(group, TILE, HD)

            in_groups(begin, end, step)
            return carry

        before = first - pl.program_id(0) * heads
        lax.fori_loop(
            jnp.clip(before, 0, heads), jnp.clip(before + count, 0, heads), one_head, 0
        )
        base = base + tiles * count


def send_off(box, outs, sems):
    @pl.when(pl.program_id(0) == pl.num_programs(0) - 1)
    def _():
        at, copies = 0, []
        for i, out in enumerate(outs):
            copies.append(pltpu.make_async_copy(box.at[pl.ds(at, out.shape[0])], out, sems.at[i]))
            at += out.shape[0]
        for copy in copies:
            copy.start()
        for copy in copies:
            copy.wait()


def first_kernel(scal, q_ref, k_ref, v_ref, cos_ref, sin_ref, *rest):
    outs, box, sems = rest[:-2], rest[-2], rest[-1]

    def get(rows, lanes):
        cosine, sine = cos_ref[rows, :], sin_ref[rows, :]
        return (
            turn(q_ref[rows, lanes], cosine, sine),
            turn(k_ref[rows, lanes], cosine, sine),
            v_ref[rows, lanes],
        )

    pack(scal, 0, box.shape[0], box, q_ref.shape[1] // HD, get)
    send_off(box, outs, sems)


def second_kernel(
    low, scal, q_ref, k_ref, v_ref, cos_ref, sin_ref, swap_ref, wt_ref, mod_ref, qr_ref, kr_ref, w_ref, shift_ref, *rest
):
    outs, box, sems = rest[:-3], rest[-2], rest[-1]
    rows = q_ref.shape[0]
    heads = q_ref.shape[1] // HD
    wide = swap_ref.shape[0]

    @pl.when(pl.program_id(0) == 0)
    def _():
        w = wt_ref[...].astype(jnp.float32)
        scaled = w * (1.0 + mod_ref[1:2, :])
        high = scaled.astype(jnp.bfloat16)
        low = (scaled - high.astype(jnp.float32)).astype(jnp.bfloat16)
        w_ref[...] = jnp.concatenate([high, low], axis=0)
        shift = jnp.sum(w * mod_ref[0:1, :], axis=1, keepdims=True)
        shift_ref[...] = jnp.broadcast_to(shift, shift_ref.shape)

    for source, to in ((q_ref, qr_ref), (k_ref, kr_ref)):
        for h in range(0, heads, wide // HD):
            for j in range(rows // BLK):
                at = slice(j * BLK, (j + 1) * BLK)
                x = source[at, h * HD : h * HD + wide]
                swapped = jnp.dot(x, swap_ref[: x.shape[1], : x.shape[1]], preferred_element_type=jnp.float32)
                for i in range(x.shape[1] // HD):
                    lanes = slice(i * HD, (i + 1) * HD)
                    to[at, (h + i) * HD : (h + i + 1) * HD] = (
                        x[:, lanes].astype(jnp.float32) * cos_ref[at, :] + swapped[:, lanes] * sin_ref[at, :]
                    ).astype(jnp.bfloat16)

    def get(rows, lanes):
        return qr_ref[rows, lanes], kr_ref[rows, lanes], v_ref[rows, lanes]

    pack(scal, low, low + box.shape[0], box, heads, get)
    send_off(box, outs, sems)


def dot_t(a, b):
    return lax.dot_general(a, b, (((1,), (1,)), ((), ())), preferred_element_type=jnp.float32)


def attend_rows(q, k, v_ones, masked):
    s = masked(dot_t(q, k))
    top = jnp.max(s, axis=1, keepdims=True)
    weight = jnp.exp2(s * SCALE2 - top * SCALE2).astype(jnp.bfloat16)
    both = jnp.dot(weight, v_ones, preferred_element_type=jnp.float32)
    return (both[:, :HD] / both[:, HD:]).astype(jnp.bfloat16)


def projected(o_ref, w_ref, out_ref, rows):
    for j in range(rows // BLK):
        at = slice(j * BLK, (j + 1) * BLK)
        z = dot_t(o_ref[at, :], w_ref[...])
        z = z + pltpu.roll(z, HD // 2, 1)
        lane = lax.broadcasted_iota(jnp.int32, z.shape, 1)
        squares = jnp.zeros(z.shape, jnp.float32)
        for h in range(o_ref.shape[1] // HD):
            wide = o_ref[at, h * HD : (h + 1) * HD].astype(jnp.float32)
            squares = squares + wide * wide
        total = jnp.sum(squares, axis=1, keepdims=True)
        out_ref[at, :] = jnp.where(lane < HD // 2, z, jnp.where(lane == HD // 2, total, 0.0))


def inner_kernel(scal, q_ref, k_ref, v_ref, w_ref, qv_ref, kv_ref, out_ref, o_ref):
    g = pl.program_id(0)
    rows, width = q_ref.shape
    ones = jnp.ones((rows, HD), jnp.bfloat16)
    for j in range(rows // BLK):
        at = pl.ds(j * BLK, BLK)
        same = qv_ref[at, :] == kv_ref[...]
        for i in range(width // HD):
            lanes = slice(i * HD, (i + 1) * HD)
            v_ones = jnp.concatenate([v_ref[:, lanes], ones], axis=1)
            o_ref[at, pl.ds(pl.multiple_of(g * width + i * HD, HD), HD)] = attend_rows(
                q_ref[at, lanes], k_ref[:, lanes], v_ones, lambda s: jnp.where(same, s, NEG)
            )

    @pl.when(g == pl.num_programs(0) - 1)
    def _():
        projected(o_ref, w_ref, out_ref, rows)


def across(scal, at, offset, low, high, sources, items, w_ref, own_sems, places, o_ref, zz):
    rows = zz.shape[0] // 2
    left, right = scal[at + LB], scal[at + RB]
    lead = left * TILE - scal[at + LROWS]
    end = left * TILE + scal[at + RROWS]
    blocks = jnp.minimum(lax.div((left + right) * TILE + BLK - 1, BLK), rows // BLK)
    own_at = jnp.where(scal[at + SIDE] == 0, rows, 0) + left * TILE
    pairs = lax.shift_right_logical(high - low + 1, 1)

    def heads_of(i):
        return [jnp.minimum(low + 2 * i + u, high - 1) for u in range(2)]

    def own_copies(i):
        slot = lax.rem(i, 2)
        to = pl.ds(pl.multiple_of(own_at, TILE), rows)
        return [
            pltpu.make_async_copy(
                source.at[:, lanes_of(scal[at + HEAD0] + s)], place.at[slot, u, to, :],
                own_sems.at[slot, u, x],
            )
            for u, s in enumerate(heads_of(i))
            for x, (source, place) in enumerate(zip(sources, places))
        ]

    @pl.when(pairs > 0)
    def _():
        for copy in own_copies(0):
            copy.start()

    def two_heads(n, i, carry):
        slot = lax.rem(i, 2)

        @pl.when(i + 1 < pairs)
        def _():
            for copy in own_copies(i + 1):
                copy.start()

        heads = heads_of(i)

        def foreign(t, group):
            to = rows_of(rows // TILE + scal[at + FAR_TO] + t, group)
            for u, s in enumerate(heads):
                item = pl.ds(scal[at + SOURCE] + offset + s * scal[at + FAR] + t, group)
                for x, place in enumerate(places):
                    part = items[item, x * TILE : (x + 1) * TILE]
                    place[slot, u, to, :] = part.reshape(group * TILE, HD)

        in_groups(0, scal[at + FAR], foreign)
        for copy in own_copies(i):
            copy.wait()
        width = n * BLK
        if width == rows:

            @pl.when((left + right) * TILE > rows)
            def _():
                row = lax.broadcasted_iota(jnp.int32, (TILE, HD), 0)
                for place in places:
                    for u in range(2):
                        first = place[slot, u, rows : rows + TILE, :]
                        last = place[slot, u, 2 * rows : 2 * rows + TILE, :]
                        place[slot, u, rows : rows + TILE, :] = jnp.where(row < lead, last, first)

        place = lax.broadcasted_iota(jnp.int32, (1, width), 1)
        valid = ((place >= lead) & (place < end)) | (place + rows < end)
        bias = jnp.where(valid, 0.0, NEG)
        ones = jnp.ones((width, HD), jnp.bfloat16)
        qs, ks, vs = places
        whole = slice(rows, rows + width)
        for j in range(n):
            mine = slice(rows + j * BLK, rows + (j + 1) * BLK)
            for u, s in enumerate(heads):
                v_ones = jnp.concatenate([vs[slot, u, whole, :], ones], axis=1)
                o_ref[j * BLK : (j + 1) * BLK, lanes_of(scal[at + HEAD0] + s)] = attend_rows(
                    qs[slot, u, mine, :], ks[slot, u, whole, :], v_ones, lambda x: x + bias
                )
        return carry

    for n in range(1, rows // BLK + 1):

        @pl.when((blocks == n) & (pairs > 0))
        def _(n=n):
            o_ref[0 : n * BLK, :] = jnp.zeros((n * BLK, o_ref.shape[1]), o_ref.dtype)
            lax.fori_loop(0, pairs, functools.partial(two_heads, n), 0)
            projected(o_ref, w_ref, zz, n * BLK)
            zz[rows : 2 * rows, :] = zz[0:rows, :]

    @pl.when(pairs <= 0)
    def _():
        zz[...] = jnp.zeros_like(zz)

    return zz[pl.ds(pl.multiple_of(left * TILE, TILE), rows), :]


def fetch(scal, at, offset, low, high, places, boxes, items, sems):
    begin = scal[at + SOURCE] + offset + low * scal[at + FAR]
    end = scal[at + SOURCE] + offset + high * scal[at + FAR]
    return [
        (
            pltpu.make_async_copy(box, items.at[pl.ds(place, box.shape[0])], sems.at[i]),
            (high > low) & (begin < place + box.shape[0]) & (end > place),
        )
        for i, (place, box) in enumerate(zip(places, boxes))
    ]


def clear(places, rows):
    for place in places:
        for slot in range(2):
            for u in range(2):
                place[slot, u, rows : 2 * rows + TILE, :] = jnp.zeros((rows + TILE, HD), place.dtype)


def of_boundary(scal, at, shape, mine):
    row = lax.broadcasted_iota(jnp.int32, shape, 0)
    tail = jnp.where(row >= shape[0] - scal[at + LROWS], 1, 0)
    head = jnp.where(row < scal[at + RROWS], 1, 0)
    right_is_mine = (scal[at + SIDE] == 0) == mine
    return jnp.where(right_is_mine, head, tail) == 1


def send_back(scal, at, z, back_ref):
    lane = lax.broadcasted_iota(jnp.int32, z.shape, 1)
    back = jnp.where(of_boundary(scal, at, z.shape, False), z, 0.0)
    high = back.astype(jnp.bfloat16).astype(jnp.float32)
    both = jnp.where(lane == HD // 2 + 1, pltpu.roll(back - high, 1, 1), high)
    back_ref[...] = both.T[: back_ref.shape[0]].astype(jnp.bfloat16)


def early_kernel(places, at, scal, q_hbm, k_hbm, v_hbm, w_ref, *rest):
    boxes, (out_ref, items, sems, own_sems, qs, ks, vs, o_ref, zz) = rest[: len(places)], rest[len(places) :]
    high = scal[at + EARLY]
    copies = fetch(scal, at, 0, 0, high, places, boxes, items, sems)
    for copy, need in copies:
        pl.when(need)(copy.start)
    clear((qs, ks, vs), zz.shape[0] // 2)
    for copy, need in copies:
        pl.when(need)(copy.wait)
    out_ref[...] = across(
        scal, at, 0, 0, high, (q_hbm, k_hbm, v_hbm), items, w_ref, own_sems, (qs, ks, vs), o_ref, zz
    )


def last_kernel(places, offsets, scal, q_hbm, k_hbm, v_hbm, w_ref, *rest):
    partials, rest = rest[:4], rest[4:]
    boxes, rest = rest[: len(places)], rest[len(places) :]
    own_ref, pass_back_ref, direct_back_ref, items, sems, own_sems, qs, ks, vs, o_ref, zz, sums, sum_sems = rest
    sum_copies = [
        pltpu.make_async_copy(part, sums.at[i], sum_sems.at[i]) for i, part in enumerate(partials)
    ]
    for copy in sum_copies:
        copy.start()
    clear((qs, ks, vs), zz.shape[0] // 2)

    def remaining(at, offset):
        low, high = scal[at + EARLY], scal[at + KEEP]
        copies = fetch(scal, at, offset, low, high, places, boxes, items, sems)
        for copy, need in copies:
            pl.when(need)(copy.start)
        for copy, need in copies:
            pl.when(need)(copy.wait)
        return across(
            scal, at, offset, low, high, (q_hbm, k_hbm, v_hbm), items, w_ref, own_sems, (qs, ks, vs), o_ref, zz
        )

    passed_z = remaining(PASS, offsets[0])
    for copy in sum_copies:
        copy.wait()
    passed_z = passed_z + sums[0]
    send_back(scal, PASS, passed_z, pass_back_ref)
    own = jnp.where(of_boundary(scal, PASS, passed_z.shape, True), passed_z, sums[2] + sums[3])
    direct_z = sums[1] + remaining(DIRECT, offsets[1])
    send_back(scal, DIRECT, direct_z, direct_back_ref)
    own = jnp.where(of_boundary(scal, DIRECT, own.shape, True), direct_z, own)
    own_ref[...] = own.T[: own_ref.shape[0]]


def step_rows(video_ids, step_sizes):
    chosen = video_ids[:, None] == jnp.arange(step_sizes.shape[0], dtype=jnp.int32)[None, :]
    return jnp.sum(jnp.where(chosen, step_sizes[None, :], 0.0), axis=1)


def call(kernel, name, mib, scalars, operands, in_specs, outs, out_specs, scratch, grid=()):
    return pl.pallas_call(
        kernel,
        out_shape=outs,
        grid_spec=pltpu.PrefetchScalarGridSpec(
            num_scalar_prefetch=1, grid=grid, in_specs=in_specs, out_specs=out_specs,
            scratch_shapes=scratch,
        ),
        compiler_params=pltpu.CompilerParams(vmem_limit_bytes=mib * MIB),
        cost_estimate=pl.CostEstimate(flops=1, bytes_accessed=1, transcendentals=0),
        name=name,
    )(scalars, *operands)


def per_device(
    query_rows, key_rows, value_rows, positions, latents, w_head, modulation,
    guide_scale, step_sizes, lengths,
):
    rows, features = query_rows.shape[1], query_rows.shape[2]
    heads = features // HD
    count = lax.axis_size("req")
    here = lax.axis_index("req")
    first_row = here * rows
    _, padded, room = sizes(rows, heads)
    chunk = padded // CHUNKS
    late_sizes = (*[chunk] * (CHUNKS - 1), MORE, room - padded - MORE)

    angle = angles(positions)
    odd = (jnp.arange(HD, dtype=jnp.int32) % 2).astype(jnp.float32)
    cosine = jnp.cos(angle)
    sine = jnp.sin(angle) * (2.0 * odd - 1.0)[None, :]

    smem = pl.BlockSpec(memory_space=pltpu.SMEM)
    vmem = pl.BlockSpec(memory_space=pltpu.VMEM)
    hbm = pl.BlockSpec(memory_space=pl.ANY)
    parity = lax.axis_index("cfg")
    tie = lax.optimization_barrier
    scalars = pl.pallas_call(
        functools.partial(plan_kernel, rows, heads, count),
        out_shape=jax.ShapeDtypeStruct((SCALARS,), jnp.int32),
        in_specs=[smem],
        out_specs=smem,
        scratch_shapes=[
            pltpu.SMEM((count + 3,), jnp.int32),
            pltpu.SMEM((count + 3,), jnp.int32),
            pltpu.VMEM(((count + 3) * 8, 128), jnp.float32),
            pltpu.VMEM(((count + 3) * 8, 128), jnp.float32),
        ],
        name="plan",
    )(lengths)

    def in_hbm(x):
        return pltpu.with_memory_space_constraint(x, pltpu.HBM)

    q, k, v = query_rows[0], key_rows[0], value_rows[0]

    def box(items):
        return jax.ShapeDtypeStruct((items, 3 * TILE, HD), jnp.bfloat16)

    def box_scratch(items):
        return pltpu.VMEM((items, 3 * TILE, HD), jnp.bfloat16)

    group = next(n for n in (5, 4, 3, 2, 1) if heads % n == 0)
    steps = heads // group
    head_block = pl.BlockSpec((rows, group * HD), lambda g, s: (0, g))
    table = pl.BlockSpec((rows, HD), lambda g, s: (0, 0))
    first = call(
        first_kernel, "pack_first", 24, scalars, (in_hbm(q), in_hbm(k), in_hbm(v), cosine, sine),
        [head_block] * 3 + [table] * 2, (box(chunk),), (hbm,),
        [box_scratch(chunk), pltpu.SemaphoreType.DMA((1,))], grid=(steps,),
    )
    pairs = [(i, i ^ 1) for i in range(count)]
    onward = [(i, i + 2) for i in range(0, count - 2, 2)] + [(i + 2, i) for i in range(1, count - 2, 2)]
    got = [lax.ppermute(first[0], "req", pairs)]

    after_first, _ = tie((scalars, first[0]))
    swap = jnp.asarray(numpy.eye(2 * HD)[numpy.arange(2 * HD) ^ 1], jnp.bfloat16)
    q_rot, k_rot, w_both, shift, *second = call(
        functools.partial(second_kernel, chunk), "turn_and_pack_rest", 32, after_first,
        (in_hbm(q), in_hbm(k), in_hbm(v), cosine, sine, swap, w_head.T, modulation),
        [head_block] * 3 + [table] * 2 + [vmem] * 3,
        (jax.ShapeDtypeStruct(q.shape, q.dtype), jax.ShapeDtypeStruct(k.shape, k.dtype),
         jax.ShapeDtypeStruct((HD, features), jnp.bfloat16),
         jax.ShapeDtypeStruct((HD // 2, HD), jnp.float32),
         *[box(n) for n in late_sizes], box(late_sizes[-1])),
        (head_block, head_block, vmem, vmem, *[hbm] * (len(late_sizes) + 1)),
        [box_scratch(sum(late_sizes)), pltpu.SemaphoreType.DMA((len(late_sizes),))], grid=(steps,),
    )
    got += [lax.ppermute(x, "req", pairs) for x in second[: CHUNKS - 1]]
    got[1], second[CHUNKS - 1] = tie((got[1], second[CHUNKS - 1]))
    got.append(lax.ppermute(second[CHUNKS - 1], "req", pairs))
    more, arriving = second[CHUNKS:]

    own_rows = first_row + jnp.arange(rows, dtype=jnp.int32)
    video = jnp.sum((jnp.cumsum(lengths)[None, :] <= own_rows[:, None]).astype(jnp.int32), axis=1)
    step_of_row = step_rows(video, step_sizes)

    def inner(when, first_step, step_count):
        block = pl.BlockSpec((rows, group * HD), lambda g, s: (0, g + first_step))
        width = step_count * group * HD
        return call(
            inner_kernel, "inner_videos", 20, when,
            (in_hbm(q_rot), in_hbm(k_rot), in_hbm(v), w_both, video[:, None], video[None, :]),
            [block] * 3 + [pl.BlockSpec((HD, width), lambda g, s: (0, first_step // step_count))] + [vmem] * 2, jax.ShapeDtypeStruct((rows, HD), jnp.float32), vmem,
            [pltpu.VMEM((rows, width), jnp.bfloat16)], grid=(step_count,),
        )

    when_a, got[0] = tie((scalars, got[0]))
    inner_a = inner(when_a, 0, steps // 2)
    got[1], inner_a = tie((got[1], inner_a))
    passed = [lax.ppermute(x, "req", onward) for x in got[:2]]
    when_b, passed[0], got[2], inner_a = tie((scalars, passed[0], got[2], inner_a))
    inner_b = inner(when_b, steps // 2, steps - steps // 2)
    got[3], inner_b = tie((got[3], inner_b))
    when_early, got[3] = tie((scalars, got[3]))
    passed += [lax.ppermute(x, "req", onward) for x in got[2:CHUNKS]]

    place = pltpu.VMEM((2, 2, 3 * rows, HD), jnp.bfloat16)
    work = [
        pltpu.SemaphoreType.DMA((2, 2, 3)), place, place, place,
        pltpu.VMEM((rows, features), jnp.bfloat16),
        pltpu.VMEM((2 * rows, HD), jnp.float32),
    ]
    partial = jax.ShapeDtypeStruct((rows, HD), jnp.float32)
    lanes = HD // 2 + TILE
    sent_back = jax.ShapeDtypeStruct((lanes, rows), jnp.bfloat16)

    def on_videos_across(kernel, name, when, boxes, outs, others=(), scratch=()):
        places = [0]
        for x in boxes:
            places.append(places[-1] + x.shape[0])
        return call(
            kernel(tuple(places[:-1])), name, 32, when,
            (in_hbm(q_rot), in_hbm(k_rot), in_hbm(v), w_both, *[in_hbm(x) for x in others], *boxes),
            [hbm] * 3 + [vmem] + [hbm] * (len(others) + len(boxes)),
            outs, jax.tree.map(lambda _: vmem, outs),
            [box_scratch(places[-1]), pltpu.SemaphoreType.DMA((len(boxes),)), *work, *scratch],
        )

    def early_on(at, name, when, boxes):
        return on_videos_across(
            lambda places: functools.partial(early_kernel, places, at), name, when, boxes,
            partial,
        )

    early = early_on(PASS, "videos_across_early", when_early, passed[:EARLY_CHUNKS])
    when_direct, early, passed[2] = tie((scalars, early, passed[2]))
    direct_z = early_on(DIRECT, "videos_across_direct", when_direct, got)

    pieces = jnp.maximum(scalars[MOST] - padded - MORE + EXTRA - 1, 0) // EXTRA
    pieces, direct_z = tie((pieces, direct_z))

    def one_more(i, arrived):
        piece = lax.dynamic_slice_in_dim(more, i * EXTRA, EXTRA, 0)
        piece = lax.ppermute(piece, "req", pairs)
        return lax.dynamic_update_slice_in_dim(arrived, piece, i * EXTRA, 0)

    arrived = lax.fori_loop(0, pieces, one_more, arriving)
    before = EARLY_CHUNKS - 1
    offsets = (-chunk * before, chunk * (CHUNKS - before))
    own, to_beyond, to_direct = on_videos_across(
        lambda places: functools.partial(last_kernel, places, offsets), "videos_across_last", scalars,
        [*passed[before:], *got, arrived],
        (jax.ShapeDtypeStruct((lanes, rows), jnp.float32), sent_back, sent_back),
        (early, direct_z, inner_a, inner_b),
        (pltpu.VMEM((4, rows, HD), jnp.float32), pltpu.SemaphoreType.DMA((4,))),
    )
    back_direct = lax.ppermute(to_direct, "req", pairs)
    beyond = [(i, i + 1) for i in range(1, count - 1, 2)] + [(i + 1, i) for i in range(1, count - 1, 2)]
    back_beyond = lax.ppermute(to_beyond, "req", beyond)
    total = own + back_direct.astype(jnp.float32) + back_beyond.astype(jnp.float32)
    values = HD // 2
    squares = total[values : values + 1] + total[values + 1 : values + 2]
    velocity = total[:values] * lax.rsqrt(squares / features + 1e-06) + shift[:, :1]

    width = latents.shape[1]
    mine = lax.dynamic_slice_in_dim(velocity, parity * width, width, 0)
    theirs = lax.dynamic_slice_in_dim(velocity, (1 - parity) * width, width, 0)
    partner = lax.ppermute(theirs, "cfg", [(0, 1), (1, 0)])
    conditional = jnp.where(parity == 0, mine, partner)
    unconditional = jnp.where(parity == 0, partner, mine)
    guided = unconditional + guide_scale[0] * (conditional - unconditional)
    return (latents.T + step_of_row[None, :] * guided).T


def solution(mesh):
    in_specs = (
        P("cfg", "req", None), P("cfg", "req", None), P("cfg", "req", None),
        P(None, "req"), P("req", "cfg"), P(), P(), P(), P(), P(),
    )
    return jax.shard_map(
        per_device, mesh=mesh, in_specs=in_specs, out_specs=P("req", "cfg"), check_vma=False
    )
```

```python
import functools
import math

import jax
import jax.numpy as jnp
import numpy
from jax import lax
from jax.experimental import pallas as pl
from jax.experimental.pallas import tpu as pltpu
from jax.sharding import PartitionSpec as P

HD = 128
TILE = 16
BLK = 128
CHUNKS = 4
MORE = 48
EXTRA = 32
EARLY_CHUNKS = 2
rope_theta = 10000.0
NEG = -1e30
SCALE2 = math.log2(math.e) / math.sqrt(HD)

PASS, DIRECT = 0, 16
LB, RB, LROWS, RROWS, HEAD0, KEEP, EARLY, SOURCE = range(8)
OWN_FROM, OWN_TO, OWN, FAR_TO, FAR, SIDE = range(8, 14)
SEND = 32
ROW, TILES, FIRST, HEADS = range(4)
MOST, INNER_FROM, INNER_TO = 40, 41, 42
SCALARS = 48
MIB = 1024 * 1024


def sizes(rows, heads):
    tiles = rows // TILE
    cap = max(
        min(max(a * n, (tiles + 1 - a) * (heads - n)) for n in range(heads + 1))
        for a in range(1, tiles + 1)
    )
    padded = -(-cap // TILE) * TILE
    return cap, padded, 2 * padded


def angles(positions):
    pair_total = HD // 2
    side_pairs = HD // 6
    time_pairs = pair_total - 2 * side_pairs
    column = jnp.arange(HD, dtype=jnp.int32) // 2
    in_time = column < time_pairs
    in_height = (column >= time_pairs) & (column < time_pairs + side_pairs)
    in_width = column >= time_pairs + side_pairs
    local_index = jnp.where(
        in_time, column, jnp.where(in_height, column - time_pairs, column - time_pairs - side_pairs)
    )
    axis_pairs = jnp.where(in_time, time_pairs, side_pairs)
    frequency = jnp.exp(
        -(local_index.astype(jnp.float32) / axis_pairs.astype(jnp.float32)) * math.log(rope_theta)
    )
    selector = jnp.stack([in_time, in_height, in_width]).astype(jnp.float32) * frequency[None, :]
    placed = positions.astype(jnp.float32)
    return (
        placed[0][:, None] * selector[0][None, :]
        + placed[1][:, None] * selector[1][None, :]
        + placed[2][:, None] * selector[2][None, :]
    )


def plan_kernel(rows, heads, count, lengths, out, ls, rs, split, least):
    cap, padded, _ = sizes(rows, heads)
    here = lax.axis_index("req")
    shift = rows.bit_length() - 1

    def clear(b, carry):
        ls[b] = 0
        rs[b] = 0
        return carry

    lax.fori_loop(0, count + 3, clear, 0)

    def one_video(v, start):
        end = start + lengths[v]
        b = lax.shift_right_logical(end - 1, shift) if rows == 1 << shift else lax.div(end - 1, rows)
        at = b * rows

        @pl.when(start < at)
        def _():
            ls[b] = at - start
            rs[b] = end - at

        return end

    lax.fori_loop(0, lengths.shape[0], one_video, 0)
    budget = 3.0 * lax.broadcasted_iota(jnp.int32, (8, 128), 1).astype(jnp.float32)
    split[...] = jnp.zeros_like(split)

    def tiles_of(x):
        return lax.shift_right_logical(x + TILE - 1, 4)

    def eight(b):
        return pl.ds(pl.multiple_of(b * 8, 8), 8)

    def per_tile(x, tiles):
        return jnp.floor((x + 0.5) / jnp.maximum(tiles, 1.0))

    def facts(b):
        direct = lax.rem(b, 2).astype(jnp.float32)
        lt, rt = tiles_of(ls[b]).astype(jnp.float32), tiles_of(rs[b]).astype(jnp.float32)
        return lt, rt, padded + direct * 1e6

    def from_right(i, load):
        b = count - 1 - i
        lt, rt, limit = facts(b)
        room = jnp.minimum(budget - load, limit)
        n = jnp.where(rt > 0.0, jnp.maximum(heads - per_tile(room, rt), 0.0), 0.0)
        least[eight(b)] = jnp.where(room >= 0.0, n, 1e6)
        return lt * n

    def from_left(b, carry):
        load, ok = carry
        lt, rt, limit = facts(b)
        room = jnp.minimum(budget - load, limit)
        most = jnp.where(lt > 0.0, jnp.minimum(per_tile(room, lt), float(heads)), 0.0)
        low = least[eight(b)]
        even = jnp.floor(heads * rt / jnp.maximum(lt + rt, 1.0) + 0.5)
        n = jnp.minimum(most, jnp.maximum(low, even))
        split[eight(b)] = n
        return rt * (heads - n), jnp.where((room >= 0.0) & (low <= most), ok, 0.0)

    zero = jnp.zeros((8, 128), jnp.float32)
    lax.fori_loop(0, count - 1, from_right, zero)
    load, ok = lax.fori_loop(1, count, from_left, (zero, zero + 1.0))
    ok = jnp.where(load <= budget, ok, 0.0)
    most = jnp.min(jnp.where(ok > 0.0, budget, 1e9))
    out[MOST] = most.astype(jnp.int32)

    def head_split(b):
        n = split[eight(b)]
        return jnp.max(jnp.where(budget == most, n, 0.0)).astype(jnp.int32)

    even = lax.rem(here, 2) == 0
    beyond = jnp.where(even, here + 2, here - 1)
    n_left, n_right, n_beyond = head_split(here), head_split(here + 1), head_split(beyond)
    partner_passes = jnp.where(
        even,
        tiles_of(ls[beyond]) * n_beyond,
        tiles_of(rs[beyond]) * (heads - n_beyond),
    )
    for side, b, n in ((0, here, n_left), (1, here + 1, n_right)):
        direct = jnp.logical_not(even) if side == 0 else even
        at = jnp.where(direct, DIRECT, PASS)
        lt, rt = tiles_of(ls[b]), tiles_of(rs[b])
        none = jnp.where(lt > 0, 0, heads)
        keep = n if side == 0 else jnp.maximum(heads - n - none, 0)
        far = lt if side == 0 else rt
        out[at + LB], out[at + RB] = lt, rt
        out[at + LROWS], out[at + RROWS] = ls[b], rs[b]
        out[at + HEAD0] = 0 if side == 0 else n
        out[at + KEEP] = keep
        source = jnp.where(direct, partner_passes, 0)
        there = jnp.where(direct, padded + MORE, padded // CHUNKS * EARLY_CHUNKS) - source
        out[at + EARLY] = jnp.minimum(keep, lax.div(jnp.maximum(there, 0), jnp.maximum(far, 1)))
        out[at + SOURCE] = source
        out[at + OWN_FROM] = 0 if side == 0 else rows // TILE - lt
        out[at + OWN_TO] = lt if side == 0 else 0
        out[at + OWN] = rt if side == 0 else lt
        out[at + FAR_TO] = 0 if side == 0 else lt
        out[at + FAR] = far
        out[at + SIDE] = side
        to = SEND + jnp.where(direct, 4, 0)
        out[to + ROW] = 0 if side == 0 else rows - TILE * lt
        out[to + TILES] = rt if side == 0 else lt
        out[to + FIRST] = n if side == 0 else 0
        out[to + HEADS] = jnp.maximum(heads - n - none, 0) if side == 0 else n
    out[INNER_FROM] = rs[here]
    out[INNER_TO] = rows - ls[here + 1]


def in_groups(low, high, step):
    count = high - low

    def run(group, times):
        def body(i, carry):
            step(jnp.minimum(low + group * i, high - group), group)
            return carry

        lax.fori_loop(0, times, body, 0)

    run(8, jnp.where(count >= 8, lax.shift_right_logical(count + 7, 3), 0))
    run(2, jnp.where((count >= 2) & (count < 8), lax.shift_right_logical(count + 1, 1), 0))
    run(1, jnp.where(count == 1, 1, 0))


def lanes_of(h):
    return pl.ds(pl.multiple_of(h * HD, HD), HD)


def rows_of(t, group):
    return pl.ds(pl.multiple_of(t * TILE, TILE), group * TILE)


def turn(x, cosine, sine):
    wide = x.astype(jnp.float32)
    even = lax.rem(lax.broadcasted_iota(jnp.int32, wide.shape, 1), 2) == 0
    swapped = jnp.where(even, pltpu.roll(wide, HD - 1, 1), pltpu.roll(wide, 1, 1))
    return (wide * cosine + swapped * sine).astype(jnp.bfloat16)


def pack(scal, low, high, box, heads, get):
    base = 0
    for what in (SEND, SEND + 4):
        first_tile = lax.shift_right_logical(scal[what + ROW], 4)
        tiles, first, count = scal[what + TILES], scal[what + FIRST], scal[what + HEADS]

        def one_head(i, carry):
            start = base + (pl.program_id(0) * heads + i - first) * tiles
            begin = jnp.clip(low - start, 0, tiles)
            end = jnp.clip(high - start, 0, tiles)
            lanes = lanes_of(i)

            def step(t, group):
                q, k, v = get(rows_of(first_tile + t, group), lanes)
                item = pl.ds(start + t - low, group)
                box[item, 0:TILE] = q.reshape(group, TILE, HD)
                box[item, TILE : 2 * TILE] = k.reshape(group, TILE, HD)
                box[item, 2 * TILE : 3 * TILE] = v.reshape(group, TILE, HD)

            in_groups(begin, end, step)
            return carry

        before = first - pl.program_id(0) * heads
        lax.fori_loop(
            jnp.clip(before, 0, heads), jnp.clip(before + count, 0, heads), one_head, 0
        )
        base = base + tiles * count


def send_off(box, outs, sems):
    @pl.when(pl.program_id(0) == pl.num_programs(0) - 1)
    def _():
        at, copies = 0, []
        for i, out in enumerate(outs):
            copies.append(pltpu.make_async_copy(box.at[pl.ds(at, out.shape[0])], out, sems.at[i]))
            at += out.shape[0]
        for copy in copies:
            copy.start()
        for copy in copies:
            copy.wait()


def first_kernel(scal, q_hbm, k_hbm, v_hbm, cos_ref, sin_ref, box, qs, ks, vs, sems):
    limit = box.shape[0]
    ahead = qs.shape[0] - 1

    def heads_in(what, base):
        tiles = jnp.maximum(scal[what + TILES], 1)
        taken = lax.div(jnp.maximum(limit - base, 0) + tiles - 1, tiles)
        return jnp.minimum(scal[what + HEADS], taken)

    passed = scal[SEND + TILES] * scal[SEND + HEADS]
    count_pass = heads_in(SEND, 0)
    count = count_pass + heads_in(SEND + 4, passed)

    def entry(w):
        direct = w >= count_pass
        what = jnp.where(direct, SEND + 4, SEND)
        slot = w - jnp.where(direct, count_pass, 0)
        tiles = scal[what + TILES]
        start = jnp.where(direct, passed, 0) + slot * tiles
        return scal[what + FIRST] + slot, scal[what + ROW], tiles, start

    def copies(w):
        at = lax.rem(w, ahead + 1)
        lanes = lanes_of(entry(w)[0])
        return [
            pltpu.make_async_copy(source.at[:, lanes], place.at[at], sems.at[at, x])
            for x, (source, place) in enumerate(((q_hbm, qs), (k_hbm, ks), (v_hbm, vs)))
        ]

    for w in range(ahead):

        @pl.when(w < count)
        def _(w=w):
            for copy in copies(w):
                copy.start()

    def one_head(w, carry):
        @pl.when(w + ahead < count)
        def _():
            for copy in copies(w + ahead):
                copy.start()

        for copy in copies(w):
            copy.wait()
        at = lax.rem(w, ahead + 1)
        _, row, tiles, start = entry(w)
        first_tile = lax.shift_right_logical(row, 4)

        def step(t, group):
            source = rows_of(first_tile + t, group)
            cosine, sine = cos_ref[source, :], sin_ref[source, :]
            item = pl.ds(start + t, group)
            q, k = turn(qs[at, source, :], cosine, sine), turn(ks[at, source, :], cosine, sine)
            box[item, 0:TILE] = q.reshape(group, TILE, HD)
            box[item, TILE : 2 * TILE] = k.reshape(group, TILE, HD)
            box[item, 2 * TILE : 3 * TILE] = vs[at, source, :].reshape(group, TILE, HD)

        in_groups(0, jnp.clip(limit - start, 0, tiles), step)
        return carry

    lax.fori_loop(0, count, one_head, 0)


def second_kernel(
    low, scal, q_ref, k_ref, v_ref, cos_ref, sin_ref, swap_ref, wt_ref, mod_ref, qr_ref, kr_ref, w_ref, shift_ref, *rest
):
    outs, box, sems = rest[:-3], rest[-2], rest[-1]
    rows = q_ref.shape[0]
    heads = q_ref.shape[1] // HD
    wide = swap_ref.shape[0]

    @pl.when(pl.program_id(0) == 0)
    def _():
        w = wt_ref[...].astype(jnp.float32)
        scaled = w * (1.0 + mod_ref[1:2, :])
        high = scaled.astype(jnp.bfloat16)
        low = (scaled - high.astype(jnp.float32)).astype(jnp.bfloat16)
        w_ref[...] = jnp.concatenate([high, low], axis=0)
        shift = jnp.sum(w * mod_ref[0:1, :], axis=1, keepdims=True)
        shift_ref[...] = jnp.broadcast_to(shift, shift_ref.shape)

    for source, to in ((q_ref, qr_ref), (k_ref, kr_ref)):
        for h in range(0, heads, wide // HD):
            for j in range(rows // BLK):
                at = slice(j * BLK, (j + 1) * BLK)
                x = source[at, h * HD : h * HD + wide]
                swapped = jnp.dot(x, swap_ref[: x.shape[1], : x.shape[1]], preferred_element_type=jnp.float32)
                for i in range(x.shape[1] // HD):
                    lanes = slice(i * HD, (i + 1) * HD)
                    to[at, (h + i) * HD : (h + i + 1) * HD] = (
                        x[:, lanes].astype(jnp.float32) * cos_ref[at, :] + swapped[:, lanes] * sin_ref[at, :]
                    ).astype(jnp.bfloat16)

    def get(rows, lanes):
        return qr_ref[rows, lanes], kr_ref[rows, lanes], v_ref[rows, lanes]

    pack(scal, low, low + box.shape[0], box, heads, get)
    send_off(box, outs, sems)


def dot_t(a, b):
    return lax.dot_general(a, b, (((1,), (1,)), ((), ())), preferred_element_type=jnp.float32)


def attend_rows(q, k, v_ones, masked):
    s = masked(dot_t(q, k))
    top = jnp.max(s, axis=1, keepdims=True)
    weight = jnp.exp2(s * SCALE2 - top * SCALE2).astype(jnp.bfloat16)
    both = jnp.dot(weight, v_ones, preferred_element_type=jnp.float32)
    return (both[:, :HD] / both[:, HD:]).astype(jnp.bfloat16)


def projected(o_ref, w_ref, out_ref, rows):
    for j in range(rows // BLK):
        at = slice(j * BLK, (j + 1) * BLK)
        z = dot_t(o_ref[at, :], w_ref[...])
        z = z + pltpu.roll(z, HD // 2, 1)
        lane = lax.broadcasted_iota(jnp.int32, z.shape, 1)
        squares = jnp.zeros(z.shape, jnp.float32)
        for h in range(o_ref.shape[1] // HD):
            wide = o_ref[at, h * HD : (h + 1) * HD].astype(jnp.float32)
            squares = squares + wide * wide
        total = jnp.sum(squares, axis=1, keepdims=True)
        out_ref[at, :] = jnp.where(lane < HD // 2, z, jnp.where(lane == HD // 2, total, 0.0))


def inner_kernel(scal, q_ref, k_ref, v_ref, w_ref, qv_ref, kv_ref, out_ref, o_ref):
    g = pl.program_id(0)
    rows, width = q_ref.shape
    ones = jnp.ones((rows, HD), jnp.bfloat16)
    for j in range(rows // BLK):
        at = pl.ds(j * BLK, BLK)
        same = qv_ref[at, :] == kv_ref[...]
        for i in range(width // HD):
            lanes = slice(i * HD, (i + 1) * HD)
            v_ones = jnp.concatenate([v_ref[:, lanes], ones], axis=1)
            o_ref[at, pl.ds(pl.multiple_of(g * width + i * HD, HD), HD)] = attend_rows(
                q_ref[at, lanes], k_ref[:, lanes], v_ones, lambda s: jnp.where(same, s, NEG)
            )

    @pl.when(g == pl.num_programs(0) - 1)
    def _():
        projected(o_ref, w_ref, out_ref, rows)


def across(scal, at, offset, low, high, sources, items, w_ref, own_sems, places, o_ref, zz):
    rows = zz.shape[0] // 2
    left, right = scal[at + LB], scal[at + RB]
    lead = left * TILE - scal[at + LROWS]
    end = left * TILE + scal[at + RROWS]
    blocks = jnp.minimum(lax.div((left + right) * TILE + BLK - 1, BLK), rows // BLK)
    own_at = jnp.where(scal[at + SIDE] == 0, rows, 0) + left * TILE
    pairs = lax.shift_right_logical(high - low + 1, 1)

    def heads_of(i):
        return [jnp.minimum(low + 2 * i + u, high - 1) for u in range(2)]

    def own_copies(i):
        slot = lax.rem(i, 2)
        to = pl.ds(pl.multiple_of(own_at, TILE), rows)
        return [
            pltpu.make_async_copy(
                source.at[:, lanes_of(scal[at + HEAD0] + s)], place.at[slot, u, to, :],
                own_sems.at[slot, u, x],
            )
            for u, s in enumerate(heads_of(i))
            for x, (source, place) in enumerate(zip(sources, places))
        ]

    @pl.when(pairs > 0)
    def _():
        for copy in own_copies(0):
            copy.start()

    def two_heads(n, i, carry):
        slot = lax.rem(i, 2)

        @pl.when(i + 1 < pairs)
        def _():
            for copy in own_copies(i + 1):
                copy.start()

        heads = heads_of(i)

        def foreign(t, group):
            to = rows_of(rows // TILE + scal[at + FAR_TO] + t, group)
            for u, s in enumerate(heads):
                item = pl.ds(scal[at + SOURCE] + offset + s * scal[at + FAR] + t, group)
                for x, place in enumerate(places):
                    part = items[item, x * TILE : (x + 1) * TILE]
                    place[slot, u, to, :] = part.reshape(group * TILE, HD)

        in_groups(0, scal[at + FAR], foreign)
        for copy in own_copies(i):
            copy.wait()
        width = n * BLK
        if width == rows:

            @pl.when((left + right) * TILE > rows)
            def _():
                row = lax.broadcasted_iota(jnp.int32, (TILE, HD), 0)
                for place in places:
                    for u in range(2):
                        first = place[slot, u, rows : rows + TILE, :]
                        last = place[slot, u, 2 * rows : 2 * rows + TILE, :]
                        place[slot, u, rows : rows + TILE, :] = jnp.where(row < lead, last, first)

        place = lax.broadcasted_iota(jnp.int32, (1, width), 1)
        valid = ((place >= lead) & (place < end)) | (place + rows < end)
        bias = jnp.where(valid, 0.0, NEG)
        ones = jnp.ones((width, HD), jnp.bfloat16)
        qs, ks, vs = places
        whole = slice(rows, rows + width)
        for j in range(n):
            mine = slice(rows + j * BLK, rows + (j + 1) * BLK)
            for u, s in enumerate(heads):
                v_ones = jnp.concatenate([vs[slot, u, whole, :], ones], axis=1)
                o_ref[j * BLK : (j + 1) * BLK, lanes_of(scal[at + HEAD0] + s)] = attend_rows(
                    qs[slot, u, mine, :], ks[slot, u, whole, :], v_ones, lambda x: x + bias
                )
        return carry

    for n in range(1, rows // BLK + 1):

        @pl.when((blocks == n) & (pairs > 0))
        def _(n=n):
            o_ref[0 : n * BLK, :] = jnp.zeros((n * BLK, o_ref.shape[1]), o_ref.dtype)
            lax.fori_loop(0, pairs, functools.partial(two_heads, n), 0)
            projected(o_ref, w_ref, zz, n * BLK)
            zz[rows : 2 * rows, :] = zz[0:rows, :]

    @pl.when(pairs <= 0)
    def _():
        zz[...] = jnp.zeros_like(zz)

    return zz[pl.ds(pl.multiple_of(left * TILE, TILE), rows), :]


def fetch(scal, at, offset, low, high, places, boxes, items, sems):
    begin = scal[at + SOURCE] + offset + low * scal[at + FAR]
    end = scal[at + SOURCE] + offset + high * scal[at + FAR]
    return [
        (
            pltpu.make_async_copy(box, items.at[pl.ds(place, box.shape[0])], sems.at[i]),
            (high > low) & (begin < place + box.shape[0]) & (end > place),
        )
        for i, (place, box) in enumerate(zip(places, boxes))
    ]


def clear(places, rows):
    for place in places:
        for slot in range(2):
            for u in range(2):
                place[slot, u, rows : 2 * rows + TILE, :] = jnp.zeros((rows + TILE, HD), place.dtype)


def of_boundary(scal, at, shape, mine):
    row = lax.broadcasted_iota(jnp.int32, shape, 0)
    tail = jnp.where(row >= shape[0] - scal[at + LROWS], 1, 0)
    head = jnp.where(row < scal[at + RROWS], 1, 0)
    right_is_mine = (scal[at + SIDE] == 0) == mine
    return jnp.where(right_is_mine, head, tail) == 1


def send_back(scal, at, z, back_ref):
    lane = lax.broadcasted_iota(jnp.int32, z.shape, 1)
    back = jnp.where(of_boundary(scal, at, z.shape, False), z, 0.0)
    high = back.astype(jnp.bfloat16).astype(jnp.float32)
    both = jnp.where(lane == HD // 2 + 1, pltpu.roll(back - high, 1, 1), high)
    back_ref[...] = both.T[: back_ref.shape[0]].astype(jnp.bfloat16)


def early_kernel(places, at, scal, q_hbm, k_hbm, v_hbm, w_ref, *rest):
    boxes, (out_ref, items, sems, own_sems, qs, ks, vs, o_ref, zz) = rest[: len(places)], rest[len(places) :]
    high = scal[at + EARLY]
    copies = fetch(scal, at, 0, 0, high, places, boxes, items, sems)
    for copy, need in copies:
        pl.when(need)(copy.start)
    clear((qs, ks, vs), zz.shape[0] // 2)
    for copy, need in copies:
        pl.when(need)(copy.wait)
    out_ref[...] = across(
        scal, at, 0, 0, high, (q_hbm, k_hbm, v_hbm), items, w_ref, own_sems, (qs, ks, vs), o_ref, zz
    )


def last_kernel(places, offsets, scal, q_hbm, k_hbm, v_hbm, w_ref, *rest):
    partials, rest = rest[:4], rest[4:]
    boxes, rest = rest[: len(places)], rest[len(places) :]
    own_ref, pass_back_ref, direct_back_ref, items, sems, own_sems, qs, ks, vs, o_ref, zz, sums, sum_sems = rest
    sum_copies = [
        pltpu.make_async_copy(part, sums.at[i], sum_sems.at[i]) for i, part in enumerate(partials)
    ]
    for copy in sum_copies:
        copy.start()
    clear((qs, ks, vs), zz.shape[0] // 2)

    def remaining(at, offset):
        low, high = scal[at + EARLY], scal[at + KEEP]
        copies = fetch(scal, at, offset, low, high, places, boxes, items, sems)
        for copy, need in copies:
            pl.when(need)(copy.start)
        for copy, need in copies:
            pl.when(need)(copy.wait)
        return across(
            scal, at, offset, low, high, (q_hbm, k_hbm, v_hbm), items, w_ref, own_sems, (qs, ks, vs), o_ref, zz
        )

    passed_z = remaining(PASS, offsets[0])
    for copy in sum_copies:
        copy.wait()
    passed_z = passed_z + sums[0]
    send_back(scal, PASS, passed_z, pass_back_ref)
    own = jnp.where(of_boundary(scal, PASS, passed_z.shape, True), passed_z, sums[2] + sums[3])
    direct_z = sums[1] + remaining(DIRECT, offsets[1])
    send_back(scal, DIRECT, direct_z, direct_back_ref)
    own = jnp.where(of_boundary(scal, DIRECT, own.shape, True), direct_z, own)
    own_ref[...] = own.T[: own_ref.shape[0]]


def step_rows(video_ids, step_sizes):
    chosen = video_ids[:, None] == jnp.arange(step_sizes.shape[0], dtype=jnp.int32)[None, :]
    return jnp.sum(jnp.where(chosen, step_sizes[None, :], 0.0), axis=1)


def call(kernel, name, mib, scalars, operands, in_specs, outs, out_specs, scratch, grid=()):
    return pl.pallas_call(
        kernel,
        out_shape=outs,
        grid_spec=pltpu.PrefetchScalarGridSpec(
            num_scalar_prefetch=1, grid=grid, in_specs=in_specs, out_specs=out_specs,
            scratch_shapes=scratch,
        ),
        compiler_params=pltpu.CompilerParams(vmem_limit_bytes=mib * MIB),
        cost_estimate=pl.CostEstimate(flops=1, bytes_accessed=1, transcendentals=0),
        name=name,
    )(scalars, *operands)


def per_device(
    query_rows, key_rows, value_rows, positions, latents, w_head, modulation,
    guide_scale, step_sizes, lengths,
):
    rows, features = query_rows.shape[1], query_rows.shape[2]
    heads = features // HD
    count = lax.axis_size("req")
    here = lax.axis_index("req")
    first_row = here * rows
    _, padded, room = sizes(rows, heads)
    chunk = padded // CHUNKS
    late_sizes = (*[chunk] * (CHUNKS - 1), MORE, room - padded - MORE)

    angle = angles(positions)
    odd = (jnp.arange(HD, dtype=jnp.int32) % 2).astype(jnp.float32)
    cosine = jnp.cos(angle)
    sine = jnp.sin(angle) * (2.0 * odd - 1.0)[None, :]

    smem = pl.BlockSpec(memory_space=pltpu.SMEM)
    vmem = pl.BlockSpec(memory_space=pltpu.VMEM)
    hbm = pl.BlockSpec(memory_space=pl.ANY)
    parity = lax.axis_index("cfg")
    tie = lax.optimization_barrier
    scalars = pl.pallas_call(
        functools.partial(plan_kernel, rows, heads, count),
        out_shape=jax.ShapeDtypeStruct((SCALARS,), jnp.int32),
        in_specs=[smem],
        out_specs=smem,
        scratch_shapes=[
            pltpu.SMEM((count + 3,), jnp.int32),
            pltpu.SMEM((count + 3,), jnp.int32),
            pltpu.VMEM(((count + 3) * 8, 128), jnp.float32),
            pltpu.VMEM(((count + 3) * 8, 128), jnp.float32),
        ],
        name="plan",
    )(lengths)

    def in_hbm(x):
        return pltpu.with_memory_space_constraint(x, pltpu.HBM)

    q, k, v = query_rows[0], key_rows[0], value_rows[0]

    def box(items):
        return jax.ShapeDtypeStruct((items, 3 * TILE, HD), jnp.bfloat16)

    def box_scratch(items):
        return pltpu.VMEM((items, 3 * TILE, HD), jnp.bfloat16)

    group = next(n for n in (5, 4, 3, 2, 1) if heads % n == 0)
    steps = heads // group
    head_block = pl.BlockSpec((rows, group * HD), lambda g, s: (0, g))
    table = pl.BlockSpec((rows, HD), lambda g, s: (0, 0))
    first = call(
        first_kernel, "pack_first", 16, scalars, (in_hbm(q), in_hbm(k), in_hbm(v), cosine, sine),
        [hbm] * 3 + [vmem] * 2, (box(chunk),), (vmem,),
        [*[pltpu.VMEM((4, rows, HD), jnp.bfloat16)] * 3, pltpu.SemaphoreType.DMA((4, 3))],
    )
    pairs = [(i, i ^ 1) for i in range(count)]
    onward = [(i, i + 2) for i in range(0, count - 2, 2)] + [(i + 2, i) for i in range(1, count - 2, 2)]
    got = [lax.ppermute(first[0], "req", pairs)]

    after_first, _ = tie((scalars, first[0]))
    swap = jnp.asarray(numpy.eye(2 * HD)[numpy.arange(2 * HD) ^ 1], jnp.bfloat16)
    q_rot, k_rot, w_both, shift, *second = call(
        functools.partial(second_kernel, chunk), "turn_and_pack_rest", 32, after_first,
        (in_hbm(q), in_hbm(k), in_hbm(v), cosine, sine, swap, w_head.T, modulation),
        [head_block] * 3 + [table] * 2 + [vmem] * 3,
        (pltpu.HBM(q.shape, q.dtype), pltpu.HBM(k.shape, k.dtype),
         jax.ShapeDtypeStruct((HD, features), jnp.bfloat16),
         jax.ShapeDtypeStruct((HD // 2, HD), jnp.float32),
         *[box(n) for n in late_sizes], box(late_sizes[-1])),
        (head_block, head_block, vmem, vmem, *[hbm] * (len(late_sizes) + 1)),
        [box_scratch(sum(late_sizes)), pltpu.SemaphoreType.DMA((len(late_sizes),))], grid=(steps,),
    )
    got += [lax.ppermute(x, "req", pairs) for x in second[: CHUNKS - 1]]
    more, arriving = second[CHUNKS:]

    own_rows = first_row + jnp.arange(rows, dtype=jnp.int32)
    video = jnp.sum((jnp.cumsum(lengths)[None, :] <= own_rows[:, None]).astype(jnp.int32), axis=1)
    step_of_row = step_rows(video, step_sizes)

    def inner(when, first_step, step_count):
        block = pl.BlockSpec((rows, group * HD), lambda g, s: (0, g + first_step))
        width = step_count * group * HD
        return call(
            inner_kernel, "inner_videos", 20, when,
            (in_hbm(q_rot), in_hbm(k_rot), in_hbm(v), w_both, video[:, None], video[None, :]),
            [block] * 3 + [pl.BlockSpec((HD, width), lambda g, s: (0, first_step // step_count))] + [vmem] * 2, pltpu.HBM((rows, HD), jnp.float32), vmem,
            [pltpu.VMEM((rows, width), jnp.bfloat16)], grid=(step_count,),
        )

    inner_a = inner(scalars, 0, steps // 2)
    got[0], inner_a = tie((got[0], inner_a))
    passed = [lax.ppermute(x, "req", onward) for x in got[:2]]
    passed[0], got[1], second[CHUNKS - 1] = tie((passed[0], got[1], second[CHUNKS - 1]))
    got.append(lax.ppermute(second[CHUNKS - 1], "req", pairs))
    when_b, passed[0], got[2], inner_a = tie((scalars, passed[0], got[2], inner_a))
    inner_b = inner(when_b, steps // 2, steps - steps // 2)
    got[3], inner_b = tie((got[3], inner_b))
    when_early, got[3] = tie((scalars, got[3]))
    passed += [lax.ppermute(x, "req", onward) for x in got[2:CHUNKS]]

    place = pltpu.VMEM((2, 2, 3 * rows, HD), jnp.bfloat16)
    work = [
        pltpu.SemaphoreType.DMA((2, 2, 3)), place, place, place,
        pltpu.VMEM((rows, features), jnp.bfloat16),
        pltpu.VMEM((2 * rows, HD), jnp.float32),
    ]
    partial = pltpu.HBM((rows, HD), jnp.float32)
    lanes = HD // 2 + TILE
    sent_back = jax.ShapeDtypeStruct((lanes, rows), jnp.bfloat16)

    def on_videos_across(kernel, name, when, boxes, outs, others=(), scratch=()):
        places = [0]
        for x in boxes:
            places.append(places[-1] + x.shape[0])
        return call(
            kernel(tuple(places[:-1])), name, 32, when,
            (in_hbm(q_rot), in_hbm(k_rot), in_hbm(v), w_both, *[in_hbm(x) for x in others], *boxes),
            [hbm] * 3 + [vmem] + [hbm] * (len(others) + len(boxes)),
            outs, jax.tree.map(lambda _: vmem, outs),
            [box_scratch(places[-1]), pltpu.SemaphoreType.DMA((len(boxes),)), *work, *scratch],
        )

    def early_on(at, name, when, boxes):
        return on_videos_across(
            lambda places: functools.partial(early_kernel, places, at), name, when, boxes,
            partial,
        )

    early = early_on(PASS, "videos_across_early", when_early, passed[:EARLY_CHUNKS])
    when_direct, early = tie((scalars, early))
    direct_z = early_on(DIRECT, "videos_across_direct", when_direct, got)

    pieces = jnp.maximum(scalars[MOST] - padded - MORE + EXTRA - 1, 0) // EXTRA
    pieces, direct_z = tie((pieces, direct_z))

    def one_more(i, arrived):
        piece = lax.dynamic_slice_in_dim(more, i * EXTRA, EXTRA, 0)
        piece = lax.ppermute(piece, "req", pairs)
        return lax.dynamic_update_slice_in_dim(arrived, piece, i * EXTRA, 0)

    arrived = lax.fori_loop(0, pieces, one_more, arriving)
    before = EARLY_CHUNKS - 1
    offsets = (-chunk * before, chunk * (CHUNKS - before))
    own, to_beyond, to_direct = on_videos_across(
        lambda places: functools.partial(last_kernel, places, offsets), "videos_across_last", scalars,
        [*passed[before:], *got, arrived],
        (jax.ShapeDtypeStruct((lanes, rows), jnp.float32), sent_back, sent_back),
        (early, direct_z, inner_a, inner_b),
        (pltpu.VMEM((4, rows, HD), jnp.float32), pltpu.SemaphoreType.DMA((4,))),
    )
    back_direct = lax.ppermute(to_direct, "req", pairs)
    beyond = [(i, i + 1) for i in range(1, count - 1, 2)] + [(i + 1, i) for i in range(1, count - 1, 2)]
    back_beyond = lax.ppermute(to_beyond, "req", beyond)
    total = own + back_direct.astype(jnp.float32) + back_beyond.astype(jnp.float32)
    values = HD // 2
    squares = total[values : values + 1] + total[values + 1 : values + 2]
    velocity = total[:values] * lax.rsqrt(squares / features + 1e-06) + shift[:, :1]

    width = latents.shape[1]
    mine = lax.dynamic_slice_in_dim(velocity, parity * width, width, 0)
    theirs = lax.dynamic_slice_in_dim(velocity, (1 - parity) * width, width, 0)
    partner = lax.ppermute(theirs, "cfg", [(0, 1), (1, 0)])
    conditional = jnp.where(parity == 0, mine, partner)
    unconditional = jnp.where(parity == 0, partner, mine)
    guided = unconditional + guide_scale[0] * (conditional - unconditional)
    return (latents.T + step_of_row[None, :] * guided).T


def solution(mesh):
    in_specs = (
        P("cfg", "req", None), P("cfg", "req", None), P("cfg", "req", None),
        P(None, "req"), P("req", "cfg"), P(), P(), P(), P(), P(),
    )
    return jax.shard_map(
        per_device, mesh=mesh, in_specs=in_specs, out_specs=P("req", "cfg"), check_vma=False
    )
```

```python
import functools
import math

import jax
import jax.numpy as jnp
import numpy
from jax import lax
from jax.experimental import pallas as pl
from jax.experimental.pallas import tpu as pltpu
from jax.sharding import PartitionSpec as P

HD = 128
TILE = 16
BLK = 128
CHUNKS = 4
MORE = 48
EXTRA = 32
EARLY_CHUNKS = 2
rope_theta = 10000.0
NEG = -1e30
SCALE2 = math.log2(math.e) / math.sqrt(HD)

PASS, DIRECT = 0, 16
LB, RB, LROWS, RROWS, HEAD0, KEEP, EARLY, SOURCE = range(8)
OWN_FROM, OWN_TO, OWN, FAR_TO, FAR, SIDE = range(8, 14)
SEND = 32
ROW, TILES, FIRST, HEADS = range(4)
MOST, INNER_FROM, INNER_TO = 40, 41, 42
SCALARS = 48
MIB = 1024 * 1024


def sizes(rows, heads):
    tiles = rows // TILE
    cap = max(
        min(max(a * n, (tiles + 1 - a) * (heads - n)) for n in range(heads + 1))
        for a in range(1, tiles + 1)
    )
    padded = -(-cap // TILE) * TILE
    return cap, padded, 2 * padded


def angles(positions):
    pair_total = HD // 2
    side_pairs = HD // 6
    time_pairs = pair_total - 2 * side_pairs
    column = jnp.arange(HD, dtype=jnp.int32) // 2
    in_time = column < time_pairs
    in_height = (column >= time_pairs) & (column < time_pairs + side_pairs)
    in_width = column >= time_pairs + side_pairs
    local_index = jnp.where(
        in_time, column, jnp.where(in_height, column - time_pairs, column - time_pairs - side_pairs)
    )
    axis_pairs = jnp.where(in_time, time_pairs, side_pairs)
    frequency = jnp.exp(
        -(local_index.astype(jnp.float32) / axis_pairs.astype(jnp.float32)) * math.log(rope_theta)
    )
    selector = jnp.stack([in_time, in_height, in_width]).astype(jnp.float32) * frequency[None, :]
    placed = positions.astype(jnp.float32)
    return (
        placed[0][:, None] * selector[0][None, :]
        + placed[1][:, None] * selector[1][None, :]
        + placed[2][:, None] * selector[2][None, :]
    )


def plan_kernel(rows, heads, count, lengths, out, ls, rs, split, least):
    cap, padded, _ = sizes(rows, heads)
    here = lax.axis_index("req")
    shift = rows.bit_length() - 1

    def clear(b, carry):
        ls[b] = 0
        rs[b] = 0
        return carry

    lax.fori_loop(0, count + 3, clear, 0)

    def one_video(v, start):
        end = start + lengths[v]
        b = lax.shift_right_logical(end - 1, shift) if rows == 1 << shift else lax.div(end - 1, rows)
        at = b * rows

        @pl.when(start < at)
        def _():
            ls[b] = at - start
            rs[b] = end - at

        return end

    lax.fori_loop(0, lengths.shape[0], one_video, 0)
    budget = 3.0 * lax.broadcasted_iota(jnp.int32, (8, 128), 1).astype(jnp.float32)
    split[...] = jnp.zeros_like(split)

    def tiles_of(x):
        return lax.shift_right_logical(x + TILE - 1, 4)

    def eight(b):
        return pl.ds(pl.multiple_of(b * 8, 8), 8)

    def per_tile(x, tiles):
        return jnp.floor((x + 0.5) / jnp.maximum(tiles, 1.0))

    def facts(b):
        direct = lax.rem(b, 2).astype(jnp.float32)
        lt, rt = tiles_of(ls[b]).astype(jnp.float32), tiles_of(rs[b]).astype(jnp.float32)
        return lt, rt, padded + direct * 1e6

    def from_right(i, load):
        b = count - 1 - i
        lt, rt, limit = facts(b)
        room = jnp.minimum(budget - load, limit)
        n = jnp.where(rt > 0.0, jnp.maximum(heads - per_tile(room, rt), 0.0), 0.0)
        least[eight(b)] = jnp.where(room >= 0.0, n, 1e6)
        return lt * n

    def from_left(b, carry):
        load, ok = carry
        lt, rt, limit = facts(b)
        room = jnp.minimum(budget - load, limit)
        most = jnp.where(lt > 0.0, jnp.minimum(per_tile(room, lt), float(heads)), 0.0)
        low = least[eight(b)]
        even = jnp.floor(heads * rt / jnp.maximum(lt + rt, 1.0) + 0.5)
        n = jnp.minimum(most, jnp.maximum(low, even))
        split[eight(b)] = n
        return rt * (heads - n), jnp.where((room >= 0.0) & (low <= most), ok, 0.0)

    zero = jnp.zeros((8, 128), jnp.float32)
    lax.fori_loop(0, count - 1, from_right, zero)
    load, ok = lax.fori_loop(1, count, from_left, (zero, zero + 1.0))
    ok = jnp.where(load <= budget, ok, 0.0)
    most = jnp.min(jnp.where(ok > 0.0, budget, 1e9))
    out[MOST] = most.astype(jnp.int32)

    def head_split(b):
        n = split[eight(b)]
        return jnp.max(jnp.where(budget == most, n, 0.0)).astype(jnp.int32)

    even = lax.rem(here, 2) == 0
    beyond = jnp.where(even, here + 2, here - 1)
    n_left, n_right, n_beyond = head_split(here), head_split(here + 1), head_split(beyond)
    partner_passes = jnp.where(
        even,
        tiles_of(ls[beyond]) * n_beyond,
        tiles_of(rs[beyond]) * (heads - n_beyond),
    )
    for side, b, n in ((0, here, n_left), (1, here + 1, n_right)):
        direct = jnp.logical_not(even) if side == 0 else even
        at = jnp.where(direct, DIRECT, PASS)
        lt, rt = tiles_of(ls[b]), tiles_of(rs[b])
        none = jnp.where(lt > 0, 0, heads)
        keep = n if side == 0 else jnp.maximum(heads - n - none, 0)
        far = lt if side == 0 else rt
        out[at + LB], out[at + RB] = lt, rt
        out[at + LROWS], out[at + RROWS] = ls[b], rs[b]
        out[at + HEAD0] = 0 if side == 0 else n
        out[at + KEEP] = keep
        source = jnp.where(direct, partner_passes, 0)
        there = jnp.where(direct, padded + MORE, padded // CHUNKS * EARLY_CHUNKS) - source
        out[at + EARLY] = jnp.minimum(keep, lax.div(jnp.maximum(there, 0), jnp.maximum(far, 1)))
        out[at + SOURCE] = source
        out[at + OWN_FROM] = 0 if side == 0 else rows // TILE - lt
        out[at + OWN_TO] = lt if side == 0 else 0
        out[at + OWN] = rt if side == 0 else lt
        out[at + FAR_TO] = 0 if side == 0 else lt
        out[at + FAR] = far
        out[at + SIDE] = side
        to = SEND + jnp.where(direct, 4, 0)
        out[to + ROW] = 0 if side == 0 else rows - TILE * lt
        out[to + TILES] = rt if side == 0 else lt
        out[to + FIRST] = n if side == 0 else 0
        out[to + HEADS] = jnp.maximum(heads - n - none, 0) if side == 0 else n
    out[INNER_FROM] = rs[here]
    out[INNER_TO] = rows - ls[here + 1]


def in_groups(low, high, step):
    count = high - low

    def run(group, times):
        def body(i, carry):
            step(jnp.minimum(low + group * i, high - group), group)
            return carry

        lax.fori_loop(0, times, body, 0)

    run(8, jnp.where(count >= 8, lax.shift_right_logical(count + 7, 3), 0))
    run(2, jnp.where((count >= 2) & (count < 8), lax.shift_right_logical(count + 1, 1), 0))
    run(1, jnp.where(count == 1, 1, 0))


def lanes_of(h):
    return pl.ds(pl.multiple_of(h * HD, HD), HD)


def rows_of(t, group):
    return pl.ds(pl.multiple_of(t * TILE, TILE), group * TILE)


def turn(x, cosine, sine):
    wide = x.astype(jnp.float32)
    even = lax.rem(lax.broadcasted_iota(jnp.int32, wide.shape, 1), 2) == 0
    swapped = jnp.where(even, pltpu.roll(wide, HD - 1, 1), pltpu.roll(wide, 1, 1))
    return (wide * cosine + swapped * sine).astype(jnp.bfloat16)


def pack(scal, low, high, box, heads, get):
    base = 0
    for what in (SEND, SEND + 4):
        first_tile = lax.shift_right_logical(scal[what + ROW], 4)
        tiles, first, count = scal[what + TILES], scal[what + FIRST], scal[what + HEADS]

        def one_head(i, carry):
            start = base + (pl.program_id(0) * heads + i - first) * tiles
            begin = jnp.clip(low - start, 0, tiles)
            end = jnp.clip(high - start, 0, tiles)
            lanes = lanes_of(i)

            def step(t, group):
                q, k, v = get(rows_of(first_tile + t, group), lanes)
                item = pl.ds(start + t - low, group)
                box[item, 0:TILE] = q.reshape(group, TILE, HD)
                box[item, TILE : 2 * TILE] = k.reshape(group, TILE, HD)
                box[item, 2 * TILE : 3 * TILE] = v.reshape(group, TILE, HD)

            in_groups(begin, end, step)
            return carry

        before = first - pl.program_id(0) * heads
        lax.fori_loop(
            jnp.clip(before, 0, heads), jnp.clip(before + count, 0, heads), one_head, 0
        )
        base = base + tiles * count


def send_off(box, outs, sems):
    @pl.when(pl.program_id(0) == pl.num_programs(0) - 1)
    def _():
        at, copies = 0, []
        for i, out in enumerate(outs):
            copies.append(pltpu.make_async_copy(box.at[pl.ds(at, out.shape[0])], out, sems.at[i]))
            at += out.shape[0]
        for copy in copies:
            copy.start()
        for copy in copies:
            copy.wait()


def first_kernel(scal, q_hbm, k_hbm, v_hbm, cos_ref, sin_ref, box, qs, ks, vs, sems):
    limit = box.shape[0]
    ahead = qs.shape[0] - 1

    def heads_in(what, base):
        tiles = jnp.maximum(scal[what + TILES], 1)
        taken = lax.div(jnp.maximum(limit - base, 0) + tiles - 1, tiles)
        return jnp.minimum(scal[what + HEADS], taken)

    passed = scal[SEND + TILES] * scal[SEND + HEADS]
    count_pass = heads_in(SEND, 0)
    count = count_pass + heads_in(SEND + 4, passed)

    def entry(w):
        direct = w >= count_pass
        what = jnp.where(direct, SEND + 4, SEND)
        slot = w - jnp.where(direct, count_pass, 0)
        tiles = scal[what + TILES]
        start = jnp.where(direct, passed, 0) + slot * tiles
        return scal[what + FIRST] + slot, scal[what + ROW], tiles, start

    def copies(w):
        at = lax.rem(w, ahead + 1)
        lanes = lanes_of(entry(w)[0])
        return [
            pltpu.make_async_copy(source.at[:, lanes], place.at[at], sems.at[at, x])
            for x, (source, place) in enumerate(((q_hbm, qs), (k_hbm, ks), (v_hbm, vs)))
        ]

    for w in range(ahead):

        @pl.when(w < count)
        def _(w=w):
            for copy in copies(w):
                copy.start()

    def one_head(w, carry):
        @pl.when(w + ahead < count)
        def _():
            for copy in copies(w + ahead):
                copy.start()

        for copy in copies(w):
            copy.wait()
        at = lax.rem(w, ahead + 1)
        _, row, tiles, start = entry(w)
        first_tile = lax.shift_right_logical(row, 4)

        def step(t, group):
            source = rows_of(first_tile + t, group)
            cosine, sine = cos_ref[source, :], sin_ref[source, :]
            item = pl.ds(start + t, group)
            q, k = turn(qs[at, source, :], cosine, sine), turn(ks[at, source, :], cosine, sine)
            box[item, 0:TILE] = q.reshape(group, TILE, HD)
            box[item, TILE : 2 * TILE] = k.reshape(group, TILE, HD)
            box[item, 2 * TILE : 3 * TILE] = vs[at, source, :].reshape(group, TILE, HD)

        in_groups(0, jnp.clip(limit - start, 0, tiles), step)
        return carry

    lax.fori_loop(0, count, one_head, 0)


def second_kernel(
    low, scal, q_ref, k_ref, v_ref, cos_ref, sin_ref, swap_ref, wt_ref, mod_ref, qr_ref, kr_ref, w_ref, shift_ref, *rest
):
    outs, box, sems = rest[:-3], rest[-2], rest[-1]
    rows = q_ref.shape[0]
    heads = q_ref.shape[1] // HD
    wide = swap_ref.shape[0]

    @pl.when(pl.program_id(0) == 0)
    def _():
        w = wt_ref[...].astype(jnp.float32)
        scaled = w * (1.0 + mod_ref[1:2, :])
        high = scaled.astype(jnp.bfloat16)
        low = (scaled - high.astype(jnp.float32)).astype(jnp.bfloat16)
        w_ref[...] = jnp.concatenate([high, low], axis=0)
        shift = jnp.sum(w * mod_ref[0:1, :], axis=1, keepdims=True)
        shift_ref[...] = jnp.broadcast_to(shift, shift_ref.shape)

    for source, to in ((q_ref, qr_ref), (k_ref, kr_ref)):
        for h in range(0, heads, wide // HD):
            for j in range(rows // BLK):
                at = slice(j * BLK, (j + 1) * BLK)
                x = source[at, h * HD : h * HD + wide]
                swapped = jnp.dot(x, swap_ref[: x.shape[1], : x.shape[1]], preferred_element_type=jnp.float32)
                for i in range(x.shape[1] // HD):
                    lanes = slice(i * HD, (i + 1) * HD)
                    to[at, (h + i) * HD : (h + i + 1) * HD] = (
                        x[:, lanes].astype(jnp.float32) * cos_ref[at, :] + swapped[:, lanes] * sin_ref[at, :]
                    ).astype(jnp.bfloat16)

    def get(rows, lanes):
        return qr_ref[rows, lanes], kr_ref[rows, lanes], v_ref[rows, lanes]

    pack(scal, low, low + box.shape[0], box, heads, get)
    send_off(box, outs, sems)


def dot_t(a, b):
    return lax.dot_general(a, b, (((1,), (1,)), ((), ())), preferred_element_type=jnp.float32)


def attend_rows(q, k, v_ones, masked):
    s = masked(dot_t(q, k))
    top = jnp.max(s, axis=1, keepdims=True)
    weight = jnp.exp2(s * SCALE2 - top * SCALE2).astype(jnp.bfloat16)
    both = jnp.dot(weight, v_ones, preferred_element_type=jnp.float32)
    return (both[:, :HD] / both[:, HD:]).astype(jnp.bfloat16)


def projected(o_ref, w_ref, out_ref, rows):
    for j in range(rows // BLK):
        at = slice(j * BLK, (j + 1) * BLK)
        z = dot_t(o_ref[at, :], w_ref[...])
        z = z + pltpu.roll(z, HD // 2, 1)
        lane = lax.broadcasted_iota(jnp.int32, z.shape, 1)
        squares = jnp.zeros(z.shape, jnp.float32)
        for h in range(o_ref.shape[1] // HD):
            wide = o_ref[at, h * HD : (h + 1) * HD].astype(jnp.float32)
            squares = squares + wide * wide
        total = jnp.sum(squares, axis=1, keepdims=True)
        out_ref[at, :] = jnp.where(lane < HD // 2, z, jnp.where(lane == HD // 2, total, 0.0))


def inner_kernel(scal, q_ref, k_ref, v_ref, w_ref, qv_ref, kv_ref, out_ref, o_ref):
    g = pl.program_id(0)
    rows, width = q_ref.shape
    ones = jnp.ones((rows, HD), jnp.bfloat16)
    for j in range(rows // BLK):
        at = pl.ds(j * BLK, BLK)
        same = qv_ref[at, :] == kv_ref[...]
        for i in range(width // HD):
            lanes = slice(i * HD, (i + 1) * HD)
            v_ones = jnp.concatenate([v_ref[:, lanes], ones], axis=1)
            o_ref[at, pl.ds(pl.multiple_of(g * width + i * HD, HD), HD)] = attend_rows(
                q_ref[at, lanes], k_ref[:, lanes], v_ones, lambda s: jnp.where(same, s, NEG)
            )

    @pl.when(g == pl.num_programs(0) - 1)
    def _():
        projected(o_ref, w_ref, out_ref, rows)


def across(scal, at, offset, low, high, sources, items, w_ref, own_sems, places, o_ref, zz):
    rows = zz.shape[0] // 2
    left, right = scal[at + LB], scal[at + RB]
    lead = left * TILE - scal[at + LROWS]
    end = left * TILE + scal[at + RROWS]
    blocks = jnp.minimum(lax.div((left + right) * TILE + BLK - 1, BLK), rows // BLK)
    own_at = jnp.where(scal[at + SIDE] == 0, rows, 0) + left * TILE
    pairs = lax.shift_right_logical(high - low + 1, 1)

    def heads_of(i):
        return [jnp.minimum(low + 2 * i + u, high - 1) for u in range(2)]

    def own_copies(i):
        slot = lax.rem(i, 2)
        to = pl.ds(pl.multiple_of(own_at, TILE), rows)
        return [
            pltpu.make_async_copy(
                source.at[:, lanes_of(scal[at + HEAD0] + s)], place.at[slot, u, to, :],
                own_sems.at[slot, u, x],
            )
            for u, s in enumerate(heads_of(i))
            for x, (source, place) in enumerate(zip(sources, places))
        ]

    @pl.when(pairs > 0)
    def _():
        for copy in own_copies(0):
            copy.start()

    def two_heads(n, i, carry):
        slot = lax.rem(i, 2)

        @pl.when(i + 1 < pairs)
        def _():
            for copy in own_copies(i + 1):
                copy.start()

        heads = heads_of(i)

        def foreign(t, group):
            to = rows_of(rows // TILE + scal[at + FAR_TO] + t, group)
            for u, s in enumerate(heads):
                item = pl.ds(scal[at + SOURCE] + offset + s * scal[at + FAR] + t, group)
                for x, place in enumerate(places):
                    part = items[item, x * TILE : (x + 1) * TILE]
                    place[slot, u, to, :] = part.reshape(group * TILE, HD)

        in_groups(0, scal[at + FAR], foreign)
        for copy in own_copies(i):
            copy.wait()
        width = n * BLK
        if width == rows:

            @pl.when((left + right) * TILE > rows)
            def _():
                row = lax.broadcasted_iota(jnp.int32, (TILE, HD), 0)
                for place in places:
                    for u in range(2):
                        first = place[slot, u, rows : rows + TILE, :]
                        last = place[slot, u, 2 * rows : 2 * rows + TILE, :]
                        place[slot, u, rows : rows + TILE, :] = jnp.where(row < lead, last, first)

        place = lax.broadcasted_iota(jnp.int32, (1, width), 1)
        valid = ((place >= lead) & (place < end)) | (place + rows < end)
        bias = jnp.where(valid, 0.0, NEG)
        ones = jnp.ones((width, HD), jnp.bfloat16)
        qs, ks, vs = places
        whole = slice(rows, rows + width)
        for j in range(n):
            mine = slice(rows + j * BLK, rows + (j + 1) * BLK)
            for u, s in enumerate(heads):
                v_ones = jnp.concatenate([vs[slot, u, whole, :], ones], axis=1)
                o_ref[j * BLK : (j + 1) * BLK, lanes_of(scal[at + HEAD0] + s)] = attend_rows(
                    qs[slot, u, mine, :], ks[slot, u, whole, :], v_ones, lambda x: x + bias
                )
        return carry

    for n in range(1, rows // BLK + 1):

        @pl.when((blocks == n) & (pairs > 0))
        def _(n=n):
            o_ref[0 : n * BLK, :] = jnp.zeros((n * BLK, o_ref.shape[1]), o_ref.dtype)
            lax.fori_loop(0, pairs, functools.partial(two_heads, n), 0)
            projected(o_ref, w_ref, zz, n * BLK)
            zz[rows : 2 * rows, :] = zz[0:rows, :]

    @pl.when(pairs <= 0)
    def _():
        zz[...] = jnp.zeros_like(zz)

    return zz[pl.ds(pl.multiple_of(left * TILE, TILE), rows), :]


def fetch(scal, at, offset, low, high, places, boxes, items, sems):
    begin = scal[at + SOURCE] + offset + low * scal[at + FAR]
    end = scal[at + SOURCE] + offset + high * scal[at + FAR]
    return [
        (
            pltpu.make_async_copy(box, items.at[pl.ds(place, box.shape[0])], sems.at[i]),
            (high > low) & (begin < place + box.shape[0]) & (end > place),
        )
        for i, (place, box) in enumerate(zip(places, boxes))
    ]


def clear(places, rows):
    for place in places:
        for slot in range(2):
            for u in range(2):
                place[slot, u, rows : 2 * rows + TILE, :] = jnp.zeros((rows + TILE, HD), place.dtype)


def of_boundary(scal, at, shape, mine):
    row = lax.broadcasted_iota(jnp.int32, shape, 0)
    tail = jnp.where(row >= shape[0] - scal[at + LROWS], 1, 0)
    head = jnp.where(row < scal[at + RROWS], 1, 0)
    right_is_mine = (scal[at + SIDE] == 0) == mine
    return jnp.where(right_is_mine, head, tail) == 1


def send_back(scal, at, z, back_ref):
    lane = lax.broadcasted_iota(jnp.int32, z.shape, 1)
    back = jnp.where(of_boundary(scal, at, z.shape, False), z, 0.0)
    high = back.astype(jnp.bfloat16).astype(jnp.float32)
    both = jnp.where(lane == HD // 2 + 1, pltpu.roll(back - high, 1, 1), high)
    back_ref[...] = both.T[: back_ref.shape[0]].astype(jnp.bfloat16)


def early_kernel(places, at, scal, q_hbm, k_hbm, v_hbm, w_ref, *rest):
    boxes, (out_ref, items, sems, own_sems, qs, ks, vs, o_ref, zz) = rest[: len(places)], rest[len(places) :]
    high = scal[at + EARLY]
    copies = fetch(scal, at, 0, 0, high, places, boxes, items, sems)
    for copy, need in copies:
        pl.when(need)(copy.start)
    clear((qs, ks, vs), zz.shape[0] // 2)
    for copy, need in copies:
        pl.when(need)(copy.wait)
    out_ref[...] = across(
        scal, at, 0, 0, high, (q_hbm, k_hbm, v_hbm), items, w_ref, own_sems, (qs, ks, vs), o_ref, zz
    )


def last_kernel(places, offsets, scal, q_hbm, k_hbm, v_hbm, w_ref, *rest):
    partials, rest = rest[:4], rest[4:]
    boxes, rest = rest[: len(places)], rest[len(places) :]
    own_ref, pass_back_ref, direct_back_ref, items, sems, own_sems, qs, ks, vs, o_ref, zz, sums, sum_sems = rest
    sum_copies = [
        pltpu.make_async_copy(part, sums.at[i], sum_sems.at[i]) for i, part in enumerate(partials)
    ]
    for copy in sum_copies:
        copy.start()
    clear((qs, ks, vs), zz.shape[0] // 2)

    def remaining(at, offset):
        low, high = scal[at + EARLY], scal[at + KEEP]
        copies = fetch(scal, at, offset, low, high, places, boxes, items, sems)
        for copy, need in copies:
            pl.when(need)(copy.start)
        for copy, need in copies:
            pl.when(need)(copy.wait)
        return across(
            scal, at, offset, low, high, (q_hbm, k_hbm, v_hbm), items, w_ref, own_sems, (qs, ks, vs), o_ref, zz
        )

    passed_z = remaining(PASS, offsets[0])
    for copy in sum_copies:
        copy.wait()
    passed_z = passed_z + sums[0]
    send_back(scal, PASS, passed_z, pass_back_ref)
    own = jnp.where(of_boundary(scal, PASS, passed_z.shape, True), passed_z, sums[2] + sums[3])
    direct_z = sums[1] + remaining(DIRECT, offsets[1])
    send_back(scal, DIRECT, direct_z, direct_back_ref)
    own = jnp.where(of_boundary(scal, DIRECT, own.shape, True), direct_z, own)
    own_ref[...] = own.T[: own_ref.shape[0]]


def step_rows(video_ids, step_sizes):
    chosen = video_ids[:, None] == jnp.arange(step_sizes.shape[0], dtype=jnp.int32)[None, :]
    return jnp.sum(jnp.where(chosen, step_sizes[None, :], 0.0), axis=1)


def call(kernel, name, mib, scalars, operands, in_specs, outs, out_specs, scratch, grid=()):
    return pl.pallas_call(
        kernel,
        out_shape=outs,
        grid_spec=pltpu.PrefetchScalarGridSpec(
            num_scalar_prefetch=1, grid=grid, in_specs=in_specs, out_specs=out_specs,
            scratch_shapes=scratch,
        ),
        compiler_params=pltpu.CompilerParams(vmem_limit_bytes=mib * MIB),
        cost_estimate=pl.CostEstimate(flops=1, bytes_accessed=1, transcendentals=0),
        name=name,
    )(scalars, *operands)


def per_device(
    query_rows, key_rows, value_rows, positions, latents, w_head, modulation,
    guide_scale, step_sizes, lengths,
):
    rows, features = query_rows.shape[1], query_rows.shape[2]
    heads = features // HD
    count = lax.axis_size("req")
    here = lax.axis_index("req")
    first_row = here * rows
    _, padded, room = sizes(rows, heads)
    chunk = padded // CHUNKS
    late_sizes = (*[chunk] * (CHUNKS - 1), MORE, room - padded - MORE)

    angle = angles(positions)
    odd = (jnp.arange(HD, dtype=jnp.int32) % 2).astype(jnp.float32)
    cosine = jnp.cos(angle)
    sine = jnp.sin(angle) * (2.0 * odd - 1.0)[None, :]

    smem = pl.BlockSpec(memory_space=pltpu.SMEM)
    vmem = pl.BlockSpec(memory_space=pltpu.VMEM)
    hbm = pl.BlockSpec(memory_space=pl.ANY)
    parity = lax.axis_index("cfg")
    tie = lax.optimization_barrier
    scalars = pl.pallas_call(
        functools.partial(plan_kernel, rows, heads, count),
        out_shape=jax.ShapeDtypeStruct((SCALARS,), jnp.int32),
        in_specs=[smem],
        out_specs=smem,
        scratch_shapes=[
            pltpu.SMEM((count + 3,), jnp.int32),
            pltpu.SMEM((count + 3,), jnp.int32),
            pltpu.VMEM(((count + 3) * 8, 128), jnp.float32),
            pltpu.VMEM(((count + 3) * 8, 128), jnp.float32),
        ],
        name="plan",
    )(lengths)

    def in_hbm(x):
        return pltpu.with_memory_space_constraint(x, pltpu.HBM)

    q, k, v = query_rows[0], key_rows[0], value_rows[0]

    def box(items):
        return jax.ShapeDtypeStruct((items, 3 * TILE, HD), jnp.bfloat16)

    def box_scratch(items):
        return pltpu.VMEM((items, 3 * TILE, HD), jnp.bfloat16)

    group = next(n for n in (5, 4, 3, 2, 1) if heads % n == 0)
    steps = heads // group
    head_block = pl.BlockSpec((rows, group * HD), lambda g, s: (0, g))
    table = pl.BlockSpec((rows, HD), lambda g, s: (0, 0))
    first = call(
        first_kernel, "pack_first", 16, scalars, (in_hbm(q), in_hbm(k), in_hbm(v), cosine, sine),
        [hbm] * 3 + [vmem] * 2, (box(chunk),), (vmem,),
        [*[pltpu.VMEM((4, rows, HD), jnp.bfloat16)] * 3, pltpu.SemaphoreType.DMA((4, 3))],
    )
    pairs = [(i, i ^ 1) for i in range(count)]
    onward = [(i, i + 2) for i in range(0, count - 2, 2)] + [(i + 2, i) for i in range(1, count - 2, 2)]
    got = [lax.ppermute(first[0], "req", pairs)]

    after_first, _ = tie((scalars, first[0]))
    swap = jnp.asarray(numpy.eye(2 * HD)[numpy.arange(2 * HD) ^ 1], jnp.bfloat16)
    q_rot, k_rot, w_both, shift, *second = call(
        functools.partial(second_kernel, chunk), "turn_and_pack_rest", 32, after_first,
        (in_hbm(q), in_hbm(k), in_hbm(v), cosine, sine, swap, w_head.T, modulation),
        [head_block] * 3 + [table] * 2 + [vmem] * 3,
        (pltpu.HBM(q.shape, q.dtype), pltpu.HBM(k.shape, k.dtype),
         jax.ShapeDtypeStruct((HD, features), jnp.bfloat16),
         jax.ShapeDtypeStruct((HD // 2, HD), jnp.float32),
         *[box(n) for n in late_sizes], box(late_sizes[-1])),
        (head_block, head_block, vmem, vmem, *[hbm] * (len(late_sizes) + 1)),
        [box_scratch(sum(late_sizes)), pltpu.SemaphoreType.DMA((len(late_sizes),))], grid=(steps,),
    )
    got += [lax.ppermute(x, "req", pairs) for x in second[: CHUNKS - 1]]
    more, arriving = second[CHUNKS:]

    own_rows = first_row + jnp.arange(rows, dtype=jnp.int32)
    video = jnp.sum((jnp.cumsum(lengths)[None, :] <= own_rows[:, None]).astype(jnp.int32), axis=1)
    step_of_row = step_rows(video, step_sizes)

    def inner(when, first_step, step_count):
        block = pl.BlockSpec((rows, group * HD), lambda g, s: (0, g + first_step))
        width = step_count * group * HD
        return call(
            inner_kernel, "inner_videos", 20, when,
            (in_hbm(q_rot), in_hbm(k_rot), in_hbm(v), w_both, video[:, None], video[None, :]),
            [block] * 3 + [pl.BlockSpec((HD, width), lambda g, s: (0, first_step // step_count))] + [vmem] * 2, pltpu.HBM((rows, HD), jnp.float32), vmem,
            [pltpu.VMEM((rows, width), jnp.bfloat16)], grid=(step_count,),
        )

    got[1], second[CHUNKS - 1] = tie((got[1], second[CHUNKS - 1]))
    got.append(lax.ppermute(second[CHUNKS - 1], "req", pairs))
    when_a, got[0] = tie((scalars, got[0]))
    inner_a = inner(when_a, 0, steps // 2)
    got[1], inner_a = tie((got[1], inner_a))
    passed = [lax.ppermute(x, "req", onward) for x in got[:2]]
    when_b, passed[0], got[2], inner_a = tie((scalars, passed[0], got[2], inner_a))
    inner_b = inner(when_b, steps // 2, steps - steps // 2)
    got[3], inner_b = tie((got[3], inner_b))
    when_early, got[3] = tie((scalars, got[3]))
    passed += [lax.ppermute(x, "req", onward) for x in got[2:CHUNKS]]

    place = pltpu.VMEM((2, 2, 3 * rows, HD), jnp.bfloat16)
    work = [
        pltpu.SemaphoreType.DMA((2, 2, 3)), place, place, place,
        pltpu.VMEM((rows, features), jnp.bfloat16),
        pltpu.VMEM((2 * rows, HD), jnp.float32),
    ]
    partial = pltpu.HBM((rows, HD), jnp.float32)
    lanes = HD // 2 + TILE
    sent_back = jax.ShapeDtypeStruct((lanes, rows), jnp.bfloat16)

    def on_videos_across(kernel, name, when, boxes, outs, others=(), scratch=()):
        places = [0]
        for x in boxes:
            places.append(places[-1] + x.shape[0])
        return call(
            kernel(tuple(places[:-1])), name, 32, when,
            (in_hbm(q_rot), in_hbm(k_rot), in_hbm(v), w_both, *[in_hbm(x) for x in others], *boxes),
            [hbm] * 3 + [vmem] + [hbm] * (len(others) + len(boxes)),
            outs, jax.tree.map(lambda _: vmem, outs),
            [box_scratch(places[-1]), pltpu.SemaphoreType.DMA((len(boxes),)), *work, *scratch],
        )

    def early_on(at, name, when, boxes):
        return on_videos_across(
            lambda places: functools.partial(early_kernel, places, at), name, when, boxes,
            partial,
        )

    early = early_on(PASS, "videos_across_early", when_early, passed[:EARLY_CHUNKS])
    when_direct, early, passed[2] = tie((scalars, early, passed[2]))
    direct_z = early_on(DIRECT, "videos_across_direct", when_direct, got)

    pieces = jnp.maximum(scalars[MOST] - padded - MORE + EXTRA - 1, 0) // EXTRA
    pieces, direct_z = tie((pieces, direct_z))

    def one_more(i, arrived):
        piece = lax.dynamic_slice_in_dim(more, i * EXTRA, EXTRA, 0)
        piece = lax.ppermute(piece, "req", pairs)
        return lax.dynamic_update_slice_in_dim(arrived, piece, i * EXTRA, 0)

    arrived = lax.fori_loop(0, pieces, one_more, arriving)
    before = EARLY_CHUNKS - 1
    offsets = (-chunk * before, chunk * (CHUNKS - before))
    own, to_beyond, to_direct = on_videos_across(
        lambda places: functools.partial(last_kernel, places, offsets), "videos_across_last", scalars,
        [*passed[before:], *got, arrived],
        (jax.ShapeDtypeStruct((lanes, rows), jnp.float32), sent_back, sent_back),
        (early, direct_z, inner_a, inner_b),
        (pltpu.VMEM((4, rows, HD), jnp.float32), pltpu.SemaphoreType.DMA((4,))),
    )
    back_direct = lax.ppermute(to_direct, "req", pairs)
    beyond = [(i, i + 1) for i in range(1, count - 1, 2)] + [(i + 1, i) for i in range(1, count - 1, 2)]
    back_beyond = lax.ppermute(to_beyond, "req", beyond)
    total = own + back_direct.astype(jnp.float32) + back_beyond.astype(jnp.float32)
    values = HD // 2
    squares = total[values : values + 1] + total[values + 1 : values + 2]
    velocity = total[:values] * lax.rsqrt(squares / features + 1e-06) + shift[:, :1]

    width = latents.shape[1]
    mine = lax.dynamic_slice_in_dim(velocity, parity * width, width, 0)
    theirs = lax.dynamic_slice_in_dim(velocity, (1 - parity) * width, width, 0)
    partner = lax.ppermute(theirs, "cfg", [(0, 1), (1, 0)])
    conditional = jnp.where(parity == 0, mine, partner)
    unconditional = jnp.where(parity == 0, partner, mine)
    guided = unconditional + guide_scale[0] * (conditional - unconditional)
    return (latents.T + step_of_row[None, :] * guided).T


def solution(mesh):
    in_specs = (
        P("cfg", "req", None), P("cfg", "req", None), P("cfg", "req", None),
        P(None, "req"), P("req", "cfg"), P(), P(), P(), P(), P(),
    )
    return jax.shard_map(
        per_device, mesh=mesh, in_specs=in_specs, out_specs=P("req", "cfg"), check_vma=False
    )
```

```python
import functools
import math

import jax
import jax.numpy as jnp
import numpy
from jax import lax
from jax.experimental import pallas as pl
from jax.experimental.pallas import tpu as pltpu
from jax.sharding import PartitionSpec as P

HD = 128
TILE = 16
BLK = 128
CHUNKS = 4
MORE = 48
EXTRA = 16
EARLY_CHUNKS = 2
rope_theta = 10000.0
NEG = -1e30
SCALE2 = math.log2(math.e) / math.sqrt(HD)

PASS, DIRECT = 0, 16
LB, RB, LROWS, RROWS, HEAD0, KEEP, EARLY, SOURCE = range(8)
OWN_FROM, OWN_TO, OWN, FAR_TO, FAR, SIDE = range(8, 14)
SEND = 32
ROW, TILES, FIRST, HEADS = range(4)
MOST, INNER_FROM, INNER_TO = 40, 41, 42
SCALARS = 48
MIB = 1024 * 1024


def sizes(rows, heads):
    tiles = rows // TILE
    cap = max(
        min(max(a * n, (tiles + 1 - a) * (heads - n)) for n in range(heads + 1))
        for a in range(1, tiles + 1)
    )
    padded = -(-cap // TILE) * TILE
    return cap, padded, 2 * padded


def pieces_of(padded):
    most = padded * 3 // 11
    return (*[most] * (CHUNKS - 1), padded - most * (CHUNKS - 1))


def angles(positions):
    pair_total = HD // 2
    side_pairs = HD // 6
    time_pairs = pair_total - 2 * side_pairs
    column = jnp.arange(HD, dtype=jnp.int32) // 2
    in_time = column < time_pairs
    in_height = (column >= time_pairs) & (column < time_pairs + side_pairs)
    in_width = column >= time_pairs + side_pairs
    local_index = jnp.where(
        in_time, column, jnp.where(in_height, column - time_pairs, column - time_pairs - side_pairs)
    )
    axis_pairs = jnp.where(in_time, time_pairs, side_pairs)
    frequency = jnp.exp(
        -(local_index.astype(jnp.float32) / axis_pairs.astype(jnp.float32)) * math.log(rope_theta)
    )
    selector = jnp.stack([in_time, in_height, in_width]).astype(jnp.float32) * frequency[None, :]
    placed = positions.astype(jnp.float32)
    return (
        placed[0][:, None] * selector[0][None, :]
        + placed[1][:, None] * selector[1][None, :]
        + placed[2][:, None] * selector[2][None, :]
    )


def plan_kernel(rows, heads, count, lengths, out, ls, rs, split, least):
    cap, padded, _ = sizes(rows, heads)
    here = lax.axis_index("req")
    shift = rows.bit_length() - 1

    def clear(b, carry):
        ls[b] = 0
        rs[b] = 0
        return carry

    lax.fori_loop(0, count + 8, clear, 0)

    def one_video(v, start):
        end = start + lengths[v]
        b = lax.shift_right_logical(end - 1, shift) if rows == 1 << shift else lax.div(end - 1, rows)
        at = b * rows

        @pl.when(start < at)
        def _():
            ls[b] = at - start
            rs[b] = end - at

        return end

    lax.fori_loop(0, lengths.shape[0], one_video, 0)
    budget = 3.0 * lax.broadcasted_iota(jnp.int32, (8, 128), 1).astype(jnp.float32)
    split[...] = jnp.zeros_like(split)

    def tiles_of(x):
        return lax.shift_right_logical(x + TILE - 1, 4)

    def eight(b):
        return pl.ds(pl.multiple_of(b * 8, 8), 8)

    def per_tile(x, tiles):
        return jnp.floor((x + 0.5) * (1.0 / jnp.maximum(tiles, 1.0)))

    def facts(b):
        direct = lax.rem(b, 2).astype(jnp.float32)
        lt, rt = (jnp.full((8, 128), tiles_of(x[b]).astype(jnp.float32)) for x in (ls, rs))
        return lt, rt, padded + direct * 1e6

    def five_at_a_time(step, carry):
        def body(i, carry):
            for u in range(5):
                carry = step(5 * i + u, carry)
            return carry

        return lax.fori_loop(0, -(-(count - 1) // 5), body, carry)

    def from_right(i, load):
        b = -(-(count - 1) // 5) * 5 - i
        lt, rt, limit = facts(b)
        room = jnp.minimum(budget - load, limit)
        n = jnp.where(rt > 0.0, jnp.maximum(heads - per_tile(room, rt), 0.0), 0.0)
        least[eight(b)] = jnp.where(room >= 0.0, n, 1e6)
        return lt * n

    def from_left(i, carry):
        load, ok = carry
        b = i + 1
        lt, rt, limit = facts(b)
        room = jnp.minimum(budget - load, limit)
        most = jnp.where(lt > 0.0, jnp.minimum(per_tile(room, lt), float(heads)), 0.0)
        low = least[eight(b)]
        even = jnp.floor(heads * rt / jnp.maximum(lt + rt, 1.0) + 0.5)
        n = jnp.minimum(most, jnp.maximum(low, even))
        split[eight(b)] = n
        return rt * (heads - n), jnp.where((room >= 0.0) & (low <= most), ok, 0.0)

    zero = jnp.zeros((8, 128), jnp.float32)
    five_at_a_time(from_right, zero)
    load, ok = five_at_a_time(from_left, (zero, zero + 1.0))
    ok = jnp.where(load <= budget, ok, 0.0)
    most = jnp.min(jnp.where((ok > 0.0) & (budget >= (padded + MORE) // 3 * 3), budget, 1e9))
    out[MOST] = most.astype(jnp.int32)

    def head_split(b):
        n = split[eight(b)]
        return jnp.max(jnp.where(budget == most, n, 0.0)).astype(jnp.int32)

    even = lax.rem(here, 2) == 0
    beyond = jnp.where(even, here + 2, here - 1)
    n_left, n_right, n_beyond = head_split(here), head_split(here + 1), head_split(beyond)
    partner_passes = jnp.where(
        even,
        tiles_of(ls[beyond]) * n_beyond,
        tiles_of(rs[beyond]) * (heads - n_beyond),
    )
    for side, b, n in ((0, here, n_left), (1, here + 1, n_right)):
        direct = jnp.logical_not(even) if side == 0 else even
        at = jnp.where(direct, DIRECT, PASS)
        lt, rt = tiles_of(ls[b]), tiles_of(rs[b])
        none = jnp.where(lt > 0, 0, heads)
        keep = n if side == 0 else jnp.maximum(heads - n - none, 0)
        far = lt if side == 0 else rt
        out[at + LB], out[at + RB] = lt, rt
        out[at + LROWS], out[at + RROWS] = ls[b], rs[b]
        out[at + HEAD0] = 0 if side == 0 else n
        out[at + KEEP] = keep
        source = jnp.where(direct, partner_passes, 0)
        there = jnp.where(direct, padded, sum(pieces_of(padded)[:EARLY_CHUNKS])) - source
        out[at + EARLY] = jnp.minimum(keep, lax.div(jnp.maximum(there, 0), jnp.maximum(far, 1)))
        out[at + SOURCE] = source
        out[at + OWN_FROM] = 0 if side == 0 else rows // TILE - lt
        out[at + OWN_TO] = lt if side == 0 else 0
        out[at + OWN] = rt if side == 0 else lt
        out[at + FAR_TO] = 0 if side == 0 else lt
        out[at + FAR] = far
        out[at + SIDE] = side
        to = SEND + jnp.where(direct, 4, 0)
        out[to + ROW] = 0 if side == 0 else rows - TILE * lt
        out[to + TILES] = rt if side == 0 else lt
        out[to + FIRST] = n if side == 0 else 0
        out[to + HEADS] = jnp.maximum(heads - n - none, 0) if side == 0 else n
    out[INNER_FROM] = rs[here]
    out[INNER_TO] = rows - ls[here + 1]


def in_groups(low, high, step):
    count = high - low

    def run(group, times):
        def body(i, carry):
            step(jnp.minimum(low + group * i, high - group), group)
            return carry

        lax.fori_loop(0, times, body, 0)

    run(8, jnp.where(count >= 8, lax.shift_right_logical(count + 7, 3), 0))
    run(2, jnp.where((count >= 2) & (count < 8), lax.shift_right_logical(count + 1, 1), 0))
    run(1, jnp.where(count == 1, 1, 0))


def lanes_of(h):
    return pl.ds(pl.multiple_of(h * HD, HD), HD)


def rows_of(t, group):
    return pl.ds(pl.multiple_of(t * TILE, TILE), group * TILE)


def turn(x, cosine, sine):
    wide = x.astype(jnp.float32)
    even = lax.rem(lax.broadcasted_iota(jnp.int32, wide.shape, 1), 2) == 0
    swapped = jnp.where(even, pltpu.roll(wide, HD - 1, 1), pltpu.roll(wide, 1, 1))
    return (wide * cosine + swapped * sine).astype(jnp.bfloat16)


def pack(scal, low, high, box, heads, get):
    base = 0
    for what in (SEND, SEND + 4):
        first_tile = lax.shift_right_logical(scal[what + ROW], 4)
        tiles, first, count = scal[what + TILES], scal[what + FIRST], scal[what + HEADS]

        def one_head(i, carry):
            start = base + (pl.program_id(0) * heads + i - first) * tiles
            begin = jnp.clip(low - start, 0, tiles)
            end = jnp.clip(high - start, 0, tiles)
            lanes = lanes_of(i)

            def step(t, group):
                q, k, v = get(rows_of(first_tile + t, group), lanes)
                item = pl.ds(start + t - low, group)
                box[item, 0:TILE] = q.reshape(group, TILE, HD)
                box[item, TILE : 2 * TILE] = k.reshape(group, TILE, HD)
                box[item, 2 * TILE : 3 * TILE] = v.reshape(group, TILE, HD)

            in_groups(begin, end, step)
            return carry

        before = first - pl.program_id(0) * heads
        lax.fori_loop(
            jnp.clip(before, 0, heads), jnp.clip(before + count, 0, heads), one_head, 0
        )
        base = base + tiles * count


def send_off(box, outs, sems):
    @pl.when(pl.program_id(0) == pl.num_programs(0) - 1)
    def _():
        at, copies = 0, []
        for i, out in enumerate(outs):
            copies.append(pltpu.make_async_copy(box.at[pl.ds(at, out.shape[0])], out, sems.at[i]))
            at += out.shape[0]
        for copy in copies:
            copy.start()
        for copy in copies:
            copy.wait()


def first_kernel(scal, q_hbm, k_hbm, v_hbm, cos_ref, sin_ref, box, qs, ks, vs, sems):
    limit = box.shape[0]
    ahead = qs.shape[0] - 1

    def heads_in(what, base):
        tiles = jnp.maximum(scal[what + TILES], 1)
        taken = lax.div(jnp.maximum(limit - base, 0) + tiles - 1, tiles)
        return jnp.minimum(scal[what + HEADS], taken)

    passed = scal[SEND + TILES] * scal[SEND + HEADS]
    count_pass = heads_in(SEND, 0)
    count = count_pass + heads_in(SEND + 4, passed)

    def entry(w):
        direct = w >= count_pass
        what = jnp.where(direct, SEND + 4, SEND)
        slot = w - jnp.where(direct, count_pass, 0)
        tiles = scal[what + TILES]
        start = jnp.where(direct, passed, 0) + slot * tiles
        return scal[what + FIRST] + slot, scal[what + ROW], tiles, start

    def copies(w):
        at = lax.rem(w, ahead + 1)
        lanes = lanes_of(entry(w)[0])
        return [
            pltpu.make_async_copy(source.at[:, lanes], place.at[at], sems.at[at, x])
            for x, (source, place) in enumerate(((q_hbm, qs), (k_hbm, ks), (v_hbm, vs)))
        ]

    for w in range(ahead):

        @pl.when(w < count)
        def _(w=w):
            for copy in copies(w):
                copy.start()

    def one_head(w, carry):
        @pl.when(w + ahead < count)
        def _():
            for copy in copies(w + ahead):
                copy.start()

        for copy in copies(w):
            copy.wait()
        at = lax.rem(w, ahead + 1)
        _, row, tiles, start = entry(w)
        first_tile = lax.shift_right_logical(row, 4)

        def step(t, group):
            source = rows_of(first_tile + t, group)
            cosine, sine = cos_ref[source, :], sin_ref[source, :]
            item = pl.ds(start + t, group)
            q, k = turn(qs[at, source, :], cosine, sine), turn(ks[at, source, :], cosine, sine)
            box[item, 0:TILE] = q.reshape(group, TILE, HD)
            box[item, TILE : 2 * TILE] = k.reshape(group, TILE, HD)
            box[item, 2 * TILE : 3 * TILE] = vs[at, source, :].reshape(group, TILE, HD)

        in_groups(0, jnp.clip(limit - start, 0, tiles), step)
        return carry

    lax.fori_loop(0, count, one_head, 0)


def second_kernel(
    low, scal, q_ref, k_ref, v_ref, cos_ref, sin_ref, swap_ref, wt_ref, mod_ref, qr_ref, kr_ref, w_ref, shift_ref, *rest
):
    outs, box, sems = rest[:-3], rest[-2], rest[-1]
    rows = q_ref.shape[0]
    heads = q_ref.shape[1] // HD
    wide = swap_ref.shape[0]

    @pl.when(pl.program_id(0) == 0)
    def _():
        w = wt_ref[...].astype(jnp.float32)
        scaled = w * (1.0 + mod_ref[1:2, :])
        high = scaled.astype(jnp.bfloat16)
        low = (scaled - high.astype(jnp.float32)).astype(jnp.bfloat16)
        w_ref[...] = jnp.concatenate([high, low], axis=0)
        shift = jnp.sum(w * mod_ref[0:1, :], axis=1, keepdims=True)
        shift_ref[...] = jnp.broadcast_to(shift, shift_ref.shape)

    for source, to in ((q_ref, qr_ref), (k_ref, kr_ref)):
        for h in range(0, heads, wide // HD):
            for j in range(rows // BLK):
                at = slice(j * BLK, (j + 1) * BLK)
                x = source[at, h * HD : h * HD + wide]
                swapped = jnp.dot(x, swap_ref[: x.shape[1], : x.shape[1]], preferred_element_type=jnp.float32)
                for i in range(x.shape[1] // HD):
                    lanes = slice(i * HD, (i + 1) * HD)
                    to[at, (h + i) * HD : (h + i + 1) * HD] = (
                        x[:, lanes].astype(jnp.float32) * cos_ref[at, :] + swapped[:, lanes] * sin_ref[at, :]
                    ).astype(jnp.bfloat16)

    def get(rows, lanes):
        return qr_ref[rows, lanes], kr_ref[rows, lanes], v_ref[rows, lanes]

    pack(scal, low, low + box.shape[0], box, heads, get)
    send_off(box, outs, sems)


def dot_t(a, b):
    return lax.dot_general(a, b, (((1,), (1,)), ((), ())), preferred_element_type=jnp.float32)


def attend_rows(q, k, v_ones, masked):
    s = masked(dot_t(q, k))
    top = jnp.max(s, axis=1, keepdims=True)
    weight = jnp.exp2(s * SCALE2 - top * SCALE2).astype(jnp.bfloat16)
    both = jnp.dot(weight, v_ones, preferred_element_type=jnp.float32)
    return (both[:, :HD] / both[:, HD:]).astype(jnp.bfloat16)


def project_block(o_ref, w_ref, out_ref, j):
    at = slice(j * BLK, (j + 1) * BLK)
    z = dot_t(o_ref[at, :], w_ref[...])
    z = z + pltpu.roll(z, HD // 2, 1)
    lane = lax.broadcasted_iota(jnp.int32, z.shape, 1)
    squares = jnp.zeros(z.shape, jnp.float32)
    for h in range(o_ref.shape[1] // HD):
        wide = o_ref[at, h * HD : (h + 1) * HD].astype(jnp.float32)
        squares = squares + wide * wide
    total = jnp.sum(squares, axis=1, keepdims=True)
    out_ref[at, :] = jnp.where(lane < HD // 2, z, jnp.where(lane == HD // 2, total, 0.0))


def inner_kernel(scal, q_ref, k_ref, v_ref, w_ref, qv_ref, kv_ref, out_ref, o_ref):
    g = pl.program_id(0)
    rows, width = q_ref.shape
    ones = jnp.ones((rows, HD), jnp.bfloat16)
    for j in range(rows // BLK):
        holds_some = (scal[INNER_FROM] < (j + 1) * BLK) & (scal[INNER_TO] > j * BLK)

        @pl.when(holds_some)
        def _(j=j):
            at = pl.ds(j * BLK, BLK)
            same = qv_ref[at, :] == kv_ref[...]
            for i in range(width // HD):
                lanes = slice(i * HD, (i + 1) * HD)
                v_ones = jnp.concatenate([v_ref[:, lanes], ones], axis=1)
                o_ref[at, pl.ds(pl.multiple_of(g * width + i * HD, HD), HD)] = attend_rows(
                    q_ref[at, lanes], k_ref[:, lanes], v_ones, lambda s: jnp.where(same, s, NEG)
                )

        @pl.when(holds_some & (g == pl.num_programs(0) - 1))
        def _(j=j):
            project_block(o_ref, w_ref, out_ref, j)


def across(scal, at, offset, low, high, sources, items, w_ref, own_sems, places, o_ref, zz):
    rows = zz.shape[0] // 2
    left, right = scal[at + LB], scal[at + RB]
    lead = left * TILE - scal[at + LROWS]
    end = left * TILE + scal[at + RROWS]
    blocks = jnp.minimum(lax.div((left + right) * TILE + BLK - 1, BLK), rows // BLK)
    own_at = jnp.where(scal[at + SIDE] == 0, rows, 0) + left * TILE
    pairs = lax.shift_right_logical(high - low + 1, 1)

    def heads_of(i):
        return [jnp.minimum(low + 2 * i + u, high - 1) for u in range(2)]

    def own_copies(i):
        slot = lax.rem(i, 2)
        to = pl.ds(pl.multiple_of(own_at, TILE), rows)
        return [
            pltpu.make_async_copy(
                source.at[:, lanes_of(scal[at + HEAD0] + s)], place.at[slot, u, to, :],
                own_sems.at[slot, u, x],
            )
            for u, s in enumerate(heads_of(i))
            for x, (source, place) in enumerate(zip(sources, places))
        ]

    @pl.when(pairs > 0)
    def _():
        for copy in own_copies(0):
            copy.start()

    def two_heads(n, i, carry):
        slot = lax.rem(i, 2)

        @pl.when(i + 1 < pairs)
        def _():
            for copy in own_copies(i + 1):
                copy.start()

        heads = heads_of(i)

        def foreign(t, group):
            to = rows_of(rows // TILE + scal[at + FAR_TO] + t, group)
            for u, s in enumerate(heads):
                item = pl.ds(scal[at + SOURCE] + offset + s * scal[at + FAR] + t, group)
                for x, place in enumerate(places):
                    part = items[item, x * TILE : (x + 1) * TILE]
                    place[slot, u, to, :] = part.reshape(group * TILE, HD)

        in_groups(0, scal[at + FAR], foreign)
        for copy in own_copies(i):
            copy.wait()
        width = n * BLK
        if width == rows:

            @pl.when((left + right) * TILE > rows)
            def _():
                row = lax.broadcasted_iota(jnp.int32, (TILE, HD), 0)
                for place in places:
                    for u in range(2):
                        first = place[slot, u, rows : rows + TILE, :]
                        last = place[slot, u, 2 * rows : 2 * rows + TILE, :]
                        place[slot, u, rows : rows + TILE, :] = jnp.where(row < lead, last, first)

        place = lax.broadcasted_iota(jnp.int32, (1, width), 1)
        valid = ((place >= lead) & (place < end)) | (place + rows < end)
        bias = jnp.where(valid, 0.0, NEG)
        ones = jnp.ones((width, HD), jnp.bfloat16)
        qs, ks, vs = places
        whole = slice(rows, rows + width)
        for j in range(n):
            mine = slice(rows + j * BLK, rows + (j + 1) * BLK)
            for u, s in enumerate(heads):
                v_ones = jnp.concatenate([vs[slot, u, whole, :], ones], axis=1)
                o_ref[j * BLK : (j + 1) * BLK, lanes_of(scal[at + HEAD0] + s)] = attend_rows(
                    qs[slot, u, mine, :], ks[slot, u, whole, :], v_ones, lambda x: x + bias
                )
        return carry

    for n in range(1, rows // BLK + 1):

        @pl.when((blocks == n) & (pairs > 0))
        def _(n=n):
            o_ref[0 : n * BLK, :] = jnp.zeros((n * BLK, o_ref.shape[1]), o_ref.dtype)
            lax.fori_loop(0, pairs, functools.partial(two_heads, n), 0)
            for j in range(n):
                project_block(o_ref, w_ref, zz, j)
            zz[rows : 2 * rows, :] = zz[0:rows, :]

    @pl.when(pairs <= 0)
    def _():
        zz[...] = jnp.zeros_like(zz)

    return zz[pl.ds(pl.multiple_of(left * TILE, TILE), rows), :]


def fetch(scal, at, offset, low, high, places, boxes, items, sems):
    begin = scal[at + SOURCE] + offset + low * scal[at + FAR]
    end = scal[at + SOURCE] + offset + high * scal[at + FAR]
    return [
        (
            pltpu.make_async_copy(box, items.at[pl.ds(place, box.shape[0])], sems.at[i]),
            (high > low) & (begin < place + box.shape[0]) & (end > place),
        )
        for i, (place, box) in enumerate(zip(places, boxes))
    ]


def clear(places, rows):
    for place in places:
        for slot in range(2):
            for u in range(2):
                place[slot, u, rows : 2 * rows + TILE, :] = jnp.zeros((rows + TILE, HD), place.dtype)


def of_boundary(scal, at, shape, mine):
    row = lax.broadcasted_iota(jnp.int32, shape, 0)
    tail = jnp.where(row >= shape[0] - scal[at + LROWS], 1, 0)
    head = jnp.where(row < scal[at + RROWS], 1, 0)
    right_is_mine = (scal[at + SIDE] == 0) == mine
    return jnp.where(right_is_mine, head, tail) == 1


def send_back(scal, at, z, back_ref):
    lane = lax.broadcasted_iota(jnp.int32, z.shape, 1)
    back = jnp.where(of_boundary(scal, at, z.shape, False), z, 0.0)
    high = back.astype(jnp.bfloat16).astype(jnp.float32)
    both = jnp.where(lane == HD // 2 + 1, pltpu.roll(back - high, 1, 1), high)
    back_ref[...] = both.T[: back_ref.shape[0]].astype(jnp.bfloat16)


def early_kernel(places, at, scal, q_hbm, k_hbm, v_hbm, w_ref, *rest):
    boxes, (out_ref, items, sems, own_sems, qs, ks, vs, o_ref, zz) = rest[: len(places)], rest[len(places) :]
    high = scal[at + EARLY]
    copies = fetch(scal, at, 0, 0, high, places, boxes, items, sems)
    for copy, need in copies:
        pl.when(need)(copy.start)
    clear((qs, ks, vs), zz.shape[0] // 2)
    for copy, need in copies:
        pl.when(need)(copy.wait)
    out_ref[...] = across(
        scal, at, 0, 0, high, (q_hbm, k_hbm, v_hbm), items, w_ref, own_sems, (qs, ks, vs), o_ref, zz
    )


def last_kernel(places, offsets, scal, q_hbm, k_hbm, v_hbm, w_ref, *rest):
    partials, rest = rest[:4], rest[4:]
    boxes, rest = rest[: len(places)], rest[len(places) :]
    own_ref, pass_back_ref, direct_back_ref, items, sems, own_sems, qs, ks, vs, o_ref, zz, sums, sum_sems = rest
    sum_copies = [
        pltpu.make_async_copy(part, sums.at[i], sum_sems.at[i]) for i, part in enumerate(partials)
    ]
    for copy in sum_copies:
        copy.start()
    clear((qs, ks, vs), zz.shape[0] // 2)

    def remaining(at, offset):
        low, high = scal[at + EARLY], scal[at + KEEP]
        copies = fetch(scal, at, offset, low, high, places, boxes, items, sems)
        for copy, need in copies:
            pl.when(need)(copy.start)
        for copy, need in copies:
            pl.when(need)(copy.wait)
        return across(
            scal, at, offset, low, high, (q_hbm, k_hbm, v_hbm), items, w_ref, own_sems, (qs, ks, vs), o_ref, zz
        )

    passed_z = remaining(PASS, offsets[0])
    for copy in sum_copies:
        copy.wait()
    passed_z = passed_z + sums[0]
    send_back(scal, PASS, passed_z, pass_back_ref)
    own = jnp.where(of_boundary(scal, PASS, passed_z.shape, True), passed_z, sums[2] + sums[3])
    direct_z = sums[1] + remaining(DIRECT, offsets[1])
    send_back(scal, DIRECT, direct_z, direct_back_ref)
    own = jnp.where(of_boundary(scal, DIRECT, own.shape, True), direct_z, own)
    own_ref[...] = own.T[: own_ref.shape[0]]


def step_rows(video_ids, step_sizes):
    chosen = video_ids[:, None] == jnp.arange(step_sizes.shape[0], dtype=jnp.int32)[None, :]
    return jnp.sum(jnp.where(chosen, step_sizes[None, :], 0.0), axis=1)


def call(kernel, name, mib, scalars, operands, in_specs, outs, out_specs, scratch, grid=()):
    return pl.pallas_call(
        kernel,
        out_shape=outs,
        grid_spec=pltpu.PrefetchScalarGridSpec(
            num_scalar_prefetch=1, grid=grid, in_specs=in_specs, out_specs=out_specs,
            scratch_shapes=scratch,
        ),
        compiler_params=pltpu.CompilerParams(vmem_limit_bytes=mib * MIB),
        cost_estimate=pl.CostEstimate(flops=1, bytes_accessed=1, transcendentals=0),
        name=name,
    )(scalars, *operands)


def per_device(
    query_rows, key_rows, value_rows, positions, latents, w_head, modulation,
    guide_scale, step_sizes, lengths,
):
    rows, features = query_rows.shape[1], query_rows.shape[2]
    heads = features // HD
    count = lax.axis_size("req")
    here = lax.axis_index("req")
    first_row = here * rows
    _, padded, room = sizes(rows, heads)
    sizes_passed = pieces_of(padded)
    late_sizes = (*sizes_passed[1:], MORE, room - padded - MORE)

    angle = angles(positions)
    odd = (jnp.arange(HD, dtype=jnp.int32) % 2).astype(jnp.float32)
    cosine = jnp.cos(angle)
    sine = jnp.sin(angle) * (2.0 * odd - 1.0)[None, :]

    smem = pl.BlockSpec(memory_space=pltpu.SMEM)
    vmem = pl.BlockSpec(memory_space=pltpu.VMEM)
    hbm = pl.BlockSpec(memory_space=pl.ANY)
    parity = lax.axis_index("cfg")
    tie = lax.optimization_barrier
    scalars = pl.pallas_call(
        functools.partial(plan_kernel, rows, heads, count),
        out_shape=jax.ShapeDtypeStruct((SCALARS,), jnp.int32),
        in_specs=[smem],
        out_specs=smem,
        scratch_shapes=[
            pltpu.SMEM((count + 8,), jnp.int32),
            pltpu.SMEM((count + 8,), jnp.int32),
            pltpu.VMEM(((count + 8) * 8, 128), jnp.float32),
            pltpu.VMEM(((count + 8) * 8, 128), jnp.float32),
        ],
        name="plan",
    )(lengths)

    def in_hbm(x):
        return pltpu.with_memory_space_constraint(x, pltpu.HBM)

    q, k, v = query_rows[0], key_rows[0], value_rows[0]

    def box(items):
        return jax.ShapeDtypeStruct((items, 3 * TILE, HD), jnp.bfloat16)

    def box_scratch(items):
        return pltpu.VMEM((items, 3 * TILE, HD), jnp.bfloat16)

    group = next(n for n in (5, 4, 3, 2, 1) if heads % n == 0)
    steps = heads // group
    head_block = pl.BlockSpec((rows, group * HD), lambda g, s: (0, g))
    table = pl.BlockSpec((rows, HD), lambda g, s: (0, 0))
    first = call(
        first_kernel, "pack_first", 16, scalars, (in_hbm(q), in_hbm(k), in_hbm(v), cosine, sine),
        [hbm] * 3 + [vmem] * 2, (box(sizes_passed[0]),), (vmem,),
        [*[pltpu.VMEM((4, rows, HD), jnp.bfloat16)] * 3, pltpu.SemaphoreType.DMA((4, 3))],
    )
    pairs = [(i, i ^ 1) for i in range(count)]
    onward = [(i, i + 2) for i in range(0, count - 2, 2)] + [(i + 2, i) for i in range(1, count - 2, 2)]
    got = [lax.ppermute(first[0], "req", pairs)]

    after_first, _ = tie((scalars, first[0]))
    swap = jnp.asarray(numpy.eye(2 * HD)[numpy.arange(2 * HD) ^ 1], jnp.bfloat16)
    q_rot, k_rot, w_both, shift, *second = call(
        functools.partial(second_kernel, sizes_passed[0]), "turn_and_pack_rest", 32, after_first,
        (in_hbm(q), in_hbm(k), in_hbm(v), cosine, sine, swap, w_head.T, modulation),
        [head_block] * 3 + [table] * 2 + [vmem] * 3,
        (pltpu.HBM(q.shape, q.dtype), pltpu.HBM(k.shape, k.dtype),
         jax.ShapeDtypeStruct((HD, features), jnp.bfloat16),
         jax.ShapeDtypeStruct((HD // 2, HD), jnp.float32),
         *[box(n) for n in late_sizes], box(late_sizes[-1])),
        (head_block, head_block, vmem, vmem, *[hbm] * (len(late_sizes) + 1)),
        [box_scratch(sum(late_sizes)), pltpu.SemaphoreType.DMA((len(late_sizes),))], grid=(steps,),
    )
    got += [lax.ppermute(x, "req", pairs) for x in second[: CHUNKS - 1]]
    more, arriving = second[CHUNKS:]

    own_rows = first_row + jnp.arange(rows, dtype=jnp.int32)
    video = jnp.sum((jnp.cumsum(lengths)[None, :] <= own_rows[:, None]).astype(jnp.int32), axis=1)
    step_of_row = step_rows(video, step_sizes)

    def inner(when, first_step, step_count):
        block = pl.BlockSpec((rows, group * HD), lambda g, s: (0, g + first_step))
        width = step_count * group * HD
        return call(
            inner_kernel, "inner_videos", 20, when,
            (in_hbm(q_rot), in_hbm(k_rot), in_hbm(v), w_both, video[:, None], video[None, :]),
            [block] * 3 + [pl.BlockSpec((HD, width), lambda g, s: (0, first_step // step_count))] + [vmem] * 2, pltpu.HBM((rows, HD), jnp.float32), vmem,
            [pltpu.VMEM((rows, width), jnp.bfloat16)], grid=(step_count,),
        )

    got[1], second[CHUNKS - 1] = tie((got[1], second[CHUNKS - 1]))
    got.append(lax.ppermute(second[CHUNKS - 1], "req", pairs))
    when_a, got[0] = tie((scalars, got[0]))
    inner_a = inner(when_a, 0, steps // 2)
    got[1], inner_a = tie((got[1], inner_a))
    passed = [lax.ppermute(x, "req", onward) for x in got[:2]]
    when_b, passed[0], got[2], inner_a = tie((scalars, passed[0], got[2], inner_a))
    inner_b = inner(when_b, steps // 2, steps - steps // 2)
    when_early, inner_b = tie((scalars, inner_b))

    place = pltpu.VMEM((2, 2, 3 * rows, HD), jnp.bfloat16)
    work = [
        pltpu.SemaphoreType.DMA((2, 2, 3)), place, place, place,
        pltpu.VMEM((rows, features), jnp.bfloat16),
        pltpu.VMEM((2 * rows, HD), jnp.float32),
    ]
    partial = pltpu.HBM((rows, HD), jnp.float32)
    lanes = HD // 2 + TILE
    sent_back = jax.ShapeDtypeStruct((lanes, rows), jnp.bfloat16)

    def on_videos_across(kernel, name, when, boxes, outs, others=(), scratch=()):
        places = [0]
        for x in boxes:
            places.append(places[-1] + x.shape[0])
        return call(
            kernel(tuple(places[:-1])), name, 32, when,
            (in_hbm(q_rot), in_hbm(k_rot), in_hbm(v), w_both, *[in_hbm(x) for x in others], *boxes),
            [hbm] * 3 + [vmem] + [hbm] * (len(others) + len(boxes)),
            outs, jax.tree.map(lambda _: vmem, outs),
            [box_scratch(places[-1]), pltpu.SemaphoreType.DMA((len(boxes),)), *work, *scratch],
        )

    def early_on(at, name, when, boxes):
        return on_videos_across(
            lambda places: functools.partial(early_kernel, places, at), name, when, boxes,
            partial,
        )

    early = early_on(PASS, "videos_across_early", when_early, passed[:EARLY_CHUNKS])
    got[3], early = tie((got[3], early))
    when_direct, got[3] = tie((scalars, got[3]))
    passed += [lax.ppermute(x, "req", onward) for x in got[2:CHUNKS]]
    when_direct, passed[2] = tie((when_direct, passed[2]))
    direct_z = early_on(DIRECT, "videos_across_direct", when_direct, got[:CHUNKS])

    pieces = jnp.maximum(scalars[MOST] - padded - MORE + EXTRA - 1, 0) // EXTRA
    pieces, direct_z = tie((pieces, direct_z))

    def one_more(i, arrived):
        piece = lax.dynamic_slice_in_dim(more, i * EXTRA, EXTRA, 0)
        piece = lax.ppermute(piece, "req", pairs)
        return lax.dynamic_update_slice_in_dim(arrived, piece, i * EXTRA, 0)

    arrived = lax.fori_loop(0, pieces, one_more, arriving)
    before = EARLY_CHUNKS - 1
    offsets = (-sum(sizes_passed[:before]), sum(sizes_passed[before:]))
    own, to_beyond, to_direct = on_videos_across(
        lambda places: functools.partial(last_kernel, places, offsets), "videos_across_last", scalars,
        [*passed[before:], *got, arrived],
        (jax.ShapeDtypeStruct((lanes, rows), jnp.float32), sent_back, sent_back),
        (early, direct_z, inner_a, inner_b),
        (pltpu.VMEM((4, rows, HD), jnp.float32), pltpu.SemaphoreType.DMA((4,))),
    )
    back_direct = lax.ppermute(to_direct, "req", pairs)
    beyond = [(i, i + 1) for i in range(1, count - 1, 2)] + [(i + 1, i) for i in range(1, count - 1, 2)]
    back_beyond = lax.ppermute(to_beyond, "req", beyond)
    total = own + back_direct.astype(jnp.float32) + back_beyond.astype(jnp.float32)
    values = HD // 2
    squares = total[values : values + 1] + total[values + 1 : values + 2]
    velocity = total[:values] * lax.rsqrt(squares / features + 1e-06) + shift[:, :1]

    width = latents.shape[1]
    mine = lax.dynamic_slice_in_dim(velocity, parity * width, width, 0)
    theirs = lax.dynamic_slice_in_dim(velocity, (1 - parity) * width, width, 0)
    partner = lax.ppermute(theirs, "cfg", [(0, 1), (1, 0)])
    conditional = jnp.where(parity == 0, mine, partner)
    unconditional = jnp.where(parity == 0, partner, mine)
    guided = unconditional + guide_scale[0] * (conditional - unconditional)
    return (latents.T + step_of_row[None, :] * guided).T


def solution(mesh):
    in_specs = (
        P("cfg", "req", None), P("cfg", "req", None), P("cfg", "req", None),
        P(None, "req"), P("req", "cfg"), P(), P(), P(), P(), P(),
    )
    return jax.shard_map(
        per_device, mesh=mesh, in_specs=in_specs, out_specs=P("req", "cfg"), check_vma=False
    )
```

```python
import functools
import math

import jax
import jax.numpy as jnp
import numpy
from jax import lax
from jax.experimental import pallas as pl
from jax.experimental.pallas import tpu as pltpu
from jax.sharding import PartitionSpec as P

HD = 128
TILE = 16
BLK = 128
CHUNKS = 4
MORE = 48
EXTRA = 16
EARLY_CHUNKS = 2
rope_theta = 10000.0
NEG = -1e30
SCALE2 = math.log2(math.e) / math.sqrt(HD)

PASS, DIRECT = 0, 16
LB, RB, LROWS, RROWS, HEAD0, KEEP, EARLY, SOURCE = range(8)
OWN_FROM, OWN_TO, OWN, FAR_TO, FAR, SIDE = range(8, 14)
SEND = 32
ROW, TILES, FIRST, HEADS = range(4)
MOST, INNER_FROM, INNER_TO = 40, 41, 42
SCALARS = 48
MIB = 1024 * 1024


def sizes(rows, heads):
    tiles = rows // TILE
    cap = max(
        min(max(a * n, (tiles + 1 - a) * (heads - n)) for n in range(heads + 1))
        for a in range(1, tiles + 1)
    )
    padded = -(-cap // TILE) * TILE
    return cap, padded, 2 * padded


def pieces_of(padded):
    most = padded * 3 // 11
    return (*[most] * (CHUNKS - 1), padded - most * (CHUNKS - 1))


def angles(positions):
    pair_total = HD // 2
    side_pairs = HD // 6
    time_pairs = pair_total - 2 * side_pairs
    column = jnp.arange(HD, dtype=jnp.int32) // 2
    in_time = column < time_pairs
    in_height = (column >= time_pairs) & (column < time_pairs + side_pairs)
    in_width = column >= time_pairs + side_pairs
    local_index = jnp.where(
        in_time, column, jnp.where(in_height, column - time_pairs, column - time_pairs - side_pairs)
    )
    axis_pairs = jnp.where(in_time, time_pairs, side_pairs)
    frequency = jnp.exp(
        -(local_index.astype(jnp.float32) / axis_pairs.astype(jnp.float32)) * math.log(rope_theta)
    )
    selector = jnp.stack([in_time, in_height, in_width]).astype(jnp.float32) * frequency[None, :]
    placed = positions.astype(jnp.float32)
    return (
        placed[0][:, None] * selector[0][None, :]
        + placed[1][:, None] * selector[1][None, :]
        + placed[2][:, None] * selector[2][None, :]
    )


def plan_kernel(rows, heads, count, lengths, out, ls, rs, split, least):
    cap, padded, _ = sizes(rows, heads)
    here = lax.axis_index("req")
    shift = rows.bit_length() - 1

    def clear(b, carry):
        ls[b] = 0
        rs[b] = 0
        return carry

    lax.fori_loop(0, count + 8, clear, 0)

    def one_video(v, start):
        end = start + lengths[v]
        b = lax.shift_right_logical(end - 1, shift) if rows == 1 << shift else lax.div(end - 1, rows)
        at = b * rows

        @pl.when(start < at)
        def _():
            ls[b] = at - start
            rs[b] = end - at

        return end

    lax.fori_loop(0, lengths.shape[0], one_video, 0)
    budget = 3.0 * lax.broadcasted_iota(jnp.int32, (8, 128), 1).astype(jnp.float32)
    split[...] = jnp.zeros_like(split)

    def tiles_of(x):
        return lax.shift_right_logical(x + TILE - 1, 4)

    def eight(b):
        return pl.ds(pl.multiple_of(b * 8, 8), 8)

    def per_tile(x, tiles):
        return jnp.floor((x + 0.5) * (1.0 / jnp.maximum(tiles, 1.0)))

    def facts(b):
        direct = lax.rem(b, 2).astype(jnp.float32)
        lt, rt = (jnp.full((8, 128), tiles_of(x[b]).astype(jnp.float32)) for x in (ls, rs))
        return lt, rt, padded + direct * 1e6

    def five_at_a_time(step, carry):
        def body(i, carry):
            for u in range(5):
                carry = step(5 * i + u, carry)
            return carry

        return lax.fori_loop(0, -(-(count - 1) // 5), body, carry)

    def from_right(i, load):
        b = -(-(count - 1) // 5) * 5 - i
        lt, rt, limit = facts(b)
        room = jnp.minimum(budget - load, limit)
        n = jnp.where(rt > 0.0, jnp.maximum(heads - per_tile(room, rt), 0.0), 0.0)
        least[eight(b)] = jnp.where(room >= 0.0, n, 1e6)
        return lt * n

    def from_left(i, carry):
        load, ok = carry
        b = i + 1
        lt, rt, limit = facts(b)
        room = jnp.minimum(budget - load, limit)
        most = jnp.where(lt > 0.0, jnp.minimum(per_tile(room, lt), float(heads)), 0.0)
        low = least[eight(b)]
        even = jnp.floor(heads * rt / jnp.maximum(lt + rt, 1.0) + 0.5)
        n = jnp.minimum(most, jnp.maximum(low, even))
        split[eight(b)] = n
        return rt * (heads - n), jnp.where((room >= 0.0) & (low <= most), ok, 0.0)

    zero = jnp.zeros((8, 128), jnp.float32)
    five_at_a_time(from_right, zero)
    load, ok = five_at_a_time(from_left, (zero, zero + 1.0))
    ok = jnp.where(load <= budget, ok, 0.0)
    most = jnp.min(jnp.where((ok > 0.0) & (budget >= (padded + MORE) // 3 * 3), budget, 1e9))
    out[MOST] = most.astype(jnp.int32)

    def head_split(b):
        n = split[eight(b)]
        return jnp.max(jnp.where(budget == most, n, 0.0)).astype(jnp.int32)

    even = lax.rem(here, 2) == 0
    beyond = jnp.where(even, here + 2, here - 1)
    n_left, n_right, n_beyond = head_split(here), head_split(here + 1), head_split(beyond)
    partner_passes = jnp.where(
        even,
        tiles_of(ls[beyond]) * n_beyond,
        tiles_of(rs[beyond]) * (heads - n_beyond),
    )
    for side, b, n in ((0, here, n_left), (1, here + 1, n_right)):
        direct = jnp.logical_not(even) if side == 0 else even
        at = jnp.where(direct, DIRECT, PASS)
        lt, rt = tiles_of(ls[b]), tiles_of(rs[b])
        none = jnp.where(lt > 0, 0, heads)
        keep = n if side == 0 else jnp.maximum(heads - n - none, 0)
        far = lt if side == 0 else rt
        out[at + LB], out[at + RB] = lt, rt
        out[at + LROWS], out[at + RROWS] = ls[b], rs[b]
        out[at + HEAD0] = 0 if side == 0 else n
        out[at + KEEP] = keep
        source = jnp.where(direct, partner_passes, 0)
        there = jnp.where(direct, padded, sum(pieces_of(padded)[:EARLY_CHUNKS])) - source
        out[at + EARLY] = jnp.minimum(keep, lax.div(jnp.maximum(there, 0), jnp.maximum(far, 1)))
        out[at + SOURCE] = source
        out[at + OWN_FROM] = 0 if side == 0 else rows // TILE - lt
        out[at + OWN_TO] = lt if side == 0 else 0
        out[at + OWN] = rt if side == 0 else lt
        out[at + FAR_TO] = 0 if side == 0 else lt
        out[at + FAR] = far
        out[at + SIDE] = side
        to = SEND + jnp.where(direct, 4, 0)
        out[to + ROW] = 0 if side == 0 else rows - TILE * lt
        out[to + TILES] = rt if side == 0 else lt
        out[to + FIRST] = n if side == 0 else 0
        out[to + HEADS] = jnp.maximum(heads - n - none, 0) if side == 0 else n
    out[INNER_FROM] = rs[here]
    out[INNER_TO] = rows - ls[here + 1]


def in_groups(low, high, step):
    count = high - low

    def run(group, times):
        def body(i, carry):
            step(jnp.minimum(low + group * i, high - group), group)
            return carry

        lax.fori_loop(0, times, body, 0)

    run(8, jnp.where(count >= 8, lax.shift_right_logical(count + 7, 3), 0))
    run(2, jnp.where((count >= 2) & (count < 8), lax.shift_right_logical(count + 1, 1), 0))
    run(1, jnp.where(count == 1, 1, 0))


def lanes_of(h):
    return pl.ds(pl.multiple_of(h * HD, HD), HD)


def rows_of(t, group):
    return pl.ds(pl.multiple_of(t * TILE, TILE), group * TILE)


def turn(x, cosine, sine):
    wide = x.astype(jnp.float32)
    even = lax.rem(lax.broadcasted_iota(jnp.int32, wide.shape, 1), 2) == 0
    swapped = jnp.where(even, pltpu.roll(wide, HD - 1, 1), pltpu.roll(wide, 1, 1))
    return (wide * cosine + swapped * sine).astype(jnp.bfloat16)


def pack(scal, low, high, box, heads, get):
    base = 0
    for what in (SEND, SEND + 4):
        first_tile = lax.shift_right_logical(scal[what + ROW], 4)
        tiles, first, count = scal[what + TILES], scal[what + FIRST], scal[what + HEADS]

        def one_head(i, carry):
            start = base + (pl.program_id(0) * heads + i - first) * tiles
            begin = jnp.clip(low - start, 0, tiles)
            end = jnp.clip(high - start, 0, tiles)
            lanes = lanes_of(i)

            def step(t, group):
                q, k, v = get(rows_of(first_tile + t, group), lanes)
                item = pl.ds(start + t - low, group)
                box[item, 0:TILE] = q.reshape(group, TILE, HD)
                box[item, TILE : 2 * TILE] = k.reshape(group, TILE, HD)
                box[item, 2 * TILE : 3 * TILE] = v.reshape(group, TILE, HD)

            in_groups(begin, end, step)
            return carry

        before = first - pl.program_id(0) * heads
        lax.fori_loop(
            jnp.clip(before, 0, heads), jnp.clip(before + count, 0, heads), one_head, 0
        )
        base = base + tiles * count


def send_off(box, outs, sems):
    @pl.when(pl.program_id(0) == pl.num_programs(0) - 1)
    def _():
        at, copies = 0, []
        for i, out in enumerate(outs):
            copies.append(pltpu.make_async_copy(box.at[pl.ds(at, out.shape[0])], out, sems.at[i]))
            at += out.shape[0]
        for copy in copies:
            copy.start()
        for copy in copies:
            copy.wait()


def first_kernel(scal, q_hbm, k_hbm, v_hbm, cos_ref, sin_ref, box, qs, ks, vs, sems):
    limit = box.shape[0]
    ahead = qs.shape[0] - 1

    def heads_in(what, base):
        tiles = jnp.maximum(scal[what + TILES], 1)
        taken = lax.div(jnp.maximum(limit - base, 0) + tiles - 1, tiles)
        return jnp.minimum(scal[what + HEADS], taken)

    passed = scal[SEND + TILES] * scal[SEND + HEADS]
    count_pass = heads_in(SEND, 0)
    count = count_pass + heads_in(SEND + 4, passed)

    def entry(w):
        direct = w >= count_pass
        what = jnp.where(direct, SEND + 4, SEND)
        slot = w - jnp.where(direct, count_pass, 0)
        tiles = scal[what + TILES]
        start = jnp.where(direct, passed, 0) + slot * tiles
        return scal[what + FIRST] + slot, scal[what + ROW], tiles, start

    rows = cos_ref.shape[0]

    def each_copy(w, act):
        at = lax.rem(w, ahead + 1)
        head, row, tiles, _ = entry(w)
        few = tiles * TILE <= BLK
        block = pl.ds(pl.multiple_of(jnp.minimum(row, rows - BLK), TILE), BLK)
        for need, some in ((few, block), (jnp.logical_not(few), pl.ds(0, rows))):

            @pl.when(need)
            def _(some=some):
                for x, (source, place) in enumerate(((q_hbm, qs), (k_hbm, ks), (v_hbm, vs))):
                    act(pltpu.make_async_copy(
                        source.at[some, lanes_of(head)], place.at[at, some, :], sems.at[at, x]
                    ))

    for w in range(ahead):

        @pl.when(w < count)
        def _(w=w):
            each_copy(w, lambda copy: copy.start())

    def one_head(w, carry):
        @pl.when(w + ahead < count)
        def _():
            each_copy(w + ahead, lambda copy: copy.start())

        each_copy(w, lambda copy: copy.wait())
        at = lax.rem(w, ahead + 1)
        _, row, tiles, start = entry(w)
        first_tile = lax.shift_right_logical(row, 4)

        def step(t, group):
            source = rows_of(first_tile + t, group)
            cosine, sine = cos_ref[source, :], sin_ref[source, :]
            item = pl.ds(start + t, group)
            q, k = turn(qs[at, source, :], cosine, sine), turn(ks[at, source, :], cosine, sine)
            box[item, 0:TILE] = q.reshape(group, TILE, HD)
            box[item, TILE : 2 * TILE] = k.reshape(group, TILE, HD)
            box[item, 2 * TILE : 3 * TILE] = vs[at, source, :].reshape(group, TILE, HD)

        in_groups(0, jnp.clip(limit - start, 0, tiles), step)
        return carry

    lax.fori_loop(0, count, one_head, 0)


def second_kernel(
    low, scal, q_ref, k_ref, v_ref, cos_ref, sin_ref, swap_ref, wt_ref, mod_ref, qr_ref, kr_ref, w_ref, shift_ref, *rest
):
    outs, box, sems = rest[:-3], rest[-2], rest[-1]
    rows = q_ref.shape[0]
    heads = q_ref.shape[1] // HD
    wide = swap_ref.shape[0]

    @pl.when(pl.program_id(0) == 0)
    def _():
        w = wt_ref[...].astype(jnp.float32)
        scaled = w * (1.0 + mod_ref[1:2, :])
        high = scaled.astype(jnp.bfloat16)
        low = (scaled - high.astype(jnp.float32)).astype(jnp.bfloat16)
        w_ref[...] = jnp.concatenate([high, low], axis=0)
        shift = jnp.sum(w * mod_ref[0:1, :], axis=1, keepdims=True)
        shift_ref[...] = jnp.broadcast_to(shift, shift_ref.shape)

    for source, to in ((q_ref, qr_ref), (k_ref, kr_ref)):
        for h in range(0, heads, wide // HD):
            for j in range(rows // BLK):
                at = slice(j * BLK, (j + 1) * BLK)
                x = source[at, h * HD : h * HD + wide]
                swapped = jnp.dot(x, swap_ref[: x.shape[1], : x.shape[1]], preferred_element_type=jnp.float32)
                for i in range(x.shape[1] // HD):
                    lanes = slice(i * HD, (i + 1) * HD)
                    to[at, (h + i) * HD : (h + i + 1) * HD] = (
                        x[:, lanes].astype(jnp.float32) * cos_ref[at, :] + swapped[:, lanes] * sin_ref[at, :]
                    ).astype(jnp.bfloat16)

    def get(rows, lanes):
        return qr_ref[rows, lanes], kr_ref[rows, lanes], v_ref[rows, lanes]

    pack(scal, low, low + box.shape[0], box, heads, get)
    send_off(box, outs, sems)


def dot_t(a, b):
    return lax.dot_general(a, b, (((1,), (1,)), ((), ())), preferred_element_type=jnp.float32)


def attend_rows(q, k, v_ones, masked):
    s = masked(dot_t(q, k))
    top = jnp.max(s, axis=1, keepdims=True)
    weight = jnp.exp2(s * SCALE2 - top * SCALE2).astype(jnp.bfloat16)
    both = jnp.dot(weight, v_ones, preferred_element_type=jnp.float32)
    return (both[:, :HD] / both[:, HD:]).astype(jnp.bfloat16)


def project_block(o_ref, w_ref, out_ref, j):
    at = slice(j * BLK, (j + 1) * BLK)
    z = dot_t(o_ref[at, :], w_ref[...])
    z = z + pltpu.roll(z, HD // 2, 1)
    lane = lax.broadcasted_iota(jnp.int32, z.shape, 1)
    squares = jnp.zeros(z.shape, jnp.float32)
    for h in range(o_ref.shape[1] // HD):
        wide = o_ref[at, h * HD : (h + 1) * HD].astype(jnp.float32)
        squares = squares + wide * wide
    total = jnp.sum(squares, axis=1, keepdims=True)
    out_ref[at, :] = jnp.where(lane < HD // 2, z, jnp.where(lane == HD // 2, total, 0.0))


def inner_kernel(scal, q_ref, k_ref, v_ref, w_ref, qv_ref, kv_ref, out_ref, o_ref):
    g = pl.program_id(0)
    rows, width = q_ref.shape
    ones = jnp.ones((rows, HD), jnp.bfloat16)
    for j in range(rows // BLK):
        holds_some = (scal[INNER_FROM] < (j + 1) * BLK) & (scal[INNER_TO] > j * BLK)

        @pl.when(holds_some)
        def _(j=j):
            at = pl.ds(j * BLK, BLK)
            same = qv_ref[at, :] == kv_ref[...]
            for i in range(width // HD):
                lanes = slice(i * HD, (i + 1) * HD)
                v_ones = jnp.concatenate([v_ref[:, lanes], ones], axis=1)
                o_ref[at, pl.ds(pl.multiple_of(g * width + i * HD, HD), HD)] = attend_rows(
                    q_ref[at, lanes], k_ref[:, lanes], v_ones, lambda s: jnp.where(same, s, NEG)
                )

        @pl.when(holds_some & (g == pl.num_programs(0) - 1))
        def _(j=j):
            project_block(o_ref, w_ref, out_ref, j)


def across(scal, at, offset, low, high, sources, items, w_ref, own_sems, places, o_ref, zz):
    rows = zz.shape[0] // 2
    left, right = scal[at + LB], scal[at + RB]
    lead = left * TILE - scal[at + LROWS]
    end = left * TILE + scal[at + RROWS]
    blocks = jnp.minimum(lax.div((left + right) * TILE + BLK - 1, BLK), rows // BLK)
    own_at = jnp.where(scal[at + SIDE] == 0, rows, 0) + left * TILE
    pairs = lax.shift_right_logical(high - low + 1, 1)

    def heads_of(i):
        return [jnp.minimum(low + 2 * i + u, high - 1) for u in range(2)]

    def own_copies(i):
        slot = lax.rem(i, 2)
        to = pl.ds(pl.multiple_of(own_at, TILE), rows)
        return [
            pltpu.make_async_copy(
                source.at[:, lanes_of(scal[at + HEAD0] + s)], place.at[slot, u, to, :],
                own_sems.at[slot, u, x],
            )
            for u, s in enumerate(heads_of(i))
            for x, (source, place) in enumerate(zip(sources, places))
        ]

    @pl.when(pairs > 0)
    def _():
        for copy in own_copies(0):
            copy.start()

    def two_heads(n, i, carry):
        slot = lax.rem(i, 2)

        @pl.when(i + 1 < pairs)
        def _():
            for copy in own_copies(i + 1):
                copy.start()

        heads = heads_of(i)

        def foreign(t, group):
            to = rows_of(rows // TILE + scal[at + FAR_TO] + t, group)
            for u, s in enumerate(heads):
                item = pl.ds(scal[at + SOURCE] + offset + s * scal[at + FAR] + t, group)
                for x, place in enumerate(places):
                    part = items[item, x * TILE : (x + 1) * TILE]
                    place[slot, u, to, :] = part.reshape(group * TILE, HD)

        in_groups(0, scal[at + FAR], foreign)
        for copy in own_copies(i):
            copy.wait()
        width = n * BLK
        if width == rows:

            @pl.when((left + right) * TILE > rows)
            def _():
                row = lax.broadcasted_iota(jnp.int32, (TILE, HD), 0)
                for place in places:
                    for u in range(2):
                        first = place[slot, u, rows : rows + TILE, :]
                        last = place[slot, u, 2 * rows : 2 * rows + TILE, :]
                        place[slot, u, rows : rows + TILE, :] = jnp.where(row < lead, last, first)

        place = lax.broadcasted_iota(jnp.int32, (1, width), 1)
        valid = ((place >= lead) & (place < end)) | (place + rows < end)
        bias = jnp.where(valid, 0.0, NEG)
        ones = jnp.ones((width, HD), jnp.bfloat16)
        qs, ks, vs = places
        whole = slice(rows, rows + width)
        for j in range(n):
            mine = slice(rows + j * BLK, rows + (j + 1) * BLK)
            for u, s in enumerate(heads):
                v_ones = jnp.concatenate([vs[slot, u, whole, :], ones], axis=1)
                o_ref[j * BLK : (j + 1) * BLK, lanes_of(scal[at + HEAD0] + s)] = attend_rows(
                    qs[slot, u, mine, :], ks[slot, u, whole, :], v_ones, lambda x: x + bias
                )
        return carry

    for n in range(1, rows // BLK + 1):

        @pl.when((blocks == n) & (pairs > 0))
        def _(n=n):
            o_ref[0 : n * BLK, :] = jnp.zeros((n * BLK, o_ref.shape[1]), o_ref.dtype)
            lax.fori_loop(0, pairs, functools.partial(two_heads, n), 0)
            for j in range(n):
                project_block(o_ref, w_ref, zz, j)
            zz[rows : 2 * rows, :] = zz[0:rows, :]

    @pl.when(pairs <= 0)
    def _():
        zz[...] = jnp.zeros_like(zz)

    return zz[pl.ds(pl.multiple_of(left * TILE, TILE), rows), :]


def fetch(scal, at, offset, low, high, places, boxes, items, sems):
    begin = scal[at + SOURCE] + offset + low * scal[at + FAR]
    end = scal[at + SOURCE] + offset + high * scal[at + FAR]
    return [
        (
            pltpu.make_async_copy(box, items.at[pl.ds(place, box.shape[0])], sems.at[i]),
            (high > low) & (begin < place + box.shape[0]) & (end > place),
        )
        for i, (place, box) in enumerate(zip(places, boxes))
    ]


def clear(places, rows):
    for place in places:
        for slot in range(2):
            for u in range(2):
                place[slot, u, rows : 2 * rows + TILE, :] = jnp.zeros((rows + TILE, HD), place.dtype)


def of_boundary(scal, at, shape, mine):
    row = lax.broadcasted_iota(jnp.int32, shape, 0)
    tail = jnp.where(row >= shape[0] - scal[at + LROWS], 1, 0)
    head = jnp.where(row < scal[at + RROWS], 1, 0)
    right_is_mine = (scal[at + SIDE] == 0) == mine
    return jnp.where(right_is_mine, head, tail) == 1


def send_back(scal, at, z, back_ref):
    lane = lax.broadcasted_iota(jnp.int32, z.shape, 1)
    back = jnp.where(of_boundary(scal, at, z.shape, False), z, 0.0)
    high = back.astype(jnp.bfloat16).astype(jnp.float32)
    both = jnp.where(lane == HD // 2 + 1, pltpu.roll(back - high, 1, 1), high)
    back_ref[...] = both.T[: back_ref.shape[0]].astype(jnp.bfloat16)


def early_kernel(places, at, scal, q_hbm, k_hbm, v_hbm, w_ref, *rest):
    boxes, (out_ref, items, sems, own_sems, qs, ks, vs, o_ref, zz) = rest[: len(places)], rest[len(places) :]
    high = scal[at + EARLY]
    copies = fetch(scal, at, 0, 0, high, places, boxes, items, sems)
    for copy, need in copies:
        pl.when(need)(copy.start)
    clear((qs, ks, vs), zz.shape[0] // 2)
    for copy, need in copies:
        pl.when(need)(copy.wait)
    out_ref[...] = across(
        scal, at, 0, 0, high, (q_hbm, k_hbm, v_hbm), items, w_ref, own_sems, (qs, ks, vs), o_ref, zz
    )


def last_kernel(places, offsets, scal, q_hbm, k_hbm, v_hbm, w_ref, *rest):
    partials, rest = rest[:4], rest[4:]
    boxes, rest = rest[: len(places)], rest[len(places) :]
    own_ref, pass_back_ref, direct_back_ref, items, sems, own_sems, qs, ks, vs, o_ref, zz, sums, sum_sems = rest
    sum_copies = [
        pltpu.make_async_copy(part, sums.at[i], sum_sems.at[i]) for i, part in enumerate(partials)
    ]
    for copy in sum_copies:
        copy.start()
    clear((qs, ks, vs), zz.shape[0] // 2)

    def remaining(at, offset):
        low, high = scal[at + EARLY], scal[at + KEEP]
        copies = fetch(scal, at, offset, low, high, places, boxes, items, sems)
        for copy, need in copies:
            pl.when(need)(copy.start)
        for copy, need in copies:
            pl.when(need)(copy.wait)
        return across(
            scal, at, offset, low, high, (q_hbm, k_hbm, v_hbm), items, w_ref, own_sems, (qs, ks, vs), o_ref, zz
        )

    passed_z = remaining(PASS, offsets[0])
    for copy in sum_copies:
        copy.wait()
    passed_z = passed_z + sums[0]
    send_back(scal, PASS, passed_z, pass_back_ref)
    own = jnp.where(of_boundary(scal, PASS, passed_z.shape, True), passed_z, sums[2] + sums[3])
    direct_z = sums[1] + remaining(DIRECT, offsets[1])
    send_back(scal, DIRECT, direct_z, direct_back_ref)
    own = jnp.where(of_boundary(scal, DIRECT, own.shape, True), direct_z, own)
    own_ref[...] = own.T[: own_ref.shape[0]]


def step_rows(video_ids, step_sizes):
    chosen = video_ids[:, None] == jnp.arange(step_sizes.shape[0], dtype=jnp.int32)[None, :]
    return jnp.sum(jnp.where(chosen, step_sizes[None, :], 0.0), axis=1)


def call(kernel, name, mib, scalars, operands, in_specs, outs, out_specs, scratch, grid=()):
    return pl.pallas_call(
        kernel,
        out_shape=outs,
        grid_spec=pltpu.PrefetchScalarGridSpec(
            num_scalar_prefetch=1, grid=grid, in_specs=in_specs, out_specs=out_specs,
            scratch_shapes=scratch,
        ),
        compiler_params=pltpu.CompilerParams(vmem_limit_bytes=mib * MIB),
        cost_estimate=pl.CostEstimate(flops=1, bytes_accessed=1, transcendentals=0),
        name=name,
    )(scalars, *operands)


def per_device(
    query_rows, key_rows, value_rows, positions, latents, w_head, modulation,
    guide_scale, step_sizes, lengths,
):
    rows, features = query_rows.shape[1], query_rows.shape[2]
    heads = features // HD
    count = lax.axis_size("req")
    here = lax.axis_index("req")
    first_row = here * rows
    _, padded, room = sizes(rows, heads)
    sizes_passed = pieces_of(padded)
    late_sizes = (*sizes_passed[1:], MORE, room - padded - MORE)

    angle = angles(positions)
    odd = (jnp.arange(HD, dtype=jnp.int32) % 2).astype(jnp.float32)
    cosine = jnp.cos(angle)
    sine = jnp.sin(angle) * (2.0 * odd - 1.0)[None, :]

    smem = pl.BlockSpec(memory_space=pltpu.SMEM)
    vmem = pl.BlockSpec(memory_space=pltpu.VMEM)
    hbm = pl.BlockSpec(memory_space=pl.ANY)
    parity = lax.axis_index("cfg")
    tie = lax.optimization_barrier
    scalars = pl.pallas_call(
        functools.partial(plan_kernel, rows, heads, count),
        out_shape=jax.ShapeDtypeStruct((SCALARS,), jnp.int32),
        in_specs=[smem],
        out_specs=smem,
        scratch_shapes=[
            pltpu.SMEM((count + 8,), jnp.int32),
            pltpu.SMEM((count + 8,), jnp.int32),
            pltpu.VMEM(((count + 8) * 8, 128), jnp.float32),
            pltpu.VMEM(((count + 8) * 8, 128), jnp.float32),
        ],
        name="plan",
    )(lengths)

    def in_hbm(x):
        return pltpu.with_memory_space_constraint(x, pltpu.HBM)

    q, k, v = query_rows[0], key_rows[0], value_rows[0]

    def box(items):
        return jax.ShapeDtypeStruct((items, 3 * TILE, HD), jnp.bfloat16)

    def box_scratch(items):
        return pltpu.VMEM((items, 3 * TILE, HD), jnp.bfloat16)

    group = next(n for n in (5, 4, 3, 2, 1) if heads % n == 0)
    steps = heads // group
    head_block = pl.BlockSpec((rows, group * HD), lambda g, s: (0, g))
    table = pl.BlockSpec((rows, HD), lambda g, s: (0, 0))
    first = call(
        first_kernel, "pack_first", 16, scalars, (in_hbm(q), in_hbm(k), in_hbm(v), cosine, sine),
        [hbm] * 3 + [vmem] * 2, (box(sizes_passed[0]),), (vmem,),
        [*[pltpu.VMEM((4, rows, HD), jnp.bfloat16)] * 3, pltpu.SemaphoreType.DMA((4, 3))],
    )
    pairs = [(i, i ^ 1) for i in range(count)]
    onward = [(i, i + 2) for i in range(0, count - 2, 2)] + [(i + 2, i) for i in range(1, count - 2, 2)]
    got = [lax.ppermute(first[0], "req", pairs)]

    after_first, _ = tie((scalars, first[0]))
    swap = jnp.asarray(numpy.eye(2 * HD)[numpy.arange(2 * HD) ^ 1], jnp.bfloat16)
    q_rot, k_rot, w_both, shift, *second = call(
        functools.partial(second_kernel, sizes_passed[0]), "turn_and_pack_rest", 32, after_first,
        (in_hbm(q), in_hbm(k), in_hbm(v), cosine, sine, swap, w_head.T, modulation),
        [head_block] * 3 + [table] * 2 + [vmem] * 3,
        (pltpu.HBM(q.shape, q.dtype), pltpu.HBM(k.shape, k.dtype),
         jax.ShapeDtypeStruct((HD, features), jnp.bfloat16),
         jax.ShapeDtypeStruct((HD // 2, HD), jnp.float32),
         *[box(n) for n in late_sizes], box(late_sizes[-1])),
        (head_block, head_block, vmem, vmem, *[hbm] * (len(late_sizes) + 1)),
        [box_scratch(sum(late_sizes)), pltpu.SemaphoreType.DMA((len(late_sizes),))], grid=(steps,),
    )
    got += [lax.ppermute(x, "req", pairs) for x in second[: CHUNKS - 1]]
    more, arriving = second[CHUNKS:]

    own_rows = first_row + jnp.arange(rows, dtype=jnp.int32)
    video = jnp.sum((jnp.cumsum(lengths)[None, :] <= own_rows[:, None]).astype(jnp.int32), axis=1)
    step_of_row = step_rows(video, step_sizes)

    def inner(when, first_step, step_count):
        block = pl.BlockSpec((rows, group * HD), lambda g, s: (0, g + first_step))
        width = step_count * group * HD
        return call(
            inner_kernel, "inner_videos", 20, when,
            (in_hbm(q_rot), in_hbm(k_rot), in_hbm(v), w_both, video[:, None], video[None, :]),
            [block] * 3 + [pl.BlockSpec((HD, width), lambda g, s: (0, first_step // step_count))] + [vmem] * 2, pltpu.HBM((rows, HD), jnp.float32), vmem,
            [pltpu.VMEM((rows, width), jnp.bfloat16)], grid=(step_count,),
        )

    got[1], second[CHUNKS - 1] = tie((got[1], second[CHUNKS - 1]))
    got.append(lax.ppermute(second[CHUNKS - 1], "req", pairs))
    when_a, got[0] = tie((scalars, got[0]))
    inner_a = inner(when_a, 0, steps // 2)
    got[1], inner_a = tie((got[1], inner_a))
    passed = [lax.ppermute(x, "req", onward) for x in got[:2]]
    when_b, passed[0], got[2], inner_a = tie((scalars, passed[0], got[2], inner_a))
    inner_b = inner(when_b, steps // 2, steps - steps // 2)
    when_early, got[3], inner_b = tie((scalars, got[3], inner_b))
    passed += [lax.ppermute(x, "req", onward) for x in got[2:CHUNKS]]

    place = pltpu.VMEM((2, 2, 3 * rows, HD), jnp.bfloat16)
    work = [
        pltpu.SemaphoreType.DMA((2, 2, 3)), place, place, place,
        pltpu.VMEM((rows, features), jnp.bfloat16),
        pltpu.VMEM((2 * rows, HD), jnp.float32),
    ]
    partial = pltpu.HBM((rows, HD), jnp.float32)
    lanes = HD // 2 + TILE
    sent_back = jax.ShapeDtypeStruct((lanes, rows), jnp.bfloat16)

    def on_videos_across(kernel, name, when, boxes, outs, others=(), scratch=()):
        places = [0]
        for x in boxes:
            places.append(places[-1] + x.shape[0])
        return call(
            kernel(tuple(places[:-1])), name, 32, when,
            (in_hbm(q_rot), in_hbm(k_rot), in_hbm(v), w_both, *[in_hbm(x) for x in others], *boxes),
            [hbm] * 3 + [vmem] + [hbm] * (len(others) + len(boxes)),
            outs, jax.tree.map(lambda _: vmem, outs),
            [box_scratch(places[-1]), pltpu.SemaphoreType.DMA((len(boxes),)), *work, *scratch],
        )

    def early_on(at, name, when, boxes):
        return on_videos_across(
            lambda places: functools.partial(early_kernel, places, at), name, when, boxes,
            partial,
        )

    early = early_on(PASS, "videos_across_early", when_early, passed[:EARLY_CHUNKS])
    when_direct, early, passed[2] = tie((scalars, early, passed[2]))
    direct_z = early_on(DIRECT, "videos_across_direct", when_direct, got[:CHUNKS])

    pieces = jnp.maximum(scalars[MOST] - padded - MORE + EXTRA - 1, 0) // EXTRA
    pieces, direct_z = tie((pieces, direct_z))

    def one_more(i, arrived):
        piece = lax.dynamic_slice_in_dim(more, i * EXTRA, EXTRA, 0)
        piece = lax.ppermute(piece, "req", pairs)
        return lax.dynamic_update_slice_in_dim(arrived, piece, i * EXTRA, 0)

    arrived = lax.fori_loop(0, pieces, one_more, arriving)
    before = EARLY_CHUNKS - 1
    offsets = (-sum(sizes_passed[:before]), sum(sizes_passed[before:]))
    own, to_beyond, to_direct = on_videos_across(
        lambda places: functools.partial(last_kernel, places, offsets), "videos_across_last", scalars,
        [*passed[before:], *got, arrived],
        (jax.ShapeDtypeStruct((lanes, rows), jnp.float32), sent_back, sent_back),
        (early, direct_z, inner_a, inner_b),
        (pltpu.VMEM((4, rows, HD), jnp.float32), pltpu.SemaphoreType.DMA((4,))),
    )
    back_direct = lax.ppermute(to_direct, "req", pairs)
    beyond = [(i, i + 1) for i in range(1, count - 1, 2)] + [(i + 1, i) for i in range(1, count - 1, 2)]
    back_beyond = lax.ppermute(to_beyond, "req", beyond)
    total = own + back_direct.astype(jnp.float32) + back_beyond.astype(jnp.float32)
    values = HD // 2
    squares = total[values : values + 1] + total[values + 1 : values + 2]
    velocity = total[:values] * lax.rsqrt(squares / features + 1e-06) + shift[:, :1]

    width = latents.shape[1]
    mine = lax.dynamic_slice_in_dim(velocity, parity * width, width, 0)
    theirs = lax.dynamic_slice_in_dim(velocity, (1 - parity) * width, width, 0)
    partner = lax.ppermute(theirs, "cfg", [(0, 1), (1, 0)])
    conditional = jnp.where(parity == 0, mine, partner)
    unconditional = jnp.where(parity == 0, partner, mine)
    guided = unconditional + guide_scale[0] * (conditional - unconditional)
    return (latents.T + step_of_row[None, :] * guided).T


def solution(mesh):
    in_specs = (
        P("cfg", "req", None), P("cfg", "req", None), P("cfg", "req", None),
        P(None, "req"), P("req", "cfg"), P(), P(), P(), P(), P(),
    )
    return jax.shard_map(
        per_device, mesh=mesh, in_specs=in_specs, out_specs=P("req", "cfg"), check_vma=False
    )
```

```python
import functools
import math

import jax
import jax.numpy as jnp
import numpy
from jax import lax
from jax.experimental import pallas as pl
from jax.experimental.pallas import tpu as pltpu
from jax.sharding import PartitionSpec as P

HD = 128
TILE = 16
BLK = 128
CHUNKS = 4
MORE = 80
EXTRA = 16
EARLY_CHUNKS = 2
rope_theta = 10000.0
NEG = -1e30
SCALE2 = math.log2(math.e) / math.sqrt(HD)

PASS, DIRECT = 0, 16
LB, RB, LROWS, RROWS, HEAD0, KEEP, EARLY, SOURCE = range(8)
OWN_FROM, OWN_TO, OWN, FAR_TO, FAR, SIDE, SOON = range(8, 15)
SEND = 32
ROW, TILES, FIRST, HEADS = range(4)
MOST, INNER_FROM, INNER_TO = 40, 41, 42
SCALARS = 48
MIB = 1024 * 1024


def sizes(rows, heads):
    tiles = rows // TILE
    cap = max(
        min(max(a * n, (tiles + 1 - a) * (heads - n)) for n in range(heads + 1))
        for a in range(1, tiles + 1)
    )
    padded = -(-cap // TILE) * TILE
    return cap, padded, 2 * padded


def pieces_of(padded):
    most = padded * 3 // 11
    return (*[most] * (CHUNKS - 1), padded - most * (CHUNKS - 1))


def angles(positions):
    pair_total = HD // 2
    side_pairs = HD // 6
    time_pairs = pair_total - 2 * side_pairs
    column = jnp.arange(HD, dtype=jnp.int32) // 2
    in_time = column < time_pairs
    in_height = (column >= time_pairs) & (column < time_pairs + side_pairs)
    in_width = column >= time_pairs + side_pairs
    local_index = jnp.where(
        in_time, column, jnp.where(in_height, column - time_pairs, column - time_pairs - side_pairs)
    )
    axis_pairs = jnp.where(in_time, time_pairs, side_pairs)
    frequency = jnp.exp(
        -(local_index.astype(jnp.float32) / axis_pairs.astype(jnp.float32)) * math.log(rope_theta)
    )
    selector = jnp.stack([in_time, in_height, in_width]).astype(jnp.float32) * frequency[None, :]
    placed = positions.astype(jnp.float32)
    return (
        placed[0][:, None] * selector[0][None, :]
        + placed[1][:, None] * selector[1][None, :]
        + placed[2][:, None] * selector[2][None, :]
    )


def plan_kernel(rows, heads, count, lengths, out, ls, rs, split, least):
    cap, padded, _ = sizes(rows, heads)
    here = lax.axis_index("req")
    shift = rows.bit_length() - 1

    def clear(b, carry):
        ls[b] = 0
        rs[b] = 0
        return carry

    lax.fori_loop(0, count + 8, clear, 0)

    def one_video(v, start):
        end = start + lengths[v]
        b = lax.shift_right_logical(end - 1, shift) if rows == 1 << shift else lax.div(end - 1, rows)
        at = b * rows

        @pl.when(start < at)
        def _():
            ls[b] = at - start
            rs[b] = end - at

        return end

    lax.fori_loop(0, lengths.shape[0], one_video, 0)
    budget = 3.0 * lax.broadcasted_iota(jnp.int32, (8, 128), 1).astype(jnp.float32)
    split[...] = jnp.zeros_like(split)

    def tiles_of(x):
        return lax.shift_right_logical(x + TILE - 1, 4)

    def eight(b):
        return pl.ds(pl.multiple_of(b * 8, 8), 8)

    def per_tile(x, tiles):
        return jnp.floor((x + 0.5) * (1.0 / jnp.maximum(tiles, 1.0)))

    def facts(b):
        direct = lax.rem(b, 2).astype(jnp.float32)
        lt, rt = (jnp.full((8, 128), tiles_of(x[b]).astype(jnp.float32)) for x in (ls, rs))
        return lt, rt, padded + direct * 1e6

    def five_at_a_time(step, carry):
        def body(i, carry):
            for u in range(5):
                carry = step(5 * i + u, carry)
            return carry

        return lax.fori_loop(0, -(-(count - 1) // 5), body, carry)

    def from_right(i, load):
        b = -(-(count - 1) // 5) * 5 - i
        lt, rt, limit = facts(b)
        room = jnp.minimum(budget - load, limit)
        n = jnp.where(rt > 0.0, jnp.maximum(heads - per_tile(room, rt), 0.0), 0.0)
        least[eight(b)] = jnp.where(room >= 0.0, n, 1e6)
        return lt * n

    def from_left(i, carry):
        load, ok = carry
        b = i + 1
        lt, rt, limit = facts(b)
        room = jnp.minimum(budget - load, limit)
        most = jnp.where(lt > 0.0, jnp.minimum(per_tile(room, lt), float(heads)), 0.0)
        low = least[eight(b)]
        even = jnp.floor(heads * rt / jnp.maximum(lt + rt, 1.0) + 0.5)
        n = jnp.minimum(most, jnp.maximum(low, even))
        split[eight(b)] = n
        return rt * (heads - n), jnp.where((room >= 0.0) & (low <= most), ok, 0.0)

    zero = jnp.zeros((8, 128), jnp.float32)
    five_at_a_time(from_right, zero)
    load, ok = five_at_a_time(from_left, (zero, zero + 1.0))
    ok = jnp.where(load <= budget, ok, 0.0)
    most = jnp.min(jnp.where((ok > 0.0) & (budget >= (padded + MORE) // 3 * 3), budget, 1e9))
    out[MOST] = most.astype(jnp.int32)

    def head_split(b):
        n = split[eight(b)]
        return jnp.max(jnp.where(budget == most, n, 0.0)).astype(jnp.int32)

    even = lax.rem(here, 2) == 0
    beyond = jnp.where(even, here + 2, here - 1)
    n_left, n_right, n_beyond = head_split(here), head_split(here + 1), head_split(beyond)
    partner_passes = jnp.where(
        even,
        tiles_of(ls[beyond]) * n_beyond,
        tiles_of(rs[beyond]) * (heads - n_beyond),
    )
    for side, b, n in ((0, here, n_left), (1, here + 1, n_right)):
        direct = jnp.logical_not(even) if side == 0 else even
        at = jnp.where(direct, DIRECT, PASS)
        lt, rt = tiles_of(ls[b]), tiles_of(rs[b])
        none = jnp.where(lt > 0, 0, heads)
        keep = n if side == 0 else jnp.maximum(heads - n - none, 0)
        far = lt if side == 0 else rt
        out[at + LB], out[at + RB] = lt, rt
        out[at + LROWS], out[at + RROWS] = ls[b], rs[b]
        out[at + HEAD0] = 0 if side == 0 else n
        out[at + KEEP] = keep
        source = jnp.where(direct, partner_passes, 0)
        there = jnp.where(direct, padded, sum(pieces_of(padded)[:EARLY_CHUNKS])) - source
        out[at + EARLY] = jnp.minimum(keep, lax.div(jnp.maximum(there, 0), jnp.maximum(far, 1)))
        out[at + SOON] = jnp.minimum(keep, lax.div(pieces_of(padded)[0], jnp.maximum(far, 1)))
        out[at + SOURCE] = source
        out[at + OWN_FROM] = 0 if side == 0 else rows // TILE - lt
        out[at + OWN_TO] = lt if side == 0 else 0
        out[at + OWN] = rt if side == 0 else lt
        out[at + FAR_TO] = 0 if side == 0 else lt
        out[at + FAR] = far
        out[at + SIDE] = side
        to = SEND + jnp.where(direct, 4, 0)
        out[to + ROW] = 0 if side == 0 else rows - TILE * lt
        out[to + TILES] = rt if side == 0 else lt
        out[to + FIRST] = n if side == 0 else 0
        out[to + HEADS] = jnp.maximum(heads - n - none, 0) if side == 0 else n
    out[INNER_FROM] = rs[here]
    out[INNER_TO] = rows - ls[here + 1]


def in_groups(low, high, step):
    count = high - low

    def run(group, times):
        def body(i, carry):
            step(jnp.minimum(low + group * i, high - group), group)
            return carry

        lax.fori_loop(0, times, body, 0)

    run(8, jnp.where(count >= 8, lax.shift_right_logical(count + 7, 3), 0))
    run(2, jnp.where((count >= 2) & (count < 8), lax.shift_right_logical(count + 1, 1), 0))
    run(1, jnp.where(count == 1, 1, 0))


def lanes_of(h):
    return pl.ds(pl.multiple_of(h * HD, HD), HD)


def rows_of(t, group):
    return pl.ds(pl.multiple_of(t * TILE, TILE), group * TILE)


def turn(x, cosine, sine):
    wide = x.astype(jnp.float32)
    even = lax.rem(lax.broadcasted_iota(jnp.int32, wide.shape, 1), 2) == 0
    swapped = jnp.where(even, pltpu.roll(wide, HD - 1, 1), pltpu.roll(wide, 1, 1))
    return (wide * cosine + swapped * sine).astype(jnp.bfloat16)


def pack(scal, low, high, box, heads, get):
    base = 0
    for what in (SEND, SEND + 4):
        first_tile = lax.shift_right_logical(scal[what + ROW], 4)
        tiles, first, count = scal[what + TILES], scal[what + FIRST], scal[what + HEADS]

        def one_head(i, carry):
            start = base + (pl.program_id(0) * heads + i - first) * tiles
            begin = jnp.clip(low - start, 0, tiles)
            end = jnp.clip(high - start, 0, tiles)
            lanes = lanes_of(i)

            def step(t, group):
                q, k, v = get(rows_of(first_tile + t, group), lanes)
                item = pl.ds(start + t - low, group)
                box[item, 0:TILE] = q.reshape(group, TILE, HD)
                box[item, TILE : 2 * TILE] = k.reshape(group, TILE, HD)
                box[item, 2 * TILE : 3 * TILE] = v.reshape(group, TILE, HD)

            in_groups(begin, end, step)
            return carry

        before = first - pl.program_id(0) * heads
        lax.fori_loop(
            jnp.clip(before, 0, heads), jnp.clip(before + count, 0, heads), one_head, 0
        )
        base = base + tiles * count


def send_off(box, outs, sems):
    @pl.when(pl.program_id(0) == pl.num_programs(0) - 1)
    def _():
        at, copies = 0, []
        for i, out in enumerate(outs):
            copies.append(pltpu.make_async_copy(box.at[pl.ds(at, out.shape[0])], out, sems.at[i]))
            at += out.shape[0]
        for copy in copies:
            copy.start()
        for copy in copies:
            copy.wait()


def first_kernel(scal, q_hbm, k_hbm, v_hbm, cos_ref, sin_ref, box, qs, ks, vs, sems):
    limit = box.shape[0]
    ahead = qs.shape[0] - 1

    def heads_in(what, base):
        tiles = jnp.maximum(scal[what + TILES], 1)
        taken = lax.div(jnp.maximum(limit - base, 0) + tiles - 1, tiles)
        return jnp.minimum(scal[what + HEADS], taken)

    passed = scal[SEND + TILES] * scal[SEND + HEADS]
    count_pass = heads_in(SEND, 0)
    count = count_pass + heads_in(SEND + 4, passed)

    def entry(w):
        direct = w >= count_pass
        what = jnp.where(direct, SEND + 4, SEND)
        slot = w - jnp.where(direct, count_pass, 0)
        tiles = scal[what + TILES]
        start = jnp.where(direct, passed, 0) + slot * tiles
        return scal[what + FIRST] + slot, scal[what + ROW], tiles, start

    rows = cos_ref.shape[0]

    def each_copy(w, act):
        at = lax.rem(w, ahead + 1)
        head, row, tiles, _ = entry(w)
        few = tiles * TILE <= BLK
        block = pl.ds(pl.multiple_of(jnp.minimum(row, rows - BLK), TILE), BLK)
        for need, some in ((few, block), (jnp.logical_not(few), pl.ds(0, rows))):

            @pl.when(need)
            def _(some=some):
                for x, (source, place) in enumerate(((q_hbm, qs), (k_hbm, ks), (v_hbm, vs))):
                    act(pltpu.make_async_copy(
                        source.at[some, lanes_of(head)], place.at[at, some, :], sems.at[at, x]
                    ))

    for w in range(ahead):

        @pl.when(w < count)
        def _(w=w):
            each_copy(w, lambda copy: copy.start())

    def one_head(w, carry):
        @pl.when(w + ahead < count)
        def _():
            each_copy(w + ahead, lambda copy: copy.start())

        each_copy(w, lambda copy: copy.wait())
        at = lax.rem(w, ahead + 1)
        _, row, tiles, start = entry(w)
        first_tile = lax.shift_right_logical(row, 4)

        def step(t, group):
            source = rows_of(first_tile + t, group)
            cosine, sine = cos_ref[source, :], sin_ref[source, :]
            item = pl.ds(start + t, group)
            q, k = turn(qs[at, source, :], cosine, sine), turn(ks[at, source, :], cosine, sine)
            box[item, 0:TILE] = q.reshape(group, TILE, HD)
            box[item, TILE : 2 * TILE] = k.reshape(group, TILE, HD)
            box[item, 2 * TILE : 3 * TILE] = vs[at, source, :].reshape(group, TILE, HD)

        in_groups(0, jnp.clip(limit - start, 0, tiles), step)
        return carry

    lax.fori_loop(0, count, one_head, 0)


def second_kernel(
    low, scal, q_ref, k_ref, v_ref, cos_ref, sin_ref, swap_ref, wt_ref, mod_ref, qr_ref, kr_ref, w_ref, shift_ref, *rest
):
    outs, box, sems = rest[:-3], rest[-2], rest[-1]
    rows = q_ref.shape[0]
    heads = q_ref.shape[1] // HD
    wide = swap_ref.shape[0]

    @pl.when(pl.program_id(0) == 0)
    def _():
        w = wt_ref[...].astype(jnp.float32)
        scaled = w * (1.0 + mod_ref[1:2, :])
        high = scaled.astype(jnp.bfloat16)
        low = (scaled - high.astype(jnp.float32)).astype(jnp.bfloat16)
        w_ref[...] = jnp.concatenate([high, low], axis=0)
        shift = jnp.sum(w * mod_ref[0:1, :], axis=1, keepdims=True)
        shift_ref[...] = jnp.broadcast_to(shift, shift_ref.shape)

    for source, to in ((q_ref, qr_ref), (k_ref, kr_ref)):
        for h in range(0, heads, wide // HD):
            for j in range(rows // BLK):
                at = slice(j * BLK, (j + 1) * BLK)
                x = source[at, h * HD : h * HD + wide]
                swapped = jnp.dot(x, swap_ref[: x.shape[1], : x.shape[1]], preferred_element_type=jnp.float32)
                for i in range(x.shape[1] // HD):
                    lanes = slice(i * HD, (i + 1) * HD)
                    to[at, (h + i) * HD : (h + i + 1) * HD] = (
                        x[:, lanes].astype(jnp.float32) * cos_ref[at, :] + swapped[:, lanes] * sin_ref[at, :]
                    ).astype(jnp.bfloat16)

    def get(rows, lanes):
        return qr_ref[rows, lanes], kr_ref[rows, lanes], v_ref[rows, lanes]

    pack(scal, low, low + box.shape[0], box, heads, get)
    send_off(box, outs, sems)


def dot_t(a, b):
    return lax.dot_general(a, b, (((1,), (1,)), ((), ())), preferred_element_type=jnp.float32)


def attend_rows(q, k, v_ones, masked):
    s = masked(dot_t(q, k))
    top = jnp.max(s, axis=1, keepdims=True)
    weight = jnp.exp2(s * SCALE2 - top * SCALE2).astype(jnp.bfloat16)
    both = jnp.dot(weight, v_ones, preferred_element_type=jnp.float32)
    return (both[:, :HD] / both[:, HD:]).astype(jnp.bfloat16)


def project_block(o_ref, w_ref, out_ref, j):
    at = slice(j * BLK, (j + 1) * BLK)
    z = dot_t(o_ref[at, :], w_ref[...])
    z = z + pltpu.roll(z, HD // 2, 1)
    lane = lax.broadcasted_iota(jnp.int32, z.shape, 1)
    squares = jnp.zeros(z.shape, jnp.float32)
    for h in range(o_ref.shape[1] // HD):
        wide = o_ref[at, h * HD : (h + 1) * HD].astype(jnp.float32)
        squares = squares + wide * wide
    total = jnp.sum(squares, axis=1, keepdims=True)
    out_ref[at, :] = jnp.where(lane < HD // 2, z, jnp.where(lane == HD // 2, total, 0.0))


def inner_kernel(scal, q_ref, k_ref, v_ref, w_ref, qv_ref, kv_ref, out_ref, o_ref):
    g = pl.program_id(0)
    rows, width = q_ref.shape
    ones = jnp.ones((rows, HD), jnp.bfloat16)
    for j in range(rows // BLK):
        holds_some = (scal[INNER_FROM] < (j + 1) * BLK) & (scal[INNER_TO] > j * BLK)

        @pl.when(holds_some)
        def _(j=j):
            at = pl.ds(j * BLK, BLK)
            same = qv_ref[at, :] == kv_ref[...]
            for i in range(width // HD):
                lanes = slice(i * HD, (i + 1) * HD)
                v_ones = jnp.concatenate([v_ref[:, lanes], ones], axis=1)
                o_ref[at, pl.ds(pl.multiple_of(g * width + i * HD, HD), HD)] = attend_rows(
                    q_ref[at, lanes], k_ref[:, lanes], v_ones, lambda s: jnp.where(same, s, NEG)
                )

        @pl.when(holds_some & (g == pl.num_programs(0) - 1))
        def _(j=j):
            project_block(o_ref, w_ref, out_ref, j)


def across(scal, at, offset, low, high, sources, items, w_ref, own_sems, places, o_ref, zz):
    rows = zz.shape[0] // 2
    left, right = scal[at + LB], scal[at + RB]
    lead = left * TILE - scal[at + LROWS]
    end = left * TILE + scal[at + RROWS]
    blocks = jnp.minimum(lax.div((left + right) * TILE + BLK - 1, BLK), rows // BLK)
    own_at = jnp.where(scal[at + SIDE] == 0, rows, 0) + left * TILE
    pairs = lax.shift_right_logical(high - low + 1, 1)

    def heads_of(i):
        return [jnp.minimum(low + 2 * i + u, high - 1) for u in range(2)]

    def own_copies(i, act):
        slot = lax.rem(i, 2)
        few = scal[at + OWN] * TILE <= rows // 2
        begin = jnp.where(scal[at + SIDE] == 0, 0, rows // 2)
        for need, begin, size in ((few, begin, rows // 2), (jnp.logical_not(few), 0, rows)):

            @pl.when(need)
            def _(begin=begin, size=size):
                source_rows = pl.ds(pl.multiple_of(begin, TILE), size)
                to = pl.ds(pl.multiple_of(own_at + begin, TILE), size)
                for u, s in enumerate(heads_of(i)):
                    lanes = lanes_of(scal[at + HEAD0] + s)
                    for x, (source, place) in enumerate(zip(sources, places)):
                        act(pltpu.make_async_copy(
                            source.at[source_rows, lanes], place.at[slot, u, to, :], own_sems.at[slot, u, x]
                        ))

    @pl.when(pairs > 0)
    def _():
        own_copies(0, lambda copy: copy.start())

    def two_heads(n, i, carry):
        slot = lax.rem(i, 2)

        @pl.when(i + 1 < pairs)
        def _():
            own_copies(i + 1, lambda copy: copy.start())

        heads = heads_of(i)

        def foreign(t, group):
            to = rows_of(rows // TILE + scal[at + FAR_TO] + t, group)
            for u, s in enumerate(heads):
                item = pl.ds(scal[at + SOURCE] + offset + s * scal[at + FAR] + t, group)
                for x, place in enumerate(places):
                    part = items[item, x * TILE : (x + 1) * TILE]
                    place[slot, u, to, :] = part.reshape(group * TILE, HD)

        in_groups(0, scal[at + FAR], foreign)
        own_copies(i, lambda copy: copy.wait())
        width = n * BLK
        if width == rows:

            @pl.when((left + right) * TILE > rows)
            def _():
                row = lax.broadcasted_iota(jnp.int32, (TILE, HD), 0)
                for place in places:
                    for u in range(2):
                        first = place[slot, u, rows : rows + TILE, :]
                        last = place[slot, u, 2 * rows : 2 * rows + TILE, :]
                        place[slot, u, rows : rows + TILE, :] = jnp.where(row < lead, last, first)

        place = lax.broadcasted_iota(jnp.int32, (1, width), 1)
        valid = ((place >= lead) & (place < end)) | (place + rows < end)
        bias = jnp.where(valid, 0.0, NEG)
        ones = jnp.ones((width, HD), jnp.bfloat16)
        qs, ks, vs = places
        whole = slice(rows, rows + width)
        for j in range(n):
            mine = slice(rows + j * BLK, rows + (j + 1) * BLK)
            for u, s in enumerate(heads):
                v_ones = jnp.concatenate([vs[slot, u, whole, :], ones], axis=1)
                o_ref[j * BLK : (j + 1) * BLK, lanes_of(scal[at + HEAD0] + s)] = attend_rows(
                    qs[slot, u, mine, :], ks[slot, u, whole, :], v_ones, lambda x: x + bias
                )
        return carry

    for n in range(1, rows // BLK + 1):

        @pl.when((blocks == n) & (pairs > 0))
        def _(n=n):
            o_ref[0 : n * BLK, :] = jnp.zeros((n * BLK, o_ref.shape[1]), o_ref.dtype)
            lax.fori_loop(0, pairs, functools.partial(two_heads, n), 0)
            for j in range(n):
                project_block(o_ref, w_ref, zz, j)
            zz[rows : 2 * rows, :] = zz[0:rows, :]

    @pl.when(pairs <= 0)
    def _():
        zz[...] = jnp.zeros_like(zz)

    return zz[pl.ds(pl.multiple_of(left * TILE, TILE), rows), :]


def fetch(scal, at, offset, low, high, places, boxes, items, sems):
    begin = scal[at + SOURCE] + offset + low * scal[at + FAR]
    end = scal[at + SOURCE] + offset + high * scal[at + FAR]
    return [
        (
            pltpu.make_async_copy(box, items.at[pl.ds(place, box.shape[0])], sems.at[i]),
            (high > low) & (begin < place + box.shape[0]) & (end > place),
        )
        for i, (place, box) in enumerate(zip(places, boxes))
    ]


def clear(places, rows):
    for place in places:
        for slot in range(2):
            for u in range(2):
                place[slot, u, rows : 2 * rows + TILE, :] = jnp.zeros((rows + TILE, HD), place.dtype)


def of_boundary(scal, at, shape, mine):
    row = lax.broadcasted_iota(jnp.int32, shape, 0)
    tail = jnp.where(row >= shape[0] - scal[at + LROWS], 1, 0)
    head = jnp.where(row < scal[at + RROWS], 1, 0)
    right_is_mine = (scal[at + SIDE] == 0) == mine
    return jnp.where(right_is_mine, head, tail) == 1


def send_back(scal, at, z, back_ref):
    lane = lax.broadcasted_iota(jnp.int32, z.shape, 1)
    back = jnp.where(of_boundary(scal, at, z.shape, False), z, 0.0)
    high = back.astype(jnp.bfloat16).astype(jnp.float32)
    both = jnp.where(lane == HD // 2 + 1, pltpu.roll(back - high, 1, 1), high)
    back_ref[...] = both.T[: back_ref.shape[0]].astype(jnp.bfloat16)


def early_kernel(places, at, since, until, scal, q_hbm, k_hbm, v_hbm, w_ref, *rest):
    boxes, (out_ref, items, sems, own_sems, qs, ks, vs, o_ref, zz) = rest[: len(places)], rest[len(places) :]
    low, high = 0 if since is None else scal[at + since], scal[at + until]
    copies = fetch(scal, at, 0, low, high, places, boxes, items, sems)
    for copy, need in copies:
        pl.when(need)(copy.start)
    clear((qs, ks, vs), zz.shape[0] // 2)
    for copy, need in copies:
        pl.when(need)(copy.wait)
    out_ref[...] = across(
        scal, at, 0, low, high, (q_hbm, k_hbm, v_hbm), items, w_ref, own_sems, (qs, ks, vs), o_ref, zz
    )


def last_kernel(places, offsets, scal, q_hbm, k_hbm, v_hbm, w_ref, *rest):
    partials, rest = rest[:5], rest[5:]
    boxes, rest = rest[: len(places)], rest[len(places) :]
    own_ref, pass_back_ref, direct_back_ref, items, sems, own_sems, qs, ks, vs, o_ref, zz, sums, sum_sems = rest
    sum_copies = [
        pltpu.make_async_copy(part, sums.at[i], sum_sems.at[i]) for i, part in enumerate(partials)
    ]
    for copy in sum_copies:
        copy.start()
    clear((qs, ks, vs), zz.shape[0] // 2)

    def remaining(at, offset):
        low, high = scal[at + EARLY], scal[at + KEEP]
        copies = fetch(scal, at, offset, low, high, places, boxes, items, sems)
        for copy, need in copies:
            pl.when(need)(copy.start)
        for copy, need in copies:
            pl.when(need)(copy.wait)
        return across(
            scal, at, offset, low, high, (q_hbm, k_hbm, v_hbm), items, w_ref, own_sems, (qs, ks, vs), o_ref, zz
        )

    passed_z = remaining(PASS, offsets[0])
    for copy in sum_copies:
        copy.wait()
    passed_z = passed_z + sums[0] + sums[4]
    send_back(scal, PASS, passed_z, pass_back_ref)
    own = jnp.where(of_boundary(scal, PASS, passed_z.shape, True), passed_z, sums[2] + sums[3])
    direct_z = sums[1] + remaining(DIRECT, offsets[1])
    send_back(scal, DIRECT, direct_z, direct_back_ref)
    own = jnp.where(of_boundary(scal, DIRECT, own.shape, True), direct_z, own)
    own_ref[...] = own.T[: own_ref.shape[0]]


def step_rows(video_ids, step_sizes):
    chosen = video_ids[:, None] == jnp.arange(step_sizes.shape[0], dtype=jnp.int32)[None, :]
    return jnp.sum(jnp.where(chosen, step_sizes[None, :], 0.0), axis=1)


def call(kernel, name, mib, scalars, operands, in_specs, outs, out_specs, scratch, grid=()):
    return pl.pallas_call(
        kernel,
        out_shape=outs,
        grid_spec=pltpu.PrefetchScalarGridSpec(
            num_scalar_prefetch=1, grid=grid, in_specs=in_specs, out_specs=out_specs,
            scratch_shapes=scratch,
        ),
        compiler_params=pltpu.CompilerParams(vmem_limit_bytes=mib * MIB),
        cost_estimate=pl.CostEstimate(flops=1, bytes_accessed=1, transcendentals=0),
        name=name,
    )(scalars, *operands)


def per_device(
    query_rows, key_rows, value_rows, positions, latents, w_head, modulation,
    guide_scale, step_sizes, lengths,
):
    rows, features = query_rows.shape[1], query_rows.shape[2]
    heads = features // HD
    count = lax.axis_size("req")
    here = lax.axis_index("req")
    first_row = here * rows
    _, padded, room = sizes(rows, heads)
    sizes_passed = pieces_of(padded)
    late_sizes = (*sizes_passed[1:], MORE, room - padded - MORE)

    angle = angles(positions)
    odd = (jnp.arange(HD, dtype=jnp.int32) % 2).astype(jnp.float32)
    cosine = jnp.cos(angle)
    sine = jnp.sin(angle) * (2.0 * odd - 1.0)[None, :]

    smem = pl.BlockSpec(memory_space=pltpu.SMEM)
    vmem = pl.BlockSpec(memory_space=pltpu.VMEM)
    hbm = pl.BlockSpec(memory_space=pl.ANY)
    parity = lax.axis_index("cfg")
    tie = lax.optimization_barrier
    scalars = pl.pallas_call(
        functools.partial(plan_kernel, rows, heads, count),
        out_shape=jax.ShapeDtypeStruct((SCALARS,), jnp.int32),
        in_specs=[smem],
        out_specs=smem,
        scratch_shapes=[
            pltpu.SMEM((count + 8,), jnp.int32),
            pltpu.SMEM((count + 8,), jnp.int32),
            pltpu.VMEM(((count + 8) * 8, 128), jnp.float32),
            pltpu.VMEM(((count + 8) * 8, 128), jnp.float32),
        ],
        name="plan",
    )(lengths)

    def in_hbm(x):
        return pltpu.with_memory_space_constraint(x, pltpu.HBM)

    q, k, v = query_rows[0], key_rows[0], value_rows[0]

    def box(items):
        return jax.ShapeDtypeStruct((items, 3 * TILE, HD), jnp.bfloat16)

    def box_scratch(items):
        return pltpu.VMEM((items, 3 * TILE, HD), jnp.bfloat16)

    group = next(n for n in (5, 4, 3, 2, 1) if heads % n == 0)
    steps = heads // group
    head_block = pl.BlockSpec((rows, group * HD), lambda g, s: (0, g))
    table = pl.BlockSpec((rows, HD), lambda g, s: (0, 0))
    first = call(
        first_kernel, "pack_first", 16, scalars, (in_hbm(q), in_hbm(k), in_hbm(v), cosine, sine),
        [hbm] * 3 + [vmem] * 2, (box(sizes_passed[0]),), (vmem,),
        [*[pltpu.VMEM((4, rows, HD), jnp.bfloat16)] * 3, pltpu.SemaphoreType.DMA((4, 3))],
    )
    pairs = [(i, i ^ 1) for i in range(count)]
    onward = [(i, i + 2) for i in range(0, count - 2, 2)] + [(i + 2, i) for i in range(1, count - 2, 2)]
    got = [lax.ppermute(first[0], "req", pairs)]

    after_first, _ = tie((scalars, first[0]))
    swap = jnp.asarray(numpy.eye(2 * HD)[numpy.arange(2 * HD) ^ 1], jnp.bfloat16)
    q_rot, k_rot, w_both, shift, *second = call(
        functools.partial(second_kernel, sizes_passed[0]), "turn_and_pack_rest", 32, after_first,
        (in_hbm(q), in_hbm(k), in_hbm(v), cosine, sine, swap, w_head.T, modulation),
        [head_block] * 3 + [table] * 2 + [vmem] * 3,
        (pltpu.HBM(q.shape, q.dtype), pltpu.HBM(k.shape, k.dtype),
         jax.ShapeDtypeStruct((HD, features), jnp.bfloat16),
         jax.ShapeDtypeStruct((HD // 2, HD), jnp.float32),
         *[box(n) for n in late_sizes], box(late_sizes[-1])),
        (head_block, head_block, vmem, vmem, *[hbm] * (len(late_sizes) + 1)),
        [box_scratch(sum(late_sizes)), pltpu.SemaphoreType.DMA((len(late_sizes),))], grid=(steps,),
    )
    got += [lax.ppermute(x, "req", pairs) for x in second[: CHUNKS - 1]]
    more, arriving = second[CHUNKS:]

    own_rows = first_row + jnp.arange(rows, dtype=jnp.int32)
    video = jnp.sum((jnp.cumsum(lengths)[None, :] <= own_rows[:, None]).astype(jnp.int32), axis=1)
    step_of_row = step_rows(video, step_sizes)

    def inner(when, first_step, step_count):
        block = pl.BlockSpec((rows, group * HD), lambda g, s: (0, g + first_step))
        width = step_count * group * HD
        return call(
            inner_kernel, "inner_videos", 20, when,
            (in_hbm(q_rot), in_hbm(k_rot), in_hbm(v), w_both, video[:, None], video[None, :]),
            [block] * 3 + [pl.BlockSpec((HD, width), lambda g, s: (0, first_step // step_count))] + [vmem] * 2, pltpu.HBM((rows, HD), jnp.float32), vmem,
            [pltpu.VMEM((rows, width), jnp.bfloat16)], grid=(step_count,),
        )

    when_a, got[0] = tie((scalars, got[0]))
    inner_a = inner(when_a, 0, steps // 2)
    got[1], inner_a = tie((got[1], inner_a))
    passed = [lax.ppermute(x, "req", onward) for x in got[:2]]
    when_b, passed[0], got[2], inner_a = tie((scalars, passed[0], got[2], inner_a))
    got[2], second[CHUNKS - 1] = tie((got[2], second[CHUNKS - 1]))
    got.append(lax.ppermute(second[CHUNKS - 1], "req", pairs))
    inner_b = inner(when_b, steps // 2, steps - steps // 2)
    when_soon, inner_b = tie((scalars, inner_b))

    place = pltpu.VMEM((2, 2, 3 * rows, HD), jnp.bfloat16)
    work = [
        pltpu.SemaphoreType.DMA((2, 2, 3)), place, place, place,
        pltpu.VMEM((rows, features), jnp.bfloat16),
        pltpu.VMEM((2 * rows, HD), jnp.float32),
    ]
    partial = pltpu.HBM((rows, HD), jnp.float32)
    lanes = HD // 2 + TILE
    sent_back = jax.ShapeDtypeStruct((lanes, rows), jnp.bfloat16)

    def on_videos_across(kernel, name, when, boxes, outs, others=(), scratch=()):
        places = [0]
        for x in boxes:
            places.append(places[-1] + x.shape[0])
        return call(
            kernel(tuple(places[:-1])), name, 32, when,
            (in_hbm(q_rot), in_hbm(k_rot), in_hbm(v), w_both, *[in_hbm(x) for x in others], *boxes),
            [hbm] * 3 + [vmem] + [hbm] * (len(others) + len(boxes)),
            outs, jax.tree.map(lambda _: vmem, outs),
            [box_scratch(places[-1]), pltpu.SemaphoreType.DMA((len(boxes),)), *work, *scratch],
        )

    def early_on(at, since, until, name, when, boxes):
        return on_videos_across(
            lambda places: functools.partial(early_kernel, places, at, since, until), name, when, boxes,
            partial,
        )

    soon = early_on(PASS, None, SOON, "videos_across_soon", when_soon, passed[:1])
    got[3], soon = tie((got[3], soon))
    when_early, got[3] = tie((scalars, got[3]))
    passed += [lax.ppermute(x, "req", onward) for x in got[2:CHUNKS]]
    early = early_on(PASS, SOON, EARLY, "videos_across_early", when_early, passed[:EARLY_CHUNKS])
    when_direct, early, passed[2] = tie((scalars, early, passed[2]))
    direct_z = early_on(DIRECT, None, EARLY, "videos_across_direct", when_direct, got[:CHUNKS])

    pieces = jnp.maximum(scalars[MOST] - padded - MORE + EXTRA - 1, 0) // EXTRA
    pieces, direct_z = tie((pieces, direct_z))

    def one_more(i, arrived):
        piece = lax.dynamic_slice_in_dim(more, i * EXTRA, EXTRA, 0)
        piece = lax.ppermute(piece, "req", pairs)
        return lax.dynamic_update_slice_in_dim(arrived, piece, i * EXTRA, 0)

    arrived = lax.fori_loop(0, pieces, one_more, arriving)
    before = EARLY_CHUNKS - 1
    offsets = (-sum(sizes_passed[:before]), sum(sizes_passed[before:]))
    own, to_beyond, to_direct = on_videos_across(
        lambda places: functools.partial(last_kernel, places, offsets), "videos_across_last", scalars,
        [*passed[before:], *got, arrived],
        (jax.ShapeDtypeStruct((lanes, rows), jnp.float32), sent_back, sent_back),
        (early, direct_z, inner_a, inner_b, soon),
        (pltpu.VMEM((5, rows, HD), jnp.float32), pltpu.SemaphoreType.DMA((5,))),
    )
    back_direct = lax.ppermute(to_direct, "req", pairs)
    beyond = [(i, i + 1) for i in range(1, count - 1, 2)] + [(i + 1, i) for i in range(1, count - 1, 2)]
    back_beyond = lax.ppermute(to_beyond, "req", beyond)
    total = own + back_direct.astype(jnp.float32) + back_beyond.astype(jnp.float32)
    values = HD // 2
    squares = total[values : values + 1] + total[values + 1 : values + 2]
    velocity = total[:values] * lax.rsqrt(squares / features + 1e-06) + shift[:, :1]

    width = latents.shape[1]
    mine = lax.dynamic_slice_in_dim(velocity, parity * width, width, 0)
    theirs = lax.dynamic_slice_in_dim(velocity, (1 - parity) * width, width, 0)
    partner = lax.ppermute(theirs, "cfg", [(0, 1), (1, 0)])
    conditional = jnp.where(parity == 0, mine, partner)
    unconditional = jnp.where(parity == 0, partner, mine)
    guided = unconditional + guide_scale[0] * (conditional - unconditional)
    return (latents.T + step_of_row[None, :] * guided).T


def solution(mesh):
    in_specs = (
        P("cfg", "req", None), P("cfg", "req", None), P("cfg", "req", None),
        P(None, "req"), P("req", "cfg"), P(), P(), P(), P(), P(),
    )
    return jax.shard_map(
        per_device, mesh=mesh, in_specs=in_specs, out_specs=P("req", "cfg"), check_vma=False
    )
```

```python
import functools
import math

import jax
import jax.numpy as jnp
import numpy
from jax import lax
from jax.experimental import pallas as pl
from jax.experimental.pallas import tpu as pltpu
from jax.sharding import PartitionSpec as P

HD = 128
TILE = 16
BLK = 128
CHUNKS = 4
MORE = 64
EXTRA = 16
EARLY_CHUNKS = 2
rope_theta = 10000.0
NEG = -1e30
SCALE2 = math.log2(math.e) / math.sqrt(HD)

PASS, DIRECT = 0, 16
LB, RB, LROWS, RROWS, HEAD0, KEEP, EARLY, SOURCE = range(8)
OWN_FROM, OWN_TO, OWN, FAR_TO, FAR, SIDE, SOON = range(8, 15)
SEND = 32
ROW, TILES, FIRST, HEADS = range(4)
MOST, INNER_FROM, INNER_TO = 40, 41, 42
SCALARS = 48
MIB = 1024 * 1024


def sizes(rows, heads):
    tiles = rows // TILE
    cap = max(
        min(max(a * n, (tiles + 1 - a) * (heads - n)) for n in range(heads + 1))
        for a in range(1, tiles + 1)
    )
    padded = -(-cap // TILE) * TILE
    return cap, padded, 2 * padded


def pieces_of(padded):
    most = padded * 3 // 11
    return (*[most] * (CHUNKS - 1), padded - most * (CHUNKS - 1))


def angles(positions):
    pair_total = HD // 2
    side_pairs = HD // 6
    time_pairs = pair_total - 2 * side_pairs
    column = jnp.arange(HD, dtype=jnp.int32) // 2
    in_time = column < time_pairs
    in_height = (column >= time_pairs) & (column < time_pairs + side_pairs)
    in_width = column >= time_pairs + side_pairs
    local_index = jnp.where(
        in_time, column, jnp.where(in_height, column - time_pairs, column - time_pairs - side_pairs)
    )
    axis_pairs = jnp.where(in_time, time_pairs, side_pairs)
    frequency = jnp.exp(
        -(local_index.astype(jnp.float32) / axis_pairs.astype(jnp.float32)) * math.log(rope_theta)
    )
    selector = jnp.stack([in_time, in_height, in_width]).astype(jnp.float32) * frequency[None, :]
    placed = positions.astype(jnp.float32)
    return (
        placed[0][:, None] * selector[0][None, :]
        + placed[1][:, None] * selector[1][None, :]
        + placed[2][:, None] * selector[2][None, :]
    )


def plan_kernel(rows, heads, count, lengths, out, ls, rs, split, least):
    cap, padded, _ = sizes(rows, heads)
    here = lax.axis_index("req")
    shift = rows.bit_length() - 1

    def clear(b, carry):
        ls[b] = 0
        rs[b] = 0
        return carry

    lax.fori_loop(0, count + 8, clear, 0)

    def one_video(v, start):
        end = start + lengths[v]
        b = lax.shift_right_logical(end - 1, shift) if rows == 1 << shift else lax.div(end - 1, rows)
        at = b * rows

        @pl.when(start < at)
        def _():
            ls[b] = at - start
            rs[b] = end - at

        return end

    lax.fori_loop(0, lengths.shape[0], one_video, 0)
    budget = 3.0 * lax.broadcasted_iota(jnp.int32, (8, 128), 1).astype(jnp.float32)
    split[...] = jnp.zeros_like(split)

    def tiles_of(x):
        return lax.shift_right_logical(x + TILE - 1, 4)

    def eight(b):
        return pl.ds(pl.multiple_of(b * 8, 8), 8)

    def per_tile(x, tiles):
        return jnp.floor((x + 0.5) * (1.0 / jnp.maximum(tiles, 1.0)))

    def facts(b):
        direct = lax.rem(b, 2).astype(jnp.float32)
        lt, rt = (jnp.full((8, 128), tiles_of(x[b]).astype(jnp.float32)) for x in (ls, rs))
        return lt, rt, padded + direct * 1e6

    def five_at_a_time(step, carry):
        def body(i, carry):
            for u in range(5):
                carry = step(5 * i + u, carry)
            return carry

        return lax.fori_loop(0, -(-(count - 1) // 5), body, carry)

    def from_right(i, load):
        b = -(-(count - 1) // 5) * 5 - i
        lt, rt, limit = facts(b)
        room = jnp.minimum(budget - load, limit)
        n = jnp.where(rt > 0.0, jnp.maximum(heads - per_tile(room, rt), 0.0), 0.0)
        least[eight(b)] = jnp.where(room >= 0.0, n, 1e6)
        return lt * n

    def from_left(i, carry):
        load, ok = carry
        b = i + 1
        lt, rt, limit = facts(b)
        room = jnp.minimum(budget - load, limit)
        most = jnp.where(lt > 0.0, jnp.minimum(per_tile(room, lt), float(heads)), 0.0)
        low = least[eight(b)]
        even = jnp.floor(heads * rt / jnp.maximum(lt + rt, 1.0) + 0.5)
        n = jnp.minimum(most, jnp.maximum(low, even))
        split[eight(b)] = n
        return rt * (heads - n), jnp.where((room >= 0.0) & (low <= most), ok, 0.0)

    zero = jnp.zeros((8, 128), jnp.float32)
    five_at_a_time(from_right, zero)
    load, ok = five_at_a_time(from_left, (zero, zero + 1.0))
    ok = jnp.where(load <= budget, ok, 0.0)
    most = jnp.min(jnp.where((ok > 0.0) & (budget >= (padded + MORE) // 3 * 3), budget, 1e9))
    out[MOST] = most.astype(jnp.int32)

    def head_split(b):
        n = split[eight(b)]
        return jnp.max(jnp.where(budget == most, n, 0.0)).astype(jnp.int32)

    even = lax.rem(here, 2) == 0
    beyond = jnp.where(even, here + 2, here - 1)
    n_left, n_right, n_beyond = head_split(here), head_split(here + 1), head_split(beyond)
    partner_passes = jnp.where(
        even,
        tiles_of(ls[beyond]) * n_beyond,
        tiles_of(rs[beyond]) * (heads - n_beyond),
    )
    for side, b, n in ((0, here, n_left), (1, here + 1, n_right)):
        direct = jnp.logical_not(even) if side == 0 else even
        at = jnp.where(direct, DIRECT, PASS)
        lt, rt = tiles_of(ls[b]), tiles_of(rs[b])
        none = jnp.where(lt > 0, 0, heads)
        keep = n if side == 0 else jnp.maximum(heads - n - none, 0)
        far = lt if side == 0 else rt
        out[at + LB], out[at + RB] = lt, rt
        out[at + LROWS], out[at + RROWS] = ls[b], rs[b]
        out[at + HEAD0] = 0 if side == 0 else n
        out[at + KEEP] = keep
        source = jnp.where(direct, partner_passes, 0)
        there = jnp.where(direct, padded, sum(pieces_of(padded)[:EARLY_CHUNKS])) - source
        out[at + EARLY] = jnp.minimum(keep, lax.div(jnp.maximum(there, 0), jnp.maximum(far, 1)))
        out[at + SOON] = jnp.minimum(keep, lax.div(pieces_of(padded)[0], jnp.maximum(far, 1)))
        out[at + SOURCE] = source
        out[at + OWN_FROM] = 0 if side == 0 else rows // TILE - lt
        out[at + OWN_TO] = lt if side == 0 else 0
        out[at + OWN] = rt if side == 0 else lt
        out[at + FAR_TO] = 0 if side == 0 else lt
        out[at + FAR] = far
        out[at + SIDE] = side
        to = SEND + jnp.where(direct, 4, 0)
        out[to + ROW] = 0 if side == 0 else rows - TILE * lt
        out[to + TILES] = rt if side == 0 else lt
        out[to + FIRST] = n if side == 0 else 0
        out[to + HEADS] = jnp.maximum(heads - n - none, 0) if side == 0 else n
    out[INNER_FROM] = rs[here]
    out[INNER_TO] = rows - ls[here + 1]


def in_groups(low, high, step):
    count = high - low

    def run(group, times):
        def body(i, carry):
            step(jnp.minimum(low + group * i, high - group), group)
            return carry

        lax.fori_loop(0, times, body, 0)

    run(8, jnp.where(count >= 8, lax.shift_right_logical(count + 7, 3), 0))
    run(2, jnp.where((count >= 2) & (count < 8), lax.shift_right_logical(count + 1, 1), 0))
    run(1, jnp.where(count == 1, 1, 0))


def lanes_of(h):
    return pl.ds(pl.multiple_of(h * HD, HD), HD)


def rows_of(t, group):
    return pl.ds(pl.multiple_of(t * TILE, TILE), group * TILE)


def turn(x, cosine, sine):
    wide = x.astype(jnp.float32)
    even = lax.rem(lax.broadcasted_iota(jnp.int32, wide.shape, 1), 2) == 0
    swapped = jnp.where(even, pltpu.roll(wide, HD - 1, 1), pltpu.roll(wide, 1, 1))
    return (wide * cosine + swapped * sine).astype(jnp.bfloat16)


def pack(scal, low, high, box, heads, get):
    base = 0
    for what in (SEND, SEND + 4):
        first_tile = lax.shift_right_logical(scal[what + ROW], 4)
        tiles, first, count = scal[what + TILES], scal[what + FIRST], scal[what + HEADS]

        def one_head(i, carry):
            start = base + (pl.program_id(0) * heads + i - first) * tiles
            begin = jnp.clip(low - start, 0, tiles)
            end = jnp.clip(high - start, 0, tiles)
            lanes = lanes_of(i)

            def step(t, group):
                q, k, v = get(rows_of(first_tile + t, group), lanes)
                item = pl.ds(start + t - low, group)
                box[item, 0:TILE] = q.reshape(group, TILE, HD)
                box[item, TILE : 2 * TILE] = k.reshape(group, TILE, HD)
                box[item, 2 * TILE : 3 * TILE] = v.reshape(group, TILE, HD)

            in_groups(begin, end, step)
            return carry

        before = first - pl.program_id(0) * heads
        lax.fori_loop(
            jnp.clip(before, 0, heads), jnp.clip(before + count, 0, heads), one_head, 0
        )
        base = base + tiles * count


def send_off(box, outs, sems):
    @pl.when(pl.program_id(0) == pl.num_programs(0) - 1)
    def _():
        at, copies = 0, []
        for i, out in enumerate(outs):
            copies.append(pltpu.make_async_copy(box.at[pl.ds(at, out.shape[0])], out, sems.at[i]))
            at += out.shape[0]
        for copy in copies:
            copy.start()
        for copy in copies:
            copy.wait()


def first_kernel(scal, q_hbm, k_hbm, v_hbm, cos_ref, sin_ref, box, qs, ks, vs, sems):
    limit = box.shape[0]
    ahead = qs.shape[0] - 1

    def heads_in(what, base):
        tiles = jnp.maximum(scal[what + TILES], 1)
        taken = lax.div(jnp.maximum(limit - base, 0) + tiles - 1, tiles)
        return jnp.minimum(scal[what + HEADS], taken)

    passed = scal[SEND + TILES] * scal[SEND + HEADS]
    count_pass = heads_in(SEND, 0)
    count = count_pass + heads_in(SEND + 4, passed)

    def entry(w):
        direct = w >= count_pass
        what = jnp.where(direct, SEND + 4, SEND)
        slot = w - jnp.where(direct, count_pass, 0)
        tiles = scal[what + TILES]
        start = jnp.where(direct, passed, 0) + slot * tiles
        return scal[what + FIRST] + slot, scal[what + ROW], tiles, start

    rows = cos_ref.shape[0]

    def each_copy(w, act):
        at = lax.rem(w, ahead + 1)
        head, row, tiles, _ = entry(w)
        few = tiles * TILE <= BLK
        block = pl.ds(pl.multiple_of(jnp.minimum(row, rows - BLK), TILE), BLK)
        for need, some in ((few, block), (jnp.logical_not(few), pl.ds(0, rows))):

            @pl.when(need)
            def _(some=some):
                for x, (source, place) in enumerate(((q_hbm, qs), (k_hbm, ks), (v_hbm, vs))):
                    act(pltpu.make_async_copy(
                        source.at[some, lanes_of(head)], place.at[at, some, :], sems.at[at, x]
                    ))

    for w in range(ahead):

        @pl.when(w < count)
        def _(w=w):
            each_copy(w, lambda copy: copy.start())

    def one_head(w, carry):
        @pl.when(w + ahead < count)
        def _():
            each_copy(w + ahead, lambda copy: copy.start())

        each_copy(w, lambda copy: copy.wait())
        at = lax.rem(w, ahead + 1)
        _, row, tiles, start = entry(w)
        first_tile = lax.shift_right_logical(row, 4)

        def step(t, group):
            source = rows_of(first_tile + t, group)
            cosine, sine = cos_ref[source, :], sin_ref[source, :]
            item = pl.ds(start + t, group)
            q, k = turn(qs[at, source, :], cosine, sine), turn(ks[at, source, :], cosine, sine)
            box[item, 0:TILE] = q.reshape(group, TILE, HD)
            box[item, TILE : 2 * TILE] = k.reshape(group, TILE, HD)
            box[item, 2 * TILE : 3 * TILE] = vs[at, source, :].reshape(group, TILE, HD)

        in_groups(0, jnp.clip(limit - start, 0, tiles), step)
        return carry

    lax.fori_loop(0, count, one_head, 0)


def second_kernel(
    low, scal, q_ref, k_ref, v_ref, cos_ref, sin_ref, swap_ref, wt_ref, mod_ref, qr_ref, kr_ref, w_ref, shift_ref, *rest
):
    outs, box, sems = rest[:-3], rest[-2], rest[-1]
    rows = q_ref.shape[0]
    heads = q_ref.shape[1] // HD
    wide = swap_ref.shape[0]

    @pl.when(pl.program_id(0) == 0)
    def _():
        w = wt_ref[...].astype(jnp.float32)
        scaled = w * (1.0 + mod_ref[1:2, :])
        high = scaled.astype(jnp.bfloat16)
        low = (scaled - high.astype(jnp.float32)).astype(jnp.bfloat16)
        w_ref[...] = jnp.concatenate([high, low], axis=0)
        shift = jnp.sum(w * mod_ref[0:1, :], axis=1, keepdims=True)
        shift_ref[...] = jnp.broadcast_to(shift, shift_ref.shape)

    for source, to in ((q_ref, qr_ref), (k_ref, kr_ref)):
        for h in range(0, heads, wide // HD):
            for j in range(rows // BLK):
                at = slice(j * BLK, (j + 1) * BLK)
                x = source[at, h * HD : h * HD + wide]
                swapped = jnp.dot(x, swap_ref[: x.shape[1], : x.shape[1]], preferred_element_type=jnp.float32)
                for i in range(x.shape[1] // HD):
                    lanes = slice(i * HD, (i + 1) * HD)
                    to[at, (h + i) * HD : (h + i + 1) * HD] = (
                        x[:, lanes].astype(jnp.float32) * cos_ref[at, :] + swapped[:, lanes] * sin_ref[at, :]
                    ).astype(jnp.bfloat16)

    def get(rows, lanes):
        return qr_ref[rows, lanes], kr_ref[rows, lanes], v_ref[rows, lanes]

    pack(scal, low, low + box.shape[0], box, heads, get)
    send_off(box, outs, sems)


def dot_t(a, b):
    return lax.dot_general(a, b, (((1,), (1,)), ((), ())), preferred_element_type=jnp.float32)


def attend_rows(q, k, v_ones, masked):
    s = masked(dot_t(q, k))
    top = jnp.max(s, axis=1, keepdims=True)
    weight = jnp.exp2(s * SCALE2 - top * SCALE2).astype(jnp.bfloat16)
    both = jnp.dot(weight, v_ones, preferred_element_type=jnp.float32)
    return (both[:, :HD] / both[:, HD:]).astype(jnp.bfloat16)


def project_block(o_ref, w_ref, out_ref, j):
    at = slice(j * BLK, (j + 1) * BLK)
    z = dot_t(o_ref[at, :], w_ref[...])
    z = z + pltpu.roll(z, HD // 2, 1)
    lane = lax.broadcasted_iota(jnp.int32, z.shape, 1)
    squares = jnp.zeros(z.shape, jnp.float32)
    for h in range(o_ref.shape[1] // HD):
        wide = o_ref[at, h * HD : (h + 1) * HD].astype(jnp.float32)
        squares = squares + wide * wide
    total = jnp.sum(squares, axis=1, keepdims=True)
    out_ref[at, :] = jnp.where(lane < HD // 2, z, jnp.where(lane == HD // 2, total, 0.0))


def inner_kernel(scal, q_ref, k_ref, v_ref, w_ref, qv_ref, kv_ref, out_ref, o_ref):
    g = pl.program_id(0)
    rows, width = q_ref.shape
    ones = jnp.ones((rows, HD), jnp.bfloat16)
    for j in range(rows // BLK):
        holds_some = (scal[INNER_FROM] < (j + 1) * BLK) & (scal[INNER_TO] > j * BLK)

        @pl.when(holds_some)
        def _(j=j):
            at = pl.ds(j * BLK, BLK)
            same = qv_ref[at, :] == kv_ref[...]
            for i in range(width // HD):
                lanes = slice(i * HD, (i + 1) * HD)
                v_ones = jnp.concatenate([v_ref[:, lanes], ones], axis=1)
                o_ref[at, pl.ds(pl.multiple_of(g * width + i * HD, HD), HD)] = attend_rows(
                    q_ref[at, lanes], k_ref[:, lanes], v_ones, lambda s: jnp.where(same, s, NEG)
                )

        @pl.when(holds_some & (g == pl.num_programs(0) - 1))
        def _(j=j):
            project_block(o_ref, w_ref, out_ref, j)


def across(scal, at, offset, low, high, sources, items, w_ref, own_sems, places, o_ref, zz):
    rows = zz.shape[0] // 2
    left, right = scal[at + LB], scal[at + RB]
    lead = left * TILE - scal[at + LROWS]
    end = left * TILE + scal[at + RROWS]
    blocks = jnp.minimum(lax.div((left + right) * TILE + BLK - 1, BLK), rows // BLK)
    own_at = jnp.where(scal[at + SIDE] == 0, rows, 0) + left * TILE
    pairs = lax.shift_right_logical(high - low + 1, 1)

    def heads_of(i):
        return [jnp.minimum(low + 2 * i + u, high - 1) for u in range(2)]

    def own_copies(i, act):
        slot = lax.rem(i, 2)
        few = scal[at + OWN] * TILE <= rows // 2
        begin = jnp.where(scal[at + SIDE] == 0, 0, rows // 2)
        for need, begin, size in ((few, begin, rows // 2), (jnp.logical_not(few), 0, rows)):

            @pl.when(need)
            def _(begin=begin, size=size):
                source_rows = pl.ds(pl.multiple_of(begin, TILE), size)
                to = pl.ds(pl.multiple_of(own_at + begin, TILE), size)
                for u, s in enumerate(heads_of(i)):
                    lanes = lanes_of(scal[at + HEAD0] + s)
                    for x, (source, place) in enumerate(zip(sources, places)):
                        act(pltpu.make_async_copy(
                            source.at[source_rows, lanes], place.at[slot, u, to, :], own_sems.at[slot, u, x]
                        ))

    @pl.when(pairs > 0)
    def _():
        own_copies(0, lambda copy: copy.start())

    def two_heads(n, i, carry):
        slot = lax.rem(i, 2)

        @pl.when(i + 1 < pairs)
        def _():
            own_copies(i + 1, lambda copy: copy.start())

        heads = heads_of(i)

        def foreign(t, group):
            to = rows_of(rows // TILE + scal[at + FAR_TO] + t, group)
            for u, s in enumerate(heads):
                item = pl.ds(scal[at + SOURCE] + offset + s * scal[at + FAR] + t, group)
                for x, place in enumerate(places):
                    part = items[item, x * TILE : (x + 1) * TILE]
                    place[slot, u, to, :] = part.reshape(group * TILE, HD)

        in_groups(0, scal[at + FAR], foreign)
        own_copies(i, lambda copy: copy.wait())
        width = n * BLK
        if width == rows:

            @pl.when((left + right) * TILE > rows)
            def _():
                row = lax.broadcasted_iota(jnp.int32, (TILE, HD), 0)
                for place in places:
                    for u in range(2):
                        first = place[slot, u, rows : rows + TILE, :]
                        last = place[slot, u, 2 * rows : 2 * rows + TILE, :]
                        place[slot, u, rows : rows + TILE, :] = jnp.where(row < lead, last, first)

        place = lax.broadcasted_iota(jnp.int32, (1, width), 1)
        valid = ((place >= lead) & (place < end)) | (place + rows < end)
        bias = jnp.where(valid, 0.0, NEG)
        ones = jnp.ones((width, HD), jnp.bfloat16)
        qs, ks, vs = places
        whole = slice(rows, rows + width)
        for j in range(n):
            mine = slice(rows + j * BLK, rows + (j + 1) * BLK)
            for u, s in enumerate(heads):
                v_ones = jnp.concatenate([vs[slot, u, whole, :], ones], axis=1)
                o_ref[j * BLK : (j + 1) * BLK, lanes_of(scal[at + HEAD0] + s)] = attend_rows(
                    qs[slot, u, mine, :], ks[slot, u, whole, :], v_ones, lambda x: x + bias
                )
        return carry

    for n in range(1, rows // BLK + 1):

        @pl.when((blocks == n) & (pairs > 0))
        def _(n=n):
            o_ref[0 : n * BLK, :] = jnp.zeros((n * BLK, o_ref.shape[1]), o_ref.dtype)
            lax.fori_loop(0, pairs, functools.partial(two_heads, n), 0)
            for j in range(n):
                project_block(o_ref, w_ref, zz, j)
            zz[rows : 2 * rows, :] = zz[0:rows, :]

    @pl.when(pairs <= 0)
    def _():
        zz[...] = jnp.zeros_like(zz)

    return zz[pl.ds(pl.multiple_of(left * TILE, TILE), rows), :]


def fetch(scal, at, offset, low, high, places, boxes, items, sems):
    begin = scal[at + SOURCE] + offset + low * scal[at + FAR]
    end = scal[at + SOURCE] + offset + high * scal[at + FAR]
    return [
        (
            pltpu.make_async_copy(box, items.at[pl.ds(place, box.shape[0])], sems.at[i]),
            (high > low) & (begin < place + box.shape[0]) & (end > place),
        )
        for i, (place, box) in enumerate(zip(places, boxes))
    ]


def clear(places, rows):
    for place in places:
        for slot in range(2):
            for u in range(2):
                place[slot, u, rows : 2 * rows + TILE, :] = jnp.zeros((rows + TILE, HD), place.dtype)


def of_boundary(scal, at, shape, mine):
    row = lax.broadcasted_iota(jnp.int32, shape, 0)
    tail = jnp.where(row >= shape[0] - scal[at + LROWS], 1, 0)
    head = jnp.where(row < scal[at + RROWS], 1, 0)
    right_is_mine = (scal[at + SIDE] == 0) == mine
    return jnp.where(right_is_mine, head, tail) == 1


def send_back(scal, at, z, back_ref):
    lane = lax.broadcasted_iota(jnp.int32, z.shape, 1)
    back = jnp.where(of_boundary(scal, at, z.shape, False), z, 0.0)
    high = back.astype(jnp.bfloat16).astype(jnp.float32)
    both = jnp.where(lane == HD // 2 + 1, pltpu.roll(back - high, 1, 1), high)
    back_ref[...] = both.T[: back_ref.shape[0]].astype(jnp.bfloat16)


def early_kernel(places, at, since, until, scal, q_hbm, k_hbm, v_hbm, w_ref, *rest):
    boxes, (out_ref, items, sems, own_sems, qs, ks, vs, o_ref, zz) = rest[: len(places)], rest[len(places) :]
    low, high = 0 if since is None else scal[at + since], scal[at + until]
    copies = fetch(scal, at, 0, low, high, places, boxes, items, sems)
    for copy, need in copies:
        pl.when(need)(copy.start)
    clear((qs, ks, vs), zz.shape[0] // 2)
    for copy, need in copies:
        pl.when(need)(copy.wait)
    out_ref[...] = across(
        scal, at, 0, low, high, (q_hbm, k_hbm, v_hbm), items, w_ref, own_sems, (qs, ks, vs), o_ref, zz
    )


def last_kernel(places, offsets, scal, q_hbm, k_hbm, v_hbm, w_ref, *rest):
    partials, rest = rest[:5], rest[5:]
    boxes, rest = rest[: len(places)], rest[len(places) :]
    own_ref, pass_back_ref, direct_back_ref, items, sems, own_sems, qs, ks, vs, o_ref, zz, sums, sum_sems = rest
    sum_copies = [
        pltpu.make_async_copy(part, sums.at[i], sum_sems.at[i]) for i, part in enumerate(partials)
    ]
    for copy in sum_copies:
        copy.start()
    clear((qs, ks, vs), zz.shape[0] // 2)

    def remaining(at, offset):
        low, high = scal[at + EARLY], scal[at + KEEP]
        copies = fetch(scal, at, offset, low, high, places, boxes, items, sems)
        for copy, need in copies:
            pl.when(need)(copy.start)
        for copy, need in copies:
            pl.when(need)(copy.wait)
        return across(
            scal, at, offset, low, high, (q_hbm, k_hbm, v_hbm), items, w_ref, own_sems, (qs, ks, vs), o_ref, zz
        )

    passed_z = remaining(PASS, offsets[0])
    for copy in sum_copies:
        copy.wait()
    passed_z = passed_z + sums[0] + sums[4]
    send_back(scal, PASS, passed_z, pass_back_ref)
    own = jnp.where(of_boundary(scal, PASS, passed_z.shape, True), passed_z, sums[2] + sums[3])
    direct_z = sums[1] + remaining(DIRECT, offsets[1])
    send_back(scal, DIRECT, direct_z, direct_back_ref)
    own = jnp.where(of_boundary(scal, DIRECT, own.shape, True), direct_z, own)
    own_ref[...] = own.T[: own_ref.shape[0]]


def step_rows(video_ids, step_sizes):
    chosen = video_ids[:, None] == jnp.arange(step_sizes.shape[0], dtype=jnp.int32)[None, :]
    return jnp.sum(jnp.where(chosen, step_sizes[None, :], 0.0), axis=1)


def call(kernel, name, mib, scalars, operands, in_specs, outs, out_specs, scratch, grid=()):
    return pl.pallas_call(
        kernel,
        out_shape=outs,
        grid_spec=pltpu.PrefetchScalarGridSpec(
            num_scalar_prefetch=1, grid=grid, in_specs=in_specs, out_specs=out_specs,
            scratch_shapes=scratch,
        ),
        compiler_params=pltpu.CompilerParams(vmem_limit_bytes=mib * MIB),
        cost_estimate=pl.CostEstimate(flops=1, bytes_accessed=1, transcendentals=0),
        name=name,
    )(scalars, *operands)


def per_device(
    query_rows, key_rows, value_rows, positions, latents, w_head, modulation,
    guide_scale, step_sizes, lengths,
):
    rows, features = query_rows.shape[1], query_rows.shape[2]
    heads = features // HD
    count = lax.axis_size("req")
    here = lax.axis_index("req")
    first_row = here * rows
    _, padded, room = sizes(rows, heads)
    sizes_passed = pieces_of(padded)
    late_sizes = (*sizes_passed[1:], MORE, room - padded - MORE)

    angle = angles(positions)
    odd = (jnp.arange(HD, dtype=jnp.int32) % 2).astype(jnp.float32)
    cosine = jnp.cos(angle)
    sine = jnp.sin(angle) * (2.0 * odd - 1.0)[None, :]

    smem = pl.BlockSpec(memory_space=pltpu.SMEM)
    vmem = pl.BlockSpec(memory_space=pltpu.VMEM)
    hbm = pl.BlockSpec(memory_space=pl.ANY)
    parity = lax.axis_index("cfg")
    tie = lax.optimization_barrier
    scalars = pl.pallas_call(
        functools.partial(plan_kernel, rows, heads, count),
        out_shape=jax.ShapeDtypeStruct((SCALARS,), jnp.int32),
        in_specs=[smem],
        out_specs=smem,
        scratch_shapes=[
            pltpu.SMEM((count + 8,), jnp.int32),
            pltpu.SMEM((count + 8,), jnp.int32),
            pltpu.VMEM(((count + 8) * 8, 128), jnp.float32),
            pltpu.VMEM(((count + 8) * 8, 128), jnp.float32),
        ],
        name="plan",
    )(lengths)

    def in_hbm(x):
        return pltpu.with_memory_space_constraint(x, pltpu.HBM)

    q, k, v = query_rows[0], key_rows[0], value_rows[0]

    def box(items):
        return jax.ShapeDtypeStruct((items, 3 * TILE, HD), jnp.bfloat16)

    def box_scratch(items):
        return pltpu.VMEM((items, 3 * TILE, HD), jnp.bfloat16)

    group = next(n for n in (5, 4, 3, 2, 1) if heads % n == 0)
    steps = heads // group
    head_block = pl.BlockSpec((rows, group * HD), lambda g, s: (0, g))
    table = pl.BlockSpec((rows, HD), lambda g, s: (0, 0))
    first = call(
        first_kernel, "pack_first", 16, scalars, (in_hbm(q), in_hbm(k), in_hbm(v), cosine, sine),
        [hbm] * 3 + [vmem] * 2, (box(sizes_passed[0]),), (vmem,),
        [*[pltpu.VMEM((4, rows, HD), jnp.bfloat16)] * 3, pltpu.SemaphoreType.DMA((4, 3))],
    )
    pairs = [(i, i ^ 1) for i in range(count)]
    onward = [(i, i + 2) for i in range(0, count - 2, 2)] + [(i + 2, i) for i in range(1, count - 2, 2)]
    got = [lax.ppermute(first[0], "req", pairs)]

    after_first, _ = tie((scalars, first[0]))
    swap = jnp.asarray(numpy.eye(2 * HD)[numpy.arange(2 * HD) ^ 1], jnp.bfloat16)
    q_rot, k_rot, w_both, shift, *second = call(
        functools.partial(second_kernel, sizes_passed[0]), "turn_and_pack_rest", 32, after_first,
        (in_hbm(q), in_hbm(k), in_hbm(v), cosine, sine, swap, w_head.T, modulation),
        [head_block] * 3 + [table] * 2 + [vmem] * 3,
        (pltpu.HBM(q.shape, q.dtype), pltpu.HBM(k.shape, k.dtype),
         jax.ShapeDtypeStruct((HD, features), jnp.bfloat16),
         jax.ShapeDtypeStruct((HD // 2, HD), jnp.float32),
         *[box(n) for n in late_sizes], box(late_sizes[-1])),
        (head_block, head_block, vmem, vmem, *[hbm] * (len(late_sizes) + 1)),
        [box_scratch(sum(late_sizes)), pltpu.SemaphoreType.DMA((len(late_sizes),))], grid=(steps,),
    )
    got += [lax.ppermute(x, "req", pairs) for x in second[: CHUNKS - 1]]
    more, arriving = second[CHUNKS:]

    own_rows = first_row + jnp.arange(rows, dtype=jnp.int32)
    video = jnp.sum((jnp.cumsum(lengths)[None, :] <= own_rows[:, None]).astype(jnp.int32), axis=1)
    step_of_row = step_rows(video, step_sizes)

    def inner(when, first_step, step_count):
        block = pl.BlockSpec((rows, group * HD), lambda g, s: (0, g + first_step))
        width = step_count * group * HD
        return call(
            inner_kernel, "inner_videos", 20, when,
            (in_hbm(q_rot), in_hbm(k_rot), in_hbm(v), w_both, video[:, None], video[None, :]),
            [block] * 3 + [pl.BlockSpec((HD, width), lambda g, s: (0, first_step // step_count))] + [vmem] * 2, pltpu.HBM((rows, HD), jnp.float32), vmem,
            [pltpu.VMEM((rows, width), jnp.bfloat16)], grid=(step_count,),
        )

    when_a, got[0] = tie((scalars, got[0]))
    inner_a = inner(when_a, 0, steps // 2)
    got[1], inner_a = tie((got[1], inner_a))
    passed = [lax.ppermute(x, "req", onward) for x in got[:2]]
    got[1], second[CHUNKS - 1], inner_a = tie((got[1], second[CHUNKS - 1], inner_a))
    got.append(lax.ppermute(second[CHUNKS - 1], "req", pairs))
    when_b, passed[0], got[2], inner_a = tie((scalars, passed[0], got[2], inner_a))
    inner_b = inner(when_b, steps // 2, steps - steps // 2)
    when_soon, inner_b = tie((scalars, inner_b))

    place = pltpu.VMEM((2, 2, 3 * rows, HD), jnp.bfloat16)
    work = [
        pltpu.SemaphoreType.DMA((2, 2, 3)), place, place, place,
        pltpu.VMEM((rows, features), jnp.bfloat16),
        pltpu.VMEM((2 * rows, HD), jnp.float32),
    ]
    partial = pltpu.HBM((rows, HD), jnp.float32)
    lanes = HD // 2 + TILE
    sent_back = jax.ShapeDtypeStruct((lanes, rows), jnp.bfloat16)

    def on_videos_across(kernel, name, when, boxes, outs, others=(), scratch=()):
        places = [0]
        for x in boxes:
            places.append(places[-1] + x.shape[0])
        return call(
            kernel(tuple(places[:-1])), name, 32, when,
            (in_hbm(q_rot), in_hbm(k_rot), in_hbm(v), w_both, *[in_hbm(x) for x in others], *boxes),
            [hbm] * 3 + [vmem] + [hbm] * (len(others) + len(boxes)),
            outs, jax.tree.map(lambda _: vmem, outs),
            [box_scratch(places[-1]), pltpu.SemaphoreType.DMA((len(boxes),)), *work, *scratch],
        )

    def early_on(at, since, until, name, when, boxes):
        return on_videos_across(
            lambda places: functools.partial(early_kernel, places, at, since, until), name, when, boxes,
            partial,
        )

    soon = early_on(PASS, None, SOON, "videos_across_soon", when_soon, passed[:1])
    got[3], soon = tie((got[3], soon))
    when_early, got[3] = tie((scalars, got[3]))
    passed += [lax.ppermute(x, "req", onward) for x in got[2:CHUNKS]]
    early = early_on(PASS, SOON, EARLY, "videos_across_early", when_early, passed[:EARLY_CHUNKS])
    when_direct, early, passed[2] = tie((scalars, early, passed[2]))
    direct_z = early_on(DIRECT, None, EARLY, "videos_across_direct", when_direct, got[:CHUNKS])

    pieces = jnp.maximum(scalars[MOST] - padded - MORE + EXTRA - 1, 0) // EXTRA
    pieces, direct_z = tie((pieces, direct_z))

    def one_more(i, arrived):
        piece = lax.dynamic_slice_in_dim(more, i * EXTRA, EXTRA, 0)
        piece = lax.ppermute(piece, "req", pairs)
        return lax.dynamic_update_slice_in_dim(arrived, piece, i * EXTRA, 0)

    arrived = lax.fori_loop(0, pieces, one_more, arriving)
    before = EARLY_CHUNKS - 1
    offsets = (-sum(sizes_passed[:before]), sum(sizes_passed[before:]))
    own, to_beyond, to_direct = on_videos_across(
        lambda places: functools.partial(last_kernel, places, offsets), "videos_across_last", scalars,
        [*passed[before:], *got, arrived],
        (jax.ShapeDtypeStruct((lanes, rows), jnp.float32), sent_back, sent_back),
        (early, direct_z, inner_a, inner_b, soon),
        (pltpu.VMEM((5, rows, HD), jnp.float32), pltpu.SemaphoreType.DMA((5,))),
    )
    back_direct = lax.ppermute(to_direct, "req", pairs)
    beyond = [(i, i + 1) for i in range(1, count - 1, 2)] + [(i + 1, i) for i in range(1, count - 1, 2)]
    back_beyond = lax.ppermute(to_beyond, "req", beyond)
    total = own + back_direct.astype(jnp.float32) + back_beyond.astype(jnp.float32)
    values = HD // 2
    squares = total[values : values + 1] + total[values + 1 : values + 2]
    velocity = total[:values] * lax.rsqrt(squares / features + 1e-06) + shift[:, :1]

    width = latents.shape[1]
    mine = lax.dynamic_slice_in_dim(velocity, parity * width, width, 0)
    theirs = lax.dynamic_slice_in_dim(velocity, (1 - parity) * width, width, 0)
    partner = lax.ppermute(theirs, "cfg", [(0, 1), (1, 0)])
    conditional = jnp.where(parity == 0, mine, partner)
    unconditional = jnp.where(parity == 0, partner, mine)
    guided = unconditional + guide_scale[0] * (conditional - unconditional)
    return (latents.T + step_of_row[None, :] * guided).T


def solution(mesh):
    in_specs = (
        P("cfg", "req", None), P("cfg", "req", None), P("cfg", "req", None),
        P(None, "req"), P("req", "cfg"), P(), P(), P(), P(), P(),
    )
    return jax.shard_map(
        per_device, mesh=mesh, in_specs=in_specs, out_specs=P("req", "cfg"), check_vma=False
    )
```

```python
import functools
import math

import jax
import jax.numpy as jnp
import numpy
from jax import lax
from jax.experimental import pallas as pl
from jax.experimental.pallas import tpu as pltpu
from jax.sharding import PartitionSpec as P

HD = 128
TILE = 16
BLK = 128
CHUNKS = 4
MORE = 48
EXTRA = 16
EARLY_CHUNKS = 2
rope_theta = 10000.0
NEG = -1e30
SCALE2 = math.log2(math.e) / math.sqrt(HD)

PASS, DIRECT = 0, 16
LB, RB, LROWS, RROWS, HEAD0, KEEP, EARLY, SOURCE = range(8)
OWN_FROM, OWN_TO, OWN, FAR_TO, FAR, SIDE = range(8, 14)
SEND = 32
ROW, TILES, FIRST, HEADS = range(4)
MOST, INNER_FROM, INNER_TO = 40, 41, 42
SCALARS = 48
MIB = 1024 * 1024


def sizes(rows, heads):
    tiles = rows // TILE
    cap = max(
        min(max(a * n, (tiles + 1 - a) * (heads - n)) for n in range(heads + 1))
        for a in range(1, tiles + 1)
    )
    padded = -(-cap // TILE) * TILE
    return cap, padded, 2 * padded


def angles(positions):
    pair_total = HD // 2
    side_pairs = HD // 6
    time_pairs = pair_total - 2 * side_pairs
    column = jnp.arange(HD, dtype=jnp.int32) // 2
    in_time = column < time_pairs
    in_height = (column >= time_pairs) & (column < time_pairs + side_pairs)
    in_width = column >= time_pairs + side_pairs
    local_index = jnp.where(
        in_time, column, jnp.where(in_height, column - time_pairs, column - time_pairs - side_pairs)
    )
    axis_pairs = jnp.where(in_time, time_pairs, side_pairs)
    frequency = jnp.exp(
        -(local_index.astype(jnp.float32) / axis_pairs.astype(jnp.float32)) * math.log(rope_theta)
    )
    selector = jnp.stack([in_time, in_height, in_width]).astype(jnp.float32) * frequency[None, :]
    placed = positions.astype(jnp.float32)
    return (
        placed[0][:, None] * selector[0][None, :]
        + placed[1][:, None] * selector[1][None, :]
        + placed[2][:, None] * selector[2][None, :]
    )


def plan_kernel(rows, heads, count, lengths, out, ls, rs, split, least):
    cap, padded, _ = sizes(rows, heads)
    here = lax.axis_index("req")
    shift = rows.bit_length() - 1

    def clear(b, carry):
        ls[b] = 0
        rs[b] = 0
        return carry

    lax.fori_loop(0, count + 8, clear, 0)

    def one_video(v, start):
        end = start + lengths[v]
        b = lax.shift_right_logical(end - 1, shift) if rows == 1 << shift else lax.div(end - 1, rows)
        at = b * rows

        @pl.when(start < at)
        def _():
            ls[b] = at - start
            rs[b] = end - at

        return end

    lax.fori_loop(0, lengths.shape[0], one_video, 0)
    budget = 3.0 * lax.broadcasted_iota(jnp.int32, (8, 128), 1).astype(jnp.float32)
    split[...] = jnp.zeros_like(split)

    def tiles_of(x):
        return lax.shift_right_logical(x + TILE - 1, 4)

    def eight(b):
        return pl.ds(pl.multiple_of(b * 8, 8), 8)

    def per_tile(x, tiles):
        return jnp.floor((x + 0.5) * (1.0 / jnp.maximum(tiles, 1.0)))

    def facts(b):
        direct = lax.rem(b, 2).astype(jnp.float32)
        lt, rt = (jnp.full((8, 128), tiles_of(x[b]).astype(jnp.float32)) for x in (ls, rs))
        return lt, rt, padded + direct * 1e6

    def five_at_a_time(step, carry):
        def body(i, carry):
            for u in range(5):
                carry = step(5 * i + u, carry)
            return carry

        return lax.fori_loop(0, -(-(count - 1) // 5), body, carry)

    def from_right(i, load):
        b = -(-(count - 1) // 5) * 5 - i
        lt, rt, limit = facts(b)
        room = jnp.minimum(budget - load, limit)
        n = jnp.where(rt > 0.0, jnp.maximum(heads - per_tile(room, rt), 0.0), 0.0)
        least[eight(b)] = jnp.where(room >= 0.0, n, 1e6)
        return lt * n

    def from_left(i, carry):
        load, ok = carry
        b = i + 1
        lt, rt, limit = facts(b)
        room = jnp.minimum(budget - load, limit)
        most = jnp.where(lt > 0.0, jnp.minimum(per_tile(room, lt), float(heads)), 0.0)
        low = least[eight(b)]
        even = jnp.floor(heads * rt / jnp.maximum(lt + rt, 1.0) + 0.5)
        n = jnp.minimum(most, jnp.maximum(low, even))
        split[eight(b)] = n
        return rt * (heads - n), jnp.where((room >= 0.0) & (low <= most), ok, 0.0)

    zero = jnp.zeros((8, 128), jnp.float32)
    five_at_a_time(from_right, zero)
    load, ok = five_at_a_time(from_left, (zero, zero + 1.0))
    ok = jnp.where(load <= budget, ok, 0.0)
    most = jnp.min(jnp.where((ok > 0.0) & (budget >= (padded + MORE) // 3 * 3), budget, 1e9))
    out[MOST] = most.astype(jnp.int32)

    def head_split(b):
        n = split[eight(b)]
        return jnp.max(jnp.where(budget == most, n, 0.0)).astype(jnp.int32)

    even = lax.rem(here, 2) == 0
    beyond = jnp.where(even, here + 2, here - 1)
    n_left, n_right, n_beyond = head_split(here), head_split(here + 1), head_split(beyond)
    partner_passes = jnp.where(
        even,
        tiles_of(ls[beyond]) * n_beyond,
        tiles_of(rs[beyond]) * (heads - n_beyond),
    )
    for side, b, n in ((0, here, n_left), (1, here + 1, n_right)):
        direct = jnp.logical_not(even) if side == 0 else even
        at = jnp.where(direct, DIRECT, PASS)
        lt, rt = tiles_of(ls[b]), tiles_of(rs[b])
        none = jnp.where(lt > 0, 0, heads)
        keep = n if side == 0 else jnp.maximum(heads - n - none, 0)
        far = lt if side == 0 else rt
        out[at + LB], out[at + RB] = lt, rt
        out[at + LROWS], out[at + RROWS] = ls[b], rs[b]
        out[at + HEAD0] = 0 if side == 0 else n
        out[at + KEEP] = keep
        source = jnp.where(direct, partner_passes, 0)
        there = jnp.where(direct, padded + MORE, padded // CHUNKS * EARLY_CHUNKS) - source
        out[at + EARLY] = jnp.minimum(keep, lax.div(jnp.maximum(there, 0), jnp.maximum(far, 1)))
        out[at + SOURCE] = source
        out[at + OWN_FROM] = 0 if side == 0 else rows // TILE - lt
        out[at + OWN_TO] = lt if side == 0 else 0
        out[at + OWN] = rt if side == 0 else lt
        out[at + FAR_TO] = 0 if side == 0 else lt
        out[at + FAR] = far
        out[at + SIDE] = side
        to = SEND + jnp.where(direct, 4, 0)
        out[to + ROW] = 0 if side == 0 else rows - TILE * lt
        out[to + TILES] = rt if side == 0 else lt
        out[to + FIRST] = n if side == 0 else 0
        out[to + HEADS] = jnp.maximum(heads - n - none, 0) if side == 0 else n
    out[INNER_FROM] = rs[here]
    out[INNER_TO] = rows - ls[here + 1]


def in_groups(low, high, step):
    count = high - low

    def run(group, times):
        def body(i, carry):
            step(jnp.minimum(low + group * i, high - group), group)
            return carry

        lax.fori_loop(0, times, body, 0)

    run(8, jnp.where(count >= 8, lax.shift_right_logical(count + 7, 3), 0))
    run(2, jnp.where((count >= 2) & (count < 8), lax.shift_right_logical(count + 1, 1), 0))
    run(1, jnp.where(count == 1, 1, 0))


def lanes_of(h):
    return pl.ds(pl.multiple_of(h * HD, HD), HD)


def rows_of(t, group):
    return pl.ds(pl.multiple_of(t * TILE, TILE), group * TILE)


def turn(x, cosine, sine):
    wide = x.astype(jnp.float32)
    even = lax.rem(lax.broadcasted_iota(jnp.int32, wide.shape, 1), 2) == 0
    swapped = jnp.where(even, pltpu.roll(wide, HD - 1, 1), pltpu.roll(wide, 1, 1))
    return (wide * cosine + swapped * sine).astype(jnp.bfloat16)


def pack(scal, low, high, box, heads, get):
    base = 0
    for what in (SEND, SEND + 4):
        first_tile = lax.shift_right_logical(scal[what + ROW], 4)
        tiles, first, count = scal[what + TILES], scal[what + FIRST], scal[what + HEADS]

        def one_head(i, carry):
            start = base + (pl.program_id(0) * heads + i - first) * tiles
            begin = jnp.clip(low - start, 0, tiles)
            end = jnp.clip(high - start, 0, tiles)
            lanes = lanes_of(i)

            def step(t, group):
                q, k, v = get(rows_of(first_tile + t, group), lanes)
                item = pl.ds(start + t - low, group)
                box[item, 0:TILE] = q.reshape(group, TILE, HD)
                box[item, TILE : 2 * TILE] = k.reshape(group, TILE, HD)
                box[item, 2 * TILE : 3 * TILE] = v.reshape(group, TILE, HD)

            in_groups(begin, end, step)
            return carry

        before = first - pl.program_id(0) * heads
        lax.fori_loop(
            jnp.clip(before, 0, heads), jnp.clip(before + count, 0, heads), one_head, 0
        )
        base = base + tiles * count


def send_off(box, outs, sems):
    @pl.when(pl.program_id(0) == pl.num_programs(0) - 1)
    def _():
        at, copies = 0, []
        for i, out in enumerate(outs):
            copies.append(pltpu.make_async_copy(box.at[pl.ds(at, out.shape[0])], out, sems.at[i]))
            at += out.shape[0]
        for copy in copies:
            copy.start()
        for copy in copies:
            copy.wait()


def first_kernel(scal, q_hbm, k_hbm, v_hbm, cos_ref, sin_ref, box, qs, ks, vs, sems):
    limit = box.shape[0]
    ahead = qs.shape[0] - 1

    def heads_in(what, base):
        tiles = jnp.maximum(scal[what + TILES], 1)
        taken = lax.div(jnp.maximum(limit - base, 0) + tiles - 1, tiles)
        return jnp.minimum(scal[what + HEADS], taken)

    passed = scal[SEND + TILES] * scal[SEND + HEADS]
    count_pass = heads_in(SEND, 0)
    count = count_pass + heads_in(SEND + 4, passed)

    def entry(w):
        direct = w >= count_pass
        what = jnp.where(direct, SEND + 4, SEND)
        slot = w - jnp.where(direct, count_pass, 0)
        tiles = scal[what + TILES]
        start = jnp.where(direct, passed, 0) + slot * tiles
        return scal[what + FIRST] + slot, scal[what + ROW], tiles, start

    rows = cos_ref.shape[0]

    def each_copy(w, act):
        at = lax.rem(w, ahead + 1)
        head, row, tiles, _ = entry(w)
        few = tiles * TILE <= BLK
        block = pl.ds(pl.multiple_of(jnp.minimum(row, rows - BLK), TILE), BLK)
        for need, some in ((few, block), (jnp.logical_not(few), pl.ds(0, rows))):

            @pl.when(need)
            def _(some=some):
                for x, (source, place) in enumerate(((q_hbm, qs), (k_hbm, ks), (v_hbm, vs))):
                    act(pltpu.make_async_copy(
                        source.at[some, lanes_of(head)], place.at[at, some, :], sems.at[at, x]
                    ))

    for w in range(ahead):

        @pl.when(w < count)
        def _(w=w):
            each_copy(w, lambda copy: copy.start())

    def one_head(w, carry):
        @pl.when(w + ahead < count)
        def _():
            each_copy(w + ahead, lambda copy: copy.start())

        each_copy(w, lambda copy: copy.wait())
        at = lax.rem(w, ahead + 1)
        _, row, tiles, start = entry(w)
        first_tile = lax.shift_right_logical(row, 4)

        def step(t, group):
            source = rows_of(first_tile + t, group)
            cosine, sine = cos_ref[source, :], sin_ref[source, :]
            item = pl.ds(start + t, group)
            q, k = turn(qs[at, source, :], cosine, sine), turn(ks[at, source, :], cosine, sine)
            box[item, 0:TILE] = q.reshape(group, TILE, HD)
            box[item, TILE : 2 * TILE] = k.reshape(group, TILE, HD)
            box[item, 2 * TILE : 3 * TILE] = vs[at, source, :].reshape(group, TILE, HD)

        in_groups(0, jnp.clip(limit - start, 0, tiles), step)
        return carry

    lax.fori_loop(0, count, one_head, 0)


def second_kernel(
    low, scal, q_ref, k_ref, v_ref, cos_ref, sin_ref, swap_ref, wt_ref, mod_ref, qr_ref, kr_ref, w_ref, shift_ref, *rest
):
    outs, box, sems = rest[:-3], rest[-2], rest[-1]
    rows = q_ref.shape[0]
    heads = q_ref.shape[1] // HD
    wide = swap_ref.shape[0]

    @pl.when(pl.program_id(0) == 0)
    def _():
        w = wt_ref[...].astype(jnp.float32)
        scaled = w * (1.0 + mod_ref[1:2, :])
        high = scaled.astype(jnp.bfloat16)
        low = (scaled - high.astype(jnp.float32)).astype(jnp.bfloat16)
        w_ref[...] = jnp.concatenate([high, low], axis=0)
        shift = jnp.sum(w * mod_ref[0:1, :], axis=1, keepdims=True)
        shift_ref[...] = jnp.broadcast_to(shift, shift_ref.shape)

    for source, to in ((q_ref, qr_ref), (k_ref, kr_ref)):
        for h in range(0, heads, wide // HD):
            for j in range(rows // BLK):
                at = slice(j * BLK, (j + 1) * BLK)
                x = source[at, h * HD : h * HD + wide]
                swapped = jnp.dot(x, swap_ref[: x.shape[1], : x.shape[1]], preferred_element_type=jnp.float32)
                for i in range(x.shape[1] // HD):
                    lanes = slice(i * HD, (i + 1) * HD)
                    to[at, (h + i) * HD : (h + i + 1) * HD] = (
                        x[:, lanes].astype(jnp.float32) * cos_ref[at, :] + swapped[:, lanes] * sin_ref[at, :]
                    ).astype(jnp.bfloat16)

    def get(rows, lanes):
        return qr_ref[rows, lanes], kr_ref[rows, lanes], v_ref[rows, lanes]

    pack(scal, low, low + box.shape[0], box, heads, get)
    send_off(box, outs, sems)


def dot_t(a, b):
    return lax.dot_general(a, b, (((1,), (1,)), ((), ())), preferred_element_type=jnp.float32)


def attend_rows(q, k, v_ones, masked):
    s = masked(dot_t(q, k))
    top = jnp.max(s, axis=1, keepdims=True)
    weight = jnp.exp2(s * SCALE2 - top * SCALE2).astype(jnp.bfloat16)
    both = jnp.dot(weight, v_ones, preferred_element_type=jnp.float32)
    return (both[:, :HD] / both[:, HD:]).astype(jnp.bfloat16)


def projected(o_ref, w_ref, out_ref, rows):
    for j in range(rows // BLK):
        at = slice(j * BLK, (j + 1) * BLK)
        z = dot_t(o_ref[at, :], w_ref[...])
        z = z + pltpu.roll(z, HD // 2, 1)
        lane = lax.broadcasted_iota(jnp.int32, z.shape, 1)
        squares = jnp.zeros(z.shape, jnp.float32)
        for h in range(o_ref.shape[1] // HD):
            wide = o_ref[at, h * HD : (h + 1) * HD].astype(jnp.float32)
            squares = squares + wide * wide
        total = jnp.sum(squares, axis=1, keepdims=True)
        out_ref[at, :] = jnp.where(lane < HD // 2, z, jnp.where(lane == HD // 2, total, 0.0))


def inner_kernel(scal, q_ref, k_ref, v_ref, w_ref, qv_ref, kv_ref, out_ref, o_ref):
    g = pl.program_id(0)
    rows, width = q_ref.shape
    ones = jnp.ones((rows, HD), jnp.bfloat16)
    for j in range(rows // BLK):
        at = pl.ds(j * BLK, BLK)
        same = qv_ref[at, :] == kv_ref[...]
        for i in range(width // HD):
            lanes = slice(i * HD, (i + 1) * HD)
            v_ones = jnp.concatenate([v_ref[:, lanes], ones], axis=1)
            o_ref[at, pl.ds(pl.multiple_of(g * width + i * HD, HD), HD)] = attend_rows(
                q_ref[at, lanes], k_ref[:, lanes], v_ones, lambda s: jnp.where(same, s, NEG)
            )

    @pl.when(g == pl.num_programs(0) - 1)
    def _():
        projected(o_ref, w_ref, out_ref, rows)


def across(scal, at, offset, low, high, sources, items, w_ref, own_sems, places, o_ref, zz):
    rows = zz.shape[0] // 2
    left, right = scal[at + LB], scal[at + RB]
    lead = left * TILE - scal[at + LROWS]
    end = left * TILE + scal[at + RROWS]
    blocks = jnp.minimum(lax.div((left + right) * TILE + BLK - 1, BLK), rows // BLK)
    own_at = jnp.where(scal[at + SIDE] == 0, rows, 0) + left * TILE
    pairs = lax.shift_right_logical(high - low + 1, 1)

    def heads_of(i):
        return [jnp.minimum(low + 2 * i + u, high - 1) for u in range(2)]

    def own_copies(i, act):
        slot = lax.rem(i, 2)
        few = scal[at + OWN] * TILE <= rows // 2
        begin = jnp.where(scal[at + SIDE] == 0, 0, rows // 2)
        for need, begin, size in ((few, begin, rows // 2), (jnp.logical_not(few), 0, rows)):

            @pl.when(need)
            def _(begin=begin, size=size):
                source_rows = pl.ds(pl.multiple_of(begin, TILE), size)
                to = pl.ds(pl.multiple_of(own_at + begin, TILE), size)
                for u, s in enumerate(heads_of(i)):
                    lanes = lanes_of(scal[at + HEAD0] + s)
                    for x, (source, place) in enumerate(zip(sources, places)):
                        act(pltpu.make_async_copy(
                            source.at[source_rows, lanes], place.at[slot, u, to, :], own_sems.at[slot, u, x]
                        ))

    @pl.when(pairs > 0)
    def _():
        own_copies(0, lambda copy: copy.start())

    def two_heads(n, i, carry):
        slot = lax.rem(i, 2)

        @pl.when(i + 1 < pairs)
        def _():
            own_copies(i + 1, lambda copy: copy.start())

        heads = heads_of(i)

        def foreign(t, group):
            to = rows_of(rows // TILE + scal[at + FAR_TO] + t, group)
            for u, s in enumerate(heads):
                item = pl.ds(scal[at + SOURCE] + offset + s * scal[at + FAR] + t, group)
                for x, place in enumerate(places):
                    part = items[item, x * TILE : (x + 1) * TILE]
                    place[slot, u, to, :] = part.reshape(group * TILE, HD)

        in_groups(0, scal[at + FAR], foreign)
        own_copies(i, lambda copy: copy.wait())
        width = n * BLK
        if width == rows:

            @pl.when((left + right) * TILE > rows)
            def _():
                row = lax.broadcasted_iota(jnp.int32, (TILE, HD), 0)
                for place in places:
                    for u in range(2):
                        first = place[slot, u, rows : rows + TILE, :]
                        last = place[slot, u, 2 * rows : 2 * rows + TILE, :]
                        place[slot, u, rows : rows + TILE, :] = jnp.where(row < lead, last, first)

        place = lax.broadcasted_iota(jnp.int32, (1, width), 1)
        valid = ((place >= lead) & (place < end)) | (place + rows < end)
        bias = jnp.where(valid, 0.0, NEG)
        ones = jnp.ones((width, HD), jnp.bfloat16)
        qs, ks, vs = places
        whole = slice(rows, rows + width)
        for j in range(n):
            mine = slice(rows + j * BLK, rows + (j + 1) * BLK)
            for u, s in enumerate(heads):
                v_ones = jnp.concatenate([vs[slot, u, whole, :], ones], axis=1)
                o_ref[j * BLK : (j + 1) * BLK, lanes_of(scal[at + HEAD0] + s)] = attend_rows(
                    qs[slot, u, mine, :], ks[slot, u, whole, :], v_ones, lambda x: x + bias
                )
        return carry

    for n in range(1, rows // BLK + 1):

        @pl.when((blocks == n) & (pairs > 0))
        def _(n=n):
            o_ref[0 : n * BLK, :] = jnp.zeros((n * BLK, o_ref.shape[1]), o_ref.dtype)
            lax.fori_loop(0, pairs, functools.partial(two_heads, n), 0)
            projected(o_ref, w_ref, zz, n * BLK)
            zz[rows : 2 * rows, :] = zz[0:rows, :]

    @pl.when(pairs <= 0)
    def _():
        zz[...] = jnp.zeros_like(zz)

    return zz[pl.ds(pl.multiple_of(left * TILE, TILE), rows), :]


def fetch(scal, at, offset, low, high, places, boxes, items, sems):
    begin = scal[at + SOURCE] + offset + low * scal[at + FAR]
    end = scal[at + SOURCE] + offset + high * scal[at + FAR]
    return [
        (
            pltpu.make_async_copy(box, items.at[pl.ds(place, box.shape[0])], sems.at[i]),
            (high > low) & (begin < place + box.shape[0]) & (end > place),
        )
        for i, (place, box) in enumerate(zip(places, boxes))
    ]


def clear(places, rows):
    for place in places:
        for slot in range(2):
            for u in range(2):
                place[slot, u, rows : 2 * rows + TILE, :] = jnp.zeros((rows + TILE, HD), place.dtype)


def of_boundary(scal, at, shape, mine):
    row = lax.broadcasted_iota(jnp.int32, shape, 0)
    tail = jnp.where(row >= shape[0] - scal[at + LROWS], 1, 0)
    head = jnp.where(row < scal[at + RROWS], 1, 0)
    right_is_mine = (scal[at + SIDE] == 0) == mine
    return jnp.where(right_is_mine, head, tail) == 1


def send_back(scal, at, z, back_ref):
    lane = lax.broadcasted_iota(jnp.int32, z.shape, 1)
    back = jnp.where(of_boundary(scal, at, z.shape, False), z, 0.0)
    high = back.astype(jnp.bfloat16).astype(jnp.float32)
    both = jnp.where(lane == HD // 2 + 1, pltpu.roll(back - high, 1, 1), high)
    back_ref[...] = both.T[: back_ref.shape[0]].astype(jnp.bfloat16)


def early_kernel(places, at, scal, q_hbm, k_hbm, v_hbm, w_ref, *rest):
    boxes, (out_ref, items, sems, own_sems, qs, ks, vs, o_ref, zz) = rest[: len(places)], rest[len(places) :]
    high = scal[at + EARLY]
    copies = fetch(scal, at, 0, 0, high, places, boxes, items, sems)
    for copy, need in copies:
        pl.when(need)(copy.start)
    clear((qs, ks, vs), zz.shape[0] // 2)
    for copy, need in copies:
        pl.when(need)(copy.wait)
    out_ref[...] = across(
        scal, at, 0, 0, high, (q_hbm, k_hbm, v_hbm), items, w_ref, own_sems, (qs, ks, vs), o_ref, zz
    )


def last_kernel(places, offsets, scal, q_hbm, k_hbm, v_hbm, w_ref, *rest):
    partials, rest = rest[:4], rest[4:]
    boxes, rest = rest[: len(places)], rest[len(places) :]
    own_ref, pass_back_ref, direct_back_ref, items, sems, own_sems, qs, ks, vs, o_ref, zz, sums, sum_sems = rest
    sum_copies = [
        pltpu.make_async_copy(part, sums.at[i], sum_sems.at[i]) for i, part in enumerate(partials)
    ]
    for copy in sum_copies:
        copy.start()
    clear((qs, ks, vs), zz.shape[0] // 2)

    def remaining(at, offset):
        low, high = scal[at + EARLY], scal[at + KEEP]
        copies = fetch(scal, at, offset, low, high, places, boxes, items, sems)
        for copy, need in copies:
            pl.when(need)(copy.start)
        for copy, need in copies:
            pl.when(need)(copy.wait)
        return across(
            scal, at, offset, low, high, (q_hbm, k_hbm, v_hbm), items, w_ref, own_sems, (qs, ks, vs), o_ref, zz
        )

    passed_z = remaining(PASS, offsets[0])
    for copy in sum_copies:
        copy.wait()
    passed_z = passed_z + sums[0]
    send_back(scal, PASS, passed_z, pass_back_ref)
    own = jnp.where(of_boundary(scal, PASS, passed_z.shape, True), passed_z, sums[2] + sums[3])
    direct_z = sums[1] + remaining(DIRECT, offsets[1])
    send_back(scal, DIRECT, direct_z, direct_back_ref)
    own = jnp.where(of_boundary(scal, DIRECT, own.shape, True), direct_z, own)
    own_ref[...] = own.T[: own_ref.shape[0]]


def step_rows(video_ids, step_sizes):
    chosen = video_ids[:, None] == jnp.arange(step_sizes.shape[0], dtype=jnp.int32)[None, :]
    return jnp.sum(jnp.where(chosen, step_sizes[None, :], 0.0), axis=1)


def call(kernel, name, mib, scalars, operands, in_specs, outs, out_specs, scratch, grid=()):
    return pl.pallas_call(
        kernel,
        out_shape=outs,
        grid_spec=pltpu.PrefetchScalarGridSpec(
            num_scalar_prefetch=1, grid=grid, in_specs=in_specs, out_specs=out_specs,
            scratch_shapes=scratch,
        ),
        compiler_params=pltpu.CompilerParams(vmem_limit_bytes=mib * MIB),
        cost_estimate=pl.CostEstimate(flops=1, bytes_accessed=1, transcendentals=0),
        name=name,
    )(scalars, *operands)


def per_device(
    query_rows, key_rows, value_rows, positions, latents, w_head, modulation,
    guide_scale, step_sizes, lengths,
):
    rows, features = query_rows.shape[1], query_rows.shape[2]
    heads = features // HD
    count = lax.axis_size("req")
    here = lax.axis_index("req")
    first_row = here * rows
    _, padded, room = sizes(rows, heads)
    chunk = padded // CHUNKS
    late_sizes = (*[chunk] * (CHUNKS - 1), MORE, room - padded - MORE)

    angle = angles(positions)
    odd = (jnp.arange(HD, dtype=jnp.int32) % 2).astype(jnp.float32)
    cosine = jnp.cos(angle)
    sine = jnp.sin(angle) * (2.0 * odd - 1.0)[None, :]

    smem = pl.BlockSpec(memory_space=pltpu.SMEM)
    vmem = pl.BlockSpec(memory_space=pltpu.VMEM)
    hbm = pl.BlockSpec(memory_space=pl.ANY)
    parity = lax.axis_index("cfg")
    tie = lax.optimization_barrier
    scalars = pl.pallas_call(
        functools.partial(plan_kernel, rows, heads, count),
        out_shape=jax.ShapeDtypeStruct((SCALARS,), jnp.int32),
        in_specs=[smem],
        out_specs=smem,
        scratch_shapes=[
            pltpu.SMEM((count + 8,), jnp.int32),
            pltpu.SMEM((count + 8,), jnp.int32),
            pltpu.VMEM(((count + 8) * 8, 128), jnp.float32),
            pltpu.VMEM(((count + 8) * 8, 128), jnp.float32),
        ],
        name="plan",
    )(lengths)

    def in_hbm(x):
        return pltpu.with_memory_space_constraint(x, pltpu.HBM)

    q, k, v = query_rows[0], key_rows[0], value_rows[0]

    def box(items):
        return jax.ShapeDtypeStruct((items, 3 * TILE, HD), jnp.bfloat16)

    def box_scratch(items):
        return pltpu.VMEM((items, 3 * TILE, HD), jnp.bfloat16)

    group = next(n for n in (5, 4, 3, 2, 1) if heads % n == 0)
    steps = heads // group
    head_block = pl.BlockSpec((rows, group * HD), lambda g, s: (0, g))
    table = pl.BlockSpec((rows, HD), lambda g, s: (0, 0))
    first = call(
        first_kernel, "pack_first", 16, scalars, (in_hbm(q), in_hbm(k), in_hbm(v), cosine, sine),
        [hbm] * 3 + [vmem] * 2, (box(chunk),), (vmem,),
        [*[pltpu.VMEM((4, rows, HD), jnp.bfloat16)] * 3, pltpu.SemaphoreType.DMA((4, 3))],
    )
    pairs = [(i, i ^ 1) for i in range(count)]
    onward = [(i, i + 2) for i in range(0, count - 2, 2)] + [(i + 2, i) for i in range(1, count - 2, 2)]
    got = [lax.ppermute(first[0], "req", pairs)]

    after_first, _ = tie((scalars, first[0]))
    swap = jnp.asarray(numpy.eye(2 * HD)[numpy.arange(2 * HD) ^ 1], jnp.bfloat16)
    q_rot, k_rot, w_both, shift, *second = call(
        functools.partial(second_kernel, chunk), "turn_and_pack_rest", 32, after_first,
        (in_hbm(q), in_hbm(k), in_hbm(v), cosine, sine, swap, w_head.T, modulation),
        [head_block] * 3 + [table] * 2 + [vmem] * 3,
        (pltpu.HBM(q.shape, q.dtype), pltpu.HBM(k.shape, k.dtype),
         jax.ShapeDtypeStruct((HD, features), jnp.bfloat16),
         jax.ShapeDtypeStruct((HD // 2, HD), jnp.float32),
         *[box(n) for n in late_sizes], box(late_sizes[-1])),
        (head_block, head_block, vmem, vmem, *[hbm] * (len(late_sizes) + 1)),
        [box_scratch(sum(late_sizes)), pltpu.SemaphoreType.DMA((len(late_sizes),))], grid=(steps,),
    )
    got += [lax.ppermute(x, "req", pairs) for x in second[: CHUNKS - 1]]
    more, arriving = second[CHUNKS:]

    own_rows = first_row + jnp.arange(rows, dtype=jnp.int32)
    video = jnp.sum((jnp.cumsum(lengths)[None, :] <= own_rows[:, None]).astype(jnp.int32), axis=1)
    step_of_row = step_rows(video, step_sizes)

    def inner(when, first_step, step_count):
        block = pl.BlockSpec((rows, group * HD), lambda g, s: (0, g + first_step))
        width = step_count * group * HD
        return call(
            inner_kernel, "inner_videos", 20, when,
            (in_hbm(q_rot), in_hbm(k_rot), in_hbm(v), w_both, video[:, None], video[None, :]),
            [block] * 3 + [pl.BlockSpec((HD, width), lambda g, s: (0, first_step // step_count))] + [vmem] * 2, pltpu.HBM((rows, HD), jnp.float32), vmem,
            [pltpu.VMEM((rows, width), jnp.bfloat16)], grid=(step_count,),
        )

    got[1], second[CHUNKS - 1] = tie((got[1], second[CHUNKS - 1]))
    got.append(lax.ppermute(second[CHUNKS - 1], "req", pairs))
    when_a, got[0] = tie((scalars, got[0]))
    inner_a = inner(when_a, 0, steps // 2)
    got[1], inner_a = tie((got[1], inner_a))
    passed = [lax.ppermute(x, "req", onward) for x in got[:2]]
    when_b, passed[0], got[2], inner_a = tie((scalars, passed[0], got[2], inner_a))
    inner_b = inner(when_b, steps // 2, steps - steps // 2)
    got[3], inner_b = tie((got[3], inner_b))
    when_early, got[3] = tie((scalars, got[3]))
    passed += [lax.ppermute(x, "req", onward) for x in got[2:CHUNKS]]

    place = pltpu.VMEM((2, 2, 3 * rows, HD), jnp.bfloat16)
    work = [
        pltpu.SemaphoreType.DMA((2, 2, 3)), place, place, place,
        pltpu.VMEM((rows, features), jnp.bfloat16),
        pltpu.VMEM((2 * rows, HD), jnp.float32),
    ]
    partial = pltpu.HBM((rows, HD), jnp.float32)
    lanes = HD // 2 + TILE
    sent_back = jax.ShapeDtypeStruct((lanes, rows), jnp.bfloat16)

    def on_videos_across(kernel, name, when, boxes, outs, others=(), scratch=()):
        places = [0]
        for x in boxes:
            places.append(places[-1] + x.shape[0])
        return call(
            kernel(tuple(places[:-1])), name, 32, when,
            (in_hbm(q_rot), in_hbm(k_rot), in_hbm(v), w_both, *[in_hbm(x) for x in others], *boxes),
            [hbm] * 3 + [vmem] + [hbm] * (len(others) + len(boxes)),
            outs, jax.tree.map(lambda _: vmem, outs),
            [box_scratch(places[-1]), pltpu.SemaphoreType.DMA((len(boxes),)), *work, *scratch],
        )

    def early_on(at, name, when, boxes):
        return on_videos_across(
            lambda places: functools.partial(early_kernel, places, at), name, when, boxes,
            partial,
        )

    early = early_on(PASS, "videos_across_early", when_early, passed[:EARLY_CHUNKS])
    when_direct, early, passed[2] = tie((scalars, early, passed[2]))
    direct_z = early_on(DIRECT, "videos_across_direct", when_direct, got)

    pieces = jnp.maximum(scalars[MOST] - padded - MORE + EXTRA - 1, 0) // EXTRA
    pieces, direct_z = tie((pieces, direct_z))

    def one_more(i, arrived):
        piece = lax.dynamic_slice_in_dim(more, i * EXTRA, EXTRA, 0)
        piece = lax.ppermute(piece, "req", pairs)
        return lax.dynamic_update_slice_in_dim(arrived, piece, i * EXTRA, 0)

    arrived = lax.fori_loop(0, pieces, one_more, arriving)
    before = EARLY_CHUNKS - 1
    offsets = (-chunk * before, chunk * (CHUNKS - before))
    own, to_beyond, to_direct = on_videos_across(
        lambda places: functools.partial(last_kernel, places, offsets), "videos_across_last", scalars,
        [*passed[before:], *got, arrived],
        (jax.ShapeDtypeStruct((lanes, rows), jnp.float32), sent_back, sent_back),
        (early, direct_z, inner_a, inner_b),
        (pltpu.VMEM((4, rows, HD), jnp.float32), pltpu.SemaphoreType.DMA((4,))),
    )
    back_direct = lax.ppermute(to_direct, "req", pairs)
    beyond = [(i, i + 1) for i in range(1, count - 1, 2)] + [(i + 1, i) for i in range(1, count - 1, 2)]
    back_beyond = lax.ppermute(to_beyond, "req", beyond)
    total = own + back_direct.astype(jnp.float32) + back_beyond.astype(jnp.float32)
    values = HD // 2
    squares = total[values : values + 1] + total[values + 1 : values + 2]
    velocity = total[:values] * lax.rsqrt(squares / features + 1e-06) + shift[:, :1]

    width = latents.shape[1]
    mine = lax.dynamic_slice_in_dim(velocity, parity * width, width, 0)
    theirs = lax.dynamic_slice_in_dim(velocity, (1 - parity) * width, width, 0)
    partner = lax.ppermute(theirs, "cfg", [(0, 1), (1, 0)])
    conditional = jnp.where(parity == 0, mine, partner)
    unconditional = jnp.where(parity == 0, partner, mine)
    guided = unconditional + guide_scale[0] * (conditional - unconditional)
    return (latents.T + step_of_row[None, :] * guided).T


def solution(mesh):
    in_specs = (
        P("cfg", "req", None), P("cfg", "req", None), P("cfg", "req", None),
        P(None, "req"), P("req", "cfg"), P(), P(), P(), P(), P(),
    )
    return jax.shard_map(
        per_device, mesh=mesh, in_specs=in_specs, out_specs=P("req", "cfg"), check_vma=False
    )
```

```python
import functools
import math

import jax
import jax.numpy as jnp
import numpy
from jax import lax
from jax.experimental import pallas as pl
from jax.experimental.pallas import tpu as pltpu
from jax.sharding import PartitionSpec as P

HD = 128
TILE = 16
BLK = 128
CHUNKS = 4
MORE = 48
EXTRA = 16
EARLY_CHUNKS = 2
rope_theta = 10000.0
NEG = -1e30
SCALE2 = math.log2(math.e) / math.sqrt(HD)

PASS, DIRECT = 0, 16
LB, RB, LROWS, RROWS, HEAD0, KEEP, EARLY, SOURCE = range(8)
OWN_FROM, OWN_TO, OWN, FAR_TO, FAR, SIDE = range(8, 14)
SEND = 32
ROW, TILES, FIRST, HEADS = range(4)
MOST, INNER_FROM, INNER_TO = 40, 41, 42
SCALARS = 48
MIB = 1024 * 1024


def sizes(rows, heads):
    tiles = rows // TILE
    cap = max(
        min(max(a * n, (tiles + 1 - a) * (heads - n)) for n in range(heads + 1))
        for a in range(1, tiles + 1)
    )
    padded = -(-cap // TILE) * TILE
    return cap, padded, 2 * padded


def pieces_of(padded):
    first = padded * 3 // 10
    rest = (padded - first) // (CHUNKS - 1)
    return (first, padded - first - rest * (CHUNKS - 2), *[rest] * (CHUNKS - 2))


def angles(positions):
    pair_total = HD // 2
    side_pairs = HD // 6
    time_pairs = pair_total - 2 * side_pairs
    column = jnp.arange(HD, dtype=jnp.int32) // 2
    in_time = column < time_pairs
    in_height = (column >= time_pairs) & (column < time_pairs + side_pairs)
    in_width = column >= time_pairs + side_pairs
    local_index = jnp.where(
        in_time, column, jnp.where(in_height, column - time_pairs, column - time_pairs - side_pairs)
    )
    axis_pairs = jnp.where(in_time, time_pairs, side_pairs)
    frequency = jnp.exp(
        -(local_index.astype(jnp.float32) / axis_pairs.astype(jnp.float32)) * math.log(rope_theta)
    )
    selector = jnp.stack([in_time, in_height, in_width]).astype(jnp.float32) * frequency[None, :]
    placed = positions.astype(jnp.float32)
    return (
        placed[0][:, None] * selector[0][None, :]
        + placed[1][:, None] * selector[1][None, :]
        + placed[2][:, None] * selector[2][None, :]
    )


def plan_kernel(rows, heads, count, lengths, out, ls, rs, split, least):
    cap, padded, _ = sizes(rows, heads)
    here = lax.axis_index("req")
    shift = rows.bit_length() - 1

    def clear(b, carry):
        ls[b] = 0
        rs[b] = 0
        return carry

    lax.fori_loop(0, count + 8, clear, 0)

    def one_video(v, start):
        end = start + lengths[v]
        b = lax.shift_right_logical(end - 1, shift) if rows == 1 << shift else lax.div(end - 1, rows)
        at = b * rows

        @pl.when(start < at)
        def _():
            ls[b] = at - start
            rs[b] = end - at

        return end

    lax.fori_loop(0, lengths.shape[0], one_video, 0)
    budget = 3.0 * lax.broadcasted_iota(jnp.int32, (8, 128), 1).astype(jnp.float32)
    split[...] = jnp.zeros_like(split)

    def tiles_of(x):
        return lax.shift_right_logical(x + TILE - 1, 4)

    def eight(b):
        return pl.ds(pl.multiple_of(b * 8, 8), 8)

    def per_tile(x, tiles):
        return jnp.floor((x + 0.5) * (1.0 / jnp.maximum(tiles, 1.0)))

    def facts(b):
        direct = lax.rem(b, 2).astype(jnp.float32)
        lt, rt = (jnp.full((8, 128), tiles_of(x[b]).astype(jnp.float32)) for x in (ls, rs))
        return lt, rt, padded + direct * 1e6

    def five_at_a_time(step, carry):
        def body(i, carry):
            for u in range(5):
                carry = step(5 * i + u, carry)
            return carry

        return lax.fori_loop(0, -(-(count - 1) // 5), body, carry)

    def from_right(i, load):
        b = -(-(count - 1) // 5) * 5 - i
        lt, rt, limit = facts(b)
        room = jnp.minimum(budget - load, limit)
        n = jnp.where(rt > 0.0, jnp.maximum(heads - per_tile(room, rt), 0.0), 0.0)
        least[eight(b)] = jnp.where(room >= 0.0, n, 1e6)
        return lt * n

    def from_left(i, carry):
        load, ok = carry
        b = i + 1
        lt, rt, limit = facts(b)
        room = jnp.minimum(budget - load, limit)
        most = jnp.where(lt > 0.0, jnp.minimum(per_tile(room, lt), float(heads)), 0.0)
        low = least[eight(b)]
        even = jnp.floor(heads * rt / jnp.maximum(lt + rt, 1.0) + 0.5)
        n = jnp.minimum(most, jnp.maximum(low, even))
        split[eight(b)] = n
        return rt * (heads - n), jnp.where((room >= 0.0) & (low <= most), ok, 0.0)

    zero = jnp.zeros((8, 128), jnp.float32)
    five_at_a_time(from_right, zero)
    load, ok = five_at_a_time(from_left, (zero, zero + 1.0))
    ok = jnp.where(load <= budget, ok, 0.0)
    most = jnp.min(jnp.where((ok > 0.0) & (budget >= (padded + MORE) // 3 * 3), budget, 1e9))
    out[MOST] = most.astype(jnp.int32)

    def head_split(b):
        n = split[eight(b)]
        return jnp.max(jnp.where(budget == most, n, 0.0)).astype(jnp.int32)

    even = lax.rem(here, 2) == 0
    beyond = jnp.where(even, here + 2, here - 1)
    n_left, n_right, n_beyond = head_split(here), head_split(here + 1), head_split(beyond)
    partner_passes = jnp.where(
        even,
        tiles_of(ls[beyond]) * n_beyond,
        tiles_of(rs[beyond]) * (heads - n_beyond),
    )
    for side, b, n in ((0, here, n_left), (1, here + 1, n_right)):
        direct = jnp.logical_not(even) if side == 0 else even
        at = jnp.where(direct, DIRECT, PASS)
        lt, rt = tiles_of(ls[b]), tiles_of(rs[b])
        none = jnp.where(lt > 0, 0, heads)
        keep = n if side == 0 else jnp.maximum(heads - n - none, 0)
        far = lt if side == 0 else rt
        out[at + LB], out[at + RB] = lt, rt
        out[at + LROWS], out[at + RROWS] = ls[b], rs[b]
        out[at + HEAD0] = 0 if side == 0 else n
        out[at + KEEP] = keep
        source = jnp.where(direct, partner_passes, 0)
        there = jnp.where(direct, padded + MORE, sum(pieces_of(padded)[:EARLY_CHUNKS])) - source
        out[at + EARLY] = jnp.minimum(keep, lax.div(jnp.maximum(there, 0), jnp.maximum(far, 1)))
        out[at + SOURCE] = source
        out[at + OWN_FROM] = 0 if side == 0 else rows // TILE - lt
        out[at + OWN_TO] = lt if side == 0 else 0
        out[at + OWN] = rt if side == 0 else lt
        out[at + FAR_TO] = 0 if side == 0 else lt
        out[at + FAR] = far
        out[at + SIDE] = side
        to = SEND + jnp.where(direct, 4, 0)
        out[to + ROW] = 0 if side == 0 else rows - TILE * lt
        out[to + TILES] = rt if side == 0 else lt
        out[to + FIRST] = n if side == 0 else 0
        out[to + HEADS] = jnp.maximum(heads - n - none, 0) if side == 0 else n
    out[INNER_FROM] = rs[here]
    out[INNER_TO] = rows - ls[here + 1]


def in_groups(low, high, step):
    count = high - low

    def run(group, times):
        def body(i, carry):
            step(jnp.minimum(low + group * i, high - group), group)
            return carry

        lax.fori_loop(0, times, body, 0)

    run(8, jnp.where(count >= 8, lax.shift_right_logical(count + 7, 3), 0))
    run(2, jnp.where((count >= 2) & (count < 8), lax.shift_right_logical(count + 1, 1), 0))
    run(1, jnp.where(count == 1, 1, 0))


def lanes_of(h):
    return pl.ds(pl.multiple_of(h * HD, HD), HD)


def rows_of(t, group):
    return pl.ds(pl.multiple_of(t * TILE, TILE), group * TILE)


def turn(x, cosine, sine):
    wide = x.astype(jnp.float32)
    even = lax.rem(lax.broadcasted_iota(jnp.int32, wide.shape, 1), 2) == 0
    swapped = jnp.where(even, pltpu.roll(wide, HD - 1, 1), pltpu.roll(wide, 1, 1))
    return (wide * cosine + swapped * sine).astype(jnp.bfloat16)


def pack(scal, low, high, box, heads, get):
    base = 0
    for what in (SEND, SEND + 4):
        first_tile = lax.shift_right_logical(scal[what + ROW], 4)
        tiles, first, count = scal[what + TILES], scal[what + FIRST], scal[what + HEADS]

        def one_head(i, carry):
            start = base + (pl.program_id(0) * heads + i - first) * tiles
            begin = jnp.clip(low - start, 0, tiles)
            end = jnp.clip(high - start, 0, tiles)
            lanes = lanes_of(i)

            def step(t, group):
                q, k, v = get(rows_of(first_tile + t, group), lanes)
                item = pl.ds(start + t - low, group)
                box[item, 0:TILE] = q.reshape(group, TILE, HD)
                box[item, TILE : 2 * TILE] = k.reshape(group, TILE, HD)
                box[item, 2 * TILE : 3 * TILE] = v.reshape(group, TILE, HD)

            in_groups(begin, end, step)
            return carry

        before = first - pl.program_id(0) * heads
        lax.fori_loop(
            jnp.clip(before, 0, heads), jnp.clip(before + count, 0, heads), one_head, 0
        )
        base = base + tiles * count


def send_off(box, outs, sems):
    @pl.when(pl.program_id(0) == pl.num_programs(0) - 1)
    def _():
        at, copies = 0, []
        for i, out in enumerate(outs):
            copies.append(pltpu.make_async_copy(box.at[pl.ds(at, out.shape[0])], out, sems.at[i]))
            at += out.shape[0]
        for copy in copies:
            copy.start()
        for copy in copies:
            copy.wait()


def first_kernel(scal, q_hbm, k_hbm, v_hbm, cos_ref, sin_ref, box, qs, ks, vs, sems):
    limit = box.shape[0]
    ahead = qs.shape[0] - 1

    def heads_in(what, base):
        tiles = jnp.maximum(scal[what + TILES], 1)
        taken = lax.div(jnp.maximum(limit - base, 0) + tiles - 1, tiles)
        return jnp.minimum(scal[what + HEADS], taken)

    passed = scal[SEND + TILES] * scal[SEND + HEADS]
    count_pass = heads_in(SEND, 0)
    count = count_pass + heads_in(SEND + 4, passed)

    def entry(w):
        direct = w >= count_pass
        what = jnp.where(direct, SEND + 4, SEND)
        slot = w - jnp.where(direct, count_pass, 0)
        tiles = scal[what + TILES]
        start = jnp.where(direct, passed, 0) + slot * tiles
        return scal[what + FIRST] + slot, scal[what + ROW], tiles, start

    rows = cos_ref.shape[0]

    def each_copy(w, act):
        at = lax.rem(w, ahead + 1)
        head, row, tiles, _ = entry(w)
        few = tiles * TILE <= BLK
        block = pl.ds(pl.multiple_of(jnp.minimum(row, rows - BLK), TILE), BLK)
        for need, some in ((few, block), (jnp.logical_not(few), pl.ds(0, rows))):

            @pl.when(need)
            def _(some=some):
                for x, (source, place) in enumerate(((q_hbm, qs), (k_hbm, ks), (v_hbm, vs))):
                    act(pltpu.make_async_copy(
                        source.at[some, lanes_of(head)], place.at[at, some, :], sems.at[at, x]
                    ))

    for w in range(ahead):

        @pl.when(w < count)
        def _(w=w):
            each_copy(w, lambda copy: copy.start())

    def one_head(w, carry):
        @pl.when(w + ahead < count)
        def _():
            each_copy(w + ahead, lambda copy: copy.start())

        each_copy(w, lambda copy: copy.wait())
        at = lax.rem(w, ahead + 1)
        _, row, tiles, start = entry(w)
        first_tile = lax.shift_right_logical(row, 4)

        def step(t, group):
            source = rows_of(first_tile + t, group)
            cosine, sine = cos_ref[source, :], sin_ref[source, :]
            item = pl.ds(start + t, group)
            q, k = turn(qs[at, source, :], cosine, sine), turn(ks[at, source, :], cosine, sine)
            box[item, 0:TILE] = q.reshape(group, TILE, HD)
            box[item, TILE : 2 * TILE] = k.reshape(group, TILE, HD)
            box[item, 2 * TILE : 3 * TILE] = vs[at, source, :].reshape(group, TILE, HD)

        in_groups(0, jnp.clip(limit - start, 0, tiles), step)
        return carry

    lax.fori_loop(0, count, one_head, 0)


def second_kernel(
    low, scal, q_ref, k_ref, v_ref, cos_ref, sin_ref, swap_ref, wt_ref, mod_ref, qr_ref, kr_ref, w_ref, shift_ref, *rest
):
    outs, box, sems = rest[:-3], rest[-2], rest[-1]
    rows = q_ref.shape[0]
    heads = q_ref.shape[1] // HD
    wide = swap_ref.shape[0]

    @pl.when(pl.program_id(0) == 0)
    def _():
        w = wt_ref[...].astype(jnp.float32)
        scaled = w * (1.0 + mod_ref[1:2, :])
        high = scaled.astype(jnp.bfloat16)
        low = (scaled - high.astype(jnp.float32)).astype(jnp.bfloat16)
        w_ref[...] = jnp.concatenate([high, low], axis=0)
        shift = jnp.sum(w * mod_ref[0:1, :], axis=1, keepdims=True)
        shift_ref[...] = jnp.broadcast_to(shift, shift_ref.shape)

    for source, to in ((q_ref, qr_ref), (k_ref, kr_ref)):
        for h in range(0, heads, wide // HD):
            for j in range(rows // BLK):
                at = slice(j * BLK, (j + 1) * BLK)
                x = source[at, h * HD : h * HD + wide]
                swapped = jnp.dot(x, swap_ref[: x.shape[1], : x.shape[1]], preferred_element_type=jnp.float32)
                for i in range(x.shape[1] // HD):
                    lanes = slice(i * HD, (i + 1) * HD)
                    to[at, (h + i) * HD : (h + i + 1) * HD] = (
                        x[:, lanes].astype(jnp.float32) * cos_ref[at, :] + swapped[:, lanes] * sin_ref[at, :]
                    ).astype(jnp.bfloat16)

    def get(rows, lanes):
        return qr_ref[rows, lanes], kr_ref[rows, lanes], v_ref[rows, lanes]

    pack(scal, low, low + box.shape[0], box, heads, get)
    send_off(box, outs, sems)


def dot_t(a, b):
    return lax.dot_general(a, b, (((1,), (1,)), ((), ())), preferred_element_type=jnp.float32)


def attend_rows(q, k, v_ones, masked):
    s = masked(dot_t(q, k))
    top = jnp.max(s, axis=1, keepdims=True)
    weight = jnp.exp2(s * SCALE2 - top * SCALE2).astype(jnp.bfloat16)
    both = jnp.dot(weight, v_ones, preferred_element_type=jnp.float32)
    return (both[:, :HD] / both[:, HD:]).astype(jnp.bfloat16)


def projected(o_ref, w_ref, out_ref, rows):
    for j in range(rows // BLK):
        at = slice(j * BLK, (j + 1) * BLK)
        z = dot_t(o_ref[at, :], w_ref[...])
        z = z + pltpu.roll(z, HD // 2, 1)
        lane = lax.broadcasted_iota(jnp.int32, z.shape, 1)
        squares = jnp.zeros(z.shape, jnp.float32)
        for h in range(o_ref.shape[1] // HD):
            wide = o_ref[at, h * HD : (h + 1) * HD].astype(jnp.float32)
            squares = squares + wide * wide
        total = jnp.sum(squares, axis=1, keepdims=True)
        out_ref[at, :] = jnp.where(lane < HD // 2, z, jnp.where(lane == HD // 2, total, 0.0))


def inner_kernel(scal, q_ref, k_ref, v_ref, w_ref, qv_ref, kv_ref, out_ref, o_ref):
    g = pl.program_id(0)
    rows, width = q_ref.shape
    ones = jnp.ones((rows, HD), jnp.bfloat16)
    for j in range(rows // BLK):
        at = pl.ds(j * BLK, BLK)
        same = qv_ref[at, :] == kv_ref[...]
        for i in range(width // HD):
            lanes = slice(i * HD, (i + 1) * HD)
            v_ones = jnp.concatenate([v_ref[:, lanes], ones], axis=1)
            o_ref[at, pl.ds(pl.multiple_of(g * width + i * HD, HD), HD)] = attend_rows(
                q_ref[at, lanes], k_ref[:, lanes], v_ones, lambda s: jnp.where(same, s, NEG)
            )

    @pl.when(g == pl.num_programs(0) - 1)
    def _():
        projected(o_ref, w_ref, out_ref, rows)


def across(scal, at, offset, low, high, sources, items, w_ref, own_sems, places, o_ref, zz):
    rows = zz.shape[0] // 2
    left, right = scal[at + LB], scal[at + RB]
    lead = left * TILE - scal[at + LROWS]
    end = left * TILE + scal[at + RROWS]
    blocks = jnp.minimum(lax.div((left + right) * TILE + BLK - 1, BLK), rows // BLK)
    own_at = jnp.where(scal[at + SIDE] == 0, rows, 0) + left * TILE
    pairs = lax.shift_right_logical(high - low + 1, 1)

    def heads_of(i):
        return [jnp.minimum(low + 2 * i + u, high - 1) for u in range(2)]

    def own_copies(i, act):
        slot = lax.rem(i, 2)
        few = scal[at + OWN] * TILE <= rows // 2
        begin = jnp.where(scal[at + SIDE] == 0, 0, rows // 2)
        for need, begin, size in ((few, begin, rows // 2), (jnp.logical_not(few), 0, rows)):

            @pl.when(need)
            def _(begin=begin, size=size):
                source_rows = pl.ds(pl.multiple_of(begin, TILE), size)
                to = pl.ds(pl.multiple_of(own_at + begin, TILE), size)
                for u, s in enumerate(heads_of(i)):
                    lanes = lanes_of(scal[at + HEAD0] + s)
                    for x, (source, place) in enumerate(zip(sources, places)):
                        act(pltpu.make_async_copy(
                            source.at[source_rows, lanes], place.at[slot, u, to, :], own_sems.at[slot, u, x]
                        ))

    @pl.when(pairs > 0)
    def _():
        own_copies(0, lambda copy: copy.start())

    def two_heads(n, i, carry):
        slot = lax.rem(i, 2)

        @pl.when(i + 1 < pairs)
        def _():
            own_copies(i + 1, lambda copy: copy.start())

        heads = heads_of(i)

        def foreign(t, group):
            to = rows_of(rows // TILE + scal[at + FAR_TO] + t, group)
            for u, s in enumerate(heads):
                item = pl.ds(scal[at + SOURCE] + offset + s * scal[at + FAR] + t, group)
                for x, place in enumerate(places):
                    part = items[item, x * TILE : (x + 1) * TILE]
                    place[slot, u, to, :] = part.reshape(group * TILE, HD)

        in_groups(0, scal[at + FAR], foreign)
        own_copies(i, lambda copy: copy.wait())
        width = n * BLK
        if width == rows:

            @pl.when((left + right) * TILE > rows)
            def _():
                row = lax.broadcasted_iota(jnp.int32, (TILE, HD), 0)
                for place in places:
                    for u in range(2):
                        first = place[slot, u, rows : rows + TILE, :]
                        last = place[slot, u, 2 * rows : 2 * rows + TILE, :]
                        place[slot, u, rows : rows + TILE, :] = jnp.where(row < lead, last, first)

        place = lax.broadcasted_iota(jnp.int32, (1, width), 1)
        valid = ((place >= lead) & (place < end)) | (place + rows < end)
        bias = jnp.where(valid, 0.0, NEG)
        ones = jnp.ones((width, HD), jnp.bfloat16)
        qs, ks, vs = places
        whole = slice(rows, rows + width)
        for j in range(n):
            mine = slice(rows + j * BLK, rows + (j + 1) * BLK)
            for u, s in enumerate(heads):
                v_ones = jnp.concatenate([vs[slot, u, whole, :], ones], axis=1)
                o_ref[j * BLK : (j + 1) * BLK, lanes_of(scal[at + HEAD0] + s)] = attend_rows(
                    qs[slot, u, mine, :], ks[slot, u, whole, :], v_ones, lambda x: x + bias
                )
        return carry

    for n in range(1, rows // BLK + 1):

        @pl.when((blocks == n) & (pairs > 0))
        def _(n=n):
            o_ref[0 : n * BLK, :] = jnp.zeros((n * BLK, o_ref.shape[1]), o_ref.dtype)
            lax.fori_loop(0, pairs, functools.partial(two_heads, n), 0)
            projected(o_ref, w_ref, zz, n * BLK)
            zz[rows : 2 * rows, :] = zz[0:rows, :]

    @pl.when(pairs <= 0)
    def _():
        zz[...] = jnp.zeros_like(zz)

    return zz[pl.ds(pl.multiple_of(left * TILE, TILE), rows), :]


def fetch(scal, at, offset, low, high, places, boxes, items, sems):
    begin = scal[at + SOURCE] + offset + low * scal[at + FAR]
    end = scal[at + SOURCE] + offset + high * scal[at + FAR]
    return [
        (
            pltpu.make_async_copy(box, items.at[pl.ds(place, box.shape[0])], sems.at[i]),
            (high > low) & (begin < place + box.shape[0]) & (end > place),
        )
        for i, (place, box) in enumerate(zip(places, boxes))
    ]


def clear(places, rows):
    for place in places:
        for slot in range(2):
            for u in range(2):
                place[slot, u, rows : 2 * rows + TILE, :] = jnp.zeros((rows + TILE, HD), place.dtype)


def of_boundary(scal, at, shape, mine):
    row = lax.broadcasted_iota(jnp.int32, shape, 0)
    tail = jnp.where(row >= shape[0] - scal[at + LROWS], 1, 0)
    head = jnp.where(row < scal[at + RROWS], 1, 0)
    right_is_mine = (scal[at + SIDE] == 0) == mine
    return jnp.where(right_is_mine, head, tail) == 1


def send_back(scal, at, z, back_ref):
    lane = lax.broadcasted_iota(jnp.int32, z.shape, 1)
    back = jnp.where(of_boundary(scal, at, z.shape, False), z, 0.0)
    high = back.astype(jnp.bfloat16).astype(jnp.float32)
    both = jnp.where(lane == HD // 2 + 1, pltpu.roll(back - high, 1, 1), high)
    back_ref[...] = both.T[: back_ref.shape[0]].astype(jnp.bfloat16)


def early_kernel(places, at, scal, q_hbm, k_hbm, v_hbm, w_ref, *rest):
    boxes, (out_ref, items, sems, own_sems, qs, ks, vs, o_ref, zz) = rest[: len(places)], rest[len(places) :]
    high = scal[at + EARLY]
    copies = fetch(scal, at, 0, 0, high, places, boxes, items, sems)
    for copy, need in copies:
        pl.when(need)(copy.start)
    clear((qs, ks, vs), zz.shape[0] // 2)
    for copy, need in copies:
        pl.when(need)(copy.wait)
    out_ref[...] = across(
        scal, at, 0, 0, high, (q_hbm, k_hbm, v_hbm), items, w_ref, own_sems, (qs, ks, vs), o_ref, zz
    )


def last_kernel(places, offsets, scal, q_hbm, k_hbm, v_hbm, w_ref, *rest):
    partials, rest = rest[:4], rest[4:]
    boxes, rest = rest[: len(places)], rest[len(places) :]
    own_ref, pass_back_ref, direct_back_ref, items, sems, own_sems, qs, ks, vs, o_ref, zz, sums, sum_sems = rest
    sum_copies = [
        pltpu.make_async_copy(part, sums.at[i], sum_sems.at[i]) for i, part in enumerate(partials)
    ]
    for copy in sum_copies:
        copy.start()
    clear((qs, ks, vs), zz.shape[0] // 2)

    def remaining(at, offset):
        low, high = scal[at + EARLY], scal[at + KEEP]
        copies = fetch(scal, at, offset, low, high, places, boxes, items, sems)
        for copy, need in copies:
            pl.when(need)(copy.start)
        for copy, need in copies:
            pl.when(need)(copy.wait)
        return across(
            scal, at, offset, low, high, (q_hbm, k_hbm, v_hbm), items, w_ref, own_sems, (qs, ks, vs), o_ref, zz
        )

    passed_z = remaining(PASS, offsets[0])
    for copy in sum_copies:
        copy.wait()
    passed_z = passed_z + sums[0]
    send_back(scal, PASS, passed_z, pass_back_ref)
    own = jnp.where(of_boundary(scal, PASS, passed_z.shape, True), passed_z, sums[2] + sums[3])
    direct_z = sums[1] + remaining(DIRECT, offsets[1])
    send_back(scal, DIRECT, direct_z, direct_back_ref)
    own = jnp.where(of_boundary(scal, DIRECT, own.shape, True), direct_z, own)
    own_ref[...] = own.T[: own_ref.shape[0]]


def step_rows(video_ids, step_sizes):
    chosen = video_ids[:, None] == jnp.arange(step_sizes.shape[0], dtype=jnp.int32)[None, :]
    return jnp.sum(jnp.where(chosen, step_sizes[None, :], 0.0), axis=1)


def call(kernel, name, mib, scalars, operands, in_specs, outs, out_specs, scratch, grid=()):
    return pl.pallas_call(
        kernel,
        out_shape=outs,
        grid_spec=pltpu.PrefetchScalarGridSpec(
            num_scalar_prefetch=1, grid=grid, in_specs=in_specs, out_specs=out_specs,
            scratch_shapes=scratch,
        ),
        compiler_params=pltpu.CompilerParams(vmem_limit_bytes=mib * MIB),
        cost_estimate=pl.CostEstimate(flops=1, bytes_accessed=1, transcendentals=0),
        name=name,
    )(scalars, *operands)


def per_device(
    query_rows, key_rows, value_rows, positions, latents, w_head, modulation,
    guide_scale, step_sizes, lengths,
):
    rows, features = query_rows.shape[1], query_rows.shape[2]
    heads = features // HD
    count = lax.axis_size("req")
    here = lax.axis_index("req")
    first_row = here * rows
    _, padded, room = sizes(rows, heads)
    sizes_passed = pieces_of(padded)
    late_sizes = (*sizes_passed[1:], MORE, room - padded - MORE)

    angle = angles(positions)
    odd = (jnp.arange(HD, dtype=jnp.int32) % 2).astype(jnp.float32)
    cosine = jnp.cos(angle)
    sine = jnp.sin(angle) * (2.0 * odd - 1.0)[None, :]

    smem = pl.BlockSpec(memory_space=pltpu.SMEM)
    vmem = pl.BlockSpec(memory_space=pltpu.VMEM)
    hbm = pl.BlockSpec(memory_space=pl.ANY)
    parity = lax.axis_index("cfg")
    tie = lax.optimization_barrier
    scalars = pl.pallas_call(
        functools.partial(plan_kernel, rows, heads, count),
        out_shape=jax.ShapeDtypeStruct((SCALARS,), jnp.int32),
        in_specs=[smem],
        out_specs=smem,
        scratch_shapes=[
            pltpu.SMEM((count + 8,), jnp.int32),
            pltpu.SMEM((count + 8,), jnp.int32),
            pltpu.VMEM(((count + 8) * 8, 128), jnp.float32),
            pltpu.VMEM(((count + 8) * 8, 128), jnp.float32),
        ],
        name="plan",
    )(lengths)

    def in_hbm(x):
        return pltpu.with_memory_space_constraint(x, pltpu.HBM)

    q, k, v = query_rows[0], key_rows[0], value_rows[0]

    def box(items):
        return jax.ShapeDtypeStruct((items, 3 * TILE, HD), jnp.bfloat16)

    def box_scratch(items):
        return pltpu.VMEM((items, 3 * TILE, HD), jnp.bfloat16)

    group = next(n for n in (5, 4, 3, 2, 1) if heads % n == 0)
    steps = heads // group
    head_block = pl.BlockSpec((rows, group * HD), lambda g, s: (0, g))
    table = pl.BlockSpec((rows, HD), lambda g, s: (0, 0))
    first = call(
        first_kernel, "pack_first", 16, scalars, (in_hbm(q), in_hbm(k), in_hbm(v), cosine, sine),
        [hbm] * 3 + [vmem] * 2, (box(sizes_passed[0]),), (vmem,),
        [*[pltpu.VMEM((4, rows, HD), jnp.bfloat16)] * 3, pltpu.SemaphoreType.DMA((4, 3))],
    )
    pairs = [(i, i ^ 1) for i in range(count)]
    onward = [(i, i + 2) for i in range(0, count - 2, 2)] + [(i + 2, i) for i in range(1, count - 2, 2)]
    got = [lax.ppermute(first[0], "req", pairs)]

    after_first, _ = tie((scalars, first[0]))
    swap = jnp.asarray(numpy.eye(2 * HD)[numpy.arange(2 * HD) ^ 1], jnp.bfloat16)
    q_rot, k_rot, w_both, shift, *second = call(
        functools.partial(second_kernel, sizes_passed[0]), "turn_and_pack_rest", 32, after_first,
        (in_hbm(q), in_hbm(k), in_hbm(v), cosine, sine, swap, w_head.T, modulation),
        [head_block] * 3 + [table] * 2 + [vmem] * 3,
        (pltpu.HBM(q.shape, q.dtype), pltpu.HBM(k.shape, k.dtype),
         jax.ShapeDtypeStruct((HD, features), jnp.bfloat16),
         jax.ShapeDtypeStruct((HD // 2, HD), jnp.float32),
         *[box(n) for n in late_sizes], box(late_sizes[-1])),
        (head_block, head_block, vmem, vmem, *[hbm] * (len(late_sizes) + 1)),
        [box_scratch(sum(late_sizes)), pltpu.SemaphoreType.DMA((len(late_sizes),))], grid=(steps,),
    )
    got += [lax.ppermute(x, "req", pairs) for x in second[: CHUNKS - 1]]
    more, arriving = second[CHUNKS:]

    own_rows = first_row + jnp.arange(rows, dtype=jnp.int32)
    video = jnp.sum((jnp.cumsum(lengths)[None, :] <= own_rows[:, None]).astype(jnp.int32), axis=1)
    step_of_row = step_rows(video, step_sizes)

    def inner(when, first_step, step_count):
        block = pl.BlockSpec((rows, group * HD), lambda g, s: (0, g + first_step))
        width = step_count * group * HD
        return call(
            inner_kernel, "inner_videos", 20, when,
            (in_hbm(q_rot), in_hbm(k_rot), in_hbm(v), w_both, video[:, None], video[None, :]),
            [block] * 3 + [pl.BlockSpec((HD, width), lambda g, s: (0, first_step // step_count))] + [vmem] * 2, pltpu.HBM((rows, HD), jnp.float32), vmem,
            [pltpu.VMEM((rows, width), jnp.bfloat16)], grid=(step_count,),
        )

    got[1], second[CHUNKS - 1] = tie((got[1], second[CHUNKS - 1]))
    got.append(lax.ppermute(second[CHUNKS - 1], "req", pairs))
    when_a, got[0] = tie((scalars, got[0]))
    inner_a = inner(when_a, 0, steps // 2)
    got[1], inner_a = tie((got[1], inner_a))
    passed = [lax.ppermute(x, "req", onward) for x in got[:2]]
    when_b, passed[0], got[2], inner_a = tie((scalars, passed[0], got[2], inner_a))
    inner_b = inner(when_b, steps // 2, steps - steps // 2)
    got[3], inner_b = tie((got[3], inner_b))
    when_early, got[3] = tie((scalars, got[3]))
    passed += [lax.ppermute(x, "req", onward) for x in got[2:CHUNKS]]

    place = pltpu.VMEM((2, 2, 3 * rows, HD), jnp.bfloat16)
    work = [
        pltpu.SemaphoreType.DMA((2, 2, 3)), place, place, place,
        pltpu.VMEM((rows, features), jnp.bfloat16),
        pltpu.VMEM((2 * rows, HD), jnp.float32),
    ]
    partial = pltpu.HBM((rows, HD), jnp.float32)
    lanes = HD // 2 + TILE
    sent_back = jax.ShapeDtypeStruct((lanes, rows), jnp.bfloat16)

    def on_videos_across(kernel, name, when, boxes, outs, others=(), scratch=()):
        places = [0]
        for x in boxes:
            places.append(places[-1] + x.shape[0])
        return call(
            kernel(tuple(places[:-1])), name, 32, when,
            (in_hbm(q_rot), in_hbm(k_rot), in_hbm(v), w_both, *[in_hbm(x) for x in others], *boxes),
            [hbm] * 3 + [vmem] + [hbm] * (len(others) + len(boxes)),
            outs, jax.tree.map(lambda _: vmem, outs),
            [box_scratch(places[-1]), pltpu.SemaphoreType.DMA((len(boxes),)), *work, *scratch],
        )

    def early_on(at, name, when, boxes):
        return on_videos_across(
            lambda places: functools.partial(early_kernel, places, at), name, when, boxes,
            partial,
        )

    early = early_on(PASS, "videos_across_early", when_early, passed[:EARLY_CHUNKS])
    when_direct, early, passed[2] = tie((scalars, early, passed[2]))
    direct_z = early_on(DIRECT, "videos_across_direct", when_direct, got)

    pieces = jnp.maximum(scalars[MOST] - padded - MORE + EXTRA - 1, 0) // EXTRA
    pieces, direct_z = tie((pieces, direct_z))

    def one_more(i, arrived):
        piece = lax.dynamic_slice_in_dim(more, i * EXTRA, EXTRA, 0)
        piece = lax.ppermute(piece, "req", pairs)
        return lax.dynamic_update_slice_in_dim(arrived, piece, i * EXTRA, 0)

    arrived = lax.fori_loop(0, pieces, one_more, arriving)
    before = EARLY_CHUNKS - 1
    offsets = (-sum(sizes_passed[:before]), sum(sizes_passed[before:]))
    own, to_beyond, to_direct = on_videos_across(
        lambda places: functools.partial(last_kernel, places, offsets), "videos_across_last", scalars,
        [*passed[before:], *got, arrived],
        (jax.ShapeDtypeStruct((lanes, rows), jnp.float32), sent_back, sent_back),
        (early, direct_z, inner_a, inner_b),
        (pltpu.VMEM((4, rows, HD), jnp.float32), pltpu.SemaphoreType.DMA((4,))),
    )
    back_direct = lax.ppermute(to_direct, "req", pairs)
    beyond = [(i, i + 1) for i in range(1, count - 1, 2)] + [(i + 1, i) for i in range(1, count - 1, 2)]
    back_beyond = lax.ppermute(to_beyond, "req", beyond)
    total = own + back_direct.astype(jnp.float32) + back_beyond.astype(jnp.float32)
    values = HD // 2
    squares = total[values : values + 1] + total[values + 1 : values + 2]
    velocity = total[:values] * lax.rsqrt(squares / features + 1e-06) + shift[:, :1]

    width = latents.shape[1]
    mine = lax.dynamic_slice_in_dim(velocity, parity * width, width, 0)
    theirs = lax.dynamic_slice_in_dim(velocity, (1 - parity) * width, width, 0)
    partner = lax.ppermute(theirs, "cfg", [(0, 1), (1, 0)])
    conditional = jnp.where(parity == 0, mine, partner)
    unconditional = jnp.where(parity == 0, partner, mine)
    guided = unconditional + guide_scale[0] * (conditional - unconditional)
    return (latents.T + step_of_row[None, :] * guided).T


def solution(mesh):
    in_specs = (
        P("cfg", "req", None), P("cfg", "req", None), P("cfg", "req", None),
        P(None, "req"), P("req", "cfg"), P(), P(), P(), P(), P(),
    )
    return jax.shard_map(
        per_device, mesh=mesh, in_specs=in_specs, out_specs=P("req", "cfg"), check_vma=False
    )
```
